32 devices in a mesh: groups: 2 (over y), key: 4 (over z), shard: 2 (over x), lane: 2 (over core).
Axes of the slice: x: 2, y: 2, z: 4, core: 2. Of those that a mesh axis runs over, the one named last changes fastest.
Arguments:
- events: bfloat16 [8192, 256], P(('groups', 'key', 'shard'), 'lane'), parts along dimension 0, may hold values from -6 to 6
- event_weight: float32 [8192], P(('groups', 'key', 'shard')), parts along dimension 0, may hold values from 0.25 to 4
- route: int32 [8192, 1], P(('groups', 'key', 'shard')), parts along dimension 0, may hold values from 0 to 7; in each aligned block of 512 rows (0 to 511, 512 to 1023, ...) at most 128 rows name the same one
- bucket: int32 [8192], P(('groups', 'key', 'shard')), parts along dimension 0, may hold values from 0 to 4095
- segment: int32 [65536], P(('groups', 'key', 'shard')), parts along dimension 0, may hold values from 0 to 63, never falling along the last dimension, each value on 1 to 2048 neighbouring positions
- decay_rate: float32 [8], P('lane'), may hold values from 0.000390625 to 0.0029296875
Outputs:
- table: bfloat16 [65536, 256], P(('groups', 'key', 'shard'), 'lane'), parts along dimension 0
- event_features: bfloat16 [8192, 256], P(('groups', 'key', 'shard'), 'lane'), parts along dimension 0
The draws below stay inside these ranges and needn't reach their ends.
There are 2 independent parts, one for each index of `groups`. The reference program is written for one: setup_inputs(seed, part) draws one part's arguments, and reference() takes and returns one part's arrays. A program takes and returns all parts, laid end to end along the dimension named above; an argument that names none is the same for every part. Nothing has to cross between parts.
Inputs may be any that keep to these rules, and one draw needn't show every extreme that they name: `route`: among the rows of one device at most 128 name the same owner, a bound that some block reaches. `segment`: never falling along the slots; each user holds 1 to 2048 slots in a row, one exactly 2048.
All inputs are finite; a program needn't handle non-finite values.
Results may differ from the reference program's by a relative error of at most 0.0056.
Values may be sent and summed in bfloat16 or wider, within the bound.
No kernel may reach another device: no remote copies, remote signals or barrier semaphores. Data moves between devices by JAX's collectives and lax.ppermute only.
A program may use at most 64 MiB of HBM per device.

```python
import math
import jax
import jax.numpy as jnp
import numpy as np
from jax import lax

F = 256
ROWS = 512
SLOTS_DEV = 4096
OWNERS = 8
CAP = 128
EVENTS = 4096
SLOTS = 32768
WIN = 1024
SPAN = 2048
USERS = 64


def place_ends(array, stream_key, smallest, top_value):
    extent = array.shape
    index_at = [jax.random.randint(jax.random.fold_in(stream_key, axis), (), 0, extent[axis]) for axis in range(len(extent))]
    array = array.at[tuple(index_at)].set(smallest)
    longest = extent.index(max(extent))
    index_at[longest] = (index_at[longest] + 1) % extent[longest]
    return array.at[tuple(index_at)].set(top_value)


def steps_of(key, dims, pieces, smallest, top_value):
    def one(axis_at, blocks):
        steps = jax.random.uniform(jax.random.fold_in(jax.random.fold_in(key, 6), axis_at), (blocks,), jnp.float32, smallest / len(pieces), top_value / len(pieces))
        return jnp.repeat(jnp.exp(steps), dims[axis_at] // blocks).reshape((-1,) + (1,) * (len(dims) - axis_at - 1))

    factor_of = one(*pieces[0])
    for cut in pieces[1:]:
        factor_of = factor_of * one(*cut)
    return factor_of


def profile(amount, total, bound, skew):
    portions = [(1 << 20) // math.isqrt(rank ** skew) + 1 for rank in range(2, amount + 1)]
    spare, given = total - bound - (amount - 1), [1] * (amount - 1)
    while spare > 0:
        movable = [i for i in range(amount - 1) if given[i] < bound]
        mass, budget = sum([portions[i] for i in movable]), spare
        for i in movable:
            extra = min(bound - given[i], max(1, budget * portions[i] // mass), spare)
            given[i] = given[i] + extra
            spare = spare - extra
    return np.array([bound] + given)


def ragged_sizes(stream_key, amount, total, most, skew):
    if amount == 2:
        one = jax.random.randint(stream_key, (), max(1, total - most), min(most, total - 1) + 1)
        return jnp.stack([one, total - one])
    tallies = jnp.asarray(profile(amount, total, most, skew), jnp.int32)
    couples = (amount - 1) // 2
    donor, sink = tallies[1:1 + 2 * couples:2], tallies[2:2 + 2 * couples:2]
    slack = jnp.minimum(donor - 1, most - sink)
    moved = jax.random.randint(jax.random.fold_in(stream_key, 1), (couples,), 0, 1 << 20) % (slack + 1)
    tallies = tallies.at[1:1 + 2 * couples:2].set(donor - moved).at[2:2 + 2 * couples:2].set(sink + moved)
    return tallies[jax.random.permutation(jax.random.fold_in(stream_key, 2), amount)]


def routed_block(rng, own, number, rows, number_of, top, limit, slope):
    sequence = jax.random.permutation(rng, number_of)
    heavy_load, ordinary = load_shares(number_of, rows * top, limit, slope, True), load_shares(number_of, rows * top, limit, slope, False)
    places = jnp.arange(number_of)

    def named(lengths, offset_by):
        used = int((lengths > 0).sum())
        fixed = max(1, used // 4)
        moved = fixed + (places - fixed + offset_by * (used - fixed)) % max(1, number_of - fixed)
        return jnp.zeros((number_of,), jnp.int32).at[sequence[jnp.where(places < fixed, places, moved)]].set(jnp.asarray(lengths, jnp.int32))

    lengths = jnp.where(number % 4 == 0, named(heavy_load, number // 4), named(ordinary, number - number // 4 - 1))
    mixed = jax.random.permutation(jax.random.fold_in(own, 3), number_of)
    source_of, receiver = mixed[0:number_of // 2 * 2:2], mixed[1:number_of // 2 * 2:2]
    slack = jnp.minimum(lengths[source_of] - 1, limit - lengths[receiver]) // 2
    slack = jnp.where((source_of == sequence[0]) | (receiver == sequence[0]) | (lengths[receiver] == 0), 0, jnp.maximum(slack, 0))
    moved = jax.random.randint(jax.random.fold_in(own, 4), (number_of // 2,), 0, 1 << 20) % (slack + 1)
    lengths = lengths.at[source_of].add(-moved).at[receiver].add(moved)
    labels = jnp.searchsorted(jnp.cumsum(lengths), jnp.arange(rows * top), side="right").astype(jnp.int32)
    listing = labels.reshape(top, rows).T
    listing = listing[jax.random.permutation(jax.random.fold_in(own, 1), rows)]
    offset_by = jax.random.randint(jax.random.fold_in(own, 2), (rows, 1), 0, top)
    return jnp.take_along_axis(listing, (jnp.arange(top)[None, :] + offset_by) % top, axis=1)


def load_shares(count, total, reach, slope, full):
    portions = [(1 << 20) // math.isqrt(rank ** slope) + 1 for rank in range(1, count + 1)]
    largest = reach if full else min(reach, max(-(-total // count), total * portions[0] // sum(portions)))
    least = 1 if total - largest >= count - 1 else 0
    counts, spare = [largest] + [least] * (count - 1), total - largest - least * (count - 1)
    while spare > 0:
        candidates = [i for i in range(1, count) if counts[i] < largest] or [i for i in range(1, count) if counts[i] < reach]
        mass, budget = sum([portions[i] for i in candidates]), spare
        for i in candidates:
            addition = min(reach - counts[i], max(1, budget * portions[i] // mass), spare)
            counts[i] = counts[i] + addition
            spare = spare - addition
    return np.array(counts)


def gaussian(own_key, shape, width, limit, split=(), kind=jnp.bfloat16):
    array = width * jax.random.normal(own_key, shape, jnp.float32)
    if split:
        array = array * steps_of(own_key, shape, split, -0.22, 0.18)
    return jnp.clip(array, -limit, limit).astype(kind)


def setup_inputs(seed: int = 0, part: int = 0) -> dict:
    keys = jax.random.split(jax.random.key(seed), 7)
    part_keys = jax.random.split(jax.random.fold_in(keys[6], part), 7)
    events = gaussian(part_keys[0], (EVENTS, F), 1.0, 6.0, ((0, 8), (1, 2)))
    event_weight = jnp.clip(jnp.exp(math.log(4.0) - 2.7725887 * jax.random.uniform(part_keys[1], (EVENTS,), jnp.float32) ** steps_of(part_keys[1], (EVENTS,), ((0, 8),), -0.2, 0.2)), 0.25, 4.0)
    route_keys = jax.random.split(jax.random.fold_in(part_keys[2], 1), EVENTS // ROWS)
    route_turns = jax.random.permutation(jax.random.fold_in(part_keys[2], 3), EVENTS // ROWS)
    route = jax.vmap(lambda own, number: routed_block(jax.random.fold_in(part_keys[2], 2), own, number, ROWS, OWNERS, 1, CAP, 2))(route_keys, route_turns).reshape((EVENTS, 1))
    bucket = place_ends(jax.random.randint(part_keys[3], (EVENTS,), 0, SLOTS_DEV), jax.random.fold_in(part_keys[3], 1), 0, SLOTS_DEV - 1).astype(jnp.int32)
    segment = jnp.searchsorted(jnp.cumsum(ragged_sizes(part_keys[4], USERS, SLOTS, SPAN, 1)), jnp.arange(SLOTS), side="right").astype(jnp.int32)
    decay_rate = jnp.clip(jnp.exp(math.log(0.0029296875) - 2.014903 * jax.random.uniform(keys[5], (F // 32,), jnp.float32) ** steps_of(keys[5], (F // 32,), ((0, 2),), -0.2, 0.2)), 0.000390625, 0.0029296875)
    return dict(events=events, event_weight=event_weight, route=route, bucket=bucket, segment=segment, decay_rate=decay_rate)


def reference(events, event_weight, route, bucket, segment, decay_rate):
    weighted = (event_weight[:, None] * events.astype(jnp.float32)).astype(jnp.bfloat16)
    place = (route[:, 0] * SLOTS_DEV + bucket).astype(jnp.int32)
    summed = jax.ops.segment_sum(weighted.astype(jnp.float32), place, num_segments=SLOTS)
    summed_round = summed.astype(jnp.bfloat16)
    window = WIN
    block = min(512, SLOTS_DEV)
    span = block + window
    groups = decay_rate.shape[0]
    group_cols = F // groups
    padded = jnp.concatenate([jnp.zeros((window, F), jnp.bfloat16), summed_round], axis=0)
    marks = jnp.concatenate([jnp.full((window,), -1, jnp.int32), segment.astype(jnp.int32)])
    gap = jnp.arange(block, dtype=jnp.int32)[:, None] + window - jnp.arange(span, dtype=jnp.int32)[None, :]
    inside = (gap >= 0) & (gap <= window)
    gap_float = gap.astype(jnp.float32)

    def one_block(start):
        source = lax.dynamic_slice_in_dim(padded, start, span, 0)
        source_marks = lax.dynamic_slice_in_dim(marks, start, span, 0)
        query_marks = lax.dynamic_slice_in_dim(marks, start + window, block, 0)
        keep = inside & (query_marks[:, None] == source_marks[None, :])
        count = lax.optimization_barrier(jnp.sum(keep.astype(jnp.float32), axis=1))
        factor = jnp.where(keep[None], jnp.exp(-decay_rate[:, None, None] * gap_float[None]), jnp.float32(0.0)).astype(jnp.bfloat16)
        mixed = jnp.einsum('gim,mgc->igc', factor.astype(jnp.float32), source.astype(jnp.float32).reshape(span, groups, group_cols), precision=lax.Precision.HIGHEST)
        return (mixed.reshape(block, F) * lax.rsqrt(count)[:, None]).astype(jnp.bfloat16)
    starts = jnp.arange(SLOTS // block, dtype=jnp.int32) * block
    table = lax.map(one_block, starts).reshape(SLOTS, F)
    return (table, table[place])
```

```python
import functools
import jax
import jax.numpy as jnp
from jax import lax
from jax.experimental import pallas as pl
from jax.experimental.pallas import tpu as pltpu
from jax.sharding import PartitionSpec as P

LANES = 128
LOW = 7
MASK = 127
F32 = jnp.float32
BF16 = jnp.bfloat16
I32 = jnp.int32
FAR = 1e9
NT = (((1,), (1,)), ((), ()))


def dims(owners, rows, slots):
    chunks = rows // LANES
    users = 8 * owners
    user_rows = -(-users // LANES)
    code_rows = -(-(3 * chunks + 2 * user_rows) // 16) * 16
    span = min(owners, 8)
    return chunks, user_rows, code_rows, span


def iota(shape, axis):
    return lax.broadcasted_iota(I32, shape, axis)


def rate_row(rate_ref):
    groups = rate_ref.shape[0]
    lane = iota((1, LANES), 1)
    row = jnp.full((1, LANES), rate_ref[0], F32)
    for g in range(1, groups):
        row = jnp.where(lane >= g * (LANES // groups), rate_ref[g], row)
    return row


def send_kernel(owners, slots, rate_ref, events_ref, weight_ref, route_ref, bucket_ref, segment_ref, out_ref):
    rows = events_ref.shape[0]
    chunks, user_rows, code_rows, span = dims(owners, rows, slots)
    rate = rate_row(rate_ref)
    route = route_ref[...]
    bucket = bucket_ref[...]
    spot = (route & (span - 1)) * slots + bucket - span * slots // 2
    columns = jnp.concatenate([weight_ref[...], spot.astype(F32)], axis=0).T
    for r in range(chunks):
        part = pl.ds(r * LANES, LANES)
        weighted = (columns[:, r : r + 1] * events_ref[part, :].astype(F32)).astype(BF16)
        grown = weighted.astype(F32) * jnp.exp(columns[:, chunks + r : chunks + r + 1] * rate)
        out_ref[part, :] = grown.astype(BF16)
    ones = jnp.ones((8, LANES), BF16)
    high, low = [], []
    for u in range(user_rows):
        user = iota((LANES, LANES), 0) + u * LANES
        below = jnp.zeros((LANES, LANES), F32)
        for r in range(slots // LANES):
            below += jnp.where(segment_ref[r : r + 1, :] < user, F32(1), F32(0))
        count = lax.dot_general(ones, below.astype(BF16), NT, preferred_element_type=F32)[0:1].astype(I32)
        high.append(count >> LOW)
        low.append(count & MASK)
    spare = code_rows - 3 * chunks - 2 * user_rows
    pad = [jnp.zeros((spare, LANES), I32)] if spare else []
    codes = jnp.concatenate([route, bucket >> LOW, bucket & MASK] + high + low + pad, axis=0)
    out_ref[pl.ds(rows, code_rows), :] = codes.astype(F32).astype(BF16)


def each(count, body):
    if count <= 8:
        for i in range(count):
            body(i)
    else:
        lax.fori_loop(0, count, lambda i, c: (body(i), c)[1], 0)


def gather_kernel(
    owners, rows, slots, me_ref, rate_ref, route_ref, bucket_ref, all_ref,
    table_ref, feature_ref,
    place_ref, until_ref, own_ref, tail_ref, codes_ref, rows_ref, from_ref, last_ref, total_ref,
):
    chunks, user_rows, code_rows, span = dims(owners, rows, slots)
    window = slots // 4
    block_rows = rows + code_rows
    capacity = 2 * rows // owners
    per_group = LANES // capacity
    groups = owners // per_group
    me = me_ref[0]
    base = (me * slots).astype(F32)
    rate = rate_row(rate_ref)

    starts = []
    for u in range(user_rows):
        def add(s, total):
            tile = all_ref[pl.ds(pl.multiple_of(s * block_rows + rows, 16), code_rows), :].astype(F32)
            at = 3 * chunks + u
            return total + F32(LANES) * tile[at : at + 1] + tile[at + user_rows : at + user_rows + 1]

        starts.append(lax.fori_loop(0, owners, add, jnp.zeros((1, LANES), F32), unroll=owners <= 8))
    start_columns = [jnp.broadcast_to(row, (8, LANES)).T[:, 0:1] for row in starts]
    steps = []
    for u in range(user_rows):
        before = pltpu.roll(starts[u], 1, 1)
        first = starts[u - 1][:, LANES - 1 : LANES] if u else jnp.zeros((1, 1), F32)
        step = (starts[u] - jnp.where(iota((1, LANES), 1) == 0, first, before)).astype(I32)
        pair = jnp.concatenate([jnp.broadcast_to(step >> LOW, (LANES, LANES)), jnp.broadcast_to(step & MASK, (LANES, LANES))], axis=0)
        steps.append(pair.astype(F32).astype(BF16))

    def run_start(position):
        total = jnp.zeros((position.shape[0], 2 * LANES), F32)
        for u in range(user_rows):
            reached = jnp.where(starts[u] <= position, F32(1), F32(0)).astype(BF16)
            total += lax.dot_general(reached, steps[u], NT, preferred_element_type=F32)
        return F32(LANES) * total[:, :LANES] + total[:, LANES:]

    def root(position):
        return lax.rsqrt(jnp.minimum(position - run_start(position), F32(window)) + F32(1))

    def decode(s):
        tile = all_ref[pl.ds(pl.multiple_of(s * block_rows + rows, 16), code_rows), :].astype(F32)
        route = tile[0:chunks]
        bucket = F32(LANES) * tile[chunks : 2 * chunks] + tile[2 * chunks : 3 * chunks]
        place = route * F32(slots) + bucket
        until = []
        for r in range(chunks):
            row = place[r : r + 1]
            after = jnp.full((1, LANES), FAR, F32)
            for column in start_columns:
                later = jnp.where(column > row, column, F32(FAR))
                after = jnp.minimum(after, jnp.min(later, axis=0, keepdims=True))
            until.append(jnp.minimum(row + F32(window), after - F32(1)))
        until = jnp.concatenate(until, axis=0)
        local = place - base
        end = until - base
        near = (local.astype(I32), end.astype(I32))
        codes = jnp.concatenate([near[0] >> LOW, near[0] & MASK, near[1] >> LOW, near[1] & MASK], axis=0)
        spare = jnp.full((8 - chunks, LANES), -1, F32)
        place_ref[s] = jnp.concatenate([place, spare], axis=0)
        until_ref[s] = jnp.concatenate([until, spare], axis=0)
        codes_ref[s] = codes.astype(F32)
        own = (local >= 0) & (local < F32(slots))
        tail = (local >= F32(-window)) & (local < 0)
        spare = jnp.zeros((8 - chunks, LANES), F32)
        own_ref[s] = jnp.concatenate([jnp.where(own, F32(1), F32(0)), spare], axis=0)
        tail_ref[s] = jnp.concatenate([jnp.where(tail, F32(1), F32(0)), spare], axis=0)

    each(owners, decode)

    upper = jnp.where(iota((LANES, LANES), 0) < iota((LANES, LANES), 1), F32(1), F32(0)).astype(BF16)
    full = jnp.ones((LANES, LANES), BF16)
    lines = owners * 8
    at, by = iota((lines, lines), 0), iota((lines, lines), 1)
    earlier = jnp.where(((at >> 3) == (by >> 3)) & (by < at), F32(1), F32(0)).astype(BF16)
    for ref in (own_ref, tail_ref):
        marked = ref[...].reshape(lines, LANES)
        mark = marked.astype(BF16)
        inner = jnp.dot(mark, upper, preferred_element_type=F32)
        sums = jnp.dot(mark, full, preferred_element_type=F32).astype(BF16)
        rank = inner + jnp.dot(earlier, sums, preferred_element_type=F32)
        source = iota((lines, LANES), 0) >> 3
        rank += ((source & (per_group - 1)) * capacity).astype(F32)
        ref[...] = jnp.where(marked > 0, rank, F32(-1)).reshape(owners, 8, LANES)

    spots = iota((LANES, LANES), 0).astype(F32)
    code_line = iota((4 * chunks, LANES), 0) & (chunks - 1)

    def pack(kind, ref, g):
        def add(i, carry):
            values, places = carry
            s = g * per_group + i
            ranks = ref[s]
            codes = codes_ref[s]
            hot = jnp.concatenate(
                [jnp.where(spots == ranks[r : r + 1], F32(1), F32(0)).astype(BF16) for r in range(chunks)], axis=1
            )
            wide = jnp.concatenate(
                [jnp.where(code_line == r, codes, F32(0)).astype(BF16) for r in range(chunks)], axis=1
            )
            block = all_ref[pl.ds(pl.multiple_of(s * block_rows, 16), rows), :]
            values += jnp.dot(hot, block, preferred_element_type=F32)
            places += lax.dot_general(wide, hot, NT, preferred_element_type=F32)
            return values, places

        zero = (jnp.zeros((LANES, LANES), F32), jnp.zeros((4 * chunks, LANES), F32))
        values, places = lax.fori_loop(0, per_group, add, zero, unroll=per_group == 1)
        line = kind * groups + g
        rows_ref[line * LANES : (line + 1) * LANES, :] = values.astype(BF16)
        part = [jnp.sum(places[k * chunks : (k + 1) * chunks], axis=0, keepdims=True) for k in range(4)]
        from_ref[line : line + 1, :] = F32(LANES) * part[0] + part[1]
        last_ref[line : line + 1, :] = F32(LANES) * part[2] + part[3]

    for kind, ref in enumerate((own_ref, tail_ref)):
        for g in range(groups):
            pack(kind, ref, g)

    block = 256
    own_offset = ((me & (span - 1)) * slots - span * slots // 2).astype(F32)
    tail_offset = (((me - 1) & (span - 1)) * slots + slots - span * slots // 2).astype(F32)
    inner = iota((block, LANES), 0)

    def summed(position, kind):
        masks = []
        for g in range(groups):
            line = kind * groups + g
            held = (position >= from_ref[line : line + 1, :]) & (position <= last_ref[line : line + 1, :])
            masks.append(jnp.where(held, F32(1), F32(0)).astype(BF16))
        held = jnp.concatenate(masks, axis=1)
        events = rows_ref[kind * groups * LANES : (kind + 1) * groups * LANES, :]
        return jnp.dot(held, events, preferred_element_type=F32)

    def table_block(b, with_tail):
        position = (inner + b * block).astype(F32)
        value = summed(position, 0) * jnp.exp(-rate * (position + own_offset))
        if with_tail:
            value += summed(position, 1) * jnp.exp(-rate * (position + tail_offset))
        value *= root(position + base)
        table_ref[pl.ds(pl.multiple_of(b * block, block), block), :] = value.astype(BF16)

    lax.fori_loop(0, window // block, lambda b, c: (table_block(b, True), c)[1], 0)
    lax.fori_loop(window // block, slots // block, lambda b, c: (table_block(b, False), c)[1], 0)

    route = route_ref[...]
    place = route * slots + bucket_ref[...]
    first = (route >> (span.bit_length() - 1)) * (span * slots)
    columns = jnp.concatenate([place, first], axis=0).astype(F32).T
    position = jnp.concatenate(
        [jnp.broadcast_to(columns[:, r : r + 1], (LANES, LANES)) for r in range(chunks)], axis=0
    )
    first = jnp.concatenate(
        [jnp.broadcast_to(columns[:, chunks + r : chunks + r + 1], (LANES, LANES)) for r in range(chunks)], axis=0
    )
    scale = root(position)
    value = jnp.zeros((rows, LANES), F32)
    for shift in (0,) if owners <= span else (0, 1):
        total_ref[...] = jnp.zeros((rows, LANES), F32)

        def add(s):
            begin, end = place_ref[s], until_ref[s]
            masks = []
            for r in range(chunks):
                held = (position >= begin[r : r + 1]) & (position <= end[r : r + 1])
                if owners > span:
                    inside = begin[r : r + 1] >= first
                    held &= inside if shift == 0 else jnp.logical_not(inside)
                masks.append(jnp.where(held, F32(1), F32(0)).astype(BF16))
            events = all_ref[pl.ds(pl.multiple_of(s * block_rows, 16), rows), :]
            total_ref[...] += jnp.dot(jnp.concatenate(masks, axis=1), events, preferred_element_type=F32)

        each(owners, add)
        center = first + F32(span * slots // 2 - shift * span * slots)
        value += total_ref[...] * jnp.exp(-rate * (position - center))
    feature_ref[...] = (value * scale).astype(BF16)


def on_device(events, event_weight, route, bucket, segment, decay_rate):
    rows, width = events.shape
    shard_count = lax.axis_size("shard")
    owners = lax.axis_size("key") * shard_count
    slots = segment.shape[0]
    chunks, user_rows, code_rows, span = dims(owners, rows, slots)
    block_rows = rows + code_rows
    smem = pl.BlockSpec(memory_space=pltpu.SMEM)
    vmem = pl.BlockSpec(memory_space=pltpu.VMEM)
    route = route.reshape(chunks, LANES)
    bucket = bucket.reshape(chunks, LANES)
    block = pl.pallas_call(
        functools.partial(send_kernel, owners, slots),
        out_shape=jax.ShapeDtypeStruct((block_rows, width), BF16),
        in_specs=[smem] + [vmem] * 5,
        out_specs=vmem,
        name="weigh",
    )(decay_rate, events, event_weight.reshape(chunks, LANES), route, bucket, segment.reshape(slots // LANES, LANES))
    gathered = lax.all_gather(block, ("key", "shard"), axis=0, tiled=True)
    me = (lax.axis_index("key") * shard_count + lax.axis_index("shard")).astype(I32).reshape(1)
    lines = 2 * rows // LANES * 2
    return pl.pallas_call(
        functools.partial(gather_kernel, owners, rows, slots),
        out_shape=(
            jax.ShapeDtypeStruct((slots, width), BF16),
            jax.ShapeDtypeStruct((rows, width), BF16),
        ),
        in_specs=[smem, smem] + [vmem] * 3,
        out_specs=(vmem, vmem),
        scratch_shapes=[
            pltpu.VMEM((owners, 8, LANES), F32),
            pltpu.VMEM((owners, 8, LANES), F32),
            pltpu.VMEM((owners, 8, LANES), F32),
            pltpu.VMEM((owners, 8, LANES), F32),
            pltpu.VMEM((owners, 4 * chunks, LANES), F32),
            pltpu.VMEM((lines * LANES, LANES), BF16),
            pltpu.VMEM((lines, LANES), F32),
            pltpu.VMEM((lines, LANES), F32),
            pltpu.VMEM((rows, LANES), F32),
        ],
        compiler_params=pltpu.CompilerParams(vmem_limit_bytes=56 * 1024 * 1024),
        name="aggregate",
    )(me, decay_rate, route, bucket, gathered)


def solution(mesh):
    placed = (
        P(("groups", "key", "shard"), "lane"),
        P(("groups", "key", "shard")),
        P(("groups", "key", "shard"), None),
        P(("groups", "key", "shard")),
        P(("groups", "key", "shard")),
        P("lane"),
    )
    return jax.shard_map(
        on_device,
        mesh=mesh,
        in_specs=placed,
        out_specs=(P(("groups", "key", "shard"), "lane"), P(("groups", "key", "shard"), "lane")),
        check_vma=False,
    )
```

```python
import functools
import jax
import jax.numpy as jnp
from jax import lax
from jax.experimental import pallas as pl
from jax.experimental.pallas import tpu as pltpu
from jax.sharding import PartitionSpec as P

LANES = 128
LOW = 7
MASK = 127
F32 = jnp.float32
BF16 = jnp.bfloat16
I32 = jnp.int32
FAR = 1e9
NT = (((1,), (1,)), ((), ()))


def dims(owners, rows, slots):
    chunks = rows // LANES
    users = 8 * owners
    user_rows = -(-users // LANES)
    code_rows = -(-(3 * chunks + 2 * user_rows + 1) // 16) * 16
    span = min(owners, 8)
    return chunks, user_rows, code_rows, span


def iota(shape, axis):
    return lax.broadcasted_iota(I32, shape, axis)


def rate_row(rate_ref):
    groups = rate_ref.shape[0]
    lane = iota((1, LANES), 1)
    row = jnp.full((1, LANES), rate_ref[0], F32)
    for g in range(1, groups):
        row = jnp.where(lane >= g * (LANES // groups), rate_ref[g], row)
    return row


def send_kernel(owners, slots, events_ref, weight_ref, route_ref, bucket_ref, segment_ref, out_ref):
    rows = events_ref.shape[0]
    chunks, user_rows, code_rows, span = dims(owners, rows, slots)
    route = route_ref[...]
    bucket = bucket_ref[...]
    columns = jnp.concatenate([weight_ref[...], jnp.zeros((8 - chunks, LANES), F32)], axis=0).T
    weighted = []
    largest = jnp.zeros((LANES, LANES), F32)
    for r in range(chunks):
        part = pl.ds(r * LANES, LANES)
        weighted.append((columns[:, r : r + 1] * events_ref[part, :].astype(F32)).astype(BF16).astype(F32))
        largest = jnp.maximum(largest, jnp.abs(weighted[-1]))
    largest = jnp.max(jnp.max(largest, axis=0, keepdims=True), axis=1, keepdims=True)
    power = jnp.zeros((1, 1), F32)
    factor = jnp.ones((1, 1), F32)
    for bits in (64, 32, 16, 8, 4, 2, 1):
        more = factor * F32(2.0**bits)
        fits = largest * more <= F32(32768)
        factor = jnp.where(fits, more, factor)
        power = jnp.where(fits, power + F32(bits), power)
    for r in range(chunks):
        out_ref[pl.ds(r * LANES, LANES), :] = (weighted[r] * factor).astype(BF16)
    ones = jnp.ones((8, LANES), BF16)
    high, low = [], []
    for u in range(user_rows):
        user = iota((LANES, LANES), 0) + u * LANES
        below = jnp.zeros((LANES, LANES), F32)
        for r in range(slots // LANES):
            below += jnp.where(segment_ref[r : r + 1, :] < user, F32(1), F32(0))
        count = lax.dot_general(ones, below.astype(BF16), NT, preferred_element_type=F32)[0:1].astype(I32)
        high.append(count >> LOW)
        low.append(count & MASK)
    spare = code_rows - 3 * chunks - 2 * user_rows
    pad = [jnp.broadcast_to(power, (spare, LANES)).astype(I32)]
    codes = jnp.concatenate([route, bucket >> LOW, bucket & MASK] + high + low + pad, axis=0)
    out_ref[pl.ds(rows, code_rows), :] = codes.astype(F32).astype(BF16)


def each(count, body):
    if count <= 8:
        for i in range(count):
            body(i)
    else:
        lax.fori_loop(0, count, lambda i, c: (body(i), c)[1], 0)


def gather_kernel(
    owners, rows, slots, me_ref, rate_ref, route_ref, bucket_ref, all_ref,
    table_ref, feature_ref,
    grown_ref, place_ref, until_ref, own_ref, tail_ref, codes_ref, rows_ref, from_ref, last_ref, total_ref,
):
    chunks, user_rows, code_rows, span = dims(owners, rows, slots)
    window = slots // 4
    block_rows = rows + code_rows
    power_row = 3 * chunks + 2 * user_rows
    capacity = 2 * rows // owners
    per_group = LANES // capacity
    groups = owners // per_group
    me = me_ref[0]
    base = (me * slots).astype(F32)
    rate = rate_row(rate_ref)

    starts = []
    for u in range(user_rows):
        def add(s, total):
            tile = all_ref[pl.ds(pl.multiple_of(s * block_rows + rows, 16), code_rows), :].astype(F32)
            at = 3 * chunks + u
            return total + F32(LANES) * tile[at : at + 1] + tile[at + user_rows : at + user_rows + 1]

        starts.append(lax.fori_loop(0, owners, add, jnp.zeros((1, LANES), F32), unroll=owners <= 8))
    start_columns = [jnp.broadcast_to(row, (8, LANES)).T[:, 0:1] for row in starts]
    steps = []
    for u in range(user_rows):
        before = pltpu.roll(starts[u], 1, 1)
        first = starts[u - 1][:, LANES - 1 : LANES] if u else jnp.zeros((1, 1), F32)
        step = (starts[u] - jnp.where(iota((1, LANES), 1) == 0, first, before)).astype(I32)
        pair = jnp.concatenate([jnp.broadcast_to(step >> LOW, (LANES, LANES)), jnp.broadcast_to(step & MASK, (LANES, LANES))], axis=0)
        steps.append(pair.astype(F32).astype(BF16))

    def run_start(position):
        total = jnp.zeros((position.shape[0], 2 * LANES), F32)
        for u in range(user_rows):
            reached = jnp.where(starts[u] <= position, F32(1), F32(0)).astype(BF16)
            total += lax.dot_general(reached, steps[u], NT, preferred_element_type=F32)
        return F32(LANES) * total[:, :LANES] + total[:, LANES:]

    def root(position):
        return lax.rsqrt(jnp.minimum(position - run_start(position), F32(window)) + F32(1))

    def decode(s):
        tile = all_ref[pl.ds(pl.multiple_of(s * block_rows + rows, 16), code_rows), :].astype(F32)
        route = tile[0:chunks]
        bucket = F32(LANES) * tile[chunks : 2 * chunks] + tile[2 * chunks : 3 * chunks]
        place = route * F32(slots) + bucket
        spot = ((route.astype(I32) & (span - 1)) * slots - span * slots // 2).astype(F32) + bucket
        shrink = jnp.broadcast_to(tile[power_row : power_row + 1] * F32(-0.6931471805599453), (8 - chunks, LANES))
        columns = jnp.concatenate([spot, shrink], axis=0).T
        for r in range(chunks):
            events = all_ref[pl.ds(pl.multiple_of(s * block_rows + r * LANES, 16), LANES), :].astype(F32)
            growth = jnp.exp(columns[:, r : r + 1] * rate + columns[:, chunks : chunks + 1])
            part = pl.ds(pl.multiple_of(s * rows + r * LANES, LANES), LANES)
            grown_ref[part, :] = (events * growth).astype(BF16)
        until = []
        for r in range(chunks):
            row = place[r : r + 1]
            after = jnp.full((1, LANES), FAR, F32)
            for column in start_columns:
                later = jnp.where(column > row, column, F32(FAR))
                after = jnp.minimum(after, jnp.min(later, axis=0, keepdims=True))
            until.append(jnp.minimum(row + F32(window), after - F32(1)))
        until = jnp.concatenate(until, axis=0)
        local = place - base
        end = until - base
        near = (local.astype(I32), end.astype(I32))
        codes = jnp.concatenate([near[0] >> LOW, near[0] & MASK, near[1] >> LOW, near[1] & MASK], axis=0)
        spare = jnp.full((8 - chunks, LANES), -1, F32)
        place_ref[s] = jnp.concatenate([place, spare], axis=0)
        until_ref[s] = jnp.concatenate([until, spare], axis=0)
        codes_ref[s] = codes.astype(F32)
        own = (local >= 0) & (local < F32(slots))
        tail = (local >= F32(-window)) & (local < 0)
        spare = jnp.zeros((8 - chunks, LANES), F32)
        own_ref[s] = jnp.concatenate([jnp.where(own, F32(1), F32(0)), spare], axis=0)
        tail_ref[s] = jnp.concatenate([jnp.where(tail, F32(1), F32(0)), spare], axis=0)

    each(owners, decode)

    upper = jnp.where(iota((LANES, LANES), 0) < iota((LANES, LANES), 1), F32(1), F32(0)).astype(BF16)
    full = jnp.ones((LANES, LANES), BF16)
    lines = owners * 8
    at, by = iota((lines, lines), 0), iota((lines, lines), 1)
    earlier = jnp.where(((at >> 3) == (by >> 3)) & (by < at), F32(1), F32(0)).astype(BF16)
    for ref in (own_ref, tail_ref):
        marked = ref[...].reshape(lines, LANES)
        mark = marked.astype(BF16)
        inner = jnp.dot(mark, upper, preferred_element_type=F32)
        sums = jnp.dot(mark, full, preferred_element_type=F32).astype(BF16)
        rank = inner + jnp.dot(earlier, sums, preferred_element_type=F32)
        source = iota((lines, LANES), 0) >> 3
        rank += ((source & (per_group - 1)) * capacity).astype(F32)
        ref[...] = jnp.where(marked > 0, rank, F32(-1)).reshape(owners, 8, LANES)

    spots = iota((LANES, LANES), 0).astype(F32)
    code_line = iota((4 * chunks, LANES), 0) & (chunks - 1)

    def pack(kind, ref, g):
        def add(i, carry):
            values, places = carry
            s = g * per_group + i
            ranks = ref[s]
            codes = codes_ref[s]
            hot = jnp.concatenate(
                [jnp.where(spots == ranks[r : r + 1], F32(1), F32(0)).astype(BF16) for r in range(chunks)], axis=1
            )
            wide = jnp.concatenate(
                [jnp.where(code_line == r, codes, F32(0)).astype(BF16) for r in range(chunks)], axis=1
            )
            block = grown_ref[pl.ds(pl.multiple_of(s * rows, LANES), rows), :]
            values += jnp.dot(hot, block, preferred_element_type=F32)
            places += lax.dot_general(wide, hot, NT, preferred_element_type=F32)
            return values, places

        zero = (jnp.zeros((LANES, LANES), F32), jnp.zeros((4 * chunks, LANES), F32))
        values, places = lax.fori_loop(0, per_group, add, zero, unroll=per_group == 1)
        line = kind * groups + g
        rows_ref[line * LANES : (line + 1) * LANES, :] = values.astype(BF16)
        part = [jnp.sum(places[k * chunks : (k + 1) * chunks], axis=0, keepdims=True) for k in range(4)]
        from_ref[line : line + 1, :] = F32(LANES) * part[0] + part[1]
        last_ref[line : line + 1, :] = F32(LANES) * part[2] + part[3]

    for kind, ref in enumerate((own_ref, tail_ref)):
        for g in range(groups):
            pack(kind, ref, g)

    block = 256
    own_offset = ((me & (span - 1)) * slots - span * slots // 2).astype(F32)
    tail_offset = (((me - 1) & (span - 1)) * slots + slots - span * slots // 2).astype(F32)
    inner = iota((block, LANES), 0)

    def summed(position, kind):
        masks = []
        for g in range(groups):
            line = kind * groups + g
            held = (position >= from_ref[line : line + 1, :]) & (position <= last_ref[line : line + 1, :])
            masks.append(jnp.where(held, F32(1), F32(0)).astype(BF16))
        held = jnp.concatenate(masks, axis=1)
        events = rows_ref[kind * groups * LANES : (kind + 1) * groups * LANES, :]
        return jnp.dot(held, events, preferred_element_type=F32)

    def table_block(b, with_tail):
        position = (inner + b * block).astype(F32)
        value = summed(position, 0) * jnp.exp(-rate * (position + own_offset))
        if with_tail:
            value += summed(position, 1) * jnp.exp(-rate * (position + tail_offset))
        value *= root(position + base)
        table_ref[pl.ds(pl.multiple_of(b * block, block), block), :] = value.astype(BF16)

    lax.fori_loop(0, window // block, lambda b, c: (table_block(b, True), c)[1], 0)
    lax.fori_loop(window // block, slots // block, lambda b, c: (table_block(b, False), c)[1], 0)

    route = route_ref[...]
    place = route * slots + bucket_ref[...]
    first = (route >> (span.bit_length() - 1)) * (span * slots)
    columns = jnp.concatenate([place, first], axis=0).astype(F32).T
    position = jnp.concatenate(
        [jnp.broadcast_to(columns[:, r : r + 1], (LANES, LANES)) for r in range(chunks)], axis=0
    )
    first = jnp.concatenate(
        [jnp.broadcast_to(columns[:, chunks + r : chunks + r + 1], (LANES, LANES)) for r in range(chunks)], axis=0
    )
    scale = root(position)
    value = jnp.zeros((rows, LANES), F32)
    for shift in (0,) if owners <= span else (0, 1):
        total_ref[...] = jnp.zeros((rows, LANES), F32)

        def add(s):
            begin, end = place_ref[s], until_ref[s]
            masks = []
            for r in range(chunks):
                held = (position >= begin[r : r + 1]) & (position <= end[r : r + 1])
                if owners > span:
                    inside = begin[r : r + 1] >= first
                    held &= inside if shift == 0 else jnp.logical_not(inside)
                masks.append(jnp.where(held, F32(1), F32(0)).astype(BF16))
            events = grown_ref[pl.ds(pl.multiple_of(s * rows, LANES), rows), :]
            total_ref[...] += jnp.dot(jnp.concatenate(masks, axis=1), events, preferred_element_type=F32)

        each(owners, add)
        center = first + F32(span * slots // 2 - shift * span * slots)
        value += total_ref[...] * jnp.exp(-rate * (position - center))
    feature_ref[...] = (value * scale).astype(BF16)


def on_device(events, event_weight, route, bucket, segment, decay_rate):
    rows, width = events.shape
    shard_count = lax.axis_size("shard")
    owners = lax.axis_size("key") * shard_count
    slots = segment.shape[0]
    chunks, user_rows, code_rows, span = dims(owners, rows, slots)
    block_rows = rows + code_rows
    smem = pl.BlockSpec(memory_space=pltpu.SMEM)
    vmem = pl.BlockSpec(memory_space=pltpu.VMEM)
    route = route.reshape(chunks, LANES)
    bucket = bucket.reshape(chunks, LANES)
    block = pl.pallas_call(
        functools.partial(send_kernel, owners, slots),
        out_shape=jax.ShapeDtypeStruct((block_rows, width), BF16),
        in_specs=[vmem] * 5,
        out_specs=vmem,
        name="weigh",
    )(events, event_weight.reshape(chunks, LANES), route, bucket, segment.reshape(slots // LANES, LANES))
    gathered = lax.all_gather(block.astype(jnp.float16), ("key", "shard"), axis=0, tiled=True).astype(BF16)
    me = (lax.axis_index("key") * shard_count + lax.axis_index("shard")).astype(I32).reshape(1)
    lines = 2 * rows // LANES * 2
    return pl.pallas_call(
        functools.partial(gather_kernel, owners, rows, slots),
        out_shape=(
            jax.ShapeDtypeStruct((slots, width), BF16),
            jax.ShapeDtypeStruct((rows, width), BF16),
        ),
        in_specs=[smem, smem] + [vmem] * 3,
        out_specs=(vmem, vmem),
        scratch_shapes=[
            pltpu.VMEM((owners * rows, LANES), BF16),
            pltpu.VMEM((owners, 8, LANES), F32),
            pltpu.VMEM((owners, 8, LANES), F32),
            pltpu.VMEM((owners, 8, LANES), F32),
            pltpu.VMEM((owners, 8, LANES), F32),
            pltpu.VMEM((owners, 4 * chunks, LANES), F32),
            pltpu.VMEM((lines * LANES, LANES), BF16),
            pltpu.VMEM((lines, LANES), F32),
            pltpu.VMEM((lines, LANES), F32),
            pltpu.VMEM((rows, LANES), F32),
        ],
        compiler_params=pltpu.CompilerParams(vmem_limit_bytes=56 * 1024 * 1024),
        name="aggregate",
    )(me, decay_rate, route, bucket, gathered)


def solution(mesh):
    placed = (
        P(("groups", "key", "shard"), "lane"),
        P(("groups", "key", "shard")),
        P(("groups", "key", "shard"), None),
        P(("groups", "key", "shard")),
        P(("groups", "key", "shard")),
        P("lane"),
    )
    return jax.shard_map(
        on_device,
        mesh=mesh,
        in_specs=placed,
        out_specs=(P(("groups", "key", "shard"), "lane"), P(("groups", "key", "shard"), "lane")),
        check_vma=False,
    )
```

```python
import functools
import jax
import jax.numpy as jnp
from jax import lax
from jax.experimental import pallas as pl
from jax.experimental.pallas import tpu as pltpu
from jax.sharding import PartitionSpec as P

LANES = 128
LOW = 7
MASK = 127
F32 = jnp.float32
BF16 = jnp.bfloat16
I32 = jnp.int32
FAR = 1e9
NT = (((1,), (1,)), ((), ()))


def dims(owners, rows, slots):
    chunks = rows // LANES
    users = 8 * owners
    user_rows = -(-users // LANES)
    code_rows = -(-(3 * chunks + 2 * user_rows) // 16) * 16
    span = min(owners, 8)
    return chunks, user_rows, code_rows, span


def iota(shape, axis):
    return lax.broadcasted_iota(I32, shape, axis)


def rate_row(rate_ref):
    groups = rate_ref.shape[0]
    lane = iota((1, LANES), 1)
    row = jnp.full((1, LANES), rate_ref[0], F32)
    for g in range(1, groups):
        row = jnp.where(lane >= g * (LANES // groups), rate_ref[g], row)
    return row


def send_kernel(owners, slots, rate_ref, events_ref, weight_ref, route_ref, bucket_ref, segment_ref, out_ref):
    rows = events_ref.shape[0]
    chunks, user_rows, code_rows, span = dims(owners, rows, slots)
    rate = rate_row(rate_ref)
    route = route_ref[...]
    bucket = bucket_ref[...]
    spot = (route & (span - 1)) * slots + bucket - span * slots // 2
    columns = jnp.concatenate([weight_ref[...], spot.astype(F32)], axis=0).T
    for r in range(chunks):
        part = pl.ds(r * LANES, LANES)
        weighted = (columns[:, r : r + 1] * events_ref[part, :].astype(F32)).astype(BF16)
        grown = weighted.astype(F32) * jnp.exp(columns[:, chunks + r : chunks + r + 1] * rate)
        grown = grown.astype(BF16)
        for o in range(owners):
            out_ref[o, part, :] = grown
    ones = jnp.ones((8, LANES), BF16)
    high, low = [], []
    for u in range(user_rows):
        user = iota((LANES, LANES), 0) + u * LANES
        below = jnp.zeros((LANES, LANES), F32)
        for r in range(slots // LANES):
            below += jnp.where(segment_ref[r : r + 1, :] < user, F32(1), F32(0))
        count = lax.dot_general(ones, below.astype(BF16), NT, preferred_element_type=F32)[0:1].astype(I32)
        high.append(count >> LOW)
        low.append(count & MASK)
    spare = code_rows - 3 * chunks - 2 * user_rows
    pad = [jnp.zeros((spare, LANES), I32)] if spare else []
    codes = jnp.concatenate([route, bucket >> LOW, bucket & MASK] + high + low + pad, axis=0)
    codes = codes.astype(F32).astype(BF16)
    for o in range(owners):
        out_ref[o, pl.ds(rows, code_rows), :] = codes


def each(count, body):
    if count <= 8:
        for i in range(count):
            body(i)
    else:
        lax.fori_loop(0, count, lambda i, c: (body(i), c)[1], 0)


def gather_kernel(
    owners, rows, slots, me_ref, rate_ref, route_ref, bucket_ref, all_ref,
    table_ref, feature_ref,
    place_ref, until_ref, own_ref, tail_ref, codes_ref, rows_ref, from_ref, last_ref, total_ref,
):
    chunks, user_rows, code_rows, span = dims(owners, rows, slots)
    window = slots // 4
    block_rows = rows + code_rows
    capacity = 2 * rows // owners
    per_group = LANES // capacity
    groups = owners // per_group
    me = me_ref[0]
    base = (me * slots).astype(F32)
    rate = rate_row(rate_ref)

    starts = []
    for u in range(user_rows):
        def add(s, total):
            tile = all_ref[pl.ds(pl.multiple_of(s * block_rows + rows, 16), code_rows), :].astype(F32)
            at = 3 * chunks + u
            return total + F32(LANES) * tile[at : at + 1] + tile[at + user_rows : at + user_rows + 1]

        starts.append(lax.fori_loop(0, owners, add, jnp.zeros((1, LANES), F32), unroll=owners <= 8))
    start_columns = [jnp.broadcast_to(row, (8, LANES)).T[:, 0:1] for row in starts]
    steps = []
    for u in range(user_rows):
        before = pltpu.roll(starts[u], 1, 1)
        first = starts[u - 1][:, LANES - 1 : LANES] if u else jnp.zeros((1, 1), F32)
        step = (starts[u] - jnp.where(iota((1, LANES), 1) == 0, first, before)).astype(I32)
        pair = jnp.concatenate([jnp.broadcast_to(step >> LOW, (LANES, LANES)), jnp.broadcast_to(step & MASK, (LANES, LANES))], axis=0)
        steps.append(pair.astype(F32).astype(BF16))

    def run_start(position):
        total = jnp.zeros((position.shape[0], 2 * LANES), F32)
        for u in range(user_rows):
            reached = jnp.where(starts[u] <= position, F32(1), F32(0)).astype(BF16)
            total += lax.dot_general(reached, steps[u], NT, preferred_element_type=F32)
        return F32(LANES) * total[:, :LANES] + total[:, LANES:]

    def root(position):
        return lax.rsqrt(jnp.minimum(position - run_start(position), F32(window)) + F32(1))

    def decode(s):
        tile = all_ref[pl.ds(pl.multiple_of(s * block_rows + rows, 16), code_rows), :].astype(F32)
        route = tile[0:chunks]
        bucket = F32(LANES) * tile[chunks : 2 * chunks] + tile[2 * chunks : 3 * chunks]
        place = route * F32(slots) + bucket
        until = []
        for r in range(chunks):
            row = place[r : r + 1]
            after = jnp.full((1, LANES), FAR, F32)
            for column in start_columns:
                later = jnp.where(column > row, column, F32(FAR))
                after = jnp.minimum(after, jnp.min(later, axis=0, keepdims=True))
            until.append(jnp.minimum(row + F32(window), after - F32(1)))
        until = jnp.concatenate(until, axis=0)
        local = place - base
        end = until - base
        near = (local.astype(I32), end.astype(I32))
        codes = jnp.concatenate([near[0] >> LOW, near[0] & MASK, near[1] >> LOW, near[1] & MASK], axis=0)
        spare = jnp.full((8 - chunks, LANES), -1, F32)
        place_ref[s] = jnp.concatenate([place, spare], axis=0)
        until_ref[s] = jnp.concatenate([until, spare], axis=0)
        codes_ref[s] = codes.astype(F32)
        own = (local >= 0) & (local < F32(slots))
        tail = (local >= F32(-window)) & (local < 0)
        spare = jnp.zeros((8 - chunks, LANES), F32)
        own_ref[s] = jnp.concatenate([jnp.where(own, F32(1), F32(0)), spare], axis=0)
        tail_ref[s] = jnp.concatenate([jnp.where(tail, F32(1), F32(0)), spare], axis=0)

    each(owners, decode)

    upper = jnp.where(iota((LANES, LANES), 0) < iota((LANES, LANES), 1), F32(1), F32(0)).astype(BF16)
    full = jnp.ones((LANES, LANES), BF16)
    lines = owners * 8
    at, by = iota((lines, lines), 0), iota((lines, lines), 1)
    earlier = jnp.where(((at >> 3) == (by >> 3)) & (by < at), F32(1), F32(0)).astype(BF16)
    for ref in (own_ref, tail_ref):
        marked = ref[...].reshape(lines, LANES)
        mark = marked.astype(BF16)
        inner = jnp.dot(mark, upper, preferred_element_type=F32)
        sums = jnp.dot(mark, full, preferred_element_type=F32).astype(BF16)
        rank = inner + jnp.dot(earlier, sums, preferred_element_type=F32)
        source = iota((lines, LANES), 0) >> 3
        rank += ((source & (per_group - 1)) * capacity).astype(F32)
        ref[...] = jnp.where(marked > 0, rank, F32(-1)).reshape(owners, 8, LANES)

    spots = iota((LANES, LANES), 0).astype(F32)
    code_line = iota((4 * chunks, LANES), 0) & (chunks - 1)

    def pack(kind, ref, g):
        def add(i, carry):
            values, places = carry
            s = g * per_group + i
            ranks = ref[s]
            codes = codes_ref[s]
            hot = jnp.concatenate(
                [jnp.where(spots == ranks[r : r + 1], F32(1), F32(0)).astype(BF16) for r in range(chunks)], axis=1
            )
            wide = jnp.concatenate(
                [jnp.where(code_line == r, codes, F32(0)).astype(BF16) for r in range(chunks)], axis=1
            )
            block = all_ref[pl.ds(pl.multiple_of(s * block_rows, 16), rows), :]
            values += jnp.dot(hot, block, preferred_element_type=F32)
            places += lax.dot_general(wide, hot, NT, preferred_element_type=F32)
            return values, places

        zero = (jnp.zeros((LANES, LANES), F32), jnp.zeros((4 * chunks, LANES), F32))
        values, places = lax.fori_loop(0, per_group, add, zero, unroll=per_group == 1)
        line = kind * groups + g
        rows_ref[line * LANES : (line + 1) * LANES, :] = values.astype(BF16)
        part = [jnp.sum(places[k * chunks : (k + 1) * chunks], axis=0, keepdims=True) for k in range(4)]
        from_ref[line : line + 1, :] = F32(LANES) * part[0] + part[1]
        last_ref[line : line + 1, :] = F32(LANES) * part[2] + part[3]

    for kind, ref in enumerate((own_ref, tail_ref)):
        for g in range(groups):
            pack(kind, ref, g)

    block = 256
    own_offset = ((me & (span - 1)) * slots - span * slots // 2).astype(F32)
    tail_offset = (((me - 1) & (span - 1)) * slots + slots - span * slots // 2).astype(F32)
    inner = iota((block, LANES), 0)

    def summed(position, kind):
        masks = []
        for g in range(groups):
            line = kind * groups + g
            held = (position >= from_ref[line : line + 1, :]) & (position <= last_ref[line : line + 1, :])
            masks.append(jnp.where(held, F32(1), F32(0)).astype(BF16))
        held = jnp.concatenate(masks, axis=1)
        events = rows_ref[kind * groups * LANES : (kind + 1) * groups * LANES, :]
        return jnp.dot(held, events, preferred_element_type=F32)

    def table_block(b, with_tail):
        position = (inner + b * block).astype(F32)
        value = summed(position, 0) * jnp.exp(-rate * (position + own_offset))
        if with_tail:
            value += summed(position, 1) * jnp.exp(-rate * (position + tail_offset))
        value *= root(position + base)
        table_ref[pl.ds(pl.multiple_of(b * block, block), block), :] = value.astype(BF16)

    lax.fori_loop(0, window // block, lambda b, c: (table_block(b, True), c)[1], 0)
    lax.fori_loop(window // block, slots // block, lambda b, c: (table_block(b, False), c)[1], 0)

    route = route_ref[...]
    place = route * slots + bucket_ref[...]
    first = (route >> (span.bit_length() - 1)) * (span * slots)
    columns = jnp.concatenate([place, first], axis=0).astype(F32).T
    position = jnp.concatenate(
        [jnp.broadcast_to(columns[:, r : r + 1], (LANES, LANES)) for r in range(chunks)], axis=0
    )
    first = jnp.concatenate(
        [jnp.broadcast_to(columns[:, chunks + r : chunks + r + 1], (LANES, LANES)) for r in range(chunks)], axis=0
    )
    scale = root(position)
    value = jnp.zeros((rows, LANES), F32)
    for shift in (0,) if owners <= span else (0, 1):
        total_ref[...] = jnp.zeros((rows, LANES), F32)

        def add(s):
            begin, end = place_ref[s], until_ref[s]
            masks = []
            for r in range(chunks):
                held = (position >= begin[r : r + 1]) & (position <= end[r : r + 1])
                if owners > span:
                    inside = begin[r : r + 1] >= first
                    held &= inside if shift == 0 else jnp.logical_not(inside)
                masks.append(jnp.where(held, F32(1), F32(0)).astype(BF16))
            events = all_ref[pl.ds(pl.multiple_of(s * block_rows, 16), rows), :]
            total_ref[...] += jnp.dot(jnp.concatenate(masks, axis=1), events, preferred_element_type=F32)

        each(owners, add)
        center = first + F32(span * slots // 2 - shift * span * slots)
        value += total_ref[...] * jnp.exp(-rate * (position - center))
    feature_ref[...] = (value * scale).astype(BF16)


def on_device(events, event_weight, route, bucket, segment, decay_rate):
    rows, width = events.shape
    shard_count = lax.axis_size("shard")
    owners = lax.axis_size("key") * shard_count
    slots = segment.shape[0]
    chunks, user_rows, code_rows, span = dims(owners, rows, slots)
    block_rows = rows + code_rows
    smem = pl.BlockSpec(memory_space=pltpu.SMEM)
    vmem = pl.BlockSpec(memory_space=pltpu.VMEM)
    route = route.reshape(chunks, LANES)
    bucket = bucket.reshape(chunks, LANES)
    block = pl.pallas_call(
        functools.partial(send_kernel, owners, slots),
        out_shape=jax.ShapeDtypeStruct((owners, block_rows, width), BF16),
        in_specs=[smem] + [vmem] * 5,
        out_specs=vmem,
        compiler_params=pltpu.CompilerParams(vmem_limit_bytes=56 * 1024 * 1024),
        name="weigh",
    )(decay_rate, events, event_weight.reshape(chunks, LANES), route, bucket, segment.reshape(slots // LANES, LANES))
    gathered = lax.all_to_all(block, ("key", "shard"), split_axis=0, concat_axis=0, tiled=True)
    gathered = gathered.reshape(owners * block_rows, width)
    me = (lax.axis_index("key") * shard_count + lax.axis_index("shard")).astype(I32).reshape(1)
    lines = 2 * rows // LANES * 2
    return pl.pallas_call(
        functools.partial(gather_kernel, owners, rows, slots),
        out_shape=(
            jax.ShapeDtypeStruct((slots, width), BF16),
            jax.ShapeDtypeStruct((rows, width), BF16),
        ),
        in_specs=[smem, smem] + [vmem] * 3,
        out_specs=(vmem, vmem),
        scratch_shapes=[
            pltpu.VMEM((owners, 8, LANES), F32),
            pltpu.VMEM((owners, 8, LANES), F32),
            pltpu.VMEM((owners, 8, LANES), F32),
            pltpu.VMEM((owners, 8, LANES), F32),
            pltpu.VMEM((owners, 4 * chunks, LANES), F32),
            pltpu.VMEM((lines * LANES, LANES), BF16),
            pltpu.VMEM((lines, LANES), F32),
            pltpu.VMEM((lines, LANES), F32),
            pltpu.VMEM((rows, LANES), F32),
        ],
        compiler_params=pltpu.CompilerParams(vmem_limit_bytes=56 * 1024 * 1024),
        name="aggregate",
    )(me, decay_rate, route, bucket, gathered)


def solution(mesh):
    placed = (
        P(("groups", "key", "shard"), "lane"),
        P(("groups", "key", "shard")),
        P(("groups", "key", "shard"), None),
        P(("groups", "key", "shard")),
        P(("groups", "key", "shard")),
        P("lane"),
    )
    return jax.shard_map(
        on_device,
        mesh=mesh,
        in_specs=placed,
        out_specs=(P(("groups", "key", "shard"), "lane"), P(("groups", "key", "shard"), "lane")),
        check_vma=False,
    )
```

```python
import functools
import jax
import jax.numpy as jnp
from jax import lax
from jax.experimental import pallas as pl
from jax.experimental.pallas import tpu as pltpu
from jax.sharding import PartitionSpec as P

LANES = 128
LOW = 7
MASK = 127
F32 = jnp.float32
BF16 = jnp.bfloat16
I32 = jnp.int32
FAR = 1e9
NT = (((1,), (1,)), ((), ()))
BLOCK = 256
CHUNK = 256
FIXED = 2


class Sizes:
    def __init__(self, owners, rows, slots):
        self.owners, self.rows, self.slots = owners, rows, slots
        self.window = slots // 4
        self.chunks = rows // LANES
        self.half = rows // 2
        self.half_chunks = self.chunks // 2
        self.user_rows = -(-8 * owners // LANES)
        self.code_rows = -(-(3 * self.chunks + 2 * self.user_rows) // 16) * 16
        self.span = min(owners, 8)
        self.shifts = 1 if owners <= self.span else 2
        self.listed = 4 * rows


def iota(shape, axis):
    return lax.broadcasted_iota(I32, shape, axis)


def rate_row(rate_ref):
    groups = rate_ref.shape[0]
    lane = iota((1, LANES), 1)
    row = jnp.full((1, LANES), rate_ref[0], F32)
    for g in range(1, groups):
        row = jnp.where(lane >= g * (LANES // groups), rate_ref[g], row)
    return row


def ones_where(condition):
    return jnp.where(condition, F32(1), F32(0)).astype(BF16)


def dot(a, b):
    return jnp.dot(a, b, preferred_element_type=F32)


def loop(count, body, carry):
    if count <= 8:
        for i in range(count):
            carry = body(i, carry)
        return carry
    return lax.fori_loop(0, count, body, carry)


def over_sources(pieces, body, carry):
    first = 0
    for ref in pieces:
        carry = loop(ref.shape[0], lambda i, c: body(ref, i, first + i, c), carry)
        first += ref.shape[0]
    return carry


def send_kernel(z, rate_ref, events_ref, weight_ref, route_ref, bucket_ref, segment_ref, first_ref, second_ref):
    copies = first_ref.shape[0]
    rate = rate_row(rate_ref)
    route = route_ref[...]
    bucket = bucket_ref[...]
    spot = (route & (z.span - 1)) * z.slots + bucket - z.span * z.slots // 2
    columns = jnp.concatenate([weight_ref[...], spot.astype(F32)], axis=0).T
    for r in range(z.chunks):
        events = events_ref[r * LANES : (r + 1) * LANES, :].astype(F32)
        weighted = (columns[:, r : r + 1] * events).astype(BF16)
        grown = weighted.astype(F32) * jnp.exp(columns[:, z.chunks + r : z.chunks + r + 1] * rate)
        grown = grown.astype(BF16)
        ref = first_ref if r < z.half_chunks else second_ref
        at = (r % z.half_chunks) * LANES
        for o in range(copies):
            ref[o, at : at + LANES, :] = grown
    ones = jnp.ones((8, LANES), BF16)
    high, low = [], []
    for u in range(z.user_rows):
        user = iota((LANES, LANES), 0) + u * LANES
        below = jnp.zeros((LANES, LANES), F32)
        for r in range(z.slots // LANES):
            below += jnp.where(segment_ref[r : r + 1, :] < user, F32(1), F32(0))
        count = lax.dot_general(ones, below.astype(BF16), NT, preferred_element_type=F32)[0:1].astype(I32)
        high.append(count >> LOW)
        low.append(count & MASK)
    spare = z.code_rows - 3 * z.chunks - 2 * z.user_rows
    pad = [jnp.zeros((spare, LANES), I32)] if spare else []
    codes = jnp.concatenate([route, bucket >> LOW, bucket & MASK] + high + low + pad, axis=0)
    codes = codes.astype(F32).astype(BF16)
    for o in range(copies):
        first_ref[o, z.half : z.half + z.code_rows, :] = codes


def table_sum(b, value, count_ref, rows_ref, from_ref, last_ref):
    position = (iota((BLOCK, LANES), 0) + b * BLOCK).astype(F32)

    def held(g):
        masks = []
        for k in range(CHUNK // LANES):
            line = g * (CHUNK // LANES) + k
            begin, end = from_ref[pl.ds(line, 1), :], last_ref[pl.ds(line, 1), :]
            masks.append(ones_where((position >= begin) & (position <= end)))
        return jnp.concatenate(masks, axis=1)

    fixed = jnp.concatenate([held(g) for g in range(FIXED)], axis=1)
    value = value + dot(fixed, rows_ref[0 : FIXED * CHUNK, :])

    def more(g, value):
        return value + dot(held(g), rows_ref[pl.ds(pl.multiple_of(g * CHUNK, CHUNK), CHUNK), :])

    return lax.fori_loop(FIXED, count_ref, more, value)


def pack_rows(z, pieces, h, g, ranks_ref, codes_ref=None, with_rows=True):
    spots = (iota((CHUNK, LANES), 0) + g * CHUNK).astype(F32)

    def add(ref, i, s, carry):
        values, places = carry
        ranks = ranks_ref[s]
        chunks = range(h * z.half_chunks, (h + 1) * z.half_chunks)
        hot = jnp.concatenate([ones_where(spots == ranks[r : r + 1]) for r in chunks], axis=1)
        if with_rows:
            values += dot(hot, ref[i, 0 : z.half, :])
        if codes_ref is not None:
            wide = jnp.concatenate([codes_ref[s, r] for r in chunks], axis=1)
            places += lax.dot_general(wide.astype(BF16), hot, NT, preferred_element_type=F32)
        return values, places

    zero = (jnp.zeros((CHUNK, LANES), F32), jnp.zeros((8, CHUNK), F32))
    values, places = over_sources(pieces, add, zero)
    begin = F32(LANES) * places[0:1] + places[1:2]
    end = F32(LANES) * places[2:3] + places[3:4]
    return values, begin, end


def store_codes(g, begin, end, from_ref, last_ref):
    for k in range(CHUNK // LANES):
        line = g * (CHUNK // LANES) + k
        from_ref[pl.ds(line, 1), :] = begin[:, k * LANES : (k + 1) * LANES]
        last_ref[pl.ds(line, 1), :] = end[:, k * LANES : (k + 1) * LANES]


def store_rows(z, g, values, from_ref, rows_ref, me, rate):
    if z.shifts > 1:
        for k in range(CHUNK // LANES):
            begin = from_ref[pl.ds(g * (CHUNK // LANES) + k, 1), :]
            column = jnp.broadcast_to(begin, (8, LANES)).T[:, 0:1]
            early = column < -((me & (z.span - 1)) * z.slots).astype(F32)
            step = jnp.exp(rate * F32(-z.span * z.slots // 2))
            part = values[k * LANES : (k + 1) * LANES]
            part = jnp.where(early, part * step * step, part)
            at = pl.multiple_of(g * CHUNK + k * LANES, LANES)
            rows_ref[pl.ds(at, LANES), :] = part.astype(BF16)
    else:
        rows_ref[pl.ds(pl.multiple_of(g * CHUNK, CHUNK), CHUNK), :] = values.astype(BF16)


def own_columns(z, route_ref, bucket_ref):
    route = route_ref[...]
    place = route * z.slots + bucket_ref[...]
    first = (route >> (z.span.bit_length() - 1)) * (z.span * z.slots)
    return jnp.concatenate([place, first], axis=0).astype(F32).T


def target_block(z, columns, t, offset):
    parts = []
    for k in range(BLOCK // LANES):
        at = offset + t * (BLOCK // LANES) + k
        parts.append(jnp.broadcast_to(columns[:, at : at + 1], (LANES, LANES)))
    return jnp.concatenate(parts, axis=0)


def feature_sum(z, pieces, h, position, first, shift, place_ref, until_ref):
    def add(ref, i, s, value):
        begin, end = place_ref[s], until_ref[s]
        masks = []
        for r in range(h * z.half_chunks, (h + 1) * z.half_chunks):
            held = (position >= begin[r : r + 1]) & (position <= end[r : r + 1])
            if z.shifts > 1:
                inside = begin[r : r + 1] >= first
                held &= inside if shift == 0 else jnp.logical_not(inside)
            masks.append(ones_where(held))
        return value + dot(jnp.concatenate(masks, axis=1), ref[i, 0 : z.half, :])

    return over_sources(pieces, add, jnp.zeros((BLOCK, LANES), F32))


def first_kernel(z, count, *refs):
    me_ref, rate_ref, route_ref, bucket_ref = refs[:4]
    pieces = refs[4 : 4 + count]
    (
        sums_ref, scale_ref, feature_ref, feature_scale_ref, place_ref, until_ref, ranks_ref,
        from2_ref, last2_ref, count2_ref, codes_ref, rows_ref, from_ref, last_ref,
    ) = refs[4 + count :]
    me = me_ref[0]
    base = (me * z.slots).astype(F32)
    rate = rate_row(rate_ref)

    starts = []
    for u in range(z.user_rows):
        def add(ref, i, s, total):
            tile = ref[i, z.half : z.half + z.code_rows, :].astype(F32)
            at = 3 * z.chunks + u
            return total + F32(LANES) * tile[at : at + 1] + tile[at + z.user_rows : at + z.user_rows + 1]

        starts.append(over_sources(pieces, add, jnp.zeros((1, LANES), F32)))
    start_columns = [jnp.broadcast_to(row, (8, LANES)).T[:, 0:1] for row in starts]
    steps = []
    for u in range(z.user_rows):
        before = pltpu.roll(starts[u], 1, 1)
        first = starts[u - 1][:, LANES - 1 : LANES] if u else jnp.zeros((1, 1), F32)
        step = (starts[u] - jnp.where(iota((1, LANES), 1) == 0, first, before)).astype(I32)
        pair = [jnp.broadcast_to(step >> LOW, (LANES, LANES)), jnp.broadcast_to(step & MASK, (LANES, LANES))]
        steps.append(jnp.concatenate(pair, axis=0).astype(F32).astype(BF16))

    def root(position):
        total = jnp.zeros((position.shape[0], 2 * LANES), F32)
        for u in range(z.user_rows):
            total += lax.dot_general(ones_where(starts[u] <= position), steps[u], NT, preferred_element_type=F32)
        start = F32(LANES) * total[:, :LANES] + total[:, LANES:]
        return lax.rsqrt(jnp.minimum(position - start, F32(z.window)) + F32(1))

    def decode(ref, i, s, carry):
        tile = ref[i, z.half : z.half + z.code_rows, :].astype(F32)
        route = tile[0 : z.chunks]
        bucket = F32(LANES) * tile[z.chunks : 2 * z.chunks] + tile[2 * z.chunks : 3 * z.chunks]
        place = route * F32(z.slots) + bucket
        until = []
        for r in range(z.chunks):
            row = place[r : r + 1]
            after = jnp.full((1, LANES), FAR, F32)
            for column in start_columns:
                users = column[: min(LANES, 8 * z.owners)]
                later = jnp.where(users > row, users, F32(FAR))
                after = jnp.minimum(after, jnp.min(later, axis=0, keepdims=True))
            until.append(jnp.minimum(row + F32(z.window), after - F32(1)))
        until = jnp.concatenate(until, axis=0)
        local = place - base
        near, far = local.astype(I32), (until - base).astype(I32)
        kinds = [(near >> LOW).astype(F32), (near & MASK).astype(F32), (far >> LOW).astype(F32), (far & MASK).astype(F32)]
        empty = jnp.zeros((4, LANES), F32)
        for r in range(z.chunks):
            codes_ref[s, r] = jnp.concatenate([kind[r : r + 1] for kind in kinds] + [empty], axis=0)
        spare = jnp.zeros((8 - z.chunks, LANES), F32)
        place_ref[s] = jnp.concatenate([place, spare], axis=0)
        until_ref[s] = jnp.concatenate([until, spare], axis=0)
        mark = jnp.where((local >= F32(-z.window)) & (local < F32(z.slots)), F32(1), F32(0))
        ranks_ref[s] = jnp.concatenate([mark, spare], axis=0)
        return carry

    over_sources(pieces, decode, 0)

    lines = z.owners * 8
    upper = ones_where(iota((LANES, LANES), 0) < iota((LANES, LANES), 1))
    at, by = iota((lines, lines), 0), iota((lines, lines), 1)
    half_of = lambda line: (line & 7) >> (z.half_chunks.bit_length() - 1)
    earlier = ones_where((half_of(at) == half_of(by)) & (by < at))
    marked = ranks_ref[...].reshape(lines, LANES)
    mark = marked.astype(BF16)
    sums = dot(mark, jnp.ones((LANES, LANES), BF16))
    rank = dot(mark, upper) + dot(earlier, sums.astype(BF16))
    ranks_ref[...] = jnp.where(marked > 0, rank, F32(-1)).reshape(z.owners, 8, LANES)
    number = []
    for h in range(2):
        own = half_of(iota((lines, LANES), 0)) == h
        total = jnp.sum(jnp.where(own, marked, F32(0))).astype(I32)
        number.append((total + CHUNK - 1) // CHUNK)
    count2_ref[0] = number[1]

    def pack(g, carry):
        values, begin, end = pack_rows(z, pieces, 0, g, ranks_ref, codes_ref)
        store_codes(g, begin, end, from_ref, last_ref)
        store_rows(z, g, values, from_ref, rows_ref, me, rate)
        return carry

    def pack_codes(g, carry):
        _, begin, end = pack_rows(z, pieces, 1, g, ranks_ref, codes_ref, False)
        store_codes(g, begin, end, from2_ref, last2_ref)
        return carry

    for g in range(FIXED):
        pack(g, 0)
        pack_codes(g, 0)
    lax.fori_loop(FIXED, number[0], pack, 0)
    lax.fori_loop(FIXED, number[1], pack_codes, 0)

    fall = jnp.exp(-rate * iota((BLOCK, LANES), 0).astype(F32))
    center = ((me & (z.span - 1)) * z.slots - z.span * z.slots // 2).astype(F32)

    def table_block(b, carry):
        part = pl.ds(pl.multiple_of(b * BLOCK, BLOCK), BLOCK)
        start = (b * BLOCK).astype(F32)
        sums_ref[part, :] = table_sum(b, jnp.zeros((BLOCK, LANES), F32), number[0], rows_ref, from_ref, last_ref)
        position = iota((BLOCK, LANES), 0).astype(F32) + (base + start)
        scale_ref[part, :] = fall * jnp.exp(-rate * (start + center)) * root(position)
        return carry

    lax.fori_loop(0, z.slots // BLOCK, table_block, 0)

    columns = own_columns(z, route_ref, bucket_ref)
    for t in range(z.rows // BLOCK):
        position = target_block(z, columns, t, 0)
        first = target_block(z, columns, t, z.chunks)
        scale = root(position)
        for shift in range(z.shifts):
            part = pl.ds(shift * z.rows + t * BLOCK, BLOCK)
            feature_ref[part, :] = feature_sum(z, pieces, 0, position, first, shift, place_ref, until_ref)
            center = first + F32(z.span * z.slots // 2 - shift * z.span * z.slots)
            feature_scale_ref[part, :] = scale * jnp.exp(-rate * (position - center))


def second_kernel(z, count, *refs):
    me_ref, rate_ref, route_ref, bucket_ref, count2_ref = refs[:5]
    sums_ref, scale_ref, partial_ref, feature_scale_ref, place_ref, until_ref, ranks_ref, from_ref, last_ref = refs[5:14]
    pieces = refs[14 : 14 + count]
    table_ref, feature_ref, rows_ref = refs[14 + count :]
    me = me_ref[0]
    rate = rate_row(rate_ref)
    number = count2_ref[0]

    def pack(g, carry):
        values, _, _ = pack_rows(z, pieces, 1, g, ranks_ref)
        store_rows(z, g, values, from_ref, rows_ref, me, rate)
        return carry

    for g in range(FIXED):
        pack(g, 0)
    lax.fori_loop(FIXED, number, pack, 0)

    def table_block(b, carry):
        part = pl.ds(pl.multiple_of(b * BLOCK, BLOCK), BLOCK)
        value = table_sum(b, sums_ref[part, :], number, rows_ref, from_ref, last_ref)
        table_ref[part, :] = (value * scale_ref[part, :]).astype(BF16)
        return carry

    lax.fori_loop(0, z.slots // BLOCK, table_block, 0)
    columns = own_columns(z, route_ref, bucket_ref)
    for t in range(z.rows // BLOCK):
        position = target_block(z, columns, t, 0)
        first = target_block(z, columns, t, z.chunks)
        total = jnp.zeros((BLOCK, LANES), F32)
        for shift in range(z.shifts):
            part = pl.ds(shift * z.rows + t * BLOCK, BLOCK)
            value = partial_ref[part, :] + feature_sum(z, pieces, 1, position, first, shift, place_ref, until_ref)
            total += value * feature_scale_ref[part, :]
        feature_ref[t * BLOCK : (t + 1) * BLOCK, :] = total.astype(BF16)


def exchange(block):
    return (lax.all_to_all(block, ("key", "shard"), split_axis=0, concat_axis=0, tiled=True),)


def on_device(events, event_weight, route, bucket, segment, decay_rate):
    rows, width = events.shape
    shard_count = lax.axis_size("shard")
    owners = lax.axis_size("key") * shard_count
    slots = segment.shape[0]
    z = Sizes(owners, rows, slots)
    copies = owners
    smem = pl.BlockSpec(memory_space=pltpu.SMEM)
    vmem = pl.BlockSpec(memory_space=pltpu.VMEM)
    grant = pltpu.CompilerParams(vmem_limit_bytes=(16 if owners <= 8 else 44) * 1024 * 1024)
    shape = jax.ShapeDtypeStruct
    route = route.reshape(z.chunks, LANES)
    bucket = bucket.reshape(z.chunks, LANES)
    first, second = pl.pallas_call(
        functools.partial(send_kernel, z),
        out_shape=(
            shape((copies, z.half + z.code_rows, width), BF16),
            shape((copies, z.half, width), BF16),
        ),
        in_specs=[smem] + [vmem] * 5,
        out_specs=(vmem, vmem),
        compiler_params=grant,
        name="weigh",
    )(decay_rate, events, event_weight.reshape(z.chunks, LANES), route, bucket, segment.reshape(slots // LANES, LANES))
    first = exchange(first)
    second = exchange(second)
    me = (lax.axis_index("key") * shard_count + lax.axis_index("shard")).astype(I32).reshape(1)
    lines = z.listed // LANES
    kept = pl.pallas_call(
        functools.partial(first_kernel, z, len(first)),
        out_shape=(
            shape((slots, width), F32),
            shape((slots, width), F32),
            shape((z.shifts * rows, width), F32),
            shape((z.shifts * rows, width), F32),
            shape((owners, 8, LANES), F32),
            shape((owners, 8, LANES), F32),
            shape((owners, 8, LANES), F32),
            shape((lines, LANES), F32),
            shape((lines, LANES), F32),
            shape((1,), I32),
        ),
        in_specs=[smem, smem, vmem, vmem] + [vmem] * len(first),
        out_specs=(vmem,) * 9 + (smem,),
        scratch_shapes=[
            pltpu.VMEM((owners, z.chunks, 8, LANES), F32),
            pltpu.VMEM((z.listed, LANES), BF16),
            pltpu.VMEM((lines, LANES), F32),
            pltpu.VMEM((lines, LANES), F32),
        ],
        compiler_params=grant,
        name="first_half",
    )(me, decay_rate, route, bucket, *first)
    return pl.pallas_call(
        functools.partial(second_kernel, z, len(second)),
        out_shape=(shape((slots, width), BF16), shape((rows, width), BF16)),
        in_specs=[smem, smem, vmem, vmem, smem] + [vmem] * (9 + len(second)),
        out_specs=(vmem, vmem),
        scratch_shapes=[pltpu.VMEM((z.listed, LANES), BF16)],
        compiler_params=grant,
        name="second_half",
    )(me, decay_rate, route, bucket, kept[9], *kept[:9], *second)


def solution(mesh):
    placed = (
        P(("groups", "key", "shard"), "lane"),
        P(("groups", "key", "shard")),
        P(("groups", "key", "shard"), None),
        P(("groups", "key", "shard")),
        P(("groups", "key", "shard")),
        P("lane"),
    )
    return jax.shard_map(
        on_device,
        mesh=mesh,
        in_specs=placed,
        out_specs=(P(("groups", "key", "shard"), "lane"), P(("groups", "key", "shard"), "lane")),
        check_vma=False,
    )
```

```python
import functools
import jax
import jax.numpy as jnp
from jax import lax
from jax.experimental import pallas as pl
from jax.experimental.pallas import tpu as pltpu
from jax.sharding import PartitionSpec as P

LANES = 128
LOW = 7
MASK = 127
F32 = jnp.float32
BF16 = jnp.bfloat16
I32 = jnp.int32
FAR = 1e9
NT = (((1,), (1,)), ((), ()))
BLOCK = 256


class Sizes:
    def __init__(self, owners, rows, slots):
        self.owners, self.rows, self.slots = owners, rows, slots
        self.window = slots // 4
        self.chunks = rows // LANES
        self.user_rows = -(-8 * owners // LANES)
        self.code_rows = -(-(3 * self.chunks + 2 * self.user_rows) // 16) * 16
        self.span = min(owners, 8)
        self.shifts = 1 if owners <= self.span else 2
        self.capacity = 2 * rows // owners
        self.per_group = LANES // self.capacity
        self.groups = owners // self.per_group


def iota(shape, axis):
    return lax.broadcasted_iota(I32, shape, axis)


def ones_where(condition):
    return jnp.where(condition, F32(1), F32(0)).astype(BF16)


def dot(a, b):
    return jnp.dot(a, b, preferred_element_type=F32)


def loop(count, body, carry):
    if count <= 8:
        for i in range(count):
            carry = body(i, carry)
        return carry
    return lax.fori_loop(0, count, body, carry)


def block_of(pieces, s):
    return (pieces[s], 0) if len(pieces) > 1 else (pieces[0], s)


def send_kernel(z, me_ref, rate_ref, events_ref, weight_ref, route_ref, bucket_ref, segment_ref, block_ref, own_ref):
    groups = rate_ref.shape[0]
    lane = iota((1, LANES), 1)
    rate = jnp.full((1, LANES), rate_ref[0], F32)
    for g in range(1, groups):
        rate = jnp.where(lane >= g * (LANES // groups), rate_ref[g], rate)
    route = route_ref[...]
    bucket = bucket_ref[...]
    place = (route * z.slots + bucket).astype(F32)
    first = ((route >> (z.span.bit_length() - 1)) * (z.span * z.slots)).astype(F32)
    me = jnp.full((8 - 1, LANES), me_ref[0], I32).astype(F32)
    own_ref[...] = jnp.concatenate([place, first, rate, me], axis=0)
    spot = place - first - F32(z.span * z.slots // 2)
    columns = jnp.concatenate([weight_ref[...], spot], axis=0).T
    for r in range(z.chunks):
        part = slice(r * LANES, (r + 1) * LANES)
        weighted = (columns[:, r : r + 1] * events_ref[part, :].astype(F32)).astype(BF16)
        grown = weighted.astype(F32) * jnp.exp(columns[:, z.chunks + r : z.chunks + r + 1] * rate)
        block_ref[part, :] = grown.astype(BF16)
    ones = jnp.ones((8, LANES), BF16)
    high, low = [], []
    for u in range(z.user_rows):
        user = iota((LANES, LANES), 0) + u * LANES
        below = jnp.zeros((LANES, LANES), F32)
        for r in range(z.slots // LANES):
            below += jnp.where(segment_ref[r : r + 1, :] < user, F32(1), F32(0))
        count = lax.dot_general(ones, below.astype(BF16), NT, preferred_element_type=F32)[0:1].astype(I32)
        high.append(count >> LOW)
        low.append(count & MASK)
    spare = z.code_rows - 3 * z.chunks - 2 * z.user_rows
    pad = [jnp.zeros((spare, LANES), I32)] if spare else []
    codes = jnp.concatenate([route, bucket >> LOW, bucket & MASK] + high + low + pad, axis=0)
    block_ref[z.rows : z.rows + z.code_rows, :] = codes.astype(F32).astype(BF16)


def gather_kernel(z, count, *refs):
    own_ref = refs[0]
    pieces = refs[1 : 1 + count]
    (
        table_ref, feature_ref,
        place_ref, until_ref, rank_ref, tail_ref, codes_ref, rows_ref, from_ref, last_ref,
    ) = refs[1 + count :]
    rate = own_ref[8:9, :]
    me = own_ref[9:10, :]
    base = me * F32(z.slots)

    def code_tile(s):
        ref, i = block_of(pieces, s)
        return ref[i, z.rows : z.rows + z.code_rows, :].astype(F32)

    def row_block(s):
        ref, i = block_of(pieces, s)
        return ref[i, 0 : z.rows, :]

    starts = []
    for u in range(z.user_rows):
        def add(s, total):
            tile = code_tile(s)
            at = 3 * z.chunks + u
            return total + F32(LANES) * tile[at : at + 1] + tile[at + z.user_rows : at + z.user_rows + 1]

        starts.append(loop(z.owners, add, jnp.zeros((1, LANES), F32)))
    start_columns = [jnp.broadcast_to(row, (8, LANES)).T[:, 0:1] for row in starts]
    steps = []
    for u in range(z.user_rows):
        before = pltpu.roll(starts[u], 1, 1)
        first = starts[u - 1][:, LANES - 1 : LANES] if u else jnp.zeros((1, 1), F32)
        step = (starts[u] - jnp.where(iota((1, LANES), 1) == 0, first, before)).astype(I32)
        pair = [jnp.broadcast_to(step >> LOW, (LANES, LANES)), jnp.broadcast_to(step & MASK, (LANES, LANES))]
        steps.append(jnp.concatenate(pair, axis=0).astype(F32).astype(BF16))

    def root(position):
        total = jnp.zeros((position.shape[0], 2 * LANES), F32)
        for u in range(z.user_rows):
            total += lax.dot_general(ones_where(starts[u] <= position), steps[u], NT, preferred_element_type=F32)
        start = F32(LANES) * total[:, :LANES] + total[:, LANES:]
        return lax.rsqrt(jnp.minimum(position - start, F32(z.window)) + F32(1))

    def decode(s, carry):
        tile = code_tile(s)
        bucket = F32(LANES) * tile[z.chunks : 2 * z.chunks] + tile[2 * z.chunks : 3 * z.chunks]
        place = tile[0 : z.chunks] * F32(z.slots) + bucket
        until = []
        for r in range(z.chunks):
            row = place[r : r + 1]
            after = jnp.full((1, LANES), FAR, F32)
            for column in start_columns:
                users = column[: min(LANES, 8 * z.owners)]
                later = jnp.where(users > row, users, F32(FAR))
                after = jnp.minimum(after, jnp.min(later, axis=0, keepdims=True))
            until.append(jnp.minimum(row + F32(z.window), after - F32(1)))
        until = jnp.concatenate(until, axis=0)
        local = place - base
        near, far = local.astype(I32), (until - base).astype(I32)
        codes = jnp.concatenate([near >> LOW, near & MASK, far >> LOW, far & MASK], axis=0)
        codes_ref[s] = codes.astype(F32)
        spare = jnp.zeros((8 - z.chunks, LANES), F32)
        place_ref[s] = jnp.concatenate([place, spare], axis=0)
        until_ref[s] = jnp.concatenate([until, spare], axis=0)
        own = (local >= 0) & (local < F32(z.slots))
        tail = (local >= F32(-z.window)) & (local < 0)
        rank_ref[s] = jnp.concatenate([jnp.where(own, F32(1), F32(0)), spare], axis=0)
        tail_ref[s] = jnp.concatenate([jnp.where(tail, F32(1), F32(0)), spare], axis=0)
        return carry

    loop(z.owners, decode, 0)

    upper = ones_where(iota((LANES, LANES), 0) < iota((LANES, LANES), 1))
    full = jnp.ones((LANES, LANES), BF16)
    lines = z.owners * 8
    at, by = iota((lines, lines), 0), iota((lines, lines), 1)
    earlier = ones_where(((at >> 3) == (by >> 3)) & (by < at))
    source = iota((lines, LANES), 0) >> 3
    offset = ((source & (z.per_group - 1)) * z.capacity).astype(F32)
    for ref in (rank_ref, tail_ref):
        marked = ref[...].reshape(lines, LANES)
        mark = marked.astype(BF16)
        rank = dot(mark, upper) + dot(earlier, dot(mark, full).astype(BF16)) + offset
        ref[...] = jnp.where(marked > 0, rank, F32(-1)).reshape(z.owners, 8, LANES)

    spots = iota((LANES, LANES), 0).astype(F32)
    code_line = iota((4 * z.chunks, LANES), 0) & (z.chunks - 1)

    def pack(kind, ref, g):
        def add(i, carry):
            values, places = carry
            s = g * z.per_group + i
            ranks = ref[s]
            codes = codes_ref[s]
            hot = jnp.concatenate([ones_where(spots == ranks[r : r + 1]) for r in range(z.chunks)], axis=1)
            wide = [jnp.where(code_line == r, codes, F32(0)).astype(BF16) for r in range(z.chunks)]
            values += dot(hot, row_block(s))
            places += lax.dot_general(jnp.concatenate(wide, axis=1), hot, NT, preferred_element_type=F32)
            return values, places

        zero = (jnp.zeros((LANES, LANES), F32), jnp.zeros((4 * z.chunks, LANES), F32))
        values, places = loop(z.per_group, add, zero)
        line = kind * z.groups + g
        rows_ref[line * LANES : (line + 1) * LANES, :] = values.astype(BF16)
        part = [jnp.sum(places[k * z.chunks : (k + 1) * z.chunks], axis=0, keepdims=True) for k in range(4)]
        from_ref[line : line + 1, :] = F32(LANES) * part[0] + part[1]
        last_ref[line : line + 1, :] = F32(LANES) * part[2] + part[3]

    for kind, ref in enumerate((rank_ref, tail_ref)):
        for g in range(z.groups):
            pack(kind, ref, g)

    middle = F32(z.span * z.slots // 2)
    span_of = lambda owner: (owner.astype(I32) >> (z.span.bit_length() - 1)).astype(F32) * F32(z.span)
    own_offset = (me - span_of(me)) * F32(z.slots) - middle
    tail_offset = (me - span_of(me - F32(1))) * F32(z.slots) - middle
    inner = iota((BLOCK, LANES), 0).astype(F32)
    fall = jnp.exp(-rate * inner)

    def summed(b, kinds):
        masks = []
        for line in range(kinds.start * z.groups, kinds.stop * z.groups):
            begin, end = from_ref[line : line + 1, :], last_ref[line : line + 1, :]
            masks.append(ones_where((inner >= begin - F32(b * BLOCK)) & (inner <= end - F32(b * BLOCK))))
        events = rows_ref[kinds.start * z.groups * LANES : kinds.stop * z.groups * LANES, :]
        return dot(jnp.concatenate(masks, axis=1), events)

    for b in range(z.slots // BLOCK):
        start = F32(b * BLOCK)
        tailed = b * BLOCK < z.window
        value = summed(b, range(0, 2 if tailed and z.shifts == 1 else 1)) * jnp.exp(-rate * (start + own_offset))
        if tailed and z.shifts > 1:
            value += summed(b, range(1, 2)) * jnp.exp(-rate * (start + tail_offset))
        value = value * fall * root(inner + (start + base))
        table_ref[b * BLOCK : (b + 1) * BLOCK, :] = value.astype(BF16)

    columns = own_ref[0:8, :].T
    wide_column = lambda at: jnp.broadcast_to(columns[:, at : at + 1], (LANES, LANES))
    for t in range(z.rows // BLOCK):
        at = t * (BLOCK // LANES)
        position = jnp.concatenate([wide_column(at + k) for k in range(BLOCK // LANES)], axis=0)
        first = jnp.concatenate([wide_column(z.chunks + at + k) for k in range(BLOCK // LANES)], axis=0)
        total = jnp.zeros((BLOCK, LANES), F32)
        for shift in range(z.shifts):
            def add(s, value):
                begin, end = place_ref[s], until_ref[s]
                masks = []
                for r in range(z.chunks):
                    held = (position >= begin[r : r + 1]) & (position <= end[r : r + 1])
                    if z.shifts > 1:
                        inside = begin[r : r + 1] >= first
                        held &= inside if shift == 0 else jnp.logical_not(inside)
                    masks.append(ones_where(held))
                return value + dot(jnp.concatenate(masks, axis=1), row_block(s))

            value = loop(z.owners, add, jnp.zeros((BLOCK, LANES), F32))
            center = first + F32(z.span * z.slots // 2 - shift * z.span * z.slots)
            total += value * jnp.exp(-rate * (position - center))
        feature_ref[t * BLOCK : (t + 1) * BLOCK, :] = (total * root(position)).astype(BF16)


def spread(blocks, axis):
    distance = lax.axis_size(axis) // 2
    while distance:
        pairs = [(i, i ^ distance) for i in range(lax.axis_size(axis))]
        blocks = blocks + [lax.ppermute(block, axis, pairs) for block in blocks]
        distance //= 2
    return blocks


def on_device(events, event_weight, route, bucket, segment, decay_rate):
    rows, width = events.shape
    shard_count = lax.axis_size("shard")
    owners = lax.axis_size("key") * shard_count
    slots = segment.shape[0]
    z = Sizes(owners, rows, slots)
    block_rows = rows + z.code_rows
    smem = pl.BlockSpec(memory_space=pltpu.SMEM)
    vmem = pl.BlockSpec(memory_space=pltpu.VMEM)
    shape = jax.ShapeDtypeStruct
    me = (lax.axis_index("key") * shard_count + lax.axis_index("shard")).astype(I32).reshape(1)
    block, own = pl.pallas_call(
        functools.partial(send_kernel, z),
        out_shape=(shape((block_rows, width), BF16), shape((16, LANES), F32)),
        in_specs=[smem, smem] + [vmem] * 5,
        out_specs=(vmem, vmem),
        compiler_params=pltpu.CompilerParams(vmem_limit_bytes=56 * 1024 * 1024),
        name="weigh",
    )(
        me, decay_rate, events, event_weight.reshape(z.chunks, LANES), route.reshape(z.chunks, LANES),
        bucket.reshape(z.chunks, LANES), segment.reshape(slots // LANES, LANES),
    )
    blocks = spread(spread([block], "key"), "shard")
    if owners > 8:
        blocks = [jnp.concatenate(blocks, axis=0)]
    blocks = [b.reshape(-1, block_rows, width) for b in blocks]
    lines = 2 * z.groups
    return pl.pallas_call(
        functools.partial(gather_kernel, z, len(blocks)),
        out_shape=(shape((slots, width), BF16), shape((rows, width), BF16)),
        in_specs=[vmem] * (1 + len(blocks)),
        out_specs=(vmem, vmem),
        scratch_shapes=[
            pltpu.VMEM((owners, 8, LANES), F32),
            pltpu.VMEM((owners, 8, LANES), F32),
            pltpu.VMEM((owners, 8, LANES), F32),
            pltpu.VMEM((owners, 8, LANES), F32),
            pltpu.VMEM((owners, 4 * z.chunks, LANES), F32),
            pltpu.VMEM((lines * LANES, LANES), BF16),
            pltpu.VMEM((lines, LANES), F32),
            pltpu.VMEM((lines, LANES), F32),
        ],
        compiler_params=pltpu.CompilerParams(vmem_limit_bytes=(16 if owners <= 8 else 48) * 1024 * 1024),
        name="aggregate",
    )(own, *blocks)


def solution(mesh):
    placed = (
        P(("groups", "key", "shard"), "lane"),
        P(("groups", "key", "shard")),
        P(("groups", "key", "shard"), None),
        P(("groups", "key", "shard")),
        P(("groups", "key", "shard")),
        P("lane"),
    )
    return jax.shard_map(
        on_device,
        mesh=mesh,
        in_specs=placed,
        out_specs=(P(("groups", "key", "shard"), "lane"), P(("groups", "key", "shard"), "lane")),
        check_vma=False,
    )
```

```python
import functools
import jax
import jax.numpy as jnp
from jax import lax
from jax.experimental import pallas as pl
from jax.experimental.pallas import tpu as pltpu
from jax.sharding import PartitionSpec as P

LANES = 128
LOW = 7
MASK = 127
F32 = jnp.float32
BF16 = jnp.bfloat16
I32 = jnp.int32
I16 = jnp.int16
FAR = 1e9
NT = (((1,), (1,)), ((), ()))
BLOCK = 256


class Sizes:
    def __init__(self, owners, rows, slots):
        self.owners, self.rows, self.slots = owners, rows, slots
        self.window = slots // 4
        self.chunks = rows // LANES
        self.user_rows = -(-8 * owners // LANES)
        self.code_rows = -(-(3 * self.chunks + 2 * self.user_rows) // 16) * 16
        self.span = min(owners, 8)
        self.shifts = 1 if owners <= self.span else 2
        self.capacity = 2 * rows // owners
        self.per_group = LANES // self.capacity
        self.groups = owners // self.per_group


def iota(shape, axis):
    return lax.broadcasted_iota(I32, shape, axis)


def ones_where(condition):
    return jnp.where(condition, F32(1), F32(0)).astype(BF16)


def dot(a, b):
    return jnp.dot(a, b, preferred_element_type=F32)


def loop(count, body, carry):
    if count <= 8:
        for i in range(count):
            carry = body(i, carry)
        return carry
    return lax.fori_loop(0, count, body, carry)


def send_kernel(z, me_ref, rate_ref, events_ref, weight_ref, route_ref, bucket_ref, segment_ref, block_ref, own_ref):
    groups = rate_ref.shape[0]
    lane = iota((1, LANES), 1)
    rate = jnp.full((1, LANES), rate_ref[0], F32)
    for g in range(1, groups):
        rate = jnp.where(lane >= g * (LANES // groups), rate_ref[g], rate)
    route = route_ref[...]
    bucket = bucket_ref[...]
    place = (route * z.slots + bucket).astype(F32)
    first = ((route >> (z.span.bit_length() - 1)) * (z.span * z.slots)).astype(F32)
    me = jnp.full((8 - 1, LANES), me_ref[0], I32).astype(F32)
    own_ref[0:16, :] = jnp.concatenate([place, first, rate, me], axis=0)
    spot = place - first - F32(z.span * z.slots // 2)
    columns = jnp.concatenate([weight_ref[...], spot], axis=0).T
    for r in range(z.chunks):
        part = slice(r * LANES, (r + 1) * LANES)
        weighted = (columns[:, r : r + 1] * events_ref[part, :].astype(F32)).astype(BF16)
        grown = weighted.astype(F32) * jnp.exp(columns[:, z.chunks + r : z.chunks + r + 1] * rate)
        block_ref[part, :] = grown.astype(BF16)
    ones = jnp.ones((8, LANES), BF16)
    high, low = [], []
    for u in range(z.user_rows):
        user = iota((LANES, LANES), 0) + u * LANES
        below = jnp.zeros((LANES, LANES), F32)
        for r in range(z.slots // LANES):
            below += jnp.where(segment_ref[r : r + 1, :] < user, F32(1), F32(0))
        count = lax.dot_general(ones, below.astype(BF16), NT, preferred_element_type=F32)[0:1]
        own_ref[16 + u : 17 + u, :] = count
        count = count.astype(I32)
        high.append(count >> LOW)
        low.append(count & MASK)
    spare = z.code_rows - 3 * z.chunks - 2 * z.user_rows
    pad = [jnp.zeros((spare, LANES), I32)] if spare else []
    codes = jnp.concatenate([route, bucket >> LOW, bucket & MASK] + high + low + pad, axis=0)
    block_ref[z.rows : z.rows + z.code_rows, :] = codes.astype(F32).astype(BF16)


class Pieces:
    def __init__(self, z, refs):
        self.z, self.refs = z, refs
        self.count = len(refs) if len(refs) != 1 else refs[0].shape[0]
        self.per_group = 1 if len(refs) != 1 else z.per_group
        self.groups = self.count // self.per_group

    def block(self, s):
        return (self.refs[s], 0) if len(self.refs) != 1 else (self.refs[0], s)

    def codes(self, s):
        ref, i = self.block(s)
        return ref[i, self.z.rows : self.z.rows + self.z.code_rows, :].astype(F32)

    def rows(self, s):
        ref, i = self.block(s)
        return ref[i, 0 : self.z.rows, :]

    def place(self, s):
        n, tile = self.z.chunks, self.codes(s)
        return tile[0:n] * F32(self.z.slots) + F32(LANES) * tile[n : 2 * n] + tile[2 * n : 3 * n]

    def below(self, s, u):
        tile, at = self.codes(s), 3 * self.z.chunks + u
        return F32(LANES) * tile[at : at + 1] + tile[at + self.z.user_rows : at + self.z.user_rows + 1]


class Runs:
    def __init__(self, z, starts):
        self.z, self.starts = z, starts
        users = min(LANES, 8 * z.owners)
        self.columns = [jnp.broadcast_to(row, (8, LANES)).T[:users, 0:1] for row in starts]
        self.steps = []
        for u, row in enumerate(starts):
            before = pltpu.roll(row, 1, 1)
            first = starts[u - 1][:, LANES - 1 : LANES] if u else jnp.zeros((1, 1), F32)
            step = (row - jnp.where(iota((1, LANES), 1) == 0, first, before)).astype(I32)
            pair = [jnp.broadcast_to(part, (LANES, LANES)) for part in (step >> LOW, step & MASK)]
            self.steps.append(jnp.concatenate(pair, axis=0).astype(F32).astype(BF16))

    def root(self, position):
        total = jnp.zeros((position.shape[0], 2 * LANES), F32)
        for row, step in zip(self.starts, self.steps):
            total += lax.dot_general(ones_where(row <= position), step, NT, preferred_element_type=F32)
        start = F32(LANES) * total[:, :LANES] + total[:, LANES:]
        return lax.rsqrt(jnp.minimum(position - start, F32(self.z.window)) + F32(1))

    def until(self, row):
        after = jnp.full((1, LANES), FAR, F32)
        for column in self.columns:
            later = jnp.where(column > row, column, F32(FAR))
            after = jnp.minimum(after, jnp.min(later, axis=0, keepdims=True))
        return jnp.minimum(row + F32(self.z.window), after - F32(1))


def pack(z, pieces, base, marks_ref, codes_ref, rows_ref, from_ref):
    if not pieces.count:
        return
    spare = jnp.zeros((8 - z.chunks, LANES), F32)

    def mark(s, carry):
        local = pieces.place(s) - base
        near = local.astype(I32)
        codes_ref[s] = jnp.concatenate([near >> LOW, near & MASK], axis=0).astype(F32)
        own = (local >= 0) & (local < F32(z.slots))
        tail = (local >= F32(-z.window)) & (local < 0)
        marks_ref[0, s] = jnp.concatenate([jnp.where(own, F32(1), F32(0)), spare], axis=0)
        marks_ref[1, s] = jnp.concatenate([jnp.where(tail, F32(1), F32(0)), spare], axis=0)
        return carry

    loop(pieces.count, mark, 0)
    upper = ones_where(iota((LANES, LANES), 0) < iota((LANES, LANES), 1))
    full = jnp.ones((LANES, LANES), BF16)
    lines = pieces.count * 8
    at, by = iota((lines, lines), 0), iota((lines, lines), 1)
    earlier = ones_where(((at >> 3) == (by >> 3)) & (by < at))
    source = iota((lines, LANES), 0) >> 3
    offset = ((source & (pieces.per_group - 1)) * z.capacity).astype(F32)
    for kind in range(2):
        marked = marks_ref[kind].reshape(lines, LANES)
        mark = marked.astype(BF16)
        rank = dot(mark, upper) + dot(earlier, dot(mark, full).astype(BF16)) + offset
        marks_ref[kind] = jnp.where(marked > 0, rank, F32(-1)).reshape(pieces.count, 8, LANES)

    spots = iota((LANES, LANES), 0).astype(F32)
    code_line = iota((2 * z.chunks, LANES), 0) & (z.chunks - 1)
    for kind in range(2):
        for g in range(pieces.groups):

            def add(i, carry):
                values, places = carry
                s = g * pieces.per_group + i
                ranks = marks_ref[kind, s]
                codes = codes_ref[s]
                hot = jnp.concatenate([ones_where(spots == ranks[r : r + 1]) for r in range(z.chunks)], axis=1)
                wide = [jnp.where(code_line == r, codes, F32(0)).astype(BF16) for r in range(z.chunks)]
                values += dot(hot, pieces.rows(s))
                places += lax.dot_general(jnp.concatenate(wide, axis=1), hot, NT, preferred_element_type=F32)
                return values, places

            zero = (jnp.zeros((LANES, LANES), F32), jnp.zeros((2 * z.chunks, LANES), F32))
            values, places = loop(pieces.per_group, add, zero)
            line = kind * pieces.groups + g
            rows_ref[line * LANES : (line + 1) * LANES, :] = values.astype(BF16)
            high = jnp.sum(places[: z.chunks], axis=0, keepdims=True)
            low = jnp.sum(places[z.chunks :], axis=0, keepdims=True)
            from_ref[line : line + 1, :] = F32(LANES) * high + low


def held(position, bounds):
    one, nothing = BF16(1), BF16(0)
    masks = [jnp.where((position >= a) & (position <= b), one, nothing) for a, b in bounds]
    return jnp.concatenate(masks, axis=1)


def anchors(z, me):
    middle = F32(z.span * z.slots // 2)
    span_of = lambda owner: (owner.astype(I32) >> (z.span.bit_length() - 1)).astype(F32) * F32(z.span)
    own = (me - span_of(me)) * F32(z.slots) - middle
    tail = (me - span_of(me - F32(1))) * F32(z.slots) - middle
    return own, tail


def short(row):
    return row.astype(I32).astype(I16)


def early_kernel(z, count, *refs):
    own_ref, pieces = refs[0], Pieces(z, refs[1 : 1 + count])
    sums_ref, scale_ref, rows_ref, from_ref, marks_ref, codes_ref = refs[1 + count :]
    rate, me = own_ref[8:9, :], own_ref[9:10, :]
    runs = Runs(z, [own_ref[16 + u : 17 + u, :] for u in range(z.user_rows)])
    pack(z, pieces, me * F32(z.slots), marks_ref, codes_ref, rows_ref, from_ref)
    own_anchor, _ = anchors(z, me)
    inner = iota((BLOCK, LANES), 0)
    fall = jnp.exp(-rate * inner.astype(F32))
    bounds = []
    for g in range(pieces.groups if pieces.count else 0):
        begin = from_ref[g : g + 1, :]
        bounds.append((short(begin), short(runs.until(begin))))
    for b in range(z.slots // BLOCK):
        part = slice(b * BLOCK, (b + 1) * BLOCK)
        if bounds:
            mask = held((inner + b * BLOCK).astype(I16), bounds)
            sums_ref[part, :] = dot(mask, rows_ref[0 : len(bounds) * LANES, :])
        else:
            sums_ref[part, :] = jnp.zeros((BLOCK, LANES), F32)
        if b * BLOCK >= z.window:
            start = F32(b * BLOCK)
            scale_ref[part, :] = fall * jnp.exp(-rate * (start + own_anchor)) * runs.root(inner.astype(F32) + start)


def late_kernel(z, early, late, *refs):
    own_ref, sums_ref, scale_ref, tail_rows_ref, tail_from_ref = refs[:5]
    blocks = refs[5 : 5 + early + late]
    table_ref, feature_ref, place_ref, until_ref, rows_ref, from_ref, marks_ref, codes_ref = refs[5 + early + late :]
    pieces, last = Pieces(z, blocks), Pieces(z, blocks[early:])
    rate, me = own_ref[8:9, :], own_ref[9:10, :]
    base = me * F32(z.slots)
    starts = []
    for u in range(z.user_rows):
        add = lambda s, total: total + pieces.below(s, u)
        starts.append(loop(pieces.count, add, jnp.zeros((1, LANES), F32)))
    runs = Runs(z, starts)
    pack(z, last, base, marks_ref, codes_ref, rows_ref, from_ref)

    own_anchor, tail_anchor = anchors(z, me)
    inner = iota((BLOCK, LANES), 0)
    fall = jnp.exp(-rate * inner.astype(F32))
    bounds = []
    for ref, first, lines in ((from_ref, 0, 2 * last.groups), (tail_from_ref, early, early)):
        for g in range(first, first + lines):
            begin = ref[g : g + 1, :]
            bounds.append((short(begin), short(runs.until(begin + base) - base)))
    n = last.groups
    for b in range(z.slots // BLOCK):
        part = slice(b * BLOCK, (b + 1) * BLOCK)
        position = (inner + b * BLOCK).astype(I16)
        start = F32(b * BLOCK)
        value = sums_ref[part, :] + dot(held(position, bounds[:n]), rows_ref[0 : n * LANES, :])
        if b * BLOCK >= z.window:
            value = value * scale_ref[part, :]
        else:
            tail = dot(held(position, bounds[n : 2 * n]), rows_ref[n * LANES : 2 * n * LANES, :])
            if early:
                tail += dot(held(position, bounds[2 * n :]), tail_rows_ref[early * LANES : 2 * early * LANES, :])
            own_fall = jnp.exp(-rate * (start + own_anchor))
            if z.shifts == 1:
                value = (value + tail) * own_fall
            else:
                value = value * own_fall + tail * jnp.exp(-rate * (start + tail_anchor))
            value = value * fall * runs.root(inner.astype(F32) + (start + base))
        table_ref[part, :] = value.astype(BF16)

    narrow = z.owners * z.slots <= 32768

    def decode(s, carry):
        place = pieces.place(s)
        until = jnp.concatenate([runs.until(place[r : r + 1]) for r in range(z.chunks)], axis=0)
        if narrow:
            until = jnp.minimum(until, F32(32767))
        spare = jnp.zeros((8 - z.chunks, LANES), F32)
        place_ref[s] = jnp.concatenate([place, spare], axis=0)
        until_ref[s] = jnp.concatenate([until, spare], axis=0)
        return carry

    loop(pieces.count, decode, 0)
    columns = own_ref[0:8, :].T
    wide_column = lambda at: jnp.broadcast_to(columns[:, at : at + 1], (LANES, LANES))
    for t in range(z.rows // BLOCK):
        at = t * (BLOCK // LANES)
        position = jnp.concatenate([wide_column(at + k) for k in range(BLOCK // LANES)], axis=0)
        first = jnp.concatenate([wide_column(z.chunks + at + k) for k in range(BLOCK // LANES)], axis=0)
        point = short(position) if narrow else position
        total = jnp.zeros((BLOCK, LANES), F32)
        for shift in range(z.shifts):

            def add(s, value):
                begin, end = place_ref[s], until_ref[s]
                bounds = [(begin[r : r + 1], end[r : r + 1]) for r in range(z.chunks)]
                if narrow:
                    mask = held(point, [(short(a), short(b)) for a, b in bounds])
                else:
                    masks = []
                    for a, b in bounds:
                        inside = a >= first if shift == 0 else a < first
                        masks.append(ones_where((point >= a) & (point <= b) & inside))
                    mask = jnp.concatenate(masks, axis=1)
                return value + dot(mask, pieces.rows(s))

            value = loop(pieces.count, add, jnp.zeros((BLOCK, LANES), F32))
            center = first + F32(z.span * z.slots // 2 - shift * z.span * z.slots)
            total += value * jnp.exp(-rate * (position - center))
        feature_ref[t * BLOCK : (t + 1) * BLOCK, :] = (total * runs.root(position)).astype(BF16)


def swap(block, axis, distance):
    return lax.ppermute(block, axis, [(i, i ^ distance) for i in range(lax.axis_size(axis))])


def spread(blocks, axis, early=None):
    distance = lax.axis_size(axis) // 2
    while distance:
        for block in list(blocks):
            if early is not None and block is not blocks[0]:
                block, early = lax.optimization_barrier((block, early))
            blocks = blocks + [swap(block, axis, distance)]
        distance //= 2
    return blocks, early


def on_device(events, event_weight, route, bucket, segment, decay_rate):
    rows, width = events.shape
    shard_count = lax.axis_size("shard")
    owners = lax.axis_size("key") * shard_count
    slots = segment.shape[0]
    z = Sizes(owners, rows, slots)
    block_rows = rows + z.code_rows
    smem = pl.BlockSpec(memory_space=pltpu.SMEM)
    vmem = pl.BlockSpec(memory_space=pltpu.VMEM)
    shape = jax.ShapeDtypeStruct
    me = (lax.axis_index("key") * shard_count + lax.axis_index("shard")).astype(I32).reshape(1)
    block, own = pl.pallas_call(
        functools.partial(send_kernel, z),
        out_shape=(shape((block_rows, width), BF16), shape((16 + z.user_rows + 7, LANES), F32)),
        in_specs=[smem, smem] + [vmem] * 5,
        out_specs=(vmem, vmem),
        compiler_params=pltpu.CompilerParams(vmem_limit_bytes=56 * 1024 * 1024),
        name="weigh",
    )(
        me, decay_rate, events, event_weight.reshape(z.chunks, LANES), route.reshape(z.chunks, LANES),
        bucket.reshape(z.chunks, LANES), segment.reshape(slots // LANES, LANES),
    )
    if shard_count == 2:
        near = swap(block, "shard", 1)
        blocks, near = spread([block], "key", near)
        across = [swap(b, "shard", 1) for b in blocks[1:]]
        early, late = blocks + [near] + across[1:-1], across[:1] + across[-1:]
    else:
        blocks, _ = spread([block], "key")
        blocks, _ = spread(blocks, "shard")
        early, late = [], [jnp.concatenate(blocks, axis=0)]
    early = [b.reshape(-1, block_rows, width) for b in early]
    late = [b.reshape(-1, block_rows, width) for b in late]
    lines = max(8, 2 * len(early))
    late_lines = 2 * (len(late) if len(late) > 1 else z.groups)
    late_count = sum(b.shape[0] for b in late)
    grant = pltpu.CompilerParams(vmem_limit_bytes=(16 if owners <= 8 else 48) * 1024 * 1024)
    kept = pl.pallas_call(
        functools.partial(early_kernel, z, len(early)),
        out_shape=(
            shape((slots, width), F32),
            shape((slots, width), F32),
            shape((lines * LANES, LANES), BF16),
            shape((lines, LANES), F32),
        ),
        in_specs=[vmem] * (1 + len(early)),
        out_specs=(vmem,) * 4,
        scratch_shapes=[
            pltpu.VMEM((2, max(1, len(early)), 8, LANES), F32),
            pltpu.VMEM((max(1, len(early)), 2 * z.chunks, LANES), F32),
        ],
        compiler_params=grant,
        cost_estimate=pl.CostEstimate(flops=2 * slots * rows * 6 * LANES, bytes_accessed=6 * slots * LANES, transcendentals=0),
        name="early_sums",
    )(own, *early)
    return pl.pallas_call(
        functools.partial(late_kernel, z, len(early), len(late)),
        out_shape=(shape((slots, width), BF16), shape((rows, width), BF16)),
        in_specs=[vmem] * (5 + len(early) + len(late)),
        out_specs=(vmem, vmem),
        scratch_shapes=[
            pltpu.VMEM((owners, 8, LANES), F32),
            pltpu.VMEM((owners, 8, LANES), F32),
            pltpu.VMEM((late_lines * LANES, LANES), BF16),
            pltpu.VMEM((late_lines, LANES), F32),
            pltpu.VMEM((2, late_count, 8, LANES), F32),
            pltpu.VMEM((late_count, 2 * z.chunks, LANES), F32),
        ],
        compiler_params=grant,
        name="table_and_rows",
    )(own, *kept, *early, *late)


def solution(mesh):
    placed = (
        P(("groups", "key", "shard"), "lane"),
        P(("groups", "key", "shard")),
        P(("groups", "key", "shard"), None),
        P(("groups", "key", "shard")),
        P(("groups", "key", "shard")),
        P("lane"),
    )
    return jax.shard_map(
        on_device,
        mesh=mesh,
        in_specs=placed,
        out_specs=(P(("groups", "key", "shard"), "lane"), P(("groups", "key", "shard"), "lane")),
        check_vma=False,
    )
```

```python
import functools
import jax
import jax.numpy as jnp
from jax import lax
from jax.experimental import pallas as pl
from jax.experimental.pallas import tpu as pltpu
from jax.sharding import PartitionSpec as P

LANES = 128
LOW = 7
MASK = 127
F32 = jnp.float32
BF16 = jnp.bfloat16
I32 = jnp.int32
I16 = jnp.int16
FAR = 1e9
NT = (((1,), (1,)), ((), ()))
BLOCK = 256
COST = 1 << 26


class Sizes:
    def __init__(self, owners, rows, slots):
        self.owners, self.rows, self.slots = owners, rows, slots
        self.window = slots // 4
        self.chunks = rows // LANES
        self.user_rows = -(-8 * owners // LANES)
        self.code_rows = -(-(3 * self.chunks + 2 * self.user_rows) // 16) * 16
        self.span = min(owners, 8)
        self.shifts = 1 if owners <= self.span else 2
        self.capacity = 2 * rows // owners
        self.per_group = LANES // self.capacity
        self.groups = owners // self.per_group


def iota(shape, axis):
    return lax.broadcasted_iota(I32, shape, axis)


def ones_where(condition):
    return jnp.where(condition, F32(1), F32(0)).astype(BF16)


def dot(a, b):
    return jnp.dot(a, b, preferred_element_type=F32)


def loop(count, body, carry):
    if count <= 8:
        for i in range(count):
            carry = body(i, carry)
        return carry
    return lax.fori_loop(0, count, body, carry)


def send_kernel(z, me_ref, rate_ref, events_ref, weight_ref, route_ref, bucket_ref, segment_ref, block_ref, first_ref, second_ref, own_ref):
    groups = rate_ref.shape[0]
    lane = iota((1, LANES), 1)
    rate = jnp.full((1, LANES), rate_ref[0], F32)
    for g in range(1, groups):
        rate = jnp.where(lane >= g * (LANES // groups), rate_ref[g], rate)
    route = route_ref[...]
    bucket = bucket_ref[...]
    place = (route * z.slots + bucket).astype(F32)
    first = ((route >> (z.span.bit_length() - 1)) * (z.span * z.slots)).astype(F32)
    me = jnp.full((8 - 1, LANES), me_ref[0], I32).astype(F32)
    own_ref[0:16, :] = jnp.concatenate([place, first, rate, me], axis=0)
    spot = place - first - F32(z.span * z.slots // 2)
    columns = jnp.concatenate([weight_ref[...], spot], axis=0).T
    for r in range(z.chunks):
        part = slice(r * LANES, (r + 1) * LANES)
        weighted = (columns[:, r : r + 1] * events_ref[part, :].astype(F32)).astype(BF16)
        grown = weighted.astype(F32) * jnp.exp(columns[:, z.chunks + r : z.chunks + r + 1] * rate)
        grown = grown.astype(BF16)
        block_ref[part, :] = grown
        ref = first_ref if r < z.chunks // 2 else second_ref
        at = r % (z.chunks // 2) * LANES
        ref[at : at + LANES, :] = grown
    ones = jnp.ones((8, LANES), BF16)
    high, low = [], []
    for u in range(z.user_rows):
        user = iota((LANES, LANES), 0) + u * LANES
        below = jnp.zeros((LANES, LANES), F32)
        for r in range(z.slots // LANES):
            below += jnp.where(segment_ref[r : r + 1, :] < user, F32(1), F32(0))
        count = lax.dot_general(ones, below.astype(BF16), NT, preferred_element_type=F32)[0:1]
        own_ref[16 + u : 17 + u, :] = count
        count = count.astype(I32)
        high.append(count >> LOW)
        low.append(count & MASK)
    spare = z.code_rows - 3 * z.chunks - 2 * z.user_rows
    pad = [jnp.zeros((spare, LANES), I32)] if spare else []
    codes = jnp.concatenate([route, bucket >> LOW, bucket & MASK] + high + low + pad, axis=0)
    codes = codes.astype(F32).astype(BF16)
    block_ref[z.rows : z.rows + z.code_rows, :] = codes
    first_ref[z.rows // 2 : z.rows // 2 + z.code_rows, :] = codes


class Pieces:
    def __init__(self, z, form, refs):
        self.z, refs = z, list(refs)
        self.parts = [[refs.pop(0) for _ in range(n)] for n in form]
        self.count = len(form) if len(form) != 1 else self.parts[0][0].shape[0]
        self.per_group = 1 if len(form) != 1 else z.per_group
        self.groups = self.count // self.per_group

    def block(self, s):
        return (self.parts[s], 0) if len(self.parts) != 1 else (self.parts[0], s)

    def codes(self, s):
        parts, i = self.block(s)
        first = parts[0].shape[1] - self.z.code_rows
        return parts[0][i, first : first + self.z.code_rows, :].astype(F32)

    def rows(self, s):
        parts, i = self.block(s)
        first = parts[0][i, 0 : parts[0].shape[1] - self.z.code_rows, :]
        return jnp.concatenate([first] + [part[i] for part in parts[1:]], axis=0)

    def place(self, s):
        n, tile = self.z.chunks, self.codes(s)
        return tile[0:n] * F32(self.z.slots) + F32(LANES) * tile[n : 2 * n] + tile[2 * n : 3 * n]

    def below(self, s, u):
        tile, at = self.codes(s), 3 * self.z.chunks + u
        return F32(LANES) * tile[at : at + 1] + tile[at + self.z.user_rows : at + self.z.user_rows + 1]


class Runs:
    def __init__(self, z, starts):
        self.z, self.starts = z, starts
        users = min(LANES, 8 * z.owners)
        self.columns = [jnp.broadcast_to(row, (8, LANES)).T[:users, 0:1] for row in starts]
        self.steps = []
        for u, row in enumerate(starts):
            before = pltpu.roll(row, 1, 1)
            first = starts[u - 1][:, LANES - 1 : LANES] if u else jnp.zeros((1, 1), F32)
            step = (row - jnp.where(iota((1, LANES), 1) == 0, first, before)).astype(I32)
            pair = [jnp.broadcast_to(part, (LANES, LANES)) for part in (step >> LOW, step & MASK)]
            self.steps.append(jnp.concatenate(pair, axis=0).astype(F32).astype(BF16))

    def root(self, position):
        total = jnp.zeros((position.shape[0], 2 * LANES), F32)
        for row, step in zip(self.starts, self.steps):
            total += lax.dot_general(ones_where(row <= position), step, NT, preferred_element_type=F32)
        start = F32(LANES) * total[:, :LANES] + total[:, LANES:]
        return lax.rsqrt(jnp.minimum(position - start, F32(self.z.window)) + F32(1))

    def until(self, row):
        after = jnp.full((1, LANES), FAR, F32)
        for column in self.columns:
            later = jnp.where(column > row, column, F32(FAR))
            after = jnp.minimum(after, jnp.min(later, axis=0, keepdims=True))
        return jnp.minimum(row + F32(self.z.window), after - F32(1))


def pack(z, pieces, base, marks_ref, codes_ref, rows_ref, from_ref):
    if not pieces.count:
        return
    spare = jnp.zeros((8 - z.chunks, LANES), F32)

    def mark(s, carry):
        local = pieces.place(s) - base
        near = local.astype(I32)
        codes_ref[s] = jnp.concatenate([near >> LOW, near & MASK], axis=0).astype(F32)
        own = (local >= 0) & (local < F32(z.slots))
        tail = (local >= F32(-z.window)) & (local < 0)
        marks_ref[0, s] = jnp.concatenate([jnp.where(own, F32(1), F32(0)), spare], axis=0)
        marks_ref[1, s] = jnp.concatenate([jnp.where(tail, F32(1), F32(0)), spare], axis=0)
        return carry

    loop(pieces.count, mark, 0)
    upper = ones_where(iota((LANES, LANES), 0) < iota((LANES, LANES), 1))
    full = jnp.ones((LANES, LANES), BF16)
    lines = pieces.count * 8
    at, by = iota((lines, lines), 0), iota((lines, lines), 1)
    earlier = ones_where(((at >> 3) == (by >> 3)) & (by < at))
    source = iota((lines, LANES), 0) >> 3
    offset = ((source & (pieces.per_group - 1)) * z.capacity).astype(F32)
    for kind in range(2):
        marked = marks_ref[kind].reshape(lines, LANES)
        mark = marked.astype(BF16)
        rank = dot(mark, upper) + dot(earlier, dot(mark, full).astype(BF16)) + offset
        marks_ref[kind] = jnp.where(marked > 0, rank, F32(-1)).reshape(pieces.count, 8, LANES)

    spots = iota((LANES, LANES), 0).astype(F32)
    code_line = iota((2 * z.chunks, LANES), 0) & (z.chunks - 1)
    for kind in range(2):
        for g in range(pieces.groups):

            def add(i, carry):
                values, places = carry
                s = g * pieces.per_group + i
                ranks = marks_ref[kind, s]
                codes = codes_ref[s]
                hot = jnp.concatenate([ones_where(spots == ranks[r : r + 1]) for r in range(z.chunks)], axis=1)
                wide = [jnp.where(code_line == r, codes, F32(0)).astype(BF16) for r in range(z.chunks)]
                values += dot(hot, pieces.rows(s))
                places += lax.dot_general(jnp.concatenate(wide, axis=1), hot, NT, preferred_element_type=F32)
                return values, places

            zero = (jnp.zeros((LANES, LANES), F32), jnp.zeros((2 * z.chunks, LANES), F32))
            values, places = loop(pieces.per_group, add, zero)
            line = kind * pieces.groups + g
            rows_ref[line * LANES : (line + 1) * LANES, :] = values.astype(BF16)
            high = jnp.sum(places[: z.chunks], axis=0, keepdims=True)
            low = jnp.sum(places[z.chunks :], axis=0, keepdims=True)
            from_ref[line : line + 1, :] = F32(LANES) * high + low


def held(position, bounds):
    one, nothing = BF16(1), BF16(0)
    masks = [jnp.where((position >= a) & (position <= b), one, nothing) for a, b in bounds]
    return jnp.concatenate(masks, axis=1)


def anchors(z, me):
    middle = F32(z.span * z.slots // 2)
    span_of = lambda owner: (owner.astype(I32) >> (z.span.bit_length() - 1)).astype(F32) * F32(z.span)
    own = (me - span_of(me)) * F32(z.slots) - middle
    tail = (me - span_of(me - F32(1))) * F32(z.slots) - middle
    return own, tail


def short(row):
    return row.astype(I32).astype(I16)


def early_kernel(z, form, before, *refs):
    count = sum(form)
    own_ref, pieces = refs[0], Pieces(z, form, refs[1 : 1 + count])
    refs = refs[1 + count :]
    if before:
        before_ref, sums_ref, rows_ref, from_ref, marks_ref, codes_ref = refs
    else:
        sums_ref, scale_ref, rows_ref, from_ref, marks_ref, codes_ref = refs
    rate, me = own_ref[8:9, :], own_ref[9:10, :]
    runs = Runs(z, [own_ref[16 + u : 17 + u, :] for u in range(z.user_rows)])
    pack(z, pieces, me * F32(z.slots), marks_ref, codes_ref, rows_ref, from_ref)
    own_anchor, _ = anchors(z, me)
    inner = iota((BLOCK, LANES), 0)
    fall = jnp.exp(-rate * inner.astype(F32))
    bounds = []
    for g in range(pieces.groups if pieces.count else 0):
        begin = from_ref[g : g + 1, :]
        bounds.append((short(begin), short(runs.until(begin))))
    for b in range(z.slots // BLOCK):
        part = slice(b * BLOCK, (b + 1) * BLOCK)
        if bounds:
            mask = held((inner + b * BLOCK).astype(I16), bounds)
            value = dot(mask, rows_ref[0 : len(bounds) * LANES, :])
        else:
            value = jnp.zeros((BLOCK, LANES), F32)
        sums_ref[part, :] = value + before_ref[part, :] if before else value
        if b * BLOCK >= z.window and not before:
            start = F32(b * BLOCK)
            scale_ref[part, :] = fall * jnp.exp(-rate * (start + own_anchor)) * runs.root(inner.astype(F32) + start)


def late_kernel(z, earlier, form, late, *refs):
    own_ref, sums_ref, scale_ref = refs[:3]
    tails = [refs[3 + 2 * i : 5 + 2 * i] for i in range(len(earlier))]
    refs = refs[3 + 2 * len(earlier) :]
    count = sum(form)
    table_ref, feature_ref, place_ref, until_ref, rows_ref, from_ref, marks_ref, codes_ref = refs[count:]
    pieces, last = Pieces(z, form, refs[:count]), Pieces(z, form[-late:], refs[count - sum(form[-late:]) : count])
    rate, me = own_ref[8:9, :], own_ref[9:10, :]
    base = me * F32(z.slots)
    starts = []
    for u in range(z.user_rows):
        add = lambda s, total: total + pieces.below(s, u)
        starts.append(loop(pieces.count, add, jnp.zeros((1, LANES), F32)))
    runs = Runs(z, starts)
    pack(z, last, base, marks_ref, codes_ref, rows_ref, from_ref)

    own_anchor, tail_anchor = anchors(z, me)
    inner = iota((BLOCK, LANES), 0)
    fall = jnp.exp(-rate * inner.astype(F32))
    bounds = []
    listed = [(from_ref, 0, 2 * last.groups)] + [(ref, count, count) for (_, ref), count in zip(tails, earlier)]
    for ref, first, lines in listed:
        for g in range(first, first + lines):
            begin = ref[g : g + 1, :]
            bounds.append((short(begin), short(runs.until(begin + base) - base)))
    n = last.groups
    for b in range(z.slots // BLOCK):
        part = slice(b * BLOCK, (b + 1) * BLOCK)
        position = (inner + b * BLOCK).astype(I16)
        start = F32(b * BLOCK)
        value = sums_ref[part, :] + dot(held(position, bounds[:n]), rows_ref[0 : n * LANES, :])
        if b * BLOCK >= z.window:
            value = value * scale_ref[part, :]
        else:
            tail = dot(held(position, bounds[n : 2 * n]), rows_ref[n * LANES : 2 * n * LANES, :])
            at = 2 * n
            for (ref, _), count in zip(tails, earlier):
                tail += dot(held(position, bounds[at : at + count]), ref[count * LANES : 2 * count * LANES, :])
                at += count
            own_fall = jnp.exp(-rate * (start + own_anchor))
            if z.shifts == 1:
                value = (value + tail) * own_fall
            else:
                value = value * own_fall + tail * jnp.exp(-rate * (start + tail_anchor))
            value = value * fall * runs.root(inner.astype(F32) + (start + base))
        table_ref[part, :] = value.astype(BF16)

    narrow = z.owners * z.slots <= 32768

    def decode(s, carry):
        place = pieces.place(s)
        until = jnp.concatenate([runs.until(place[r : r + 1]) for r in range(z.chunks)], axis=0)
        if narrow:
            until = jnp.minimum(until, F32(32767))
        spare = jnp.zeros((8 - z.chunks, LANES), F32)
        place_ref[s] = jnp.concatenate([place, spare], axis=0)
        until_ref[s] = jnp.concatenate([until, spare], axis=0)
        return carry

    loop(pieces.count, decode, 0)
    columns = own_ref[0:8, :].T
    wide_column = lambda at: jnp.broadcast_to(columns[:, at : at + 1], (LANES, LANES))
    for t in range(z.rows // BLOCK):
        at = t * (BLOCK // LANES)
        position = jnp.concatenate([wide_column(at + k) for k in range(BLOCK // LANES)], axis=0)
        first = jnp.concatenate([wide_column(z.chunks + at + k) for k in range(BLOCK // LANES)], axis=0)
        point = short(position) if narrow else position
        total = jnp.zeros((BLOCK, LANES), F32)
        for shift in range(z.shifts):

            def add(s, value):
                begin, end = place_ref[s], until_ref[s]
                bounds = [(begin[r : r + 1], end[r : r + 1]) for r in range(z.chunks)]
                if narrow:
                    mask = held(point, [(short(a), short(b)) for a, b in bounds])
                else:
                    masks = []
                    for a, b in bounds:
                        inside = a >= first if shift == 0 else a < first
                        masks.append(ones_where((point >= a) & (point <= b) & inside))
                    mask = jnp.concatenate(masks, axis=1)
                return value + dot(mask, pieces.rows(s))

            value = loop(pieces.count, add, jnp.zeros((BLOCK, LANES), F32))
            center = first + F32(z.span * z.slots // 2 - shift * z.span * z.slots)
            total += value * jnp.exp(-rate * (position - center))
        feature_ref[t * BLOCK : (t + 1) * BLOCK, :] = (total * runs.root(position)).astype(BF16)


def swap(block, axis, distance):
    return lax.ppermute(block, axis, [(i, i ^ distance) for i in range(lax.axis_size(axis))])


def spread(blocks, axis):
    distance = lax.axis_size(axis) // 2
    while distance:
        blocks = blocks + [swap(block, axis, distance) for block in blocks]
        distance //= 2
    return blocks


def on_device(events, event_weight, route, bucket, segment, decay_rate):
    rows, width = events.shape
    key_count, shard_count = lax.axis_size("key"), lax.axis_size("shard")
    owners = key_count * shard_count
    slots = segment.shape[0]
    z = Sizes(owners, rows, slots)
    block_rows = rows + z.code_rows
    smem = pl.BlockSpec(memory_space=pltpu.SMEM)
    vmem = pl.BlockSpec(memory_space=pltpu.VMEM)
    shape = jax.ShapeDtypeStruct
    grant = pltpu.CompilerParams(vmem_limit_bytes=(16 if owners <= 8 else 48) * 1024 * 1024)
    me = (lax.axis_index("key") * shard_count + lax.axis_index("shard")).astype(I32).reshape(1)
    half = rows // 2
    block, upper, lower, own = pl.pallas_call(
        functools.partial(send_kernel, z),
        out_shape=(
            shape((block_rows, width), BF16),
            shape((half + z.code_rows, width), BF16),
            shape((half, width), BF16),
            shape((16 + z.user_rows + 7, LANES), F32),
        ),
        in_specs=[smem, smem] + [vmem] * 5,
        out_specs=(vmem,) * 4,
        compiler_params=pltpu.CompilerParams(vmem_limit_bytes=56 * 1024 * 1024),
        name="weigh",
    )(
        me, decay_rate, events, event_weight.reshape(z.chunks, LANES), route.reshape(z.chunks, LANES),
        bucket.reshape(z.chunks, LANES), segment.reshape(slots // LANES, LANES),
    )

    def flat(blocks):
        return [part[None] if part.ndim == 2 else part for parts in blocks for part in parts]

    def sums(blocks, before=()):
        blocks, form, count = flat(blocks), tuple(map(len, blocks)), len(blocks)
        lines = max(8, 2 * count)
        whole = shape((slots, width), F32)
        kept = (shape((lines * LANES, LANES), BF16), shape((lines, LANES), F32))
        return pl.pallas_call(
            functools.partial(early_kernel, z, form, len(before)),
            out_shape=((whole,) if before else (whole, whole)) + kept,
            in_specs=[vmem] * (1 + len(blocks) + len(before)),
            out_specs=(vmem,) * (3 if before else 4),
            scratch_shapes=[
                pltpu.VMEM((2, max(1, count), 8, LANES), F32),
                pltpu.VMEM((max(1, count), 2 * z.chunks, LANES), F32),
            ],
            compiler_params=grant,
            cost_estimate=pl.CostEstimate(flops=COST * count, bytes_accessed=0, transcendentals=0),
            name="more_sums" if before else "first_sums",
        )(own, *blocks, *before)

    if (key_count, shard_count) == (4, 2):
        tie = lax.optimization_barrier
        far = [swap(upper, "key", 2)]
        side = swap(block, "shard", 1)
        near = swap(block, "key", 1)
        far.append(swap(lower, "key", 2))
        side_near = swap(near, "shard", 1)
        first = [(block,), (side,)]
        total, scale, *tail = sums(first)
        last = [swap(far[0], "key", 1)]
        far[1], total = tie((far[1], total))
        last.append(swap(far[1], "key", 1))
        second = [far, (near,), (side_near,), last]
        late = [[swap(part, "shard", 1) for part in parts] for parts in (far, last)]
        total, *tail2 = sums(second, (total,))
        early, earlier, tails = first + second, (2, 4), tail + tail2
    else:
        blocks = spread(spread([block], "key"), "shard")
        total, scale, *_ = sums([])
        early, earlier, tails = [], (), []
        late = [(jnp.concatenate(blocks, axis=0).reshape(owners, block_rows, width),)]
    late_lines = 2 * (len(late) if len(late) > 1 else z.groups)
    late_count = len(late) if len(late) > 1 else owners
    form = tuple(map(len, early + late))
    return pl.pallas_call(
        functools.partial(late_kernel, z, earlier, form, len(late)),
        out_shape=(shape((slots, width), BF16), shape((rows, width), BF16)),
        in_specs=[vmem] * (3 + len(tails) + sum(form)),
        out_specs=(vmem, vmem),
        scratch_shapes=[
            pltpu.VMEM((owners, 8, LANES), F32),
            pltpu.VMEM((owners, 8, LANES), F32),
            pltpu.VMEM((late_lines * LANES, LANES), BF16),
            pltpu.VMEM((late_lines, LANES), F32),
            pltpu.VMEM((2, late_count, 8, LANES), F32),
            pltpu.VMEM((late_count, 2 * z.chunks, LANES), F32),
        ],
        compiler_params=grant,
        name="table_and_rows",
    )(own, total, scale, *tails, *flat(early + late))


def solution(mesh):
    placed = (
        P(("groups", "key", "shard"), "lane"),
        P(("groups", "key", "shard")),
        P(("groups", "key", "shard"), None),
        P(("groups", "key", "shard")),
        P(("groups", "key", "shard")),
        P("lane"),
    )
    return jax.shard_map(
        on_device,
        mesh=mesh,
        in_specs=placed,
        out_specs=(P(("groups", "key", "shard"), "lane"), P(("groups", "key", "shard"), "lane")),
        check_vma=False,
    )
```

```python
import functools
import jax
import jax.numpy as jnp
from jax import lax
from jax.experimental import pallas as pl
from jax.experimental.pallas import tpu as pltpu
from jax.sharding import PartitionSpec as P

LANES = 128
LOW = 7
MASK = 127
F32 = jnp.float32
BF16 = jnp.bfloat16
I32 = jnp.int32
I16 = jnp.int16
FAR = 1e9
NT = (((1,), (1,)), ((), ()))
BLOCK = 256
COST = 1


class Sizes:
    def __init__(self, owners, rows, slots):
        self.owners, self.rows, self.slots = owners, rows, slots
        self.window = slots // 4
        self.chunks = rows // LANES
        self.user_rows = -(-8 * owners // LANES)
        self.code_rows = -(-(3 * self.chunks + 2 * self.user_rows) // 16) * 16
        self.span = min(owners, 8)
        self.shifts = 1 if owners <= self.span else 2
        self.capacity = 2 * rows // owners
        self.per_group = LANES // self.capacity
        self.groups = owners // self.per_group


def iota(shape, axis):
    return lax.broadcasted_iota(I32, shape, axis)


def ones_where(condition):
    return jnp.where(condition, F32(1), F32(0)).astype(BF16)


def dot(a, b):
    return jnp.dot(a, b, preferred_element_type=F32)


def loop(count, body, carry):
    if count <= 8:
        for i in range(count):
            carry = body(i, carry)
        return carry
    return lax.fori_loop(0, count, body, carry)


def send_kernel(z, me_ref, rate_ref, events_ref, weight_ref, route_ref, bucket_ref, segment_ref, block_ref, own_ref):
    groups = rate_ref.shape[0]
    lane = iota((1, LANES), 1)
    rate = jnp.full((1, LANES), rate_ref[0], F32)
    for g in range(1, groups):
        rate = jnp.where(lane >= g * (LANES // groups), rate_ref[g], rate)
    route = route_ref[...]
    bucket = bucket_ref[...]
    place = (route * z.slots + bucket).astype(F32)
    first = ((route >> (z.span.bit_length() - 1)) * (z.span * z.slots)).astype(F32)
    me = jnp.full((8 - 1, LANES), me_ref[0], I32).astype(F32)
    own_ref[0:16, :] = jnp.concatenate([place, first, rate, me], axis=0)
    spot = place - first - F32(z.span * z.slots // 2)
    columns = jnp.concatenate([weight_ref[...], spot], axis=0).T
    for r in range(z.chunks):
        part = slice(r * LANES, (r + 1) * LANES)
        weighted = (columns[:, r : r + 1] * events_ref[part, :].astype(F32)).astype(BF16)
        grown = weighted.astype(F32) * jnp.exp(columns[:, z.chunks + r : z.chunks + r + 1] * rate)
        block_ref[part, :] = grown.astype(BF16)
    ones = jnp.ones((8, LANES), BF16)
    high, low = [], []
    for u in range(z.user_rows):
        user = iota((LANES, LANES), 0) + u * LANES
        below = jnp.zeros((LANES, LANES), F32)
        for r in range(z.slots // LANES):
            below += jnp.where(segment_ref[r : r + 1, :] < user, F32(1), F32(0))
        count = lax.dot_general(ones, below.astype(BF16), NT, preferred_element_type=F32)[0:1]
        own_ref[16 + u : 17 + u, :] = count
        count = count.astype(I32)
        high.append(count >> LOW)
        low.append(count & MASK)
    spare = z.code_rows - 3 * z.chunks - 2 * z.user_rows
    pad = [jnp.zeros((spare, LANES), I32)] if spare else []
    codes = jnp.concatenate([route, bucket >> LOW, bucket & MASK] + high + low + pad, axis=0)
    block_ref[z.rows : z.rows + z.code_rows, :] = codes.astype(F32).astype(BF16)


class Pieces:
    def __init__(self, z, form, refs):
        self.z, refs = z, list(refs)
        self.parts = [[refs.pop(0) for _ in range(n)] for n in form]
        self.count = len(form) if len(form) != 1 else self.parts[0][0].shape[0]
        self.per_group = 1 if len(form) != 1 else z.per_group
        self.groups = self.count // self.per_group

    def block(self, s):
        return (self.parts[s], 0) if len(self.parts) != 1 else (self.parts[0], s)

    def codes(self, s):
        parts, i = self.block(s)
        first = parts[0].shape[1] - self.z.code_rows
        return parts[0][i, first : first + self.z.code_rows, :].astype(F32)

    def rows(self, s):
        parts, i = self.block(s)
        first = parts[0][i, 0 : parts[0].shape[1] - self.z.code_rows, :]
        return jnp.concatenate([first] + [part[i] for part in parts[1:]], axis=0)

    def place(self, s):
        n, tile = self.z.chunks, self.codes(s)
        return tile[0:n] * F32(self.z.slots) + F32(LANES) * tile[n : 2 * n] + tile[2 * n : 3 * n]

    def below(self, s, u):
        tile, at = self.codes(s), 3 * self.z.chunks + u
        return F32(LANES) * tile[at : at + 1] + tile[at + self.z.user_rows : at + self.z.user_rows + 1]


class Runs:
    def __init__(self, z, starts):
        self.z, self.starts = z, starts
        users = min(LANES, 8 * z.owners)
        self.columns = [jnp.broadcast_to(row, (8, LANES)).T[:users, 0:1] for row in starts]
        self.steps = []
        for u, row in enumerate(starts):
            before = pltpu.roll(row, 1, 1)
            first = starts[u - 1][:, LANES - 1 : LANES] if u else jnp.zeros((1, 1), F32)
            step = (row - jnp.where(iota((1, LANES), 1) == 0, first, before)).astype(I32)
            pair = [jnp.broadcast_to(part, (LANES, LANES)) for part in (step >> LOW, step & MASK)]
            self.steps.append(jnp.concatenate(pair, axis=0).astype(F32).astype(BF16))

    def root(self, position):
        total = jnp.zeros((position.shape[0], 2 * LANES), F32)
        for row, step in zip(self.starts, self.steps):
            total += lax.dot_general(ones_where(row <= position), step, NT, preferred_element_type=F32)
        start = F32(LANES) * total[:, :LANES] + total[:, LANES:]
        return lax.rsqrt(jnp.minimum(position - start, F32(self.z.window)) + F32(1))

    def until(self, row):
        after = jnp.full((1, LANES), FAR, F32)
        for column in self.columns:
            later = jnp.where(column > row, column, F32(FAR))
            after = jnp.minimum(after, jnp.min(later, axis=0, keepdims=True))
        return jnp.minimum(row + F32(self.z.window), after - F32(1))


def pack(z, pieces, base, marks_ref, codes_ref, rows_ref, from_ref):
    if not pieces.count:
        return
    spare = jnp.zeros((8 - z.chunks, LANES), F32)

    def mark(s, carry):
        local = pieces.place(s) - base
        near = local.astype(I32)
        codes_ref[s] = jnp.concatenate([near >> LOW, near & MASK], axis=0).astype(F32)
        own = (local >= 0) & (local < F32(z.slots))
        tail = (local >= F32(-z.window)) & (local < 0)
        marks_ref[0, s] = jnp.concatenate([jnp.where(own, F32(1), F32(0)), spare], axis=0)
        marks_ref[1, s] = jnp.concatenate([jnp.where(tail, F32(1), F32(0)), spare], axis=0)
        return carry

    loop(pieces.count, mark, 0)
    upper = ones_where(iota((LANES, LANES), 0) < iota((LANES, LANES), 1))
    full = jnp.ones((LANES, LANES), BF16)
    lines = pieces.count * 8
    at, by = iota((lines, lines), 0), iota((lines, lines), 1)
    earlier = ones_where(((at >> 3) == (by >> 3)) & (by < at))
    source = iota((lines, LANES), 0) >> 3
    offset = ((source & (pieces.per_group - 1)) * z.capacity).astype(F32)
    for kind in range(2):
        marked = marks_ref[kind].reshape(lines, LANES)
        mark = marked.astype(BF16)
        rank = dot(mark, upper) + dot(earlier, dot(mark, full).astype(BF16)) + offset
        marks_ref[kind] = jnp.where(marked > 0, rank, F32(-1)).reshape(pieces.count, 8, LANES)

    spots = iota((LANES, LANES), 0).astype(F32)
    code_line = iota((2 * z.chunks, LANES), 0) & (z.chunks - 1)
    for kind in range(2):
        for g in range(pieces.groups):

            def add(i, carry):
                values, places = carry
                s = g * pieces.per_group + i
                ranks = marks_ref[kind, s]
                codes = codes_ref[s]
                hot = jnp.concatenate([ones_where(spots == ranks[r : r + 1]) for r in range(z.chunks)], axis=1)
                wide = [jnp.where(code_line == r, codes, F32(0)).astype(BF16) for r in range(z.chunks)]
                values += dot(hot, pieces.rows(s))
                places += lax.dot_general(jnp.concatenate(wide, axis=1), hot, NT, preferred_element_type=F32)
                return values, places

            zero = (jnp.zeros((LANES, LANES), F32), jnp.zeros((2 * z.chunks, LANES), F32))
            values, places = loop(pieces.per_group, add, zero)
            line = kind * pieces.groups + g
            rows_ref[line * LANES : (line + 1) * LANES, :] = values.astype(BF16)
            high = jnp.sum(places[: z.chunks], axis=0, keepdims=True)
            low = jnp.sum(places[z.chunks :], axis=0, keepdims=True)
            from_ref[line : line + 1, :] = F32(LANES) * high + low


def held(position, bounds):
    one, nothing = BF16(1), BF16(0)
    masks = [jnp.where((position >= a) & (position <= b), one, nothing) for a, b in bounds]
    return jnp.concatenate(masks, axis=1)


def anchors(z, me):
    middle = F32(z.span * z.slots // 2)
    span_of = lambda owner: (owner.astype(I32) >> (z.span.bit_length() - 1)).astype(F32) * F32(z.span)
    own = (me - span_of(me)) * F32(z.slots) - middle
    tail = (me - span_of(me - F32(1))) * F32(z.slots) - middle
    return own, tail


def short(row):
    return row.astype(I32).astype(I16)


def early_kernel(z, form, before, *refs):
    count = sum(form)
    own_ref, pieces = refs[0], Pieces(z, form, refs[1 : 1 + count])
    refs = refs[1 + count :]
    if before:
        before_ref, sums_ref, rows_ref, from_ref, marks_ref, codes_ref = refs
    else:
        sums_ref, scale_ref, rows_ref, from_ref, marks_ref, codes_ref = refs
    rate, me = own_ref[8:9, :], own_ref[9:10, :]
    runs = Runs(z, [own_ref[16 + u : 17 + u, :] for u in range(z.user_rows)])
    pack(z, pieces, me * F32(z.slots), marks_ref, codes_ref, rows_ref, from_ref)
    own_anchor, _ = anchors(z, me)
    inner = iota((BLOCK, LANES), 0)
    fall = jnp.exp(-rate * inner.astype(F32))
    bounds = []
    for g in range(pieces.groups if pieces.count else 0):
        begin = from_ref[g : g + 1, :]
        bounds.append((short(begin), short(runs.until(begin))))
    for b in range(z.slots // BLOCK):
        part = slice(b * BLOCK, (b + 1) * BLOCK)
        if bounds:
            mask = held((inner + b * BLOCK).astype(I16), bounds)
            value = dot(mask, rows_ref[0 : len(bounds) * LANES, :])
        else:
            value = jnp.zeros((BLOCK, LANES), F32)
        sums_ref[part, :] = value + before_ref[part, :] if before else value
        if b * BLOCK >= z.window and not before:
            start = F32(b * BLOCK)
            scale_ref[part, :] = fall * jnp.exp(-rate * (start + own_anchor)) * runs.root(inner.astype(F32) + start)


def late_kernel(z, earlier, form, late, *refs):
    own_ref, sums_ref, scale_ref = refs[:3]
    tails = [refs[3 + 2 * i : 5 + 2 * i] for i in range(len(earlier))]
    refs = refs[3 + 2 * len(earlier) :]
    count = sum(form)
    table_ref, feature_ref, place_ref, until_ref, rows_ref, from_ref, marks_ref, codes_ref = refs[count:]
    pieces, last = Pieces(z, form, refs[:count]), Pieces(z, form[-late:], refs[count - sum(form[-late:]) : count])
    rate, me = own_ref[8:9, :], own_ref[9:10, :]
    base = me * F32(z.slots)
    starts = []
    for u in range(z.user_rows):
        add = lambda s, total: total + pieces.below(s, u)
        starts.append(loop(pieces.count, add, jnp.zeros((1, LANES), F32)))
    runs = Runs(z, starts)
    pack(z, last, base, marks_ref, codes_ref, rows_ref, from_ref)

    own_anchor, tail_anchor = anchors(z, me)
    inner = iota((BLOCK, LANES), 0)
    fall = jnp.exp(-rate * inner.astype(F32))
    bounds = []
    listed = [(from_ref, 0, 2 * last.groups)] + [(ref, count, count) for (_, ref), count in zip(tails, earlier)]
    for ref, first, lines in listed:
        for g in range(first, first + lines):
            begin = ref[g : g + 1, :]
            bounds.append((short(begin), short(runs.until(begin + base) - base)))
    n = last.groups
    for b in range(z.slots // BLOCK):
        part = slice(b * BLOCK, (b + 1) * BLOCK)
        position = (inner + b * BLOCK).astype(I16)
        start = F32(b * BLOCK)
        value = sums_ref[part, :] + dot(held(position, bounds[:n]), rows_ref[0 : n * LANES, :])
        if b * BLOCK >= z.window:
            value = value * scale_ref[part, :]
        else:
            tail = dot(held(position, bounds[n : 2 * n]), rows_ref[n * LANES : 2 * n * LANES, :])
            at = 2 * n
            for (ref, _), count in zip(tails, earlier):
                tail += dot(held(position, bounds[at : at + count]), ref[count * LANES : 2 * count * LANES, :])
                at += count
            own_fall = jnp.exp(-rate * (start + own_anchor))
            if z.shifts == 1:
                value = (value + tail) * own_fall
            else:
                value = value * own_fall + tail * jnp.exp(-rate * (start + tail_anchor))
            value = value * fall * runs.root(inner.astype(F32) + (start + base))
        table_ref[part, :] = value.astype(BF16)

    narrow = z.owners * z.slots <= 32768

    def decode(s, carry):
        place = pieces.place(s)
        until = jnp.concatenate([runs.until(place[r : r + 1]) for r in range(z.chunks)], axis=0)
        if narrow:
            until = jnp.minimum(until, F32(32767))
        spare = jnp.zeros((8 - z.chunks, LANES), F32)
        place_ref[s] = jnp.concatenate([place, spare], axis=0)
        until_ref[s] = jnp.concatenate([until, spare], axis=0)
        return carry

    loop(pieces.count, decode, 0)
    columns = own_ref[0:8, :].T
    wide_column = lambda at: jnp.broadcast_to(columns[:, at : at + 1], (LANES, LANES))
    for t in range(z.rows // BLOCK):
        at = t * (BLOCK // LANES)
        position = jnp.concatenate([wide_column(at + k) for k in range(BLOCK // LANES)], axis=0)
        first = jnp.concatenate([wide_column(z.chunks + at + k) for k in range(BLOCK // LANES)], axis=0)
        point = short(position) if narrow else position
        total = jnp.zeros((BLOCK, LANES), F32)
        for shift in range(z.shifts):

            def add(s, value):
                begin, end = place_ref[s], until_ref[s]
                bounds = [(begin[r : r + 1], end[r : r + 1]) for r in range(z.chunks)]
                if narrow:
                    mask = held(point, [(short(a), short(b)) for a, b in bounds])
                else:
                    masks = []
                    for a, b in bounds:
                        inside = a >= first if shift == 0 else a < first
                        masks.append(ones_where((point >= a) & (point <= b) & inside))
                    mask = jnp.concatenate(masks, axis=1)
                return value + dot(mask, pieces.rows(s))

            value = loop(pieces.count, add, jnp.zeros((BLOCK, LANES), F32))
            center = first + F32(z.span * z.slots // 2 - shift * z.span * z.slots)
            total += value * jnp.exp(-rate * (position - center))
        feature_ref[t * BLOCK : (t + 1) * BLOCK, :] = (total * runs.root(position)).astype(BF16)


def swap(block, axis, distance):
    return lax.ppermute(block, axis, [(i, i ^ distance) for i in range(lax.axis_size(axis))])


def spread(blocks, axis):
    distance = lax.axis_size(axis) // 2
    while distance:
        blocks = blocks + [swap(block, axis, distance) for block in blocks]
        distance //= 2
    return blocks


def on_device(events, event_weight, route, bucket, segment, decay_rate):
    rows, width = events.shape
    key_count, shard_count = lax.axis_size("key"), lax.axis_size("shard")
    owners = key_count * shard_count
    slots = segment.shape[0]
    z = Sizes(owners, rows, slots)
    block_rows = rows + z.code_rows
    smem = pl.BlockSpec(memory_space=pltpu.SMEM)
    vmem = pl.BlockSpec(memory_space=pltpu.VMEM)
    shape = jax.ShapeDtypeStruct
    grant = pltpu.CompilerParams(vmem_limit_bytes=(16 if owners <= 8 else 48) * 1024 * 1024)
    me = (lax.axis_index("key") * shard_count + lax.axis_index("shard")).astype(I32).reshape(1)
    block, own = pl.pallas_call(
        functools.partial(send_kernel, z),
        out_shape=(
            shape((block_rows, width), BF16),
            shape((16 + z.user_rows + 7, LANES), F32),
        ),
        in_specs=[smem, smem] + [vmem] * 5,
        out_specs=(vmem, vmem),
        compiler_params=pltpu.CompilerParams(vmem_limit_bytes=56 * 1024 * 1024),
        name="weigh",
    )(
        me, decay_rate, events, event_weight.reshape(z.chunks, LANES), route.reshape(z.chunks, LANES),
        bucket.reshape(z.chunks, LANES), segment.reshape(slots // LANES, LANES),
    )

    def flat(blocks):
        return [part[None] if part.ndim == 2 else part for parts in blocks for part in parts]

    def sums(blocks, before=()):
        blocks, form, count = flat(blocks), tuple(map(len, blocks)), len(blocks)
        lines = max(8, 2 * count)
        whole = shape((slots, width), F32)
        kept = (shape((lines * LANES, LANES), BF16), shape((lines, LANES), F32))
        return pl.pallas_call(
            functools.partial(early_kernel, z, form, len(before)),
            out_shape=((whole,) if before else (whole, whole)) + kept,
            in_specs=[vmem] * (1 + len(blocks) + len(before)),
            out_specs=(vmem,) * (3 if before else 4),
            scratch_shapes=[
                pltpu.VMEM((2, max(1, count), 8, LANES), F32),
                pltpu.VMEM((max(1, count), 2 * z.chunks, LANES), F32),
            ],
            compiler_params=grant,
            cost_estimate=pl.CostEstimate(flops=COST * count, bytes_accessed=0, transcendentals=0),
            name="more_sums" if before else "first_sums",
        )(own, *blocks, *before)

    if (key_count, shard_count) == (4, 2):
        tie = lax.optimization_barrier
        far = swap(block, "key", 2)
        side = swap(block, "shard", 1)
        near = swap(block, "key", 1)
        side_near = swap(near, "shard", 1)
        first = [(block,), (near,)]
        total, scale, *tail = sums(first)
        far, total = tie((far, total))
        last = swap(far, "key", 1)
        sent, side_near, side = tie((far, side_near, side))
        side_far = swap(sent, "shard", 1)
        side_last = swap(last, "shard", 1)
        second = [(far,), (side,), (side_near,), (last,), (side_far,)]
        late = [(side_last,)]
        total, *tail2 = sums(second, (total,))
        early, earlier, tails = first + second, (len(first), len(second)), tail + tail2
    else:
        blocks = spread(spread([block], "key"), "shard")
        total, scale, *_ = sums([])
        early, earlier, tails = [], (), []
        late = [(jnp.concatenate(blocks, axis=0).reshape(owners, block_rows, width),)]
    late_lines = 2 * (len(late) if earlier else z.groups)
    late_count = len(late) if earlier else owners
    form = tuple(map(len, early + late))
    return pl.pallas_call(
        functools.partial(late_kernel, z, earlier, form, len(late)),
        out_shape=(shape((slots, width), BF16), shape((rows, width), BF16)),
        in_specs=[vmem] * (3 + len(tails) + sum(form)),
        out_specs=(vmem, vmem),
        scratch_shapes=[
            pltpu.VMEM((owners, 8, LANES), F32),
            pltpu.VMEM((owners, 8, LANES), F32),
            pltpu.VMEM((late_lines * LANES, LANES), BF16),
            pltpu.VMEM((late_lines, LANES), F32),
            pltpu.VMEM((2, late_count, 8, LANES), F32),
            pltpu.VMEM((late_count, 2 * z.chunks, LANES), F32),
        ],
        compiler_params=grant,
        name="table_and_rows",
    )(own, total, scale, *tails, *flat(early + late))


def solution(mesh):
    placed = (
        P(("groups", "key", "shard"), "lane"),
        P(("groups", "key", "shard")),
        P(("groups", "key", "shard"), None),
        P(("groups", "key", "shard")),
        P(("groups", "key", "shard")),
        P("lane"),
    )
    return jax.shard_map(
        on_device,
        mesh=mesh,
        in_specs=placed,
        out_specs=(P(("groups", "key", "shard"), "lane"), P(("groups", "key", "shard"), "lane")),
        check_vma=False,
    )
```

```python
import functools
import jax
import jax.numpy as jnp
from jax import lax
from jax.experimental import pallas as pl
from jax.experimental.pallas import tpu as pltpu
from jax.sharding import PartitionSpec as P

LANES = 128
LOW = 7
MASK = 127
F32 = jnp.float32
BF16 = jnp.bfloat16
I32 = jnp.int32
I16 = jnp.int16
FAR = 1e9
NT = (((1,), (1,)), ((), ()))
BLOCK = 256
COST = 1


class Sizes:
    def __init__(self, owners, rows, slots):
        self.owners, self.rows, self.slots = owners, rows, slots
        self.window = slots // 4
        self.chunks = rows // LANES
        self.user_rows = -(-8 * owners // LANES)
        self.code_rows = -(-(3 * self.chunks + 2 * self.user_rows) // 16) * 16
        self.span = min(owners, 8)
        self.shifts = 1 if owners <= self.span else 2
        self.capacity = 2 * rows // owners
        self.per_group = LANES // self.capacity
        self.groups = owners // self.per_group


def iota(shape, axis):
    return lax.broadcasted_iota(I32, shape, axis)


def ones_where(condition):
    return jnp.where(condition, F32(1), F32(0)).astype(BF16)


def dot(a, b):
    return jnp.dot(a, b, preferred_element_type=F32)


def loop(count, body, carry):
    if count <= 8:
        for i in range(count):
            carry = body(i, carry)
        return carry
    return lax.fori_loop(0, count, body, carry)


def send_kernel(z, me_ref, rate_ref, events_ref, weight_ref, route_ref, bucket_ref, segment_ref, block_ref, own_ref):
    groups = rate_ref.shape[0]
    lane = iota((1, LANES), 1)
    rate = jnp.full((1, LANES), rate_ref[0], F32)
    for g in range(1, groups):
        rate = jnp.where(lane >= g * (LANES // groups), rate_ref[g], rate)
    route = route_ref[...]
    bucket = bucket_ref[...]
    place = (route * z.slots + bucket).astype(F32)
    first = ((route >> (z.span.bit_length() - 1)) * (z.span * z.slots)).astype(F32)
    me = jnp.full((8 - 1, LANES), me_ref[0], I32).astype(F32)
    own_ref[0:16, :] = jnp.concatenate([place, first, rate, me], axis=0)
    spot = place - first - F32(z.span * z.slots // 2)
    columns = jnp.concatenate([weight_ref[...], spot], axis=0).T
    for r in range(z.chunks):
        part = slice(r * LANES, (r + 1) * LANES)
        weighted = (columns[:, r : r + 1] * events_ref[part, :].astype(F32)).astype(BF16)
        grown = weighted.astype(F32) * jnp.exp(columns[:, z.chunks + r : z.chunks + r + 1] * rate)
        block_ref[part, :] = grown.astype(BF16)
    ones = jnp.ones((8, LANES), BF16)
    high, low = [], []
    for u in range(z.user_rows):
        user = iota((LANES, LANES), 0) + u * LANES
        below = jnp.zeros((LANES, LANES), F32)
        for r in range(z.slots // LANES):
            below += jnp.where(segment_ref[r : r + 1, :] < user, F32(1), F32(0))
        count = lax.dot_general(ones, below.astype(BF16), NT, preferred_element_type=F32)[0:1]
        own_ref[16 + u : 17 + u, :] = count
        count = count.astype(I32)
        high.append(count >> LOW)
        low.append(count & MASK)
    spare = z.code_rows - 3 * z.chunks - 2 * z.user_rows
    pad = [jnp.zeros((spare, LANES), I32)] if spare else []
    codes = jnp.concatenate([route, bucket >> LOW, bucket & MASK] + high + low + pad, axis=0)
    block_ref[z.rows : z.rows + z.code_rows, :] = codes.astype(F32).astype(BF16)


class Pieces:
    def __init__(self, z, form, refs):
        self.z, refs = z, list(refs)
        self.parts = [[refs.pop(0) for _ in range(n)] for n in form]
        self.count = len(form) if len(form) != 1 else self.parts[0][0].shape[0]
        self.per_group = 1 if len(form) != 1 else z.per_group
        self.groups = self.count // self.per_group

    def block(self, s):
        return (self.parts[s], 0) if len(self.parts) != 1 else (self.parts[0], s)

    def codes(self, s):
        parts, i = self.block(s)
        first = parts[0].shape[1] - self.z.code_rows
        return parts[0][i, first : first + self.z.code_rows, :].astype(F32)

    def rows(self, s):
        parts, i = self.block(s)
        first = parts[0][i, 0 : parts[0].shape[1] - self.z.code_rows, :]
        return jnp.concatenate([first] + [part[i] for part in parts[1:]], axis=0)

    def place(self, s):
        n, tile = self.z.chunks, self.codes(s)
        return tile[0:n] * F32(self.z.slots) + F32(LANES) * tile[n : 2 * n] + tile[2 * n : 3 * n]

    def below(self, s, u):
        tile, at = self.codes(s), 3 * self.z.chunks + u
        return F32(LANES) * tile[at : at + 1] + tile[at + self.z.user_rows : at + self.z.user_rows + 1]


class Runs:
    def __init__(self, z, starts):
        self.z, self.starts = z, starts
        users = min(LANES, 8 * z.owners)
        self.columns = [jnp.broadcast_to(row, (8, LANES)).T[:users, 0:1] for row in starts]
        self.steps = []
        for u, row in enumerate(starts):
            before = pltpu.roll(row, 1, 1)
            first = starts[u - 1][:, LANES - 1 : LANES] if u else jnp.zeros((1, 1), F32)
            step = (row - jnp.where(iota((1, LANES), 1) == 0, first, before)).astype(I32)
            pair = [jnp.broadcast_to(part, (LANES, LANES)) for part in (step >> LOW, step & MASK)]
            self.steps.append(jnp.concatenate(pair, axis=0).astype(F32).astype(BF16))

    def root(self, position):
        total = jnp.zeros((position.shape[0], 2 * LANES), F32)
        for row, step in zip(self.starts, self.steps):
            total += lax.dot_general(ones_where(row <= position), step, NT, preferred_element_type=F32)
        start = F32(LANES) * total[:, :LANES] + total[:, LANES:]
        return lax.rsqrt(jnp.minimum(position - start, F32(self.z.window)) + F32(1))

    def until(self, row):
        after = jnp.full((1, LANES), FAR, F32)
        for column in self.columns:
            later = jnp.where(column > row, column, F32(FAR))
            after = jnp.minimum(after, jnp.min(later, axis=0, keepdims=True))
        return jnp.minimum(row + F32(self.z.window), after - F32(1))


def pack(z, pieces, base, marks_ref, codes_ref, rows_ref, from_ref):
    if not pieces.count:
        return
    spare = jnp.zeros((8 - z.chunks, LANES), F32)

    def mark(s, carry):
        local = pieces.place(s) - base
        near = local.astype(I32)
        codes_ref[s] = jnp.concatenate([near >> LOW, near & MASK], axis=0).astype(F32)
        own = (local >= 0) & (local < F32(z.slots))
        tail = (local >= F32(-z.window)) & (local < 0)
        marks_ref[0, s] = jnp.concatenate([jnp.where(own, F32(1), F32(0)), spare], axis=0)
        marks_ref[1, s] = jnp.concatenate([jnp.where(tail, F32(1), F32(0)), spare], axis=0)
        return carry

    loop(pieces.count, mark, 0)
    upper = ones_where(iota((LANES, LANES), 0) < iota((LANES, LANES), 1))
    full = jnp.ones((LANES, LANES), BF16)
    lines = pieces.count * 8
    at, by = iota((lines, lines), 0), iota((lines, lines), 1)
    earlier = ones_where(((at >> 3) == (by >> 3)) & (by < at))
    source = iota((lines, LANES), 0) >> 3
    offset = ((source & (pieces.per_group - 1)) * z.capacity).astype(F32)
    for kind in range(2):
        marked = marks_ref[kind].reshape(lines, LANES)
        mark = marked.astype(BF16)
        rank = dot(mark, upper) + dot(earlier, dot(mark, full).astype(BF16)) + offset
        marks_ref[kind] = jnp.where(marked > 0, rank, F32(-1)).reshape(pieces.count, 8, LANES)

    spots = iota((LANES, LANES), 0).astype(F32)
    code_line = iota((2 * z.chunks, LANES), 0) & (z.chunks - 1)
    for kind in range(2):
        for g in range(pieces.groups):

            def add(i, carry):
                values, places = carry
                s = g * pieces.per_group + i
                ranks = marks_ref[kind, s]
                codes = codes_ref[s]
                hot = jnp.concatenate([ones_where(spots == ranks[r : r + 1]) for r in range(z.chunks)], axis=1)
                wide = [jnp.where(code_line == r, codes, F32(0)).astype(BF16) for r in range(z.chunks)]
                values += dot(hot, pieces.rows(s))
                places += lax.dot_general(jnp.concatenate(wide, axis=1), hot, NT, preferred_element_type=F32)
                return values, places

            zero = (jnp.zeros((LANES, LANES), F32), jnp.zeros((2 * z.chunks, LANES), F32))
            values, places = loop(pieces.per_group, add, zero)
            line = kind * pieces.groups + g
            rows_ref[line * LANES : (line + 1) * LANES, :] = values.astype(BF16)
            high = jnp.sum(places[: z.chunks], axis=0, keepdims=True)
            low = jnp.sum(places[z.chunks :], axis=0, keepdims=True)
            from_ref[line : line + 1, :] = F32(LANES) * high + low


def held(position, bounds):
    one, nothing = BF16(1), BF16(0)
    masks = [jnp.where((position >= a) & (position <= b), one, nothing) for a, b in bounds]
    return jnp.concatenate(masks, axis=1)


def anchors(z, me):
    middle = F32(z.span * z.slots // 2)
    span_of = lambda owner: (owner.astype(I32) >> (z.span.bit_length() - 1)).astype(F32) * F32(z.span)
    own = (me - span_of(me)) * F32(z.slots) - middle
    tail = (me - span_of(me - F32(1))) * F32(z.slots) - middle
    return own, tail


def short(row):
    return row.astype(I32).astype(I16)


def early_kernel(z, form, before, *refs):
    count = sum(form)
    own_ref, pieces = refs[0], Pieces(z, form, refs[1 : 1 + count])
    refs = refs[1 + count :]
    if before:
        before_ref, sums_ref, rows_ref, from_ref, marks_ref, codes_ref = refs
    else:
        sums_ref, scale_ref, rows_ref, from_ref, marks_ref, codes_ref = refs
    rate, me = own_ref[8:9, :], own_ref[9:10, :]
    runs = Runs(z, [own_ref[16 + u : 17 + u, :] for u in range(z.user_rows)])
    pack(z, pieces, me * F32(z.slots), marks_ref, codes_ref, rows_ref, from_ref)
    own_anchor, _ = anchors(z, me)
    inner = iota((BLOCK, LANES), 0)
    fall = jnp.exp(-rate * inner.astype(F32))
    bounds = []
    for g in range(pieces.groups if pieces.count else 0):
        begin = from_ref[g : g + 1, :]
        bounds.append((short(begin), short(runs.until(begin))))
    for b in range(z.slots // BLOCK):
        part = slice(b * BLOCK, (b + 1) * BLOCK)
        if bounds:
            mask = held((inner + b * BLOCK).astype(I16), bounds)
            value = dot(mask, rows_ref[0 : len(bounds) * LANES, :])
        else:
            value = jnp.zeros((BLOCK, LANES), F32)
        sums_ref[part, :] = value + before_ref[part, :] if before else value
        if b * BLOCK >= z.window and not before:
            start = F32(b * BLOCK)
            scale_ref[part, :] = fall * jnp.exp(-rate * (start + own_anchor)) * runs.root(inner.astype(F32) + start)


def late_kernel(z, earlier, form, late, *refs):
    own_ref, sums_ref, scale_ref = refs[:3]
    tails = [refs[3 + 2 * i : 5 + 2 * i] for i in range(len(earlier))]
    refs = refs[3 + 2 * len(earlier) :]
    count = sum(form)
    (
        out_ref, feature_ref, place_ref, until_ref, rows_ref, from_ref, marks_ref, codes_ref, table_ref, sems,
    ) = refs[count:]
    pieces, last = Pieces(z, form, refs[:count]), Pieces(z, form[-late:], refs[count - sum(form[-late:]) : count])
    rate, me = own_ref[8:9, :], own_ref[9:10, :]
    base = me * F32(z.slots)
    starts = []
    for u in range(z.user_rows):
        add = lambda s, total: total + pieces.below(s, u)
        starts.append(loop(pieces.count, add, jnp.zeros((1, LANES), F32)))
    runs = Runs(z, starts)
    pack(z, last, base, marks_ref, codes_ref, rows_ref, from_ref)

    own_anchor, tail_anchor = anchors(z, me)
    inner = iota((BLOCK, LANES), 0)
    fall = jnp.exp(-rate * inner.astype(F32))
    bounds = []
    listed = [(from_ref, 0, 2 * last.groups)] + [(ref, count, count) for (_, ref), count in zip(tails, earlier)]
    for ref, first, lines in listed:
        for g in range(first, first + lines):
            begin = ref[g : g + 1, :]
            bounds.append((short(begin), short(runs.until(begin + base) - base)))
    n = last.groups
    copies = []
    for b in range(z.slots // BLOCK):
        part = slice(b * BLOCK, (b + 1) * BLOCK)
        position = (inner + b * BLOCK).astype(I16)
        start = F32(b * BLOCK)
        value = sums_ref[part, :] + dot(held(position, bounds[:n]), rows_ref[0 : n * LANES, :])
        if b * BLOCK >= z.window:
            value = value * scale_ref[part, :]
        else:
            tail = dot(held(position, bounds[n : 2 * n]), rows_ref[n * LANES : 2 * n * LANES, :])
            at = 2 * n
            for (ref, _), count in zip(tails, earlier):
                tail += dot(held(position, bounds[at : at + count]), ref[count * LANES : 2 * count * LANES, :])
                at += count
            own_fall = jnp.exp(-rate * (start + own_anchor))
            if z.shifts == 1:
                value = (value + tail) * own_fall
            else:
                value = value * own_fall + tail * jnp.exp(-rate * (start + tail_anchor))
            value = value * fall * runs.root(inner.astype(F32) + (start + base))
        table_ref[part, :] = value.astype(BF16)
        if (b + 1) * BLOCK % z.window == 0:
            done = slice((b + 1) * BLOCK - z.window, (b + 1) * BLOCK)
            copy = pltpu.make_async_copy(table_ref.at[done, :], out_ref.at[done, :], sems.at[len(copies)])
            copy.start()
            copies.append(copy)

    narrow = z.owners * z.slots <= 32768

    def decode(s, carry):
        place = pieces.place(s)
        until = jnp.concatenate([runs.until(place[r : r + 1]) for r in range(z.chunks)], axis=0)
        if narrow:
            until = jnp.minimum(until, F32(32767))
        spare = jnp.zeros((8 - z.chunks, LANES), F32)
        place_ref[s] = jnp.concatenate([place, spare], axis=0)
        until_ref[s] = jnp.concatenate([until, spare], axis=0)
        return carry

    loop(pieces.count, decode, 0)
    columns = own_ref[0:8, :].T
    wide_column = lambda at: jnp.broadcast_to(columns[:, at : at + 1], (LANES, LANES))
    for t in range(z.rows // BLOCK):
        at = t * (BLOCK // LANES)
        position = jnp.concatenate([wide_column(at + k) for k in range(BLOCK // LANES)], axis=0)
        first = jnp.concatenate([wide_column(z.chunks + at + k) for k in range(BLOCK // LANES)], axis=0)
        point = short(position) if narrow else position
        total = jnp.zeros((BLOCK, LANES), F32)
        for shift in range(z.shifts):

            def add(s, value):
                begin, end = place_ref[s], until_ref[s]
                bounds = [(begin[r : r + 1], end[r : r + 1]) for r in range(z.chunks)]
                if narrow:
                    mask = held(point, [(short(a), short(b)) for a, b in bounds])
                else:
                    masks = []
                    for a, b in bounds:
                        inside = a >= first if shift == 0 else a < first
                        masks.append(ones_where((point >= a) & (point <= b) & inside))
                    mask = jnp.concatenate(masks, axis=1)
                return value + dot(mask, pieces.rows(s))

            value = loop(pieces.count, add, jnp.zeros((BLOCK, LANES), F32))
            center = first + F32(z.span * z.slots // 2 - shift * z.span * z.slots)
            total += value * jnp.exp(-rate * (position - center))
        feature_ref[t * BLOCK : (t + 1) * BLOCK, :] = (total * runs.root(position)).astype(BF16)
    for copy in copies:
        copy.wait()


def swap(block, axis, distance):
    return lax.ppermute(block, axis, [(i, i ^ distance) for i in range(lax.axis_size(axis))])


def spread(blocks, axis):
    distance = lax.axis_size(axis) // 2
    while distance:
        blocks = blocks + [swap(block, axis, distance) for block in blocks]
        distance //= 2
    return blocks


def on_device(events, event_weight, route, bucket, segment, decay_rate):
    rows, width = events.shape
    key_count, shard_count = lax.axis_size("key"), lax.axis_size("shard")
    owners = key_count * shard_count
    slots = segment.shape[0]
    z = Sizes(owners, rows, slots)
    block_rows = rows + z.code_rows
    smem = pl.BlockSpec(memory_space=pltpu.SMEM)
    vmem = pl.BlockSpec(memory_space=pltpu.VMEM)
    shape = jax.ShapeDtypeStruct
    grant = pltpu.CompilerParams(vmem_limit_bytes=(16 if owners <= 8 else 48) * 1024 * 1024)
    me = (lax.axis_index("key") * shard_count + lax.axis_index("shard")).astype(I32).reshape(1)
    block, own = pl.pallas_call(
        functools.partial(send_kernel, z),
        out_shape=(
            shape((block_rows, width), BF16),
            shape((16 + z.user_rows + 7, LANES), F32),
        ),
        in_specs=[smem, smem] + [vmem] * 5,
        out_specs=(vmem, vmem),
        compiler_params=pltpu.CompilerParams(vmem_limit_bytes=56 * 1024 * 1024),
        name="weigh",
    )(
        me, decay_rate, events, event_weight.reshape(z.chunks, LANES), route.reshape(z.chunks, LANES),
        bucket.reshape(z.chunks, LANES), segment.reshape(slots // LANES, LANES),
    )

    def flat(blocks):
        return [part[None] if part.ndim == 2 else part for parts in blocks for part in parts]

    def sums(blocks, before=()):
        blocks, form, count = flat(blocks), tuple(map(len, blocks)), len(blocks)
        lines = max(8, 2 * count)
        whole = shape((slots, width), F32)
        kept = (shape((lines * LANES, LANES), BF16), shape((lines, LANES), F32))
        return pl.pallas_call(
            functools.partial(early_kernel, z, form, len(before)),
            out_shape=((whole,) if before else (whole, whole)) + kept,
            in_specs=[vmem] * (1 + len(blocks) + len(before)),
            out_specs=(vmem,) * (3 if before else 4),
            scratch_shapes=[
                pltpu.VMEM((2, max(1, count), 8, LANES), F32),
                pltpu.VMEM((max(1, count), 2 * z.chunks, LANES), F32),
            ],
            compiler_params=grant,
            cost_estimate=pl.CostEstimate(flops=COST * count, bytes_accessed=0, transcendentals=0),
            name="more_sums" if before else "first_sums",
        )(own, *blocks, *before)

    if (key_count, shard_count) == (4, 2):
        tie = lax.optimization_barrier
        far = swap(block, "key", 2)
        side = swap(block, "shard", 1)
        near = swap(block, "key", 1)
        side_near = swap(side, "key", 1)
        held, waited = tie((block, far))
        first = [(held,), (side,), (near,)]
        total, scale, *tail = sums(first)

        last = swap(far, "key", 1)
        last, total = tie((last, total))
        sent = far
        side_far = swap(sent, "shard", 1)
        side_last = swap(last, "shard", 1)
        second = [(far,), (last,), (side_far,)]
        late = [(side_near,), (side_last,)]
        total, *tail2 = sums(second, (total,))
        early, earlier, tails = first + second, (len(first), len(second)), tail + tail2
    else:
        blocks = spread(spread([block], "key"), "shard")
        total, scale, *_ = sums([])
        early, earlier, tails = [], (), []
        late = [(jnp.concatenate(blocks, axis=0).reshape(owners, block_rows, width),)]
    late_lines = 2 * (len(late) if earlier else z.groups)
    late_count = len(late) if earlier else owners
    form = tuple(map(len, early + late))
    return pl.pallas_call(
        functools.partial(late_kernel, z, earlier, form, len(late)),
        out_shape=(shape((slots, width), BF16), shape((rows, width), BF16)),
        in_specs=[vmem] * (3 + len(tails) + sum(form)),
        out_specs=(pl.BlockSpec(memory_space=pl.ANY), vmem),
        scratch_shapes=[
            pltpu.VMEM((owners, 8, LANES), F32),
            pltpu.VMEM((owners, 8, LANES), F32),
            pltpu.VMEM((late_lines * LANES, LANES), BF16),
            pltpu.VMEM((late_lines, LANES), F32),
            pltpu.VMEM((2, late_count, 8, LANES), F32),
            pltpu.VMEM((late_count, 2 * z.chunks, LANES), F32),
            pltpu.VMEM((slots, width), BF16),
            pltpu.SemaphoreType.DMA((slots // z.window,)),
        ],
        compiler_params=grant,
        name="table_and_rows",
    )(own, total, scale, *tails, *flat(early + late))


def solution(mesh):
    placed = (
        P(("groups", "key", "shard"), "lane"),
        P(("groups", "key", "shard")),
        P(("groups", "key", "shard"), None),
        P(("groups", "key", "shard")),
        P(("groups", "key", "shard")),
        P("lane"),
    )
    return jax.shard_map(
        on_device,
        mesh=mesh,
        in_specs=placed,
        out_specs=(P(("groups", "key", "shard"), "lane"), P(("groups", "key", "shard"), "lane")),
        check_vma=False,
    )
```

```python
import functools
import jax
import jax.numpy as jnp
from jax import lax
from jax.experimental import pallas as pl
from jax.experimental.pallas import tpu as pltpu
from jax.sharding import PartitionSpec as P

LANES = 128
LOW = 7
MASK = 127
F32 = jnp.float32
BF16 = jnp.bfloat16
I32 = jnp.int32
I16 = jnp.int16
FAR = 1e9
NT = (((1,), (1,)), ((), ()))
BLOCK = 512
COST = 1


class Sizes:
    def __init__(self, owners, rows, slots):
        self.owners, self.rows, self.slots = owners, rows, slots
        self.window = slots // 4
        self.chunks = rows // LANES
        self.user_rows = -(-8 * owners // LANES)
        self.code_rows = -(-(3 * self.chunks + 2 * self.user_rows) // 16) * 16
        self.span = min(owners, 8)
        self.shifts = 1 if owners <= self.span else 2
        self.capacity = 2 * rows // owners
        self.per_group = LANES // self.capacity
        self.groups = owners // self.per_group


def iota(shape, axis):
    return lax.broadcasted_iota(I32, shape, axis)


def ones_where(condition):
    return jnp.where(condition, F32(1), F32(0)).astype(BF16)


def dot(a, b):
    return jnp.dot(a, b, preferred_element_type=F32)


def loop(count, body, carry):
    if count <= 8:
        for i in range(count):
            carry = body(i, carry)
        return carry
    return lax.fori_loop(0, count, body, carry)


def send_kernel(z, me_ref, rate_ref, events_ref, weight_ref, route_ref, bucket_ref, segment_ref, block_ref, own_ref):
    groups = rate_ref.shape[0]
    lane = iota((1, LANES), 1)
    rate = jnp.full((1, LANES), rate_ref[0], F32)
    for g in range(1, groups):
        rate = jnp.where(lane >= g * (LANES // groups), rate_ref[g], rate)
    route = route_ref[...]
    bucket = bucket_ref[...]
    place = (route * z.slots + bucket).astype(F32)
    first = ((route >> (z.span.bit_length() - 1)) * (z.span * z.slots)).astype(F32)
    me = jnp.full((8 - 1, LANES), me_ref[0], I32).astype(F32)
    own_ref[0:16, :] = jnp.concatenate([place, first, rate, me], axis=0)
    spot = place - first - F32(z.span * z.slots // 2)
    columns = jnp.concatenate([weight_ref[...], spot], axis=0).T
    for r in range(z.chunks):
        part = slice(r * LANES, (r + 1) * LANES)
        weighted = (columns[:, r : r + 1] * events_ref[part, :].astype(F32)).astype(BF16)
        grown = weighted.astype(F32) * jnp.exp(columns[:, z.chunks + r : z.chunks + r + 1] * rate)
        block_ref[part, :] = grown.astype(BF16)
    ones = jnp.ones((8, LANES), BF16)
    high, low = [], []
    for u in range(z.user_rows):
        user = iota((LANES, LANES), 0) + u * LANES
        below = jnp.zeros((LANES, LANES), F32)
        for r in range(z.slots // LANES):
            below += jnp.where(segment_ref[r : r + 1, :] < user, F32(1), F32(0))
        count = lax.dot_general(ones, below.astype(BF16), NT, preferred_element_type=F32)[0:1]
        own_ref[16 + u : 17 + u, :] = count
        count = count.astype(I32)
        high.append(count >> LOW)
        low.append(count & MASK)
    spare = z.code_rows - 3 * z.chunks - 2 * z.user_rows
    pad = [jnp.zeros((spare, LANES), I32)] if spare else []
    codes = jnp.concatenate([route, bucket >> LOW, bucket & MASK] + high + low + pad, axis=0)
    block_ref[z.rows : z.rows + z.code_rows, :] = codes.astype(F32).astype(BF16)


class Pieces:
    def __init__(self, z, form, refs):
        self.z, refs = z, list(refs)
        self.parts = [[refs.pop(0) for _ in range(n)] for n in form]
        self.count = len(form) if len(form) != 1 else self.parts[0][0].shape[0]
        self.per_group = 1 if len(form) != 1 else z.per_group
        self.groups = self.count // self.per_group

    def block(self, s):
        return (self.parts[s], 0) if len(self.parts) != 1 else (self.parts[0], s)

    def codes(self, s):
        parts, i = self.block(s)
        first = parts[0].shape[1] - self.z.code_rows
        return parts[0][i, first : first + self.z.code_rows, :].astype(F32)

    def rows(self, s):
        parts, i = self.block(s)
        first = parts[0][i, 0 : parts[0].shape[1] - self.z.code_rows, :]
        return jnp.concatenate([first] + [part[i] for part in parts[1:]], axis=0)

    def place(self, s):
        n, tile = self.z.chunks, self.codes(s)
        return tile[0:n] * F32(self.z.slots) + F32(LANES) * tile[n : 2 * n] + tile[2 * n : 3 * n]

    def below(self, s, u):
        tile, at = self.codes(s), 3 * self.z.chunks + u
        return F32(LANES) * tile[at : at + 1] + tile[at + self.z.user_rows : at + self.z.user_rows + 1]


class Runs:
    def __init__(self, z, starts):
        self.z, self.starts = z, starts
        users = min(LANES, 8 * z.owners)
        self.columns = [jnp.broadcast_to(row, (8, LANES)).T[:users, 0:1] for row in starts]
        self.steps = []
        for u, row in enumerate(starts):
            before = pltpu.roll(row, 1, 1)
            first = starts[u - 1][:, LANES - 1 : LANES] if u else jnp.zeros((1, 1), F32)
            step = (row - jnp.where(iota((1, LANES), 1) == 0, first, before)).astype(I32)
            pair = [jnp.broadcast_to(part, (LANES, LANES)) for part in (step >> LOW, step & MASK)]
            self.steps.append(jnp.concatenate(pair, axis=0).astype(F32).astype(BF16))

    def root(self, position):
        total = jnp.zeros((position.shape[0], 2 * LANES), F32)
        for row, step in zip(self.starts, self.steps):
            total += lax.dot_general(ones_where(row <= position), step, NT, preferred_element_type=F32)
        start = F32(LANES) * total[:, :LANES] + total[:, LANES:]
        return lax.rsqrt(jnp.minimum(position - start, F32(self.z.window)) + F32(1))

    def until(self, row):
        after = jnp.full((1, LANES), FAR, F32)
        for column in self.columns:
            later = jnp.where(column > row, column, F32(FAR))
            after = jnp.minimum(after, jnp.min(later, axis=0, keepdims=True))
        return jnp.minimum(row + F32(self.z.window), after - F32(1))


def pack(z, pieces, base, marks_ref, codes_ref, rows_ref, from_ref):
    if not pieces.count:
        return
    spare = jnp.zeros((8 - z.chunks, LANES), F32)

    def mark(s, carry):
        local = pieces.place(s) - base
        near = local.astype(I32)
        codes_ref[s] = jnp.concatenate([near >> LOW, near & MASK], axis=0).astype(F32)
        own = (local >= 0) & (local < F32(z.slots))
        tail = (local >= F32(-z.window)) & (local < 0)
        marks_ref[0, s] = jnp.concatenate([jnp.where(own, F32(1), F32(0)), spare], axis=0)
        marks_ref[1, s] = jnp.concatenate([jnp.where(tail, F32(1), F32(0)), spare], axis=0)
        return carry

    loop(pieces.count, mark, 0)
    upper = ones_where(iota((LANES, LANES), 0) < iota((LANES, LANES), 1))
    full = jnp.ones((LANES, LANES), BF16)
    lines = pieces.count * 8
    at, by = iota((lines, lines), 0), iota((lines, lines), 1)
    earlier = ones_where(((at >> 3) == (by >> 3)) & (by < at))
    source = iota((lines, LANES), 0) >> 3
    offset = ((source & (pieces.per_group - 1)) * z.capacity).astype(F32)
    for kind in range(2):
        marked = marks_ref[kind].reshape(lines, LANES)
        mark = marked.astype(BF16)
        rank = dot(mark, upper) + dot(earlier, dot(mark, full).astype(BF16)) + offset
        marks_ref[kind] = jnp.where(marked > 0, rank, F32(-1)).reshape(pieces.count, 8, LANES)

    spots = iota((LANES, LANES), 0).astype(F32)
    code_line = iota((2 * z.chunks, LANES), 0) & (z.chunks - 1)
    for kind in range(2):
        for g in range(pieces.groups):

            def add(i, carry):
                values, places = carry
                s = g * pieces.per_group + i
                ranks = marks_ref[kind, s]
                codes = codes_ref[s]
                hot = jnp.concatenate([ones_where(spots == ranks[r : r + 1]) for r in range(z.chunks)], axis=1)
                wide = [jnp.where(code_line == r, codes, F32(0)).astype(BF16) for r in range(z.chunks)]
                values += dot(hot, pieces.rows(s))
                places += lax.dot_general(jnp.concatenate(wide, axis=1), hot, NT, preferred_element_type=F32)
                return values, places

            zero = (jnp.zeros((LANES, LANES), F32), jnp.zeros((2 * z.chunks, LANES), F32))
            values, places = loop(pieces.per_group, add, zero)
            line = kind * pieces.groups + g
            rows_ref[line * LANES : (line + 1) * LANES, :] = values.astype(BF16)
            high = jnp.sum(places[: z.chunks], axis=0, keepdims=True)
            low = jnp.sum(places[z.chunks :], axis=0, keepdims=True)
            from_ref[line : line + 1, :] = F32(LANES) * high + low


def held(position, bounds):
    one, nothing = BF16(1), BF16(0)
    masks = [jnp.where((position >= a) & (position <= b), one, nothing) for a, b in bounds]
    return jnp.concatenate(masks, axis=1)


def anchors(z, me):
    middle = F32(z.span * z.slots // 2)
    span_of = lambda owner: (owner.astype(I32) >> (z.span.bit_length() - 1)).astype(F32) * F32(z.span)
    own = (me - span_of(me)) * F32(z.slots) - middle
    tail = (me - span_of(me - F32(1))) * F32(z.slots) - middle
    return own, tail


def short(row):
    return row.astype(I32).astype(I16)


def early_kernel(z, form, before, *refs):
    count = sum(form)
    own_ref, pieces = refs[0], Pieces(z, form, refs[1 : 1 + count])
    refs = refs[1 + count :]
    if before:
        before_ref, sums_ref, rows_ref, from_ref, marks_ref, codes_ref = refs
    else:
        sums_ref, scale_ref, rows_ref, from_ref, marks_ref, codes_ref = refs
    rate, me = own_ref[8:9, :], own_ref[9:10, :]
    runs = Runs(z, [own_ref[16 + u : 17 + u, :] for u in range(z.user_rows)])
    pack(z, pieces, me * F32(z.slots), marks_ref, codes_ref, rows_ref, from_ref)
    own_anchor, _ = anchors(z, me)
    inner = iota((BLOCK, LANES), 0)
    fall = jnp.exp(-rate * inner.astype(F32))
    bounds = []
    for g in range(pieces.groups if pieces.count else 0):
        begin = from_ref[g : g + 1, :]
        bounds.append((short(begin), short(runs.until(begin))))
    for b in range(z.slots // BLOCK):
        part = slice(b * BLOCK, (b + 1) * BLOCK)
        if bounds:
            mask = held((inner + b * BLOCK).astype(I16), bounds)
            value = dot(mask, rows_ref[0 : len(bounds) * LANES, :])
        else:
            value = jnp.zeros((BLOCK, LANES), F32)
        sums_ref[part, :] = value + before_ref[part, :] if before else value
        if b * BLOCK >= z.window and not before:
            start = F32(b * BLOCK)
            scale_ref[part, :] = fall * jnp.exp(-rate * (start + own_anchor)) * runs.root(inner.astype(F32) + start)


def late_kernel(z, earlier, form, late, *refs):
    own_ref, sums_ref, scale_ref = refs[:3]
    tails = [refs[3 + 2 * i : 5 + 2 * i] for i in range(len(earlier))]
    refs = refs[3 + 2 * len(earlier) :]
    count = sum(form)
    (
        out_ref, feature_ref, place_ref, until_ref, rows_ref, from_ref, marks_ref, codes_ref, table_ref, sems,
    ) = refs[count:]
    pieces, last = Pieces(z, form, refs[:count]), Pieces(z, form[-late:], refs[count - sum(form[-late:]) : count])
    rate, me = own_ref[8:9, :], own_ref[9:10, :]
    base = me * F32(z.slots)
    starts = []
    for u in range(z.user_rows):
        add = lambda s, total: total + pieces.below(s, u)
        starts.append(loop(pieces.count, add, jnp.zeros((1, LANES), F32)))
    runs = Runs(z, starts)
    pack(z, last, base, marks_ref, codes_ref, rows_ref, from_ref)

    own_anchor, tail_anchor = anchors(z, me)
    inner = iota((BLOCK, LANES), 0)
    fall = jnp.exp(-rate * inner.astype(F32))
    bounds = []
    listed = [(from_ref, 0, 2 * last.groups)] + [(ref, count, count) for (_, ref), count in zip(tails, earlier)]
    for ref, first, lines in listed:
        for g in range(first, first + lines):
            begin = ref[g : g + 1, :]
            bounds.append((short(begin), short(runs.until(begin + base) - base)))
    n = last.groups
    copies = []
    for b in range(z.slots // BLOCK):
        part = slice(b * BLOCK, (b + 1) * BLOCK)
        position = (inner + b * BLOCK).astype(I16)
        start = F32(b * BLOCK)
        value = sums_ref[part, :] + dot(held(position, bounds[:n]), rows_ref[0 : n * LANES, :])
        if b * BLOCK >= z.window:
            value = value * scale_ref[part, :]
        else:
            tail = dot(held(position, bounds[n : 2 * n]), rows_ref[n * LANES : 2 * n * LANES, :])
            at = 2 * n
            for (ref, _), count in zip(tails, earlier):
                tail += dot(held(position, bounds[at : at + count]), ref[count * LANES : 2 * count * LANES, :])
                at += count
            own_fall = jnp.exp(-rate * (start + own_anchor))
            if z.shifts == 1:
                value = (value + tail) * own_fall
            else:
                value = value * own_fall + tail * jnp.exp(-rate * (start + tail_anchor))
            value = value * fall * runs.root(inner.astype(F32) + (start + base))
        table_ref[part, :] = value.astype(BF16)
        if (b + 1) * BLOCK % z.window == 0:
            done = slice((b + 1) * BLOCK - z.window, (b + 1) * BLOCK)
            copy = pltpu.make_async_copy(table_ref.at[done, :], out_ref.at[done, :], sems.at[len(copies)])
            copy.start()
            copies.append(copy)

    narrow = z.owners * z.slots <= 32768

    def decode(s, carry):
        place = pieces.place(s)
        until = jnp.concatenate([runs.until(place[r : r + 1]) for r in range(z.chunks)], axis=0)
        if narrow:
            until = jnp.minimum(until, F32(32767))
        spare = jnp.zeros((8 - z.chunks, LANES), F32)
        place_ref[s] = jnp.concatenate([place, spare], axis=0)
        until_ref[s] = jnp.concatenate([until, spare], axis=0)
        return carry

    loop(pieces.count, decode, 0)
    columns = own_ref[0:8, :].T
    wide_column = lambda at: jnp.broadcast_to(columns[:, at : at + 1], (LANES, LANES))
    for t in range(z.rows // BLOCK):
        at = t * (BLOCK // LANES)
        position = jnp.concatenate([wide_column(at + k) for k in range(BLOCK // LANES)], axis=0)
        first = jnp.concatenate([wide_column(z.chunks + at + k) for k in range(BLOCK // LANES)], axis=0)
        point = short(position) if narrow else position
        total = jnp.zeros((BLOCK, LANES), F32)
        for shift in range(z.shifts):

            def add(s, value):
                begin, end = place_ref[s], until_ref[s]
                bounds = [(begin[r : r + 1], end[r : r + 1]) for r in range(z.chunks)]
                if narrow:
                    mask = held(point, [(short(a), short(b)) for a, b in bounds])
                else:
                    masks = []
                    for a, b in bounds:
                        inside = a >= first if shift == 0 else a < first
                        masks.append(ones_where((point >= a) & (point <= b) & inside))
                    mask = jnp.concatenate(masks, axis=1)
                return value + dot(mask, pieces.rows(s))

            value = loop(pieces.count, add, jnp.zeros((BLOCK, LANES), F32))
            center = first + F32(z.span * z.slots // 2 - shift * z.span * z.slots)
            total += value * jnp.exp(-rate * (position - center))
        feature_ref[t * BLOCK : (t + 1) * BLOCK, :] = (total * runs.root(position)).astype(BF16)
    for copy in copies:
        copy.wait()


def swap(block, axis, distance):
    return lax.ppermute(block, axis, [(i, i ^ distance) for i in range(lax.axis_size(axis))])


def spread(blocks, axis):
    distance = lax.axis_size(axis) // 2
    while distance:
        blocks = blocks + [swap(block, axis, distance) for block in blocks]
        distance //= 2
    return blocks


def on_device(events, event_weight, route, bucket, segment, decay_rate):
    rows, width = events.shape
    key_count, shard_count = lax.axis_size("key"), lax.axis_size("shard")
    owners = key_count * shard_count
    slots = segment.shape[0]
    z = Sizes(owners, rows, slots)
    block_rows = rows + z.code_rows
    smem = pl.BlockSpec(memory_space=pltpu.SMEM)
    vmem = pl.BlockSpec(memory_space=pltpu.VMEM)
    shape = jax.ShapeDtypeStruct
    grant = pltpu.CompilerParams(vmem_limit_bytes=(16 if owners <= 8 else 48) * 1024 * 1024)
    me = (lax.axis_index("key") * shard_count + lax.axis_index("shard")).astype(I32).reshape(1)
    block, own = pl.pallas_call(
        functools.partial(send_kernel, z),
        out_shape=(
            shape((block_rows, width), BF16),
            shape((16 + z.user_rows + 7, LANES), F32),
        ),
        in_specs=[smem, smem] + [vmem] * 5,
        out_specs=(vmem, vmem),
        compiler_params=pltpu.CompilerParams(vmem_limit_bytes=56 * 1024 * 1024),
        name="weigh",
    )(
        me, decay_rate, events, event_weight.reshape(z.chunks, LANES), route.reshape(z.chunks, LANES),
        bucket.reshape(z.chunks, LANES), segment.reshape(slots // LANES, LANES),
    )

    def flat(blocks):
        return [part[None] if part.ndim == 2 else part for parts in blocks for part in parts]

    def sums(blocks, before=()):
        blocks, form, count = flat(blocks), tuple(map(len, blocks)), len(blocks)
        lines = max(8, 2 * count)
        whole = shape((slots, width), F32)
        kept = (shape((lines * LANES, LANES), BF16), shape((lines, LANES), F32))
        return pl.pallas_call(
            functools.partial(early_kernel, z, form, len(before)),
            out_shape=((whole,) if before else (whole, whole)) + kept,
            in_specs=[vmem] * (1 + len(blocks) + len(before)),
            out_specs=(vmem,) * (3 if before else 4),
            scratch_shapes=[
                pltpu.VMEM((2, max(1, count), 8, LANES), F32),
                pltpu.VMEM((max(1, count), 2 * z.chunks, LANES), F32),
            ],
            compiler_params=grant,
            cost_estimate=pl.CostEstimate(flops=COST * count, bytes_accessed=0, transcendentals=0),
            name="more_sums" if before else "first_sums",
        )(own, *blocks, *before)

    if (key_count, shard_count) == (4, 2):
        tie = lax.optimization_barrier
        far = swap(block, "key", 2)
        side = swap(block, "shard", 1)
        near = swap(block, "key", 1)
        side_near = swap(side, "key", 1)
        total, scale, *tail = sums([(block,)])
        far, total = tie((far, total))
        last = swap(far, "key", 1)
        side_far = swap(far, "shard", 1)
        total, *tail2 = sums([(side,), (near,)], (total,))
        last, total = tie((last, total))
        side_last = swap(last, "shard", 1)
        second = [(far,), (last,), (side_far,)]
        late = [(side_near,), (side_last,)]
        total, *tail3 = sums(second, (total,))
        early, earlier, tails = [(block,), (side,), (near,)] + second, (1, 2, 3), tail + tail2 + tail3
    else:
        blocks = spread(spread([block], "key"), "shard")
        total, scale, *_ = sums([])
        early, earlier, tails = [], (), []
        late = [(jnp.concatenate(blocks, axis=0).reshape(owners, block_rows, width),)]
    late_lines = 2 * (len(late) if earlier else z.groups)
    late_count = len(late) if earlier else owners
    form = tuple(map(len, early + late))
    return pl.pallas_call(
        functools.partial(late_kernel, z, earlier, form, len(late)),
        out_shape=(shape((slots, width), BF16), shape((rows, width), BF16)),
        in_specs=[vmem] * (3 + len(tails) + sum(form)),
        out_specs=(pl.BlockSpec(memory_space=pl.ANY), vmem),
        scratch_shapes=[
            pltpu.VMEM((owners, 8, LANES), F32),
            pltpu.VMEM((owners, 8, LANES), F32),
            pltpu.VMEM((late_lines * LANES, LANES), BF16),
            pltpu.VMEM((late_lines, LANES), F32),
            pltpu.VMEM((2, late_count, 8, LANES), F32),
            pltpu.VMEM((late_count, 2 * z.chunks, LANES), F32),
            pltpu.VMEM((slots, width), BF16),
            pltpu.SemaphoreType.DMA((slots // z.window,)),
        ],
        compiler_params=grant,
        name="table_and_rows",
    )(own, total, scale, *tails, *flat(early + late))


def solution(mesh):
    placed = (
        P(("groups", "key", "shard"), "lane"),
        P(("groups", "key", "shard")),
        P(("groups", "key", "shard"), None),
        P(("groups", "key", "shard")),
        P(("groups", "key", "shard")),
        P("lane"),
    )
    return jax.shard_map(
        on_device,
        mesh=mesh,
        in_specs=placed,
        out_specs=(P(("groups", "key", "shard"), "lane"), P(("groups", "key", "shard"), "lane")),
        check_vma=False,
    )
```

```python
import functools
import jax
import jax.numpy as jnp
from jax import lax
from jax.experimental import pallas as pl
from jax.experimental.pallas import tpu as pltpu
from jax.sharding import PartitionSpec as P

LANES = 128
LOW = 7
MASK = 127
F32 = jnp.float32
BF16 = jnp.bfloat16
I32 = jnp.int32
I16 = jnp.int16
FAR = 1e9
NT = (((1,), (1,)), ((), ()))
BLOCK = 512
LATE_BLOCK = 256
COST = 1


class Sizes:
    def __init__(self, owners, rows, slots):
        self.owners, self.rows, self.slots = owners, rows, slots
        self.window = slots // 4
        self.chunks = rows // LANES
        self.user_rows = -(-8 * owners // LANES)
        self.code_rows = -(-(3 * self.chunks + 2 * self.user_rows) // 16) * 16
        self.span = min(owners, 8)
        self.shifts = 1 if owners <= self.span else 2
        self.capacity = 2 * rows // owners
        self.per_group = LANES // self.capacity
        self.groups = owners // self.per_group
        self.narrow = owners * slots <= 32768


def iota(shape, axis):
    return lax.broadcasted_iota(I32, shape, axis)


def ones_where(condition):
    return jnp.where(condition, F32(1), F32(0)).astype(BF16)


def dot(a, b):
    return jnp.dot(a, b, preferred_element_type=F32)


def loop(count, body, carry):
    if count <= 8:
        for i in range(count):
            carry = body(i, carry)
        return carry
    return lax.fori_loop(0, count, body, carry)


def send_kernel(z, me_ref, rate_ref, events_ref, weight_ref, route_ref, bucket_ref, segment_ref, out_ref, own_ref, block_ref, sems):
    groups = rate_ref.shape[0]
    lane = iota((1, LANES), 1)
    rate = jnp.full((1, LANES), rate_ref[0], F32)
    for g in range(1, groups):
        rate = jnp.where(lane >= g * (LANES // groups), rate_ref[g], rate)
    route = route_ref[...]
    bucket = bucket_ref[...]
    place = (route * z.slots + bucket).astype(F32)
    first = ((route >> (z.span.bit_length() - 1)) * (z.span * z.slots)).astype(F32)
    me = jnp.full((8 - 1, LANES), me_ref[0], I32).astype(F32)
    own_ref[0:16, :] = jnp.concatenate([place, first, rate, me], axis=0)
    spot = place - first - F32(z.span * z.slots // 2)
    columns = jnp.concatenate([weight_ref[...], spot], axis=0).T
    copies = []

    def send(first, count):
        part = pl.ds(first, count)
        copies.append(pltpu.make_async_copy(block_ref.at[part, :], out_ref.at[part, :], sems.at[len(copies)]))
        copies[-1].start()

    for r in range(z.chunks):
        part = slice(r * LANES, (r + 1) * LANES)
        weighted = (columns[:, r : r + 1] * events_ref[part, :].astype(F32)).astype(BF16)
        grown = weighted.astype(F32) * jnp.exp(columns[:, z.chunks + r : z.chunks + r + 1] * rate)
        block_ref[part, :] = grown.astype(BF16)
        if (r + 1) % (z.chunks // 2) == 0:
            send((r + 1) * LANES - z.rows // 2, z.rows // 2)
    ones = jnp.ones((8, LANES), BF16)
    high, low = [], []
    users = min(LANES, 8 * z.owners)
    for u in range(z.user_rows):
        user = iota((users, LANES), 0) + u * LANES
        below = jnp.zeros((users, LANES), F32)
        for r in range(z.slots // LANES):
            below += jnp.where(segment_ref[r : r + 1, :] < user, F32(1), F32(0))
        count = lax.dot_general(ones, below.astype(BF16), NT, preferred_element_type=F32)[0:1]
        if users < LANES:
            count = jnp.concatenate([count, jnp.full((1, LANES - users), z.slots, F32)], axis=1)
        own_ref[16 + u : 17 + u, :] = count
        count = count.astype(I32)
        high.append(count >> LOW)
        low.append(count & MASK)
    spare = z.code_rows - 3 * z.chunks - 2 * z.user_rows
    pad = [jnp.zeros((spare, LANES), I32)] if spare else []
    codes = jnp.concatenate([route, bucket >> LOW, bucket & MASK] + high + low + pad, axis=0)
    block_ref[z.rows : z.rows + z.code_rows, :] = codes.astype(F32).astype(BF16)
    send(z.rows, z.code_rows)
    for copy in copies:
        copy.wait()


class Pieces:
    def __init__(self, z, form, refs):
        self.z, refs = z, list(refs)
        self.parts = [[refs.pop(0) for _ in range(n)] for n in form]
        self.count = len(form) if len(form) != 1 else self.parts[0][0].shape[0]
        self.per_group = 1 if len(form) != 1 else z.per_group
        self.groups = self.count // self.per_group

    def block(self, s):
        return (self.parts[s], 0) if len(self.parts) != 1 else (self.parts[0], s)

    def codes(self, s):
        parts, i = self.block(s)
        first = parts[0].shape[1] - self.z.code_rows
        return parts[0][i, first : first + self.z.code_rows, :].astype(F32)

    def rows(self, s):
        parts, i = self.block(s)
        first = parts[0][i, 0 : parts[0].shape[1] - self.z.code_rows, :]
        return jnp.concatenate([first] + [part[i] for part in parts[1:]], axis=0)

    def place(self, s):
        n, tile = self.z.chunks, self.codes(s)
        return tile[0:n] * F32(self.z.slots) + F32(LANES) * tile[n : 2 * n] + tile[2 * n : 3 * n]

    def below(self, s, u):
        tile, at = self.codes(s), 3 * self.z.chunks + u
        return F32(LANES) * tile[at : at + 1] + tile[at + self.z.user_rows : at + self.z.user_rows + 1]


class Runs:
    def __init__(self, z, starts):
        self.z, self.starts = z, starts
        users = min(LANES, 8 * z.owners)
        self.columns = [jnp.broadcast_to(row, (8, LANES)).T[:users, 0:1] for row in starts]
        self.steps = []
        for u, row in enumerate(starts):
            before = pltpu.roll(row, 1, 1)
            first = starts[u - 1][:, LANES - 1 : LANES] if u else jnp.zeros((1, 1), F32)
            step = (row - jnp.where(iota((1, LANES), 1) == 0, first, before)).astype(I32)
            pair = [jnp.broadcast_to(part, (LANES, LANES)) for part in (step >> LOW, step & MASK)]
            self.steps.append(jnp.concatenate(pair, axis=0).astype(F32).astype(BF16))

    def start(self, position):
        total = jnp.zeros((position.shape[0], 2 * LANES), F32)
        for row, step in zip(self.starts, self.steps):
            total += lax.dot_general(ones_where(row <= position), step, NT, preferred_element_type=F32)
        return F32(LANES) * total[:, :LANES] + total[:, LANES:]

    def start_row(self, row):
        start = jnp.zeros((1, LANES), F32)
        for column in self.columns:
            start = jnp.maximum(start, jnp.max(jnp.where(column <= row, column, F32(0)), axis=0, keepdims=True))
        return start

    def until(self, row):
        after = jnp.full((1, LANES), FAR, F32)
        for column in self.columns:
            later = jnp.where(column > row, column, F32(FAR))
            after = jnp.minimum(after, jnp.min(later, axis=0, keepdims=True))
        return jnp.minimum(row + F32(self.z.window), after - F32(1))


def root(z, distance):
    return lax.rsqrt(jnp.minimum(distance, F32(z.window)) + F32(1))


def pack(z, pieces, base, marks_ref, codes_ref, rows_ref, from_ref):
    if not pieces.count:
        return
    spare = jnp.zeros((8 - z.chunks, LANES), F32)

    def mark(s, carry):
        local = pieces.place(s) - base
        near = local.astype(I32)
        codes_ref[s] = jnp.concatenate([near >> LOW, near & MASK], axis=0).astype(F32)
        own = (local >= 0) & (local < F32(z.slots))
        tail = (local >= F32(-z.window)) & (local < 0)
        marks_ref[0, s] = jnp.concatenate([jnp.where(own, F32(1), F32(0)), spare], axis=0)
        marks_ref[1, s] = jnp.concatenate([jnp.where(tail, F32(1), F32(0)), spare], axis=0)
        return carry

    loop(pieces.count, mark, 0)
    upper = ones_where(iota((LANES, LANES), 0) < iota((LANES, LANES), 1))
    full = jnp.ones((LANES, LANES), BF16)
    lines = pieces.count * 8
    at, by = iota((lines, lines), 0), iota((lines, lines), 1)
    earlier = ones_where(((at >> 3) == (by >> 3)) & (by < at))
    source = iota((lines, LANES), 0) >> 3
    offset = ((source & (pieces.per_group - 1)) * z.capacity).astype(F32)
    for kind in range(2):
        marked = marks_ref[kind].reshape(lines, LANES)
        mark = marked.astype(BF16)
        rank = dot(mark, upper) + dot(earlier, dot(mark, full).astype(BF16)) + offset
        marks_ref[kind] = jnp.where(marked > 0, rank, F32(-1)).reshape(pieces.count, 8, LANES)

    spots = iota((LANES, LANES), 0).astype(F32)
    code_line = iota((2 * z.chunks, LANES), 0) & (z.chunks - 1)
    for kind in range(2):
        for g in range(pieces.groups):

            def add(i, carry):
                values, places = carry
                s = g * pieces.per_group + i
                ranks = marks_ref[kind, s]
                codes = codes_ref[s]
                hot = jnp.concatenate([ones_where(spots == ranks[r : r + 1]) for r in range(z.chunks)], axis=1)
                wide = [jnp.where(code_line == r, codes, F32(0)).astype(BF16) for r in range(z.chunks)]
                values += dot(hot, pieces.rows(s))
                places += lax.dot_general(jnp.concatenate(wide, axis=1), hot, NT, preferred_element_type=F32)
                return values, places

            zero = (jnp.zeros((LANES, LANES), F32), jnp.zeros((2 * z.chunks, LANES), F32))
            values, places = loop(pieces.per_group, add, zero)
            line = kind * pieces.groups + g
            rows_ref[line * LANES : (line + 1) * LANES, :] = values.astype(BF16)
            high = jnp.sum(places[: z.chunks], axis=0, keepdims=True)
            low = jnp.sum(places[z.chunks :], axis=0, keepdims=True)
            from_ref[line : line + 1, :] = F32(LANES) * high + low


def held(position, bounds):
    one, nothing = BF16(1), BF16(0)
    masks = [jnp.where((position >= a) & (position <= b), one, nothing) for a, b in bounds]
    return jnp.concatenate(masks, axis=1)


def within(low, high, rows):
    if low.dtype == I16:
        one, nothing = BF16(1), BF16(0)
        return jnp.concatenate([jnp.where((low <= row) & (high >= row), one, nothing) for row in rows], axis=1)
    return jnp.concatenate([ones_where((low <= row) & (high >= row)) for row in rows], axis=1)


def wide_columns(rows):
    count = rows.shape[0]
    columns = jnp.concatenate([rows, jnp.zeros((8 - count, LANES), F32)], axis=0).T
    return jnp.concatenate([jnp.broadcast_to(columns[:, r : r + 1], (LANES, LANES)) for r in range(count)], axis=0)


def anchors(z, me):
    middle = F32(z.span * z.slots // 2)
    span_of = lambda owner: (owner.astype(I32) >> (z.span.bit_length() - 1)).astype(F32) * F32(z.span)
    own = (me - span_of(me)) * F32(z.slots) - middle
    tail = (me - span_of(me - F32(1))) * F32(z.slots) - middle
    return own, tail


def short(row):
    return row.astype(I32).astype(I16)


def early_kernel(z, form, before, *refs):
    count = sum(form)
    own_ref, pieces = refs[0], Pieces(z, form, refs[1 : 1 + count])
    refs = refs[1 + count :]
    if before:
        before_ref, sums_ref, rows_ref, from_ref, marks_ref, codes_ref = refs
    else:
        sums_ref, scale_ref, rows_ref, from_ref, high_ref, factor_ref, marks_ref, codes_ref = refs
    rate, me = own_ref[8:9, :], own_ref[9:10, :]
    runs = Runs(z, [own_ref[16 + u : 17 + u, :] for u in range(z.user_rows)])
    pack(z, pieces, me * F32(z.slots), marks_ref, codes_ref, rows_ref, from_ref)
    own_anchor, _ = anchors(z, me)
    inner = iota((BLOCK, LANES), 0)
    fall = jnp.exp(-rate * inner.astype(F32))
    bounds = []
    for g in range(pieces.groups if pieces.count else 0):
        begin = from_ref[g : g + 1, :]
        bounds.append((short(begin), short(runs.until(begin))))
    for b in range(z.slots // BLOCK):
        part = slice(b * BLOCK, (b + 1) * BLOCK)
        if bounds:
            mask = held((inner + b * BLOCK).astype(I16), bounds)
            value = dot(mask, rows_ref[0 : len(bounds) * LANES, :])
        else:
            value = jnp.zeros((BLOCK, LANES), F32)
        sums_ref[part, :] = value + before_ref[part, :] if before else value
        if not before:
            first = F32(b * BLOCK)
            position = inner.astype(F32) + first
            start = runs.start(position)
            if b * BLOCK < z.window:
                scale_ref[part, :] = start
            else:
                scale_ref[part, :] = fall * jnp.exp(-rate * (first + own_anchor)) * root(z, position - start)
    if not before:
        position, span_start = wide_columns(own_ref[0 : z.chunks, :]), wide_columns(own_ref[z.chunks : 2 * z.chunks, :])
        for shift in range(z.shifts):
            part = slice(shift * z.rows, (shift + 1) * z.rows)
            center = span_start + F32(z.span * z.slots // 2 - shift * z.span * z.slots)
            factor_ref[part, :] = jnp.exp(-rate * (position - center))
            top = position if shift == 0 else span_start - F32(1)
            high_ref[part, :] = short(top) if z.narrow else top


def late_kernel(z, earlier, form, late, *refs):
    own_ref, sums_ref, scale_ref, high_ref, factor_ref = refs[:5]
    tails = [refs[5 + 2 * i : 7 + 2 * i] for i in range(len(earlier))]
    refs = refs[5 + 2 * len(earlier) :]
    count = sum(form)
    table_out, feature_out, rows_ref, from_ref, marks_ref, codes_ref, table_ref, feature_ref, sems = refs[count:]
    pieces, last = Pieces(z, form, refs[:count]), Pieces(z, form[-late:], refs[count - sum(form[-late:]) : count])
    rate, me = own_ref[8:9, :], own_ref[9:10, :]
    base = me * F32(z.slots)
    starts = []
    for u in range(z.user_rows):
        add = lambda s, total: total + pieces.below(s, u)
        starts.append(loop(pieces.count, add, jnp.zeros((1, LANES), F32)))
    runs = Runs(z, starts)
    copies = []

    def send(ref, out, part):
        copies.append(pltpu.make_async_copy(ref.at[part, :], out.at[part, :], sems.at[len(copies)]))
        copies[-1].start()

    place = own_ref[0 : z.chunks, :]
    start = jnp.concatenate([runs.start_row(place[r : r + 1]) for r in range(z.chunks)], axis=0)
    scale = wide_columns(root(z, place - start))
    low = wide_columns(jnp.maximum(place - F32(z.window), start))
    span_start = wide_columns(own_ref[z.chunks : 2 * z.chunks, :]) if z.shifts > 1 else None
    kind = short if z.narrow else lambda row: row
    total = jnp.zeros((z.rows, LANES), F32)
    for shift in range(z.shifts):
        part = slice(shift * z.rows, (shift + 1) * z.rows)
        bottom = kind(jnp.maximum(low, span_start) if shift == 0 and z.shifts > 1 else low)
        top = high_ref[part, :]

        def add(s, value):
            rows = pieces.place(s)
            mask = within(bottom, top, [kind(rows[r : r + 1]) for r in range(z.chunks)])
            return value + dot(mask, pieces.rows(s))

        total += loop(pieces.count, add, jnp.zeros((z.rows, LANES), F32)) * factor_ref[part, :]
    feature_ref[...] = (total * scale).astype(BF16)
    send(feature_ref, feature_out, slice(0, z.rows))

    pack(z, last, base, marks_ref, codes_ref, rows_ref, from_ref)
    own_anchor, tail_anchor = anchors(z, me)
    inner = iota((LATE_BLOCK, LANES), 0)
    fall = jnp.exp(-rate * inner.astype(F32))
    first_start = jnp.max(runs.start_row(base), axis=1, keepdims=True) - base
    bounds = []
    listed = [(from_ref, 0, 2 * last.groups)] + [(ref, count, count) for (_, ref), count in zip(tails, earlier)]
    for ref, first, lines in listed:
        for g in range(first, first + lines):
            begin = ref[g : g + 1, :]
            bounds.append((short(begin), short(runs.until(begin + base) - base)))
    n = last.groups
    own_rows = rows_ref[0 : n * LANES, :]
    tail_rows = [rows_ref[n * LANES : 2 * n * LANES, :]]
    tail_rows += [ref[count * LANES : 2 * count * LANES, :] for (ref, _), count in zip(tails, earlier)]
    tail_rows = jnp.concatenate(tail_rows, axis=0)
    for b in range(z.slots // LATE_BLOCK):
        part = slice(b * LATE_BLOCK, (b + 1) * LATE_BLOCK)
        position = (inner + b * LATE_BLOCK).astype(I16)
        first = F32(b * LATE_BLOCK)
        value = sums_ref[part, :]
        if b * LATE_BLOCK >= z.window:
            value = (value + dot(held(position, bounds[:n]), own_rows)) * scale_ref[part, :]
        else:
            own_fall = jnp.exp(-rate * (first + own_anchor))
            if z.shifts == 1:
                value += dot(held(position, bounds), jnp.concatenate([own_rows, tail_rows], axis=0))
                value *= own_fall
            else:
                value = (value + dot(held(position, bounds[:n]), own_rows)) * own_fall
                value += dot(held(position, bounds[n:]), tail_rows) * jnp.exp(-rate * (first + tail_anchor))
            start = scale_ref[part, :]
            start = jnp.where(start > 0, start, first_start)
            value = value * fall * root(z, inner.astype(F32) + first - start)
        table_ref[part, :] = value.astype(BF16)
        if (b + 1) * LATE_BLOCK % z.window == 0:
            send(table_ref, table_out, slice((b + 1) * LATE_BLOCK - z.window, (b + 1) * LATE_BLOCK))
    for copy in copies:
        copy.wait()


def swap(block, axis, distance):
    return lax.ppermute(block, axis, [(i, i ^ distance) for i in range(lax.axis_size(axis))])


def spread(blocks, axis):
    distance = lax.axis_size(axis) // 2
    while distance:
        blocks = blocks + [swap(block, axis, distance) for block in blocks]
        distance //= 2
    return blocks


def on_device(events, event_weight, route, bucket, segment, decay_rate):
    rows, width = events.shape
    key_count, shard_count = lax.axis_size("key"), lax.axis_size("shard")
    owners = key_count * shard_count
    slots = segment.shape[0]
    z = Sizes(owners, rows, slots)
    block_rows = rows + z.code_rows
    smem = pl.BlockSpec(memory_space=pltpu.SMEM)
    vmem = pl.BlockSpec(memory_space=pltpu.VMEM)
    shape = jax.ShapeDtypeStruct
    grant = pltpu.CompilerParams(vmem_limit_bytes=(16 if owners <= 8 else 48) * 1024 * 1024)
    me = (lax.axis_index("key") * shard_count + lax.axis_index("shard")).astype(I32).reshape(1)
    block, own = pl.pallas_call(
        functools.partial(send_kernel, z),
        out_shape=(
            shape((block_rows, width), BF16),
            shape((16 + z.user_rows + 7, LANES), F32),
        ),
        in_specs=[smem, smem] + [vmem] * 5,
        out_specs=(pl.BlockSpec(memory_space=pl.ANY), vmem),
        scratch_shapes=[pltpu.VMEM((block_rows, width), BF16), pltpu.SemaphoreType.DMA((3,))],
        compiler_params=pltpu.CompilerParams(vmem_limit_bytes=56 * 1024 * 1024),
        name="weigh",
    )(
        me, decay_rate, events, event_weight.reshape(z.chunks, LANES), route.reshape(z.chunks, LANES),
        bucket.reshape(z.chunks, LANES), segment.reshape(slots // LANES, LANES),
    )

    def flat(blocks):
        return [part[None] if part.ndim == 2 else part for parts in blocks for part in parts]

    def sums(blocks, before=()):
        blocks, form, count = flat(blocks), tuple(map(len, blocks)), len(blocks)
        lines = max(8, 2 * count)
        whole = shape((slots, width), F32)
        kept = (shape((lines * LANES, LANES), BF16), shape((lines, LANES), F32))
        factors = shape((z.shifts * rows, width), F32)
        tops = shape((z.shifts * rows, width), I16 if z.narrow else F32)
        return pl.pallas_call(
            functools.partial(early_kernel, z, form, len(before)),
            out_shape=(whole,) + kept if before else (whole, whole) + kept + (tops, factors),
            in_specs=[vmem] * (1 + len(blocks) + len(before)),
            out_specs=(vmem,) * (3 if before else 6),
            scratch_shapes=[
                pltpu.VMEM((2, max(1, count), 8, LANES), F32),
                pltpu.VMEM((max(1, count), 2 * z.chunks, LANES), F32),
            ],
            compiler_params=grant,
            cost_estimate=pl.CostEstimate(flops=COST * count, bytes_accessed=0, transcendentals=0),
            name="more_sums" if before else "first_sums",
        )(own, *blocks, *before)

    if (key_count, shard_count) == (4, 2):
        tie = lax.optimization_barrier
        far = swap(block, "key", 2)
        side = swap(block, "shard", 1)
        near = swap(block, "key", 1)
        side_near = swap(side, "key", 1)
        total, scale, *tail, tops, factors = sums([(block,)])
        far, total = tie((far, total))
        last = swap(far, "key", 1)
        side_far = swap(far, "shard", 1)
        total, *tail2 = sums([(side,), (near,)], (total,))
        last, total = tie((last, total))
        side_last = swap(last, "shard", 1)
        second = [(far,), (last,), (side_far,)]
        late = [(side_near,), (side_last,)]
        total, *tail3 = sums(second, (total,))
        early, earlier, tails = [(block,), (side,), (near,)] + second, (1, 2, 3), tail + tail2 + tail3
    else:
        blocks = spread(spread([block], "key"), "shard")
        total, scale, _, _, tops, factors = sums([])
        early, earlier, tails = [], (), []
        late = [(jnp.concatenate(blocks, axis=0).reshape(owners, block_rows, width),)]
    late_lines = 2 * (len(late) if earlier else z.groups)
    late_count = len(late) if earlier else owners
    form = tuple(map(len, early + late))
    return pl.pallas_call(
        functools.partial(late_kernel, z, earlier, form, len(late)),
        out_shape=(shape((slots, width), BF16), shape((rows, width), BF16)),
        in_specs=[vmem] * (5 + len(tails) + sum(form)),
        out_specs=(pl.BlockSpec(memory_space=pl.ANY),) * 2,
        scratch_shapes=[
            pltpu.VMEM((late_lines * LANES, LANES), BF16),
            pltpu.VMEM((late_lines, LANES), F32),
            pltpu.VMEM((2, late_count, 8, LANES), F32),
            pltpu.VMEM((late_count, 2 * z.chunks, LANES), F32),
            pltpu.VMEM((slots, width), BF16),
            pltpu.VMEM((rows, width), BF16),
            pltpu.SemaphoreType.DMA((1 + slots // z.window,)),
        ],
        compiler_params=grant,
        name="table_and_rows",
    )(own, total, scale, tops, factors, *tails, *flat(early + late))


def solution(mesh):
    placed = (
        P(("groups", "key", "shard"), "lane"),
        P(("groups", "key", "shard")),
        P(("groups", "key", "shard"), None),
        P(("groups", "key", "shard")),
        P(("groups", "key", "shard")),
        P("lane"),
    )
    return jax.shard_map(
        on_device,
        mesh=mesh,
        in_specs=placed,
        out_specs=(P(("groups", "key", "shard"), "lane"), P(("groups", "key", "shard"), "lane")),
        check_vma=False,
    )
```

```python
import functools
import jax
import jax.numpy as jnp
from jax import lax
from jax.experimental import pallas as pl
from jax.experimental.pallas import tpu as pltpu
from jax.sharding import PartitionSpec as P

LANES = 128
LOW = 7
MASK = 127
F32 = jnp.float32
BF16 = jnp.bfloat16
I32 = jnp.int32
I16 = jnp.int16
FAR = 1e9
NT = (((1,), (1,)), ((), ()))
BLOCK = 512
LATE_BLOCK = 256
COST = 1


class Sizes:
    def __init__(self, owners, rows, slots):
        self.owners, self.rows, self.slots = owners, rows, slots
        self.window = slots // 4
        self.chunks = rows // LANES
        self.user_rows = -(-8 * owners // LANES)
        self.code_rows = -(-(3 * self.chunks + 2 * self.user_rows) // 16) * 16
        self.span = min(owners, 8)
        self.shifts = 1 if owners <= self.span else 2
        self.capacity = 2 * rows // owners
        self.per_group = LANES // self.capacity
        self.groups = owners // self.per_group
        self.narrow = owners * slots <= 32768


def iota(shape, axis):
    return lax.broadcasted_iota(I32, shape, axis)


def ones_where(condition):
    return jnp.where(condition, F32(1), F32(0)).astype(BF16)


def dot(a, b):
    return jnp.dot(a, b, preferred_element_type=F32)


def loop(count, body, carry):
    if count <= 8:
        for i in range(count):
            carry = body(i, carry)
        return carry
    return lax.fori_loop(0, count, body, carry)


def send_kernel(z, me_ref, rate_ref, events_ref, weight_ref, route_ref, bucket_ref, segment_ref, block_ref, own_ref):
    groups = rate_ref.shape[0]
    lane = iota((1, LANES), 1)
    rate = jnp.full((1, LANES), rate_ref[0], F32)
    for g in range(1, groups):
        rate = jnp.where(lane >= g * (LANES // groups), rate_ref[g], rate)
    route = route_ref[...]
    bucket = bucket_ref[...]
    place = (route * z.slots + bucket).astype(F32)
    first = ((route >> (z.span.bit_length() - 1)) * (z.span * z.slots)).astype(F32)
    me = jnp.full((8 - 1, LANES), me_ref[0], I32).astype(F32)
    own_ref[0:16, :] = jnp.concatenate([place, first, rate, me], axis=0)
    spot = place - first - F32(z.span * z.slots // 2)
    columns = jnp.concatenate([weight_ref[...], spot], axis=0).T
    for r in range(z.chunks):
        part = slice(r * LANES, (r + 1) * LANES)
        weighted = (columns[:, r : r + 1] * events_ref[part, :].astype(F32)).astype(BF16)
        grown = weighted.astype(F32) * jnp.exp(columns[:, z.chunks + r : z.chunks + r + 1] * rate)
        block_ref[part, :] = grown.astype(BF16)
    ones = jnp.ones((8, LANES), BF16)
    high, low = [], []
    users = min(LANES, 8 * z.owners)
    for u in range(z.user_rows):
        user = iota((users, LANES), 0) + u * LANES
        below = jnp.zeros((users, LANES), F32)
        for r in range(z.slots // LANES):
            below += jnp.where(segment_ref[r : r + 1, :] < user, F32(1), F32(0))
        count = lax.dot_general(ones, below.astype(BF16), NT, preferred_element_type=F32)[0:1]
        if users < LANES:
            count = jnp.concatenate([count, jnp.full((1, LANES - users), z.slots, F32)], axis=1)
        own_ref[16 + u : 17 + u, :] = count
        count = count.astype(I32)
        high.append(count >> LOW)
        low.append(count & MASK)
    spare = z.code_rows - 3 * z.chunks - 2 * z.user_rows
    pad = [jnp.zeros((spare, LANES), I32)] if spare else []
    codes = jnp.concatenate([route, bucket >> LOW, bucket & MASK] + high + low + pad, axis=0)
    block_ref[z.rows : z.rows + z.code_rows, :] = codes.astype(F32).astype(BF16)


class Pieces:
    def __init__(self, z, form, refs):
        self.z, refs = z, list(refs)
        self.parts = [[refs.pop(0) for _ in range(n)] for n in form]
        self.count = len(form) if len(form) != 1 else self.parts[0][0].shape[0]
        self.per_group = 1 if len(form) != 1 else z.per_group
        self.groups = self.count // self.per_group

    def block(self, s):
        return (self.parts[s], 0) if len(self.parts) != 1 else (self.parts[0], s)

    def codes(self, s):
        parts, i = self.block(s)
        first = parts[0].shape[1] - self.z.code_rows
        return parts[0][i, first : first + self.z.code_rows, :].astype(F32)

    def rows(self, s):
        parts, i = self.block(s)
        first = parts[0][i, 0 : parts[0].shape[1] - self.z.code_rows, :]
        return jnp.concatenate([first] + [part[i] for part in parts[1:]], axis=0)

    def place(self, s):
        n, tile = self.z.chunks, self.codes(s)
        return tile[0:n] * F32(self.z.slots) + F32(LANES) * tile[n : 2 * n] + tile[2 * n : 3 * n]

    def below(self, s, u):
        tile, at = self.codes(s), 3 * self.z.chunks + u
        return F32(LANES) * tile[at : at + 1] + tile[at + self.z.user_rows : at + self.z.user_rows + 1]


class Runs:
    def __init__(self, z, starts):
        self.z, self.starts = z, starts
        users = min(LANES, 8 * z.owners)
        self.columns = [jnp.broadcast_to(row, (8, LANES)).T[:users, 0:1] for row in starts]
        self.steps = []
        for u, row in enumerate(starts):
            before = pltpu.roll(row, 1, 1)
            first = starts[u - 1][:, LANES - 1 : LANES] if u else jnp.zeros((1, 1), F32)
            step = (row - jnp.where(iota((1, LANES), 1) == 0, first, before)).astype(I32)
            pair = [jnp.broadcast_to(part, (LANES, LANES)) for part in (step >> LOW, step & MASK)]
            self.steps.append(jnp.concatenate(pair, axis=0).astype(F32).astype(BF16))

    def start(self, position):
        total = jnp.zeros((position.shape[0], 2 * LANES), F32)
        for row, step in zip(self.starts, self.steps):
            total += lax.dot_general(ones_where(row <= position), step, NT, preferred_element_type=F32)
        return F32(LANES) * total[:, :LANES] + total[:, LANES:]

    def start_row(self, row):
        start = jnp.zeros((1, LANES), F32)
        for column in self.columns:
            start = jnp.maximum(start, jnp.max(jnp.where(column <= row, column, F32(0)), axis=0, keepdims=True))
        return start

    def until(self, row):
        after = jnp.full((1, LANES), FAR, F32)
        for column in self.columns:
            later = jnp.where(column > row, column, F32(FAR))
            after = jnp.minimum(after, jnp.min(later, axis=0, keepdims=True))
        return jnp.minimum(row + F32(self.z.window), after - F32(1))


def root(z, distance):
    return lax.rsqrt(jnp.minimum(distance, F32(z.window)) + F32(1))


def pack(z, pieces, base, marks_ref, codes_ref, rows_ref, from_ref):
    if not pieces.count:
        return
    spare = jnp.zeros((8 - z.chunks, LANES), F32)

    def mark(s, carry):
        local = pieces.place(s) - base
        near = local.astype(I32)
        codes_ref[s] = jnp.concatenate([near >> LOW, near & MASK], axis=0).astype(F32)
        own = (local >= 0) & (local < F32(z.slots))
        tail = (local >= F32(-z.window)) & (local < 0)
        marks_ref[0, s] = jnp.concatenate([jnp.where(own, F32(1), F32(0)), spare], axis=0)
        marks_ref[1, s] = jnp.concatenate([jnp.where(tail, F32(1), F32(0)), spare], axis=0)
        return carry

    loop(pieces.count, mark, 0)
    upper = ones_where(iota((LANES, LANES), 0) < iota((LANES, LANES), 1))
    full = jnp.ones((LANES, LANES), BF16)
    lines = pieces.count * 8
    at, by = iota((lines, lines), 0), iota((lines, lines), 1)
    earlier = ones_where(((at >> 3) == (by >> 3)) & (by < at))
    source = iota((lines, LANES), 0) >> 3
    offset = ((source & (pieces.per_group - 1)) * z.capacity).astype(F32)
    for kind in range(2):
        marked = marks_ref[kind].reshape(lines, LANES)
        mark = marked.astype(BF16)
        rank = dot(mark, upper) + dot(earlier, dot(mark, full).astype(BF16)) + offset
        marks_ref[kind] = jnp.where(marked > 0, rank, F32(-1)).reshape(pieces.count, 8, LANES)

    spots = iota((LANES, LANES), 0).astype(F32)
    code_line = iota((2 * z.chunks, LANES), 0) & (z.chunks - 1)
    for kind in range(2):
        for g in range(pieces.groups):

            def add(i, carry):
                values, places = carry
                s = g * pieces.per_group + i
                ranks = marks_ref[kind, s]
                codes = codes_ref[s]
                hot = jnp.concatenate([ones_where(spots == ranks[r : r + 1]) for r in range(z.chunks)], axis=1)
                wide = [jnp.where(code_line == r, codes, F32(0)).astype(BF16) for r in range(z.chunks)]
                values += dot(hot, pieces.rows(s))
                places += lax.dot_general(jnp.concatenate(wide, axis=1), hot, NT, preferred_element_type=F32)
                return values, places

            zero = (jnp.zeros((LANES, LANES), F32), jnp.zeros((2 * z.chunks, LANES), F32))
            values, places = loop(pieces.per_group, add, zero)
            line = kind * pieces.groups + g
            rows_ref[line * LANES : (line + 1) * LANES, :] = values.astype(BF16)
            high = jnp.sum(places[: z.chunks], axis=0, keepdims=True)
            low = jnp.sum(places[z.chunks :], axis=0, keepdims=True)
            from_ref[line : line + 1, :] = F32(LANES) * high + low


def held(position, bounds):
    one, nothing = BF16(1), BF16(0)
    masks = [jnp.where((position >= a) & (position <= b), one, nothing) for a, b in bounds]
    return jnp.concatenate(masks, axis=1)


def within(low, high, rows):
    if low.dtype == I16:
        one, nothing = BF16(1), BF16(0)
        return jnp.concatenate([jnp.where((low <= row) & (high >= row), one, nothing) for row in rows], axis=1)
    return jnp.concatenate([ones_where((low <= row) & (high >= row)) for row in rows], axis=1)


def wide_columns(rows):
    count = rows.shape[0]
    columns = jnp.concatenate([rows, jnp.zeros((8 - count, LANES), F32)], axis=0).T
    return jnp.concatenate([jnp.broadcast_to(columns[:, r : r + 1], (LANES, LANES)) for r in range(count)], axis=0)


def anchors(z, me):
    middle = F32(z.span * z.slots // 2)
    span_of = lambda owner: (owner.astype(I32) >> (z.span.bit_length() - 1)).astype(F32) * F32(z.span)
    own = (me - span_of(me)) * F32(z.slots) - middle
    tail = (me - span_of(me - F32(1))) * F32(z.slots) - middle
    return own, tail


def short(row):
    return row.astype(I32).astype(I16)


def early_kernel(z, form, before, *refs):
    count = sum(form)
    own_ref, pieces = refs[0], Pieces(z, form, refs[1 : 1 + count])
    refs = refs[1 + count :]
    if before:
        before_ref, sums_ref, rows_ref, from_ref, marks_ref, codes_ref = refs
    else:
        sums_ref, scale_ref, rows_ref, from_ref, high_ref, factor_ref, marks_ref, codes_ref = refs
    rate, me = own_ref[8:9, :], own_ref[9:10, :]
    runs = Runs(z, [own_ref[16 + u : 17 + u, :] for u in range(z.user_rows)])
    pack(z, pieces, me * F32(z.slots), marks_ref, codes_ref, rows_ref, from_ref)
    own_anchor, _ = anchors(z, me)
    inner = iota((BLOCK, LANES), 0)
    fall = jnp.exp(-rate * inner.astype(F32))
    bounds = []
    for g in range(pieces.groups if pieces.count else 0):
        begin = from_ref[g : g + 1, :]
        bounds.append((short(begin), short(runs.until(begin))))
    for b in range(z.slots // BLOCK):
        part = slice(b * BLOCK, (b + 1) * BLOCK)
        if bounds:
            mask = held((inner + b * BLOCK).astype(I16), bounds)
            value = dot(mask, rows_ref[0 : len(bounds) * LANES, :])
        else:
            value = jnp.zeros((BLOCK, LANES), F32)
        sums_ref[part, :] = value + before_ref[part, :] if before else value
        if not before:
            first = F32(b * BLOCK)
            position = inner.astype(F32) + first
            start = runs.start(position)
            if b * BLOCK < z.window:
                scale_ref[part, :] = start
            else:
                scale_ref[part, :] = fall * jnp.exp(-rate * (first + own_anchor)) * root(z, position - start)
    if not before:
        position, span_start = wide_columns(own_ref[0 : z.chunks, :]), wide_columns(own_ref[z.chunks : 2 * z.chunks, :])
        for shift in range(z.shifts):
            part = slice(shift * z.rows, (shift + 1) * z.rows)
            center = span_start + F32(z.span * z.slots // 2 - shift * z.span * z.slots)
            factor_ref[part, :] = jnp.exp(-rate * (position - center))
            top = position if shift == 0 else span_start - F32(1)
            high_ref[part, :] = short(top) if z.narrow else top


def late_kernel(z, earlier, form, late, *refs):
    own_ref, sums_ref, scale_ref, high_ref, factor_ref = refs[:5]
    tails = [refs[5 + 2 * i : 7 + 2 * i] for i in range(len(earlier))]
    refs = refs[5 + 2 * len(earlier) :]
    count = sum(form)
    table_ref, feature_ref, rows_ref, from_ref, marks_ref, codes_ref = refs[count:]
    pieces, last = Pieces(z, form, refs[:count]), Pieces(z, form[-late:], refs[count - sum(form[-late:]) : count])
    rate, me = own_ref[8:9, :], own_ref[9:10, :]
    base = me * F32(z.slots)
    starts = []
    for u in range(z.user_rows):
        add = lambda s, total: total + pieces.below(s, u)
        starts.append(loop(pieces.count, add, jnp.zeros((1, LANES), F32)))
    runs = Runs(z, starts)

    place = own_ref[0 : z.chunks, :]
    start = jnp.concatenate([runs.start_row(place[r : r + 1]) for r in range(z.chunks)], axis=0)
    scale = wide_columns(root(z, place - start))
    low = wide_columns(jnp.maximum(place - F32(z.window), start))
    span_start = wide_columns(own_ref[z.chunks : 2 * z.chunks, :]) if z.shifts > 1 else None
    kind = short if z.narrow else lambda row: row
    total = jnp.zeros((z.rows, LANES), F32)
    for shift in range(z.shifts):
        part = slice(shift * z.rows, (shift + 1) * z.rows)
        bottom = kind(jnp.maximum(low, span_start) if shift == 0 and z.shifts > 1 else low)
        top = high_ref[part, :]

        def add(s, value):
            rows = pieces.place(s)
            mask = within(bottom, top, [kind(rows[r : r + 1]) for r in range(z.chunks)])
            return value + dot(mask, pieces.rows(s))

        total += loop(pieces.count, add, jnp.zeros((z.rows, LANES), F32)) * factor_ref[part, :]
    feature_ref[...] = (total * scale).astype(BF16)

    pack(z, last, base, marks_ref, codes_ref, rows_ref, from_ref)
    own_anchor, tail_anchor = anchors(z, me)
    inner = iota((LATE_BLOCK, LANES), 0)
    fall = jnp.exp(-rate * inner.astype(F32))
    first_start = jnp.max(runs.start_row(base), axis=1, keepdims=True) - base
    bounds = []
    listed = [(from_ref, 0, 2 * last.groups)] + [(ref, count, count) for (_, ref), count in zip(tails, earlier)]
    for ref, first, lines in listed:
        for g in range(first, first + lines):
            begin = ref[g : g + 1, :]
            bounds.append((short(begin), short(runs.until(begin + base) - base)))
    n = last.groups
    own_rows = rows_ref[0 : n * LANES, :]
    tail_rows = [rows_ref[n * LANES : 2 * n * LANES, :]]
    tail_rows += [ref[count * LANES : 2 * count * LANES, :] for (ref, _), count in zip(tails, earlier)]
    tail_rows = jnp.concatenate(tail_rows, axis=0)
    for b in range(z.slots // LATE_BLOCK):
        part = slice(b * LATE_BLOCK, (b + 1) * LATE_BLOCK)
        position = (inner + b * LATE_BLOCK).astype(I16)
        first = F32(b * LATE_BLOCK)
        value = sums_ref[part, :]
        if b * LATE_BLOCK >= z.window:
            value = (value + dot(held(position, bounds[:n]), own_rows)) * scale_ref[part, :]
        else:
            own_fall = jnp.exp(-rate * (first + own_anchor))
            if z.shifts == 1:
                value += dot(held(position, bounds), jnp.concatenate([own_rows, tail_rows], axis=0))
                value *= own_fall
            else:
                value = (value + dot(held(position, bounds[:n]), own_rows)) * own_fall
                value += dot(held(position, bounds[n:]), tail_rows) * jnp.exp(-rate * (first + tail_anchor))
            start = scale_ref[part, :]
            start = jnp.where(start > 0, start, first_start)
            value = value * fall * root(z, inner.astype(F32) + first - start)
        table_ref[part, :] = value.astype(BF16)


def swap(block, axis, distance):
    return lax.ppermute(block, axis, [(i, i ^ distance) for i in range(lax.axis_size(axis))])


def spread(blocks, axis):
    distance = lax.axis_size(axis) // 2
    while distance:
        blocks = blocks + [swap(block, axis, distance) for block in blocks]
        distance //= 2
    return blocks


def on_device(events, event_weight, route, bucket, segment, decay_rate):
    rows, width = events.shape
    key_count, shard_count = lax.axis_size("key"), lax.axis_size("shard")
    owners = key_count * shard_count
    slots = segment.shape[0]
    z = Sizes(owners, rows, slots)
    block_rows = rows + z.code_rows
    smem = pl.BlockSpec(memory_space=pltpu.SMEM)
    vmem = pl.BlockSpec(memory_space=pltpu.VMEM)
    shape = jax.ShapeDtypeStruct
    grant = pltpu.CompilerParams(vmem_limit_bytes=(16 if owners <= 8 else 48) * 1024 * 1024)
    me = (lax.axis_index("key") * shard_count + lax.axis_index("shard")).astype(I32).reshape(1)
    block, own = pl.pallas_call(
        functools.partial(send_kernel, z),
        out_shape=(
            shape((block_rows, width), BF16),
            shape((16 + z.user_rows + 7, LANES), F32),
        ),
        in_specs=[smem, smem] + [vmem] * 5,
        out_specs=(vmem, vmem),
        compiler_params=pltpu.CompilerParams(vmem_limit_bytes=56 * 1024 * 1024),
        name="weigh",
    )(
        me, decay_rate, events, event_weight.reshape(z.chunks, LANES), route.reshape(z.chunks, LANES),
        bucket.reshape(z.chunks, LANES), segment.reshape(slots // LANES, LANES),
    )

    def flat(blocks):
        return [part[None] if part.ndim == 2 else part for parts in blocks for part in parts]

    def sums(blocks, before=()):
        blocks, form, count = flat(blocks), tuple(map(len, blocks)), len(blocks)
        lines = max(8, 2 * count)
        whole = shape((slots, width), F32)
        kept = (shape((lines * LANES, LANES), BF16), shape((lines, LANES), F32))
        factors = shape((z.shifts * rows, width), F32)
        tops = shape((z.shifts * rows, width), I16 if z.narrow else F32)
        return pl.pallas_call(
            functools.partial(early_kernel, z, form, len(before)),
            out_shape=(whole,) + kept if before else (whole, whole) + kept + (tops, factors),
            in_specs=[vmem] * (1 + len(blocks) + len(before)),
            out_specs=(vmem,) * (3 if before else 6),
            scratch_shapes=[
                pltpu.VMEM((2, max(1, count), 8, LANES), F32),
                pltpu.VMEM((max(1, count), 2 * z.chunks, LANES), F32),
            ],
            compiler_params=grant,
            cost_estimate=pl.CostEstimate(flops=COST * count, bytes_accessed=0, transcendentals=0),
            name="more_sums" if before else "first_sums",
        )(own, *blocks, *before)

    if (key_count, shard_count) == (4, 2):
        tie = lax.optimization_barrier
        far = swap(block, "key", 2)
        side = swap(block, "shard", 1)
        near = swap(block, "key", 1)
        side_near = swap(side, "key", 1)
        total, scale, *tail, tops, factors = sums([(block,)])
        far, total = tie((far, total))
        last = swap(far, "key", 1)
        side_far = swap(far, "shard", 1)
        total, *tail2 = sums([(side,), (near,)], (total,))
        last, total = tie((last, total))
        side_last = swap(last, "shard", 1)
        second = [(far,), (last,), (side_far,)]
        late = [(side_near,), (side_last,)]
        total, *tail3 = sums(second, (total,))
        early, earlier, tails = [(block,), (side,), (near,)] + second, (1, 2, 3), tail + tail2 + tail3
    else:
        blocks = spread(spread([block], "key"), "shard")
        total, scale, _, _, tops, factors = sums([])
        early, earlier, tails = [], (), []
        late = [(jnp.concatenate(blocks, axis=0).reshape(owners, block_rows, width),)]
    late_lines = 2 * (len(late) if earlier else z.groups)
    late_count = len(late) if earlier else owners
    form = tuple(map(len, early + late))
    return pl.pallas_call(
        functools.partial(late_kernel, z, earlier, form, len(late)),
        out_shape=(shape((slots, width), BF16), shape((rows, width), BF16)),
        in_specs=[vmem] * (5 + len(tails) + sum(form)),
        out_specs=(vmem, vmem),
        scratch_shapes=[
            pltpu.VMEM((late_lines * LANES, LANES), BF16),
            pltpu.VMEM((late_lines, LANES), F32),
            pltpu.VMEM((2, late_count, 8, LANES), F32),
            pltpu.VMEM((late_count, 2 * z.chunks, LANES), F32),
        ],
        compiler_params=grant,
        name="table_and_rows",
    )(own, total, scale, tops, factors, *tails, *flat(early + late))


def solution(mesh):
    placed = (
        P(("groups", "key", "shard"), "lane"),
        P(("groups", "key", "shard")),
        P(("groups", "key", "shard"), None),
        P(("groups", "key", "shard")),
        P(("groups", "key", "shard")),
        P("lane"),
    )
    return jax.shard_map(
        on_device,
        mesh=mesh,
        in_specs=placed,
        out_specs=(P(("groups", "key", "shard"), "lane"), P(("groups", "key", "shard"), "lane")),
        check_vma=False,
    )
```

```python
import functools
import jax
import jax.numpy as jnp
from jax import lax
from jax.experimental import pallas as pl
from jax.experimental.pallas import tpu as pltpu
from jax.sharding import PartitionSpec as P

LANES = 128
LOW = 7
MASK = 127
F32 = jnp.float32
BF16 = jnp.bfloat16
I32 = jnp.int32
I16 = jnp.int16
FAR = 1e9
NT = (((1,), (1,)), ((), ()))
BLOCK = 512
LATE_BLOCK = 256
COST = 1


class Sizes:
    def __init__(self, owners, rows, slots):
        self.owners, self.rows, self.slots = owners, rows, slots
        self.window = slots // 4
        self.chunks = rows // LANES
        self.user_rows = -(-8 * owners // LANES)
        self.code_rows = -(-(3 * self.chunks + 2 * self.user_rows) // 16) * 16
        self.span = min(owners, 8)
        self.shifts = 1 if owners <= self.span else 2
        self.capacity = 2 * rows // owners
        self.per_group = LANES // self.capacity
        self.groups = owners // self.per_group
        self.narrow = owners * slots <= 32768


def iota(shape, axis):
    return lax.broadcasted_iota(I32, shape, axis)


def ones_where(condition):
    return jnp.where(condition, F32(1), F32(0)).astype(BF16)


def dot(a, b):
    return jnp.dot(a, b, preferred_element_type=F32)


def loop(count, body, carry):
    if count <= 8:
        for i in range(count):
            carry = body(i, carry)
        return carry
    return lax.fori_loop(0, count, body, carry)


def send_kernel(z, me_ref, rate_ref, events_ref, weight_ref, route_ref, bucket_ref, segment_ref, block_ref, own_ref):
    groups = rate_ref.shape[0]
    lane = iota((1, LANES), 1)
    rate = jnp.full((1, LANES), rate_ref[0], F32)
    for g in range(1, groups):
        rate = jnp.where(lane >= g * (LANES // groups), rate_ref[g], rate)
    route = route_ref[...]
    bucket = bucket_ref[...]
    place = (route * z.slots + bucket).astype(F32)
    first = ((route >> (z.span.bit_length() - 1)) * (z.span * z.slots)).astype(F32)
    me = jnp.full((8 - 1, LANES), me_ref[0], I32).astype(F32)
    own_ref[0:16, :] = jnp.concatenate([place, first, rate, me], axis=0)
    spot = place - first - F32(z.span * z.slots // 2)
    columns = jnp.concatenate([weight_ref[...], spot], axis=0).T
    for r in range(z.chunks):
        part = slice(r * LANES, (r + 1) * LANES)
        weighted = (columns[:, r : r + 1] * events_ref[part, :].astype(F32)).astype(BF16)
        grown = weighted.astype(F32) * jnp.exp(columns[:, z.chunks + r : z.chunks + r + 1] * rate)
        block_ref[part, :] = grown.astype(BF16)
    ones = jnp.ones((8, LANES), BF16)
    high, low = [], []
    users = min(LANES, 8 * z.owners)
    for u in range(z.user_rows):
        user = iota((users, LANES), 0) + u * LANES
        below = jnp.zeros((users, LANES), F32)
        for r in range(z.slots // LANES):
            below += jnp.where(segment_ref[r : r + 1, :] < user, F32(1), F32(0))
        count = lax.dot_general(ones, below.astype(BF16), NT, preferred_element_type=F32)[0:1]
        if users < LANES:
            count = jnp.concatenate([count, jnp.full((1, LANES - users), z.slots, F32)], axis=1)
        own_ref[16 + u : 17 + u, :] = count
        count = count.astype(I32)
        high.append(count >> LOW)
        low.append(count & MASK)
    spare = z.code_rows - 3 * z.chunks - 2 * z.user_rows
    pad = [jnp.zeros((spare, LANES), I32)] if spare else []
    codes = jnp.concatenate([route, bucket >> LOW, bucket & MASK] + high + low + pad, axis=0)
    block_ref[z.rows : z.rows + z.code_rows, :] = codes.astype(F32).astype(BF16)


class Pieces:
    def __init__(self, z, form, refs):
        self.z, refs = z, list(refs)
        self.parts = [[refs.pop(0) for _ in range(n)] for n in form]
        self.count = len(form) if len(form) != 1 else self.parts[0][0].shape[0]
        self.per_group = 1 if len(form) != 1 else z.per_group
        self.groups = self.count // self.per_group

    def block(self, s):
        return (self.parts[s], 0) if len(self.parts) != 1 else (self.parts[0], s)

    def codes(self, s):
        parts, i = self.block(s)
        first = parts[0].shape[1] - self.z.code_rows
        return parts[0][i, first : first + self.z.code_rows, :].astype(F32)

    def rows(self, s):
        parts, i = self.block(s)
        first = parts[0][i, 0 : parts[0].shape[1] - self.z.code_rows, :]
        return jnp.concatenate([first] + [part[i] for part in parts[1:]], axis=0)

    def place(self, s):
        n, tile = self.z.chunks, self.codes(s)
        return tile[0:n] * F32(self.z.slots) + F32(LANES) * tile[n : 2 * n] + tile[2 * n : 3 * n]

    def below(self, s, u):
        tile, at = self.codes(s), 3 * self.z.chunks + u
        return F32(LANES) * tile[at : at + 1] + tile[at + self.z.user_rows : at + self.z.user_rows + 1]


class Runs:
    def __init__(self, z, starts):
        self.z, self.starts = z, starts
        users = min(LANES, 8 * z.owners)
        self.columns = [jnp.broadcast_to(row, (8, LANES)).T[:users, 0:1] for row in starts]
        self.steps = []
        for u, row in enumerate(starts):
            before = pltpu.roll(row, 1, 1)
            first = starts[u - 1][:, LANES - 1 : LANES] if u else jnp.zeros((1, 1), F32)
            step = (row - jnp.where(iota((1, LANES), 1) == 0, first, before)).astype(I32)
            pair = [jnp.broadcast_to(part, (LANES, LANES)) for part in (step >> LOW, step & MASK)]
            self.steps.append(jnp.concatenate(pair, axis=0).astype(F32).astype(BF16))

    def start(self, position):
        total = jnp.zeros((position.shape[0], 2 * LANES), F32)
        for row, step in zip(self.starts, self.steps):
            total += lax.dot_general(ones_where(row <= position), step, NT, preferred_element_type=F32)
        return F32(LANES) * total[:, :LANES] + total[:, LANES:]

    def start_row(self, row):
        start = jnp.zeros((1, LANES), F32)
        for column in self.columns:
            start = jnp.maximum(start, jnp.max(jnp.where(column <= row, column, F32(0)), axis=0, keepdims=True))
        return start

    def until(self, row):
        after = jnp.full((1, LANES), FAR, F32)
        for column in self.columns:
            later = jnp.where(column > row, column, F32(FAR))
            after = jnp.minimum(after, jnp.min(later, axis=0, keepdims=True))
        return jnp.minimum(row + F32(self.z.window), after - F32(1))


def root(z, distance):
    return lax.rsqrt(jnp.minimum(distance, F32(z.window)) + F32(1))


def pack(z, pieces, base, marks_ref, codes_ref, rows_ref, from_ref):
    if not pieces.count:
        return
    spare = jnp.zeros((8 - z.chunks, LANES), F32)

    def mark(s, carry):
        local = pieces.place(s) - base
        near = local.astype(I32)
        codes_ref[s] = jnp.concatenate([near >> LOW, near & MASK], axis=0).astype(F32)
        own = (local >= 0) & (local < F32(z.slots))
        tail = (local >= F32(-z.window)) & (local < 0)
        marks_ref[0, s] = jnp.concatenate([jnp.where(own, F32(1), F32(0)), spare], axis=0)
        marks_ref[1, s] = jnp.concatenate([jnp.where(tail, F32(1), F32(0)), spare], axis=0)
        return carry

    loop(pieces.count, mark, 0)
    upper = ones_where(iota((LANES, LANES), 0) < iota((LANES, LANES), 1))
    full = jnp.ones((LANES, LANES), BF16)
    lines = pieces.count * 8
    at, by = iota((lines, lines), 0), iota((lines, lines), 1)
    earlier = ones_where(((at >> 3) == (by >> 3)) & (by < at))
    source = iota((lines, LANES), 0) >> 3
    offset = ((source & (pieces.per_group - 1)) * z.capacity).astype(F32)
    for kind in range(2):
        marked = marks_ref[kind].reshape(lines, LANES)
        mark = marked.astype(BF16)
        rank = dot(mark, upper) + dot(earlier, dot(mark, full).astype(BF16)) + offset
        marks_ref[kind] = jnp.where(marked > 0, rank, F32(-1)).reshape(pieces.count, 8, LANES)

    spots = iota((LANES, LANES), 0).astype(F32)
    code_line = iota((2 * z.chunks, LANES), 0) & (z.chunks - 1)
    for kind in range(2):
        for g in range(pieces.groups):

            def add(i, carry):
                values, places = carry
                s = g * pieces.per_group + i
                ranks = marks_ref[kind, s]
                codes = codes_ref[s]
                hot = jnp.concatenate([ones_where(spots == ranks[r : r + 1]) for r in range(z.chunks)], axis=1)
                wide = [jnp.where(code_line == r, codes, F32(0)).astype(BF16) for r in range(z.chunks)]
                values += dot(hot, pieces.rows(s))
                places += lax.dot_general(jnp.concatenate(wide, axis=1), hot, NT, preferred_element_type=F32)
                return values, places

            zero = (jnp.zeros((LANES, LANES), F32), jnp.zeros((2 * z.chunks, LANES), F32))
            values, places = loop(pieces.per_group, add, zero)
            line = kind * pieces.groups + g
            rows_ref[line * LANES : (line + 1) * LANES, :] = values.astype(BF16)
            high = jnp.sum(places[: z.chunks], axis=0, keepdims=True)
            low = jnp.sum(places[z.chunks :], axis=0, keepdims=True)
            from_ref[line : line + 1, :] = F32(LANES) * high + low


def held(position, bounds):
    one, nothing = BF16(1), BF16(0)
    masks = [jnp.where((position >= a) & (position <= b), one, nothing) for a, b in bounds]
    return jnp.concatenate(masks, axis=1)


def within(low, high, rows):
    if low.dtype == I16:
        one, nothing = BF16(1), BF16(0)
        return jnp.concatenate([jnp.where((low <= row) & (high >= row), one, nothing) for row in rows], axis=1)
    return jnp.concatenate([ones_where((low <= row) & (high >= row)) for row in rows], axis=1)


def wide_columns(rows):
    count = rows.shape[0]
    columns = jnp.concatenate([rows, jnp.zeros((8 - count, LANES), F32)], axis=0).T
    return jnp.concatenate([jnp.broadcast_to(columns[:, r : r + 1], (LANES, LANES)) for r in range(count)], axis=0)


def anchors(z, me):
    middle = F32(z.span * z.slots // 2)
    span_of = lambda owner: (owner.astype(I32) >> (z.span.bit_length() - 1)).astype(F32) * F32(z.span)
    own = (me - span_of(me)) * F32(z.slots) - middle
    tail = (me - span_of(me - F32(1))) * F32(z.slots) - middle
    return own, tail


def short(row):
    return row.astype(I32).astype(I16)


def early_kernel(z, form, before, *refs):
    count = sum(form)
    own_ref, pieces = refs[0], Pieces(z, form, refs[1 : 1 + count])
    refs = refs[1 + count :]
    if before:
        before_ref, sums_ref, rows_ref, from_ref, marks_ref, codes_ref = refs
    else:
        sums_ref, scale_ref, rows_ref, from_ref, high_ref, factor_ref, marks_ref, codes_ref = refs
    rate, me = own_ref[8:9, :], own_ref[9:10, :]
    runs = Runs(z, [own_ref[16 + u : 17 + u, :] for u in range(z.user_rows)])
    pack(z, pieces, me * F32(z.slots), marks_ref, codes_ref, rows_ref, from_ref)
    own_anchor, _ = anchors(z, me)
    inner = iota((BLOCK, LANES), 0)
    fall = jnp.exp(-rate * inner.astype(F32))
    bounds = []
    for g in range(pieces.groups if pieces.count else 0):
        begin = from_ref[g : g + 1, :]
        bounds.append((short(begin), short(runs.until(begin))))
    for b in range(z.slots // BLOCK):
        part = slice(b * BLOCK, (b + 1) * BLOCK)
        if bounds:
            mask = held((inner + b * BLOCK).astype(I16), bounds)
            value = dot(mask, rows_ref[0 : len(bounds) * LANES, :])
        else:
            value = jnp.zeros((BLOCK, LANES), F32)
        sums_ref[part, :] = value + before_ref[part, :] if before else value
        if not before:
            first = F32(b * BLOCK)
            position = inner.astype(F32) + first
            start = runs.start(position)
            if b * BLOCK < z.window:
                scale_ref[part, :] = start
            else:
                scale_ref[part, :] = fall * jnp.exp(-rate * (first + own_anchor)) * root(z, position - start)
    if not before:
        position, span_start = wide_columns(own_ref[0 : z.chunks, :]), wide_columns(own_ref[z.chunks : 2 * z.chunks, :])
        for shift in range(z.shifts):
            part = slice(shift * z.rows, (shift + 1) * z.rows)
            center = span_start + F32(z.span * z.slots // 2 - shift * z.span * z.slots)
            factor_ref[part, :] = jnp.exp(-rate * (position - center))
            top = position if shift == 0 else span_start - F32(1)
            high_ref[part, :] = short(top) if z.narrow else top


def late_kernel(z, earlier, form, late, *refs):
    own_ref, sums_ref, scale_ref, high_ref, factor_ref = refs[:5]
    tails = [refs[5 + 2 * i : 7 + 2 * i] for i in range(len(earlier))]
    refs = refs[5 + 2 * len(earlier) :]
    count = sum(form)
    table_out, feature_out, rows_ref, from_ref, marks_ref, codes_ref, table_ref, feature_ref, sems = refs[count:]
    pieces, last = Pieces(z, form, refs[:count]), Pieces(z, form[-late:], refs[count - sum(form[-late:]) : count])
    rate, me = own_ref[8:9, :], own_ref[9:10, :]
    base = me * F32(z.slots)
    starts = []
    for u in range(z.user_rows):
        add = lambda s, total: total + pieces.below(s, u)
        starts.append(loop(pieces.count, add, jnp.zeros((1, LANES), F32)))
    runs = Runs(z, starts)
    copies = []

    def send(ref, out, part):
        copies.append(pltpu.make_async_copy(ref.at[part, :], out.at[part, :], sems.at[len(copies)]))
        copies[-1].start()

    pack(z, last, base, marks_ref, codes_ref, rows_ref, from_ref)

    place = own_ref[0 : z.chunks, :]
    start = jnp.concatenate([runs.start_row(place[r : r + 1]) for r in range(z.chunks)], axis=0)
    scale = wide_columns(root(z, place - start))
    low = wide_columns(jnp.maximum(place - F32(z.window), start))
    span_start = wide_columns(own_ref[z.chunks : 2 * z.chunks, :]) if z.shifts > 1 else None
    kind = short if z.narrow else lambda row: row
    total = jnp.zeros((z.rows, LANES), F32)
    for shift in range(z.shifts):
        part = slice(shift * z.rows, (shift + 1) * z.rows)
        bottom = kind(jnp.maximum(low, span_start) if shift == 0 and z.shifts > 1 else low)
        top = high_ref[part, :]

        def add(s, value):
            rows = pieces.place(s)
            mask = within(bottom, top, [kind(rows[r : r + 1]) for r in range(z.chunks)])
            return value + dot(mask, pieces.rows(s))

        total += loop(pieces.count, add, jnp.zeros((z.rows, LANES), F32)) * factor_ref[part, :]
    feature_ref[...] = (total * scale).astype(BF16)
    send(feature_ref, feature_out, slice(0, z.rows))

    own_anchor, tail_anchor = anchors(z, me)
    inner = iota((LATE_BLOCK, LANES), 0)
    fall = jnp.exp(-rate * inner.astype(F32))
    first_start = jnp.max(runs.start_row(base), axis=1, keepdims=True) - base
    bounds = []
    listed = [(from_ref, 0, 2 * last.groups)] + [(ref, count, count) for (_, ref), count in zip(tails, earlier)]
    for ref, first, lines in listed:
        for g in range(first, first + lines):
            begin = ref[g : g + 1, :]
            bounds.append((short(begin), short(runs.until(begin + base) - base)))
    n = last.groups
    own_rows = rows_ref[0 : n * LANES, :]
    tail_rows = [rows_ref[n * LANES : 2 * n * LANES, :]]
    tail_rows += [ref[count * LANES : 2 * count * LANES, :] for (ref, _), count in zip(tails, earlier)]
    tail_rows = jnp.concatenate(tail_rows, axis=0)
    for b in range(z.slots // LATE_BLOCK):
        part = slice(b * LATE_BLOCK, (b + 1) * LATE_BLOCK)
        position = (inner + b * LATE_BLOCK).astype(I16)
        first = F32(b * LATE_BLOCK)
        value = sums_ref[part, :]
        if b * LATE_BLOCK >= z.window:
            value = (value + dot(held(position, bounds[:n]), own_rows)) * scale_ref[part, :]
        else:
            own_fall = jnp.exp(-rate * (first + own_anchor))
            if z.shifts == 1:
                value += dot(held(position, bounds), jnp.concatenate([own_rows, tail_rows], axis=0))
                value *= own_fall
            else:
                value = (value + dot(held(position, bounds[:n]), own_rows)) * own_fall
                value += dot(held(position, bounds[n:]), tail_rows) * jnp.exp(-rate * (first + tail_anchor))
            start = scale_ref[part, :]
            start = jnp.where(start > 0, start, first_start)
            value = value * fall * root(z, inner.astype(F32) + first - start)
        table_ref[part, :] = value.astype(BF16)
        if (b + 1) * LATE_BLOCK % z.window == 0:
            send(table_ref, table_out, slice((b + 1) * LATE_BLOCK - z.window, (b + 1) * LATE_BLOCK))
    for copy in copies:
        copy.wait()


def swap(block, axis, distance):
    return lax.ppermute(block, axis, [(i, i ^ distance) for i in range(lax.axis_size(axis))])


def spread(blocks, axis):
    distance = lax.axis_size(axis) // 2
    while distance:
        blocks = blocks + [swap(block, axis, distance) for block in blocks]
        distance //= 2
    return blocks


def on_device(events, event_weight, route, bucket, segment, decay_rate):
    rows, width = events.shape
    key_count, shard_count = lax.axis_size("key"), lax.axis_size("shard")
    owners = key_count * shard_count
    slots = segment.shape[0]
    z = Sizes(owners, rows, slots)
    block_rows = rows + z.code_rows
    smem = pl.BlockSpec(memory_space=pltpu.SMEM)
    vmem = pl.BlockSpec(memory_space=pltpu.VMEM)
    shape = jax.ShapeDtypeStruct
    grant = pltpu.CompilerParams(vmem_limit_bytes=(16 if owners <= 8 else 48) * 1024 * 1024)
    me = (lax.axis_index("key") * shard_count + lax.axis_index("shard")).astype(I32).reshape(1)
    block, own = pl.pallas_call(
        functools.partial(send_kernel, z),
        out_shape=(
            shape((block_rows, width), BF16),
            shape((16 + z.user_rows + 7, LANES), F32),
        ),
        in_specs=[smem, smem] + [vmem] * 5,
        out_specs=(vmem, vmem),
        compiler_params=pltpu.CompilerParams(vmem_limit_bytes=56 * 1024 * 1024),
        name="weigh",
    )(
        me, decay_rate, events, event_weight.reshape(z.chunks, LANES), route.reshape(z.chunks, LANES),
        bucket.reshape(z.chunks, LANES), segment.reshape(slots // LANES, LANES),
    )

    def flat(blocks):
        return [part[None] if part.ndim == 2 else part for parts in blocks for part in parts]

    def sums(blocks, before=()):
        blocks, form, count = flat(blocks), tuple(map(len, blocks)), len(blocks)
        lines = max(8, 2 * count)
        whole = shape((slots, width), F32)
        kept = (shape((lines * LANES, LANES), BF16), shape((lines, LANES), F32))
        factors = shape((z.shifts * rows, width), F32)
        tops = shape((z.shifts * rows, width), I16 if z.narrow else F32)
        return pl.pallas_call(
            functools.partial(early_kernel, z, form, len(before)),
            out_shape=(whole,) + kept if before else (whole, whole) + kept + (tops, factors),
            in_specs=[vmem] * (1 + len(blocks) + len(before)),
            out_specs=(vmem,) * (3 if before else 6),
            scratch_shapes=[
                pltpu.VMEM((2, max(1, count), 8, LANES), F32),
                pltpu.VMEM((max(1, count), 2 * z.chunks, LANES), F32),
            ],
            compiler_params=grant,
            cost_estimate=pl.CostEstimate(flops=COST * count, bytes_accessed=0, transcendentals=0),
            name="more_sums" if before else "first_sums",
        )(own, *blocks, *before)

    if (key_count, shard_count) == (4, 2):
        tie = lax.optimization_barrier
        far = swap(block, "key", 2)
        side = swap(block, "shard", 1)
        near = swap(block, "key", 1)
        side_near = swap(side, "key", 1)
        total, scale, *tail, tops, factors = sums([(block,)])
        far, total = tie((far, total))
        last = swap(far, "key", 1)
        side_far = swap(far, "shard", 1)
        total, *tail2 = sums([(side,), (near,)], (total,))
        last, total = tie((last, total))
        side_last = swap(last, "shard", 1)
        second = [(far,), (last,), (side_far,)]
        total, *tail3 = sums(second, (total,))
        total, *tail4 = sums([(side_near,)], (total,))
        early = [(block,), (side,), (near,)] + second + [(side_near,)]
        earlier, tails, late = (1, 2, 3, 1), tail + tail2 + tail3 + tail4, [(side_last,)]
    else:
        blocks = spread(spread([block], "key"), "shard")
        total, scale, _, _, tops, factors = sums([])
        early, earlier, tails = [], (), []
        late = [(jnp.concatenate(blocks, axis=0).reshape(owners, block_rows, width),)]
    late_lines = 2 * (len(late) if earlier else z.groups)
    late_count = len(late) if earlier else owners
    form = tuple(map(len, early + late))
    return pl.pallas_call(
        functools.partial(late_kernel, z, earlier, form, len(late)),
        out_shape=(shape((slots, width), BF16), shape((rows, width), BF16)),
        in_specs=[vmem] * (5 + len(tails) + sum(form)),
        out_specs=(pl.BlockSpec(memory_space=pl.ANY),) * 2,
        scratch_shapes=[
            pltpu.VMEM((late_lines * LANES, LANES), BF16),
            pltpu.VMEM((late_lines, LANES), F32),
            pltpu.VMEM((2, late_count, 8, LANES), F32),
            pltpu.VMEM((late_count, 2 * z.chunks, LANES), F32),
            pltpu.VMEM((slots, width), BF16),
            pltpu.VMEM((rows, width), BF16),
            pltpu.SemaphoreType.DMA((1 + slots // z.window,)),
        ],
        compiler_params=grant,
        name="table_and_rows",
    )(own, total, scale, tops, factors, *tails, *flat(early + late))


def solution(mesh):
    placed = (
        P(("groups", "key", "shard"), "lane"),
        P(("groups", "key", "shard")),
        P(("groups", "key", "shard"), None),
        P(("groups", "key", "shard")),
        P(("groups", "key", "shard")),
        P("lane"),
    )
    return jax.shard_map(
        on_device,
        mesh=mesh,
        in_specs=placed,
        out_specs=(P(("groups", "key", "shard"), "lane"), P(("groups", "key", "shard"), "lane")),
        check_vma=False,
    )
```

```python
import functools
import jax
import jax.numpy as jnp
from jax import lax
from jax.experimental import pallas as pl
from jax.experimental.pallas import tpu as pltpu
from jax.sharding import PartitionSpec as P

LANES = 128
LOW = 7
MASK = 127
F32 = jnp.float32
BF16 = jnp.bfloat16
I32 = jnp.int32
I16 = jnp.int16
FAR = 1e9
NT = (((1,), (1,)), ((), ()))
BLOCK = 512
LATE_BLOCK = 256
COST = 1


class Sizes:
    def __init__(self, owners, rows, slots):
        self.owners, self.rows, self.slots = owners, rows, slots
        self.window = slots // 4
        self.chunks = rows // LANES
        self.user_rows = -(-8 * owners // LANES)
        self.code_rows = -(-(3 * self.chunks + 2 * self.user_rows) // 16) * 16
        self.span = min(owners, 8)
        self.shifts = 1 if owners <= self.span else 2
        self.capacity = 2 * rows // owners
        self.per_group = LANES // self.capacity
        self.groups = owners // self.per_group
        self.narrow = owners * slots <= 32768


def iota(shape, axis):
    return lax.broadcasted_iota(I32, shape, axis)


def ones_where(condition):
    return jnp.where(condition, F32(1), F32(0)).astype(BF16)


def dot(a, b):
    return jnp.dot(a, b, preferred_element_type=F32)


def loop(count, body, carry):
    if count <= 8:
        for i in range(count):
            carry = body(i, carry)
        return carry
    return lax.fori_loop(0, count, body, carry)


def send_kernel(z, me_ref, rate_ref, events_ref, weight_ref, route_ref, bucket_ref, segment_ref, block_ref, own_ref):
    groups = rate_ref.shape[0]
    lane = iota((1, LANES), 1)
    rate = jnp.full((1, LANES), rate_ref[0], F32)
    for g in range(1, groups):
        rate = jnp.where(lane >= g * (LANES // groups), rate_ref[g], rate)
    route = route_ref[...]
    bucket = bucket_ref[...]
    place = (route * z.slots + bucket).astype(F32)
    first = ((route >> (z.span.bit_length() - 1)) * (z.span * z.slots)).astype(F32)
    me = jnp.full((8 - 1, LANES), me_ref[0], I32).astype(F32)
    own_ref[0:16, :] = jnp.concatenate([place, first, rate, me], axis=0)
    spot = place - first - F32(z.span * z.slots // 2)
    columns = jnp.concatenate([weight_ref[...], spot], axis=0).T
    for r in range(z.chunks):
        part = slice(r * LANES, (r + 1) * LANES)
        weighted = (columns[:, r : r + 1] * events_ref[part, :].astype(F32)).astype(BF16)
        grown = weighted.astype(F32) * jnp.exp(columns[:, z.chunks + r : z.chunks + r + 1] * rate)
        block_ref[part, :] = grown.astype(BF16)
    ones = jnp.ones((8, LANES), BF16)
    high, low = [], []
    users = min(LANES, 8 * z.owners)
    for u in range(z.user_rows):
        user = iota((users, LANES), 0) + u * LANES
        below = jnp.zeros((users, LANES), F32)
        for r in range(z.slots // LANES):
            below += jnp.where(segment_ref[r : r + 1, :] < user, F32(1), F32(0))
        count = lax.dot_general(ones, below.astype(BF16), NT, preferred_element_type=F32)[0:1]
        if users < LANES:
            count = jnp.concatenate([count, jnp.full((1, LANES - users), z.slots, F32)], axis=1)
        own_ref[16 + u : 17 + u, :] = count
        count = count.astype(I32)
        high.append(count >> LOW)
        low.append(count & MASK)
    spare = z.code_rows - 3 * z.chunks - 2 * z.user_rows
    pad = [jnp.zeros((spare, LANES), I32)] if spare else []
    codes = jnp.concatenate([route, bucket >> LOW, bucket & MASK] + high + low + pad, axis=0)
    block_ref[z.rows : z.rows + z.code_rows, :] = codes.astype(F32).astype(BF16)


class Pieces:
    def __init__(self, z, form, refs):
        self.z, refs = z, list(refs)
        self.parts = [[refs.pop(0) for _ in range(n)] for n in form]
        self.count = len(form) if len(form) != 1 else self.parts[0][0].shape[0]
        self.per_group = 1 if len(form) != 1 else z.per_group
        self.groups = self.count // self.per_group

    def block(self, s):
        return (self.parts[s], 0) if len(self.parts) != 1 else (self.parts[0], s)

    def codes(self, s):
        parts, i = self.block(s)
        first = parts[0].shape[1] - self.z.code_rows
        return parts[0][i, first : first + self.z.code_rows, :].astype(F32)

    def rows(self, s):
        parts, i = self.block(s)
        first = parts[0][i, 0 : parts[0].shape[1] - self.z.code_rows, :]
        return jnp.concatenate([first] + [part[i] for part in parts[1:]], axis=0)

    def place(self, s):
        n, tile = self.z.chunks, self.codes(s)
        return tile[0:n] * F32(self.z.slots) + F32(LANES) * tile[n : 2 * n] + tile[2 * n : 3 * n]

    def below(self, s, u):
        tile, at = self.codes(s), 3 * self.z.chunks + u
        return F32(LANES) * tile[at : at + 1] + tile[at + self.z.user_rows : at + self.z.user_rows + 1]


class Runs:
    def __init__(self, z, starts):
        self.z, self.starts = z, starts
        users = min(LANES, 8 * z.owners)
        self.columns = [jnp.broadcast_to(row, (8, LANES)).T[:users, 0:1] for row in starts]
        self.steps = []
        for u, row in enumerate(starts):
            before = pltpu.roll(row, 1, 1)
            first = starts[u - 1][:, LANES - 1 : LANES] if u else jnp.zeros((1, 1), F32)
            step = (row - jnp.where(iota((1, LANES), 1) == 0, first, before)).astype(I32)
            pair = [jnp.broadcast_to(part, (LANES, LANES)) for part in (step >> LOW, step & MASK)]
            self.steps.append(jnp.concatenate(pair, axis=0).astype(F32).astype(BF16))

    def start(self, position):
        total = jnp.zeros((position.shape[0], 2 * LANES), F32)
        for row, step in zip(self.starts, self.steps):
            total += lax.dot_general(ones_where(row <= position), step, NT, preferred_element_type=F32)
        return F32(LANES) * total[:, :LANES] + total[:, LANES:]

    def start_row(self, row):
        start = jnp.zeros((1, LANES), F32)
        for column in self.columns:
            start = jnp.maximum(start, jnp.max(jnp.where(column <= row, column, F32(0)), axis=0, keepdims=True))
        return start

    def until(self, row):
        after = jnp.full((1, LANES), FAR, F32)
        for column in self.columns:
            later = jnp.where(column > row, column, F32(FAR))
            after = jnp.minimum(after, jnp.min(later, axis=0, keepdims=True))
        return jnp.minimum(row + F32(self.z.window), after - F32(1))


def root(z, distance):
    return lax.rsqrt(jnp.minimum(distance, F32(z.window)) + F32(1))


def pack(z, pieces, base, marks_ref, codes_ref, rows_ref, from_ref):
    if not pieces.count:
        return
    spare = jnp.zeros((8 - z.chunks, LANES), F32)

    def mark(s, carry):
        local = pieces.place(s) - base
        near = local.astype(I32)
        codes_ref[s] = jnp.concatenate([near >> LOW, near & MASK], axis=0).astype(F32)
        own = (local >= 0) & (local < F32(z.slots))
        tail = (local >= F32(-z.window)) & (local < 0)
        marks_ref[0, s] = jnp.concatenate([jnp.where(own, F32(1), F32(0)), spare], axis=0)
        marks_ref[1, s] = jnp.concatenate([jnp.where(tail, F32(1), F32(0)), spare], axis=0)
        return carry

    loop(pieces.count, mark, 0)
    upper = ones_where(iota((LANES, LANES), 0) < iota((LANES, LANES), 1))
    full = jnp.ones((LANES, LANES), BF16)
    lines = pieces.count * 8
    at, by = iota((lines, lines), 0), iota((lines, lines), 1)
    earlier = ones_where(((at >> 3) == (by >> 3)) & (by < at))
    source = iota((lines, LANES), 0) >> 3
    offset = ((source & (pieces.per_group - 1)) * z.capacity).astype(F32)
    for kind in range(2):
        marked = marks_ref[kind].reshape(lines, LANES)
        mark = marked.astype(BF16)
        rank = dot(mark, upper) + dot(earlier, dot(mark, full).astype(BF16)) + offset
        marks_ref[kind] = jnp.where(marked > 0, rank, F32(-1)).reshape(pieces.count, 8, LANES)

    spots = iota((LANES, LANES), 0).astype(F32)
    code_line = iota((2 * z.chunks, LANES), 0) & (z.chunks - 1)
    for kind in range(2):
        for g in range(pieces.groups):

            def add(i, carry):
                values, places = carry
                s = g * pieces.per_group + i
                ranks = marks_ref[kind, s]
                codes = codes_ref[s]
                hot = jnp.concatenate([ones_where(spots == ranks[r : r + 1]) for r in range(z.chunks)], axis=1)
                wide = [jnp.where(code_line == r, codes, F32(0)).astype(BF16) for r in range(z.chunks)]
                values += dot(hot, pieces.rows(s))
                places += lax.dot_general(jnp.concatenate(wide, axis=1), hot, NT, preferred_element_type=F32)
                return values, places

            zero = (jnp.zeros((LANES, LANES), F32), jnp.zeros((2 * z.chunks, LANES), F32))
            values, places = loop(pieces.per_group, add, zero)
            line = kind * pieces.groups + g
            rows_ref[line * LANES : (line + 1) * LANES, :] = values.astype(BF16)
            high = jnp.sum(places[: z.chunks], axis=0, keepdims=True)
            low = jnp.sum(places[z.chunks :], axis=0, keepdims=True)
            from_ref[line : line + 1, :] = F32(LANES) * high + low


def held(position, bounds):
    one, nothing = BF16(1), BF16(0)
    masks = [jnp.where((position >= a) & (position <= b), one, nothing) for a, b in bounds]
    return jnp.concatenate(masks, axis=1)


def within(low, high, rows):
    if low.dtype == I16:
        one, nothing = BF16(1), BF16(0)
        return jnp.concatenate([jnp.where((low <= row) & (high >= row), one, nothing) for row in rows], axis=1)
    return jnp.concatenate([ones_where((low <= row) & (high >= row)) for row in rows], axis=1)


def wide_columns(rows):
    count = rows.shape[0]
    columns = jnp.concatenate([rows, jnp.zeros((8 - count, LANES), F32)], axis=0).T
    return jnp.concatenate([jnp.broadcast_to(columns[:, r : r + 1], (LANES, LANES)) for r in range(count)], axis=0)


def anchors(z, me):
    middle = F32(z.span * z.slots // 2)
    span_of = lambda owner: (owner.astype(I32) >> (z.span.bit_length() - 1)).astype(F32) * F32(z.span)
    own = (me - span_of(me)) * F32(z.slots) - middle
    tail = (me - span_of(me - F32(1))) * F32(z.slots) - middle
    return own, tail


def short(row):
    return row.astype(I32).astype(I16)


def early_kernel(z, form, before, *refs):
    count = sum(form)
    own_ref, pieces = refs[0], Pieces(z, form, refs[1 : 1 + count])
    refs = refs[1 + count :]
    if before:
        before_ref, sums_ref, rows_ref, from_ref, marks_ref, codes_ref = refs
    else:
        sums_ref, scale_ref, rows_ref, from_ref, high_ref, factor_ref, marks_ref, codes_ref = refs
    rate, me = own_ref[8:9, :], own_ref[9:10, :]
    runs = Runs(z, [own_ref[16 + u : 17 + u, :] for u in range(z.user_rows)])
    pack(z, pieces, me * F32(z.slots), marks_ref, codes_ref, rows_ref, from_ref)
    own_anchor, _ = anchors(z, me)
    inner = iota((BLOCK, LANES), 0)
    fall = jnp.exp(-rate * inner.astype(F32))
    bounds = []
    for g in range(pieces.groups if pieces.count else 0):
        begin = from_ref[g : g + 1, :]
        bounds.append((short(begin), short(runs.until(begin))))
    for b in range(z.slots // BLOCK):
        part = slice(b * BLOCK, (b + 1) * BLOCK)
        if bounds:
            mask = held((inner + b * BLOCK).astype(I16), bounds)
            value = dot(mask, rows_ref[0 : len(bounds) * LANES, :])
        else:
            value = jnp.zeros((BLOCK, LANES), F32)
        sums_ref[part, :] = value + before_ref[part, :] if before else value
        if not before:
            first = F32(b * BLOCK)
            position = inner.astype(F32) + first
            start = runs.start(position)
            if b * BLOCK < z.window:
                scale_ref[part, :] = start
            else:
                scale_ref[part, :] = fall * jnp.exp(-rate * (first + own_anchor)) * root(z, position - start)
    if not before:
        position, span_start = wide_columns(own_ref[0 : z.chunks, :]), wide_columns(own_ref[z.chunks : 2 * z.chunks, :])
        for shift in range(z.shifts):
            part = slice(shift * z.rows, (shift + 1) * z.rows)
            center = span_start + F32(z.span * z.slots // 2 - shift * z.span * z.slots)
            factor_ref[part, :] = jnp.exp(-rate * (position - center))
            top = position if shift == 0 else span_start - F32(1)
            high_ref[part, :] = short(top) if z.narrow else top


def late_kernel(z, earlier, form, late, *refs):
    own_ref, sums_ref, scale_ref, high_ref, factor_ref = refs[:5]
    tails = [refs[5 + 2 * i : 7 + 2 * i] for i in range(len(earlier))]
    refs = refs[5 + 2 * len(earlier) :]
    count = sum(form)
    table_out, feature_out, rows_ref, from_ref, marks_ref, codes_ref, table_ref, feature_ref, sems = refs[count:]
    pieces, last = Pieces(z, form, refs[:count]), Pieces(z, form[-late:], refs[count - sum(form[-late:]) : count])
    rate, me = own_ref[8:9, :], own_ref[9:10, :]
    base = me * F32(z.slots)
    starts = []
    for u in range(z.user_rows):
        add = lambda s, total: total + pieces.below(s, u)
        starts.append(loop(pieces.count, add, jnp.zeros((1, LANES), F32)))
    runs = Runs(z, starts)
    copies = []

    def send(ref, out, part):
        copies.append(pltpu.make_async_copy(ref.at[part, :], out.at[part, :], sems.at[len(copies)]))
        copies[-1].start()

    place = own_ref[0 : z.chunks, :]
    start = jnp.concatenate([runs.start_row(place[r : r + 1]) for r in range(z.chunks)], axis=0)
    scale = wide_columns(root(z, place - start))
    low = wide_columns(jnp.maximum(place - F32(z.window), start))
    span_start = wide_columns(own_ref[z.chunks : 2 * z.chunks, :]) if z.shifts > 1 else None
    kind = short if z.narrow else lambda row: row
    total = jnp.zeros((z.rows, LANES), F32)
    for shift in range(z.shifts):
        part = slice(shift * z.rows, (shift + 1) * z.rows)
        bottom = kind(jnp.maximum(low, span_start) if shift == 0 and z.shifts > 1 else low)
        top = high_ref[part, :]

        def add(s, value):
            rows = pieces.place(s)
            mask = within(bottom, top, [kind(rows[r : r + 1]) for r in range(z.chunks)])
            return value + dot(mask, pieces.rows(s))

        total += loop(pieces.count, add, jnp.zeros((z.rows, LANES), F32)) * factor_ref[part, :]
    feature_ref[...] = (total * scale).astype(BF16)
    send(feature_ref, feature_out, slice(0, z.rows))

    pack(z, last, base, marks_ref, codes_ref, rows_ref, from_ref)
    own_anchor, tail_anchor = anchors(z, me)
    inner = iota((LATE_BLOCK, LANES), 0)
    fall = jnp.exp(-rate * inner.astype(F32))
    first_start = jnp.max(runs.start_row(base), axis=1, keepdims=True) - base
    bounds = []
    listed = [(from_ref, 0, 2 * last.groups)] + [(ref, count, count) for (_, ref), count in zip(tails, earlier)]
    for ref, first, lines in listed:
        for g in range(first, first + lines):
            begin = ref[g : g + 1, :]
            bounds.append((short(begin), short(runs.until(begin + base) - base)))
    n = last.groups
    own_rows = rows_ref[0 : n * LANES, :]
    tail_rows = [rows_ref[n * LANES : 2 * n * LANES, :]]
    tail_rows += [ref[count * LANES : 2 * count * LANES, :] for (ref, _), count in zip(tails, earlier)]
    tail_rows = jnp.concatenate(tail_rows, axis=0)
    steps = z.window // LATE_BLOCK
    for b in range(steps):
        part = slice(b * LATE_BLOCK, (b + 1) * LATE_BLOCK)
        position = (inner + b * LATE_BLOCK).astype(I16)
        first = F32(b * LATE_BLOCK)
        value = sums_ref[part, :]
        own_fall = jnp.exp(-rate * (first + own_anchor))
        if z.shifts == 1:
            value += dot(held(position, bounds), jnp.concatenate([own_rows, tail_rows], axis=0))
            value *= own_fall
        else:
            value = (value + dot(held(position, bounds[:n]), own_rows)) * own_fall
            value += dot(held(position, bounds[n:]), tail_rows) * jnp.exp(-rate * (first + tail_anchor))
        start = scale_ref[part, :]
        start = jnp.where(start > 0, start, first_start)
        value = value * fall * root(z, inner.astype(F32) + first - start)
        table_ref[part, :] = value.astype(BF16)
    send(table_ref, table_out, slice(0, z.window))

    def window(w, carry):
        for k in range(steps):
            first = w * z.window + k * LATE_BLOCK
            part = pl.ds(pl.multiple_of(first, LATE_BLOCK), LATE_BLOCK)
            position = (inner + first).astype(I16)
            value = sums_ref[part, :] + dot(held(position, bounds[:n]), own_rows)
            table_ref[part, :] = (value * scale_ref[part, :]).astype(BF16)
        return carry

    lax.fori_loop(1, z.slots // z.window, window, 0)
    send(table_ref, table_out, slice(z.window, z.slots))
    for copy in copies:
        copy.wait()


def swap(block, axis, distance):
    return lax.ppermute(block, axis, [(i, i ^ distance) for i in range(lax.axis_size(axis))])


def spread(blocks, axis):
    distance = lax.axis_size(axis) // 2
    while distance:
        blocks = blocks + [swap(block, axis, distance) for block in blocks]
        distance //= 2
    return blocks


def on_device(events, event_weight, route, bucket, segment, decay_rate):
    rows, width = events.shape
    key_count, shard_count = lax.axis_size("key"), lax.axis_size("shard")
    owners = key_count * shard_count
    slots = segment.shape[0]
    z = Sizes(owners, rows, slots)
    block_rows = rows + z.code_rows
    smem = pl.BlockSpec(memory_space=pltpu.SMEM)
    vmem = pl.BlockSpec(memory_space=pltpu.VMEM)
    shape = jax.ShapeDtypeStruct
    grant = pltpu.CompilerParams(vmem_limit_bytes=(16 if owners <= 8 else 48) * 1024 * 1024)
    me = (lax.axis_index("key") * shard_count + lax.axis_index("shard")).astype(I32).reshape(1)
    block, own = pl.pallas_call(
        functools.partial(send_kernel, z),
        out_shape=(
            shape((block_rows, width), BF16),
            shape((16 + z.user_rows + 7, LANES), F32),
        ),
        in_specs=[smem, smem] + [vmem] * 5,
        out_specs=(vmem, vmem),
        compiler_params=pltpu.CompilerParams(vmem_limit_bytes=56 * 1024 * 1024),
        name="weigh",
    )(
        me, decay_rate, events, event_weight.reshape(z.chunks, LANES), route.reshape(z.chunks, LANES),
        bucket.reshape(z.chunks, LANES), segment.reshape(slots // LANES, LANES),
    )

    def flat(blocks):
        return [part[None] if part.ndim == 2 else part for parts in blocks for part in parts]

    def sums(blocks, before=()):
        blocks, form, count = flat(blocks), tuple(map(len, blocks)), len(blocks)
        lines = max(8, 2 * count)
        whole = shape((slots, width), F32)
        kept = (shape((lines * LANES, LANES), BF16), shape((lines, LANES), F32))
        factors = shape((z.shifts * rows, width), F32)
        tops = shape((z.shifts * rows, width), I16 if z.narrow else F32)
        return pl.pallas_call(
            functools.partial(early_kernel, z, form, len(before)),
            out_shape=(whole,) + kept if before else (whole, whole) + kept + (tops, factors),
            in_specs=[vmem] * (1 + len(blocks) + len(before)),
            out_specs=(vmem,) * (3 if before else 6),
            scratch_shapes=[
                pltpu.VMEM((2, max(1, count), 8, LANES), F32),
                pltpu.VMEM((max(1, count), 2 * z.chunks, LANES), F32),
            ],
            compiler_params=grant,
            cost_estimate=pl.CostEstimate(flops=COST * count, bytes_accessed=0, transcendentals=0),
            name="more_sums" if before else "first_sums",
        )(own, *blocks, *before)

    if (key_count, shard_count) == (4, 2):
        tie = lax.optimization_barrier
        far = swap(block, "key", 2)
        side = swap(block, "shard", 1)
        near = swap(block, "key", 1)
        side_near = swap(side, "key", 1)
        total, scale, *tail, tops, factors = sums([(block,)])
        far, total = tie((far, total))
        last = swap(far, "key", 1)
        side_far = swap(far, "shard", 1)
        total, *tail2 = sums([(side,), (near,)], (total,))
        last, total = tie((last, total))
        side_last = swap(last, "shard", 1)
        second = [(far,), (last,), (side_far,)]
        late = [(side_near,), (side_last,)]
        total, *tail3 = sums(second, (total,))
        early, earlier, tails = [(block,), (side,), (near,)] + second, (1, 2, 3), tail + tail2 + tail3
    else:
        blocks = spread(spread([block], "key"), "shard")
        total, scale, _, _, tops, factors = sums([])
        early, earlier, tails = [], (), []
        late = [(jnp.concatenate(blocks, axis=0).reshape(owners, block_rows, width),)]
    late_lines = 2 * (len(late) if earlier else z.groups)
    late_count = len(late) if earlier else owners
    form = tuple(map(len, early + late))
    return pl.pallas_call(
        functools.partial(late_kernel, z, earlier, form, len(late)),
        out_shape=(shape((slots, width), BF16), shape((rows, width), BF16)),
        in_specs=[vmem] * (5 + len(tails) + sum(form)),
        out_specs=(pl.BlockSpec(memory_space=pl.ANY),) * 2,
        scratch_shapes=[
            pltpu.VMEM((late_lines * LANES, LANES), BF16),
            pltpu.VMEM((late_lines, LANES), F32),
            pltpu.VMEM((2, late_count, 8, LANES), F32),
            pltpu.VMEM((late_count, 2 * z.chunks, LANES), F32),
            pltpu.VMEM((slots, width), BF16),
            pltpu.VMEM((rows, width), BF16),
            pltpu.SemaphoreType.DMA((3,)),
        ],
        compiler_params=grant,
        name="table_and_rows",
    )(own, total, scale, tops, factors, *tails, *flat(early + late))


def solution(mesh):
    placed = (
        P(("groups", "key", "shard"), "lane"),
        P(("groups", "key", "shard")),
        P(("groups", "key", "shard"), None),
        P(("groups", "key", "shard")),
        P(("groups", "key", "shard")),
        P("lane"),
    )
    return jax.shard_map(
        on_device,
        mesh=mesh,
        in_specs=placed,
        out_specs=(P(("groups", "key", "shard"), "lane"), P(("groups", "key", "shard"), "lane")),
        check_vma=False,
    )
```

```python
import functools
import jax
import jax.numpy as jnp
from jax import lax
from jax.experimental import pallas as pl
from jax.experimental.pallas import tpu as pltpu
from jax.sharding import PartitionSpec as P

LANES = 128
LOW = 7
MASK = 127
F32 = jnp.float32
BF16 = jnp.bfloat16
I32 = jnp.int32
I16 = jnp.int16
FAR = 1e9
TOP = 32768
NT = (((1,), (1,)), ((), ()))
BLOCK = 512
LATE_BLOCK = 256
COST = 1


class Sizes:
    def __init__(self, owners, rows, slots):
        self.owners, self.rows, self.slots = owners, rows, slots
        self.window = slots // 4
        self.chunks = rows // LANES
        self.user_rows = -(-8 * owners // LANES)
        self.code_rows = -(-(3 * self.chunks + 2 * self.user_rows) // 16) * 16
        self.span = min(owners, 8)
        self.shifts = 1 if owners <= self.span else 2
        self.capacity = 2 * rows // owners
        self.per_group = LANES // self.capacity
        self.groups = owners // self.per_group
        self.narrow = owners * slots <= 32768


def iota(shape, axis):
    return lax.broadcasted_iota(I32, shape, axis)


def ones_where(condition):
    return jnp.where(condition, F32(1), F32(0)).astype(BF16)


def dot(a, b):
    return jnp.dot(a, b, preferred_element_type=F32)


def loop(count, body, carry):
    if count <= 8:
        for i in range(count):
            carry = body(i, carry)
        return carry
    return lax.fori_loop(0, count, body, carry)


def send_kernel(z, me_ref, rate_ref, events_ref, weight_ref, route_ref, bucket_ref, segment_ref, block_ref, own_ref):
    groups = rate_ref.shape[0]
    lane = iota((1, LANES), 1)
    rate = jnp.full((1, LANES), rate_ref[0], F32)
    for g in range(1, groups):
        rate = jnp.where(lane >= g * (LANES // groups), rate_ref[g], rate)
    route = route_ref[...]
    bucket = bucket_ref[...]
    place = (route * z.slots + bucket).astype(F32)
    first = ((route >> (z.span.bit_length() - 1)) * (z.span * z.slots)).astype(F32)
    me = jnp.full((8 - 1, LANES), me_ref[0], I32).astype(F32)
    own_ref[0:16, :] = jnp.concatenate([place, first, rate, me], axis=0)
    spot = place - first - F32(z.span * z.slots // 2)
    columns = jnp.concatenate([weight_ref[...], spot], axis=0).T
    for r in range(z.chunks):
        part = slice(r * LANES, (r + 1) * LANES)
        weighted = (columns[:, r : r + 1] * events_ref[part, :].astype(F32)).astype(BF16)
        grown = weighted.astype(F32) * jnp.exp(columns[:, z.chunks + r : z.chunks + r + 1] * rate)
        block_ref[part, :] = grown.astype(BF16)
    ones = jnp.ones((8, LANES), BF16)
    high, low = [], []
    users = min(LANES, 8 * z.owners)
    for u in range(z.user_rows):
        user = iota((users, LANES), 0) + u * LANES
        below = jnp.zeros((users, LANES), F32)
        for r in range(z.slots // LANES):
            below += jnp.where(segment_ref[r : r + 1, :] < user, F32(1), F32(0))
        count = lax.dot_general(ones, below.astype(BF16), NT, preferred_element_type=F32)[0:1]
        if users < LANES:
            count = jnp.concatenate([count, jnp.full((1, LANES - users), z.slots, F32)], axis=1)
        own_ref[16 + u : 17 + u, :] = count
        count = count.astype(I32)
        high.append(count >> LOW)
        low.append(count & MASK)
    spare = z.code_rows - 3 * z.chunks - 2 * z.user_rows
    pad = [jnp.zeros((spare, LANES), I32)] if spare else []
    codes = jnp.concatenate([route, bucket >> LOW, bucket & MASK] + high + low + pad, axis=0)
    block_ref[z.rows : z.rows + z.code_rows, :] = codes.astype(F32).astype(BF16)


class Pieces:
    def __init__(self, z, form, refs):
        self.z, refs = z, list(refs)
        self.parts = [[refs.pop(0) for _ in range(n)] for n in form]
        self.count = len(form) if len(form) != 1 else self.parts[0][0].shape[0]
        self.per_group = 1 if len(form) != 1 else z.per_group
        self.groups = self.count // self.per_group

    def block(self, s):
        return (self.parts[s], 0) if len(self.parts) != 1 else (self.parts[0], s)

    def codes(self, s):
        parts, i = self.block(s)
        first = parts[0].shape[1] - self.z.code_rows
        return parts[0][i, first : first + self.z.code_rows, :].astype(F32)

    def rows(self, s):
        parts, i = self.block(s)
        first = parts[0][i, 0 : parts[0].shape[1] - self.z.code_rows, :]
        return jnp.concatenate([first] + [part[i] for part in parts[1:]], axis=0)

    def place(self, s):
        n, tile = self.z.chunks, self.codes(s)
        return tile[0:n] * F32(self.z.slots) + F32(LANES) * tile[n : 2 * n] + tile[2 * n : 3 * n]

    def below(self, s, u):
        tile, at = self.codes(s), 3 * self.z.chunks + u
        return F32(LANES) * tile[at : at + 1] + tile[at + self.z.user_rows : at + self.z.user_rows + 1]


class Runs:
    def __init__(self, z, starts):
        self.z, self.starts = z, starts
        users = min(LANES, 8 * z.owners)
        self.columns = [jnp.broadcast_to(row, (8, LANES)).T[:users, 0:1] for row in starts]
        self.steps = []
        for u, row in enumerate(starts):
            before = pltpu.roll(row, 1, 1)
            first = starts[u - 1][:, LANES - 1 : LANES] if u else jnp.zeros((1, 1), F32)
            step = (row - jnp.where(iota((1, LANES), 1) == 0, first, before)).astype(I32)
            pair = [jnp.broadcast_to(part, (LANES, LANES)) for part in (step >> LOW, step & MASK)]
            self.steps.append(jnp.concatenate(pair, axis=0).astype(F32).astype(BF16))

    def start(self, position):
        total = jnp.zeros((position.shape[0], 2 * LANES), F32)
        for row, step in zip(self.starts, self.steps):
            total += lax.dot_general(ones_where(row <= position), step, NT, preferred_element_type=F32)
        return F32(LANES) * total[:, :LANES] + total[:, LANES:]

    def start_row(self, row):
        start = jnp.zeros((1, LANES), F32)
        for column in self.columns:
            start = jnp.maximum(start, jnp.max(jnp.where(column <= row, column, F32(0)), axis=0, keepdims=True))
        return start

    def until(self, row):
        after = jnp.full((1, LANES), FAR, F32)
        for column in self.columns:
            later = jnp.where(column > row, column, F32(FAR))
            after = jnp.minimum(after, jnp.min(later, axis=0, keepdims=True))
        return jnp.minimum(row + F32(self.z.window), after - F32(1))


def root(z, distance):
    return lax.rsqrt(jnp.minimum(distance, F32(z.window)) + F32(1))


def pack(z, pieces, base, marks_ref, codes_ref, rows_ref, from_ref):
    if not pieces.count:
        return
    spare = jnp.zeros((8 - z.chunks, LANES), F32)

    def mark(s, carry):
        local = pieces.place(s) - base
        near = local.astype(I32)
        codes_ref[s] = jnp.concatenate([near >> LOW, near & MASK], axis=0).astype(F32)
        own = (local >= 0) & (local < F32(z.slots))
        tail = (local >= F32(-z.window)) & (local < 0)
        marks_ref[0, s] = jnp.concatenate([jnp.where(own, F32(1), F32(0)), spare], axis=0)
        marks_ref[1, s] = jnp.concatenate([jnp.where(tail, F32(1), F32(0)), spare], axis=0)
        return carry

    loop(pieces.count, mark, 0)
    upper = ones_where(iota((LANES, LANES), 0) < iota((LANES, LANES), 1))
    full = jnp.ones((LANES, LANES), BF16)
    lines = pieces.count * 8
    at, by = iota((lines, lines), 0), iota((lines, lines), 1)
    earlier = ones_where(((at >> 3) == (by >> 3)) & (by < at))
    source = iota((lines, LANES), 0) >> 3
    offset = ((source & (pieces.per_group - 1)) * z.capacity).astype(F32)
    for kind in range(2):
        marked = marks_ref[kind].reshape(lines, LANES)
        mark = marked.astype(BF16)
        rank = dot(mark, upper) + dot(earlier, dot(mark, full).astype(BF16)) + offset
        marks_ref[kind] = jnp.where(marked > 0, rank, F32(-1)).reshape(pieces.count, 8, LANES)

    spots = iota((LANES, LANES), 0).astype(F32)
    code_line = iota((2 * z.chunks, LANES), 0) & (z.chunks - 1)
    for kind in range(2):
        for g in range(pieces.groups):

            def add(i, carry):
                values, places = carry
                s = g * pieces.per_group + i
                ranks = marks_ref[kind, s]
                codes = codes_ref[s]
                hot = jnp.concatenate([ones_where(spots == ranks[r : r + 1]) for r in range(z.chunks)], axis=1)
                wide = [jnp.where(code_line == r, codes, F32(0)).astype(BF16) for r in range(z.chunks)]
                values += dot(hot, pieces.rows(s))
                places += lax.dot_general(jnp.concatenate(wide, axis=1), hot, NT, preferred_element_type=F32)
                return values, places

            zero = (jnp.zeros((LANES, LANES), F32), jnp.zeros((2 * z.chunks, LANES), F32))
            values, places = loop(pieces.per_group, add, zero)
            line = kind * pieces.groups + g
            rows_ref[line * LANES : (line + 1) * LANES, :] = values.astype(BF16)
            high = jnp.sum(places[: z.chunks], axis=0, keepdims=True)
            low = jnp.sum(places[z.chunks :], axis=0, keepdims=True)
            from_ref[line : line + 1, :] = F32(LANES) * high + low


def held(position, bounds):
    one, nothing = BF16(1), BF16(0)
    masks = [jnp.where(position - first <= length, one, nothing) for first, length in bounds]
    return jnp.concatenate(masks, axis=1)


def within(top, span, rows):
    if top.dtype == I16:
        one, nothing = BF16(1), BF16(0)
        return jnp.concatenate([jnp.where(top - row <= span, one, nothing) for row in rows], axis=1)
    return jnp.concatenate([ones_where((top - row >= 0) & (top - row <= span)) for row in rows], axis=1)


def wide_columns(*sets):
    count = sets[0].shape[0]
    columns = jnp.concatenate(sets, axis=0).T
    wide = lambda at: jnp.broadcast_to(columns[:, at : at + 1], (LANES, LANES))
    return [jnp.concatenate([wide(i * count + r) for r in range(count)], axis=0) for i in range(len(sets))]


def anchors(z, me):
    middle = F32(z.span * z.slots // 2)
    span_of = lambda owner: (owner.astype(I32) >> (z.span.bit_length() - 1)).astype(F32) * F32(z.span)
    own = (me - span_of(me)) * F32(z.slots) - middle
    tail = (me - span_of(me - F32(1))) * F32(z.slots) - middle
    return own, tail


def short(row):
    return row.astype(I32).astype(I16)


def early_kernel(z, form, before, *refs):
    count = sum(form)
    own_ref, pieces = refs[0], Pieces(z, form, refs[1 : 1 + count])
    refs = refs[1 + count :]
    if before:
        before_ref, sums_ref, rows_ref, from_ref, marks_ref, codes_ref = refs
    else:
        sums_ref, scale_ref, rows_ref, from_ref, high_ref, factor_ref, marks_ref, codes_ref = refs
    rate, me = own_ref[8:9, :], own_ref[9:10, :]
    runs = Runs(z, [own_ref[16 + u : 17 + u, :] for u in range(z.user_rows)])
    pack(z, pieces, me * F32(z.slots), marks_ref, codes_ref, rows_ref, from_ref)
    own_anchor, _ = anchors(z, me)
    inner = iota((BLOCK, LANES), 0)
    fall = jnp.exp(-rate * inner.astype(F32))
    bounds = []
    for g in range(pieces.groups if pieces.count else 0):
        begin = from_ref[g : g + 1, :]
        bounds.append((short(begin), short(runs.until(begin) - begin - F32(TOP))))
    for b in range(z.slots // BLOCK):
        part = slice(b * BLOCK, (b + 1) * BLOCK)
        if bounds:
            mask = held((inner + (b * BLOCK - TOP)).astype(I16), bounds)
            value = dot(mask, rows_ref[0 : len(bounds) * LANES, :])
        else:
            value = jnp.zeros((BLOCK, LANES), F32)
        sums_ref[part, :] = value + before_ref[part, :] if before else value
        if not before:
            first = F32(b * BLOCK)
            position = inner.astype(F32) + first
            start = runs.start(position)
            if b * BLOCK < z.window:
                scale_ref[part, :] = start
            else:
                scale_ref[part, :] = fall * jnp.exp(-rate * (first + own_anchor)) * root(z, position - start)
    if not before:
        position, span_start = wide_columns(own_ref[0 : z.chunks, :], own_ref[z.chunks : 2 * z.chunks, :])
        for shift in range(z.shifts):
            part = slice(shift * z.rows, (shift + 1) * z.rows)
            center = span_start + F32(z.span * z.slots // 2 - shift * z.span * z.slots)
            factor_ref[part, :] = jnp.exp(-rate * (position - center))
            top = position if shift == 0 else span_start - F32(1)
            high_ref[part, :] = short(top - F32(TOP)) if z.narrow else top


def late_kernel(z, earlier, form, late, *refs):
    own_ref, sums_ref, scale_ref, high_ref, factor_ref = refs[:5]
    tails = [refs[5 + 2 * i : 7 + 2 * i] for i in range(len(earlier))]
    refs = refs[5 + 2 * len(earlier) :]
    count = sum(form)
    table_out, feature_out, rows_ref, from_ref, marks_ref, codes_ref, table_ref, feature_ref, sems = refs[count:]
    pieces, last = Pieces(z, form, refs[:count]), Pieces(z, form[-late:], refs[count - sum(form[-late:]) : count])
    rate, me = own_ref[8:9, :], own_ref[9:10, :]
    base = me * F32(z.slots)
    starts = []
    for u in range(z.user_rows):
        add = lambda s, total: total + pieces.below(s, u)
        starts.append(loop(pieces.count, add, jnp.zeros((1, LANES), F32)))
    runs = Runs(z, starts)
    copies = []

    def send(ref, out, part):
        copies.append(pltpu.make_async_copy(ref.at[part, :], out.at[part, :], sems.at[len(copies)]))
        copies[-1].start()

    place = own_ref[0 : z.chunks, :]
    start = jnp.concatenate([runs.start_row(place[r : r + 1]) for r in range(z.chunks)], axis=0)
    distance = place - start
    reach = jnp.minimum(distance, F32(z.window))
    scale, reach = wide_columns(root(z, distance), reach - F32(TOP) if z.narrow else reach)
    position, span_start = (None, None) if z.narrow else wide_columns(place, own_ref[z.chunks : 2 * z.chunks, :])
    kind = short if z.narrow else lambda row: row
    total = jnp.zeros((z.rows, LANES), F32)
    for shift in range(z.shifts):
        part = slice(shift * z.rows, (shift + 1) * z.rows)
        top = high_ref[part, :]
        if z.narrow:
            span = short(reach)
        else:
            low = position - reach
            span = top - (jnp.maximum(low, span_start) if shift == 0 else low)

        def add(s, value):
            rows = pieces.place(s)
            mask = within(top, span, [kind(rows[r : r + 1]) for r in range(z.chunks)])
            return value + dot(mask, pieces.rows(s))

        total += loop(pieces.count, add, jnp.zeros((z.rows, LANES), F32)) * factor_ref[part, :]
    feature_ref[...] = (total * scale).astype(BF16)
    send(feature_ref, feature_out, slice(0, z.rows))

    pack(z, last, base, marks_ref, codes_ref, rows_ref, from_ref)
    own_anchor, tail_anchor = anchors(z, me)
    inner = iota((LATE_BLOCK, LANES), 0)
    fall = jnp.exp(-rate * inner.astype(F32))
    first_start = jnp.max(runs.start_row(base), axis=1, keepdims=True) - base
    bounds = []
    listed = [(from_ref, 0, 2 * last.groups)] + [(ref, count, count) for (_, ref), count in zip(tails, earlier)]
    for ref, first, lines in listed:
        for g in range(first, first + lines):
            begin = ref[g : g + 1, :]
            bounds.append((short(begin), short(runs.until(begin + base) - (begin + base) - F32(TOP))))
    n = last.groups
    own_rows = rows_ref[0 : n * LANES, :]
    tail_rows = [rows_ref[n * LANES : 2 * n * LANES, :]]
    tail_rows += [ref[count * LANES : 2 * count * LANES, :] for (ref, _), count in zip(tails, earlier)]
    tail_rows = jnp.concatenate(tail_rows, axis=0)
    for b in range(z.slots // LATE_BLOCK):
        part = slice(b * LATE_BLOCK, (b + 1) * LATE_BLOCK)
        position = (inner + (b * LATE_BLOCK - TOP)).astype(I16)
        first = F32(b * LATE_BLOCK)
        value = sums_ref[part, :]
        if b * LATE_BLOCK >= z.window:
            value = (value + dot(held(position, bounds[:n]), own_rows)) * scale_ref[part, :]
        else:
            own_fall = jnp.exp(-rate * (first + own_anchor))
            if z.shifts == 1:
                value += dot(held(position, bounds), jnp.concatenate([own_rows, tail_rows], axis=0))
                value *= own_fall
            else:
                value = (value + dot(held(position, bounds[:n]), own_rows)) * own_fall
                value += dot(held(position, bounds[n:]), tail_rows) * jnp.exp(-rate * (first + tail_anchor))
            start = scale_ref[part, :]
            start = jnp.where(start > 0, start, first_start)
            value = value * fall * root(z, inner.astype(F32) + first - start)
        table_ref[part, :] = value.astype(BF16)
        if (b + 1) * LATE_BLOCK % z.window == 0:
            send(table_ref, table_out, slice((b + 1) * LATE_BLOCK - z.window, (b + 1) * LATE_BLOCK))
    for copy in copies:
        copy.wait()


def swap(block, axis, distance):
    return lax.ppermute(block, axis, [(i, i ^ distance) for i in range(lax.axis_size(axis))])


def spread(blocks, axis):
    distance = lax.axis_size(axis) // 2
    while distance:
        blocks = blocks + [swap(block, axis, distance) for block in blocks]
        distance //= 2
    return blocks


def on_device(events, event_weight, route, bucket, segment, decay_rate):
    rows, width = events.shape
    key_count, shard_count = lax.axis_size("key"), lax.axis_size("shard")
    owners = key_count * shard_count
    slots = segment.shape[0]
    z = Sizes(owners, rows, slots)
    block_rows = rows + z.code_rows
    smem = pl.BlockSpec(memory_space=pltpu.SMEM)
    vmem = pl.BlockSpec(memory_space=pltpu.VMEM)
    shape = jax.ShapeDtypeStruct
    grant = pltpu.CompilerParams(vmem_limit_bytes=(16 if owners <= 8 else 48) * 1024 * 1024)
    me = (lax.axis_index("key") * shard_count + lax.axis_index("shard")).astype(I32).reshape(1)
    block, own = pl.pallas_call(
        functools.partial(send_kernel, z),
        out_shape=(
            shape((block_rows, width), BF16),
            shape((16 + z.user_rows + 7, LANES), F32),
        ),
        in_specs=[smem, smem] + [vmem] * 5,
        out_specs=(vmem, vmem),
        compiler_params=pltpu.CompilerParams(vmem_limit_bytes=56 * 1024 * 1024),
        name="weigh",
    )(
        me, decay_rate, events, event_weight.reshape(z.chunks, LANES), route.reshape(z.chunks, LANES),
        bucket.reshape(z.chunks, LANES), segment.reshape(slots // LANES, LANES),
    )

    def flat(blocks):
        return [part[None] if part.ndim == 2 else part for parts in blocks for part in parts]

    def sums(blocks, before=()):
        blocks, form, count = flat(blocks), tuple(map(len, blocks)), len(blocks)
        lines = max(8, 2 * count)
        whole = shape((slots, width), F32)
        kept = (shape((lines * LANES, LANES), BF16), shape((lines, LANES), F32))
        factors = shape((z.shifts * rows, width), F32)
        tops = shape((z.shifts * rows, width), I16 if z.narrow else F32)
        return pl.pallas_call(
            functools.partial(early_kernel, z, form, len(before)),
            out_shape=(whole,) + kept if before else (whole, whole) + kept + (tops, factors),
            in_specs=[vmem] * (1 + len(blocks) + len(before)),
            out_specs=(vmem,) * (3 if before else 6),
            scratch_shapes=[
                pltpu.VMEM((2, max(1, count), 8, LANES), F32),
                pltpu.VMEM((max(1, count), 2 * z.chunks, LANES), F32),
            ],
            compiler_params=grant,
            cost_estimate=pl.CostEstimate(flops=COST * count, bytes_accessed=0, transcendentals=0),
            name="more_sums" if before else "first_sums",
        )(own, *blocks, *before)

    if (key_count, shard_count) == (4, 2):
        tie = lax.optimization_barrier
        far = swap(block, "key", 2)
        side = swap(block, "shard", 1)
        near = swap(block, "key", 1)
        side_near = swap(side, "key", 1)
        total, scale, *tail, tops, factors = sums([(block,)])
        far, total = tie((far, total))
        last = swap(far, "key", 1)
        side_far = swap(far, "shard", 1)
        total, *tail2 = sums([(side,), (near,)], (total,))
        last, total = tie((last, total))
        side_last = swap(last, "shard", 1)
        second = [(far,), (last,), (side_far,)]
        late = [(side_near,), (side_last,)]
        total, *tail3 = sums(second, (total,))
        early, earlier, tails = [(block,), (side,), (near,)] + second, (1, 2, 3), tail + tail2 + tail3
    else:
        blocks = spread(spread([block], "key"), "shard")
        total, scale, _, _, tops, factors = sums([])
        early, earlier, tails = [], (), []
        late = [(jnp.concatenate(blocks, axis=0).reshape(owners, block_rows, width),)]
    late_lines = 2 * (len(late) if earlier else z.groups)
    late_count = len(late) if earlier else owners
    form = tuple(map(len, early + late))
    return pl.pallas_call(
        functools.partial(late_kernel, z, earlier, form, len(late)),
        out_shape=(shape((slots, width), BF16), shape((rows, width), BF16)),
        in_specs=[vmem] * (5 + len(tails) + sum(form)),
        out_specs=(pl.BlockSpec(memory_space=pl.ANY),) * 2,
        scratch_shapes=[
            pltpu.VMEM((late_lines * LANES, LANES), BF16),
            pltpu.VMEM((late_lines, LANES), F32),
            pltpu.VMEM((2, late_count, 8, LANES), F32),
            pltpu.VMEM((late_count, 2 * z.chunks, LANES), F32),
            pltpu.VMEM((slots, width), BF16),
            pltpu.VMEM((rows, width), BF16),
            pltpu.SemaphoreType.DMA((1 + slots // z.window,)),
        ],
        compiler_params=grant,
        name="table_and_rows",
    )(own, total, scale, tops, factors, *tails, *flat(early + late))


def solution(mesh):
    placed = (
        P(("groups", "key", "shard"), "lane"),
        P(("groups", "key", "shard")),
        P(("groups", "key", "shard"), None),
        P(("groups", "key", "shard")),
        P(("groups", "key", "shard")),
        P("lane"),
    )
    return jax.shard_map(
        on_device,
        mesh=mesh,
        in_specs=placed,
        out_specs=(P(("groups", "key", "shard"), "lane"), P(("groups", "key", "shard"), "lane")),
        check_vma=False,
    )
```

```python
import functools
import jax
import jax.numpy as jnp
from jax import lax
from jax.experimental import pallas as pl
from jax.experimental.pallas import tpu as pltpu
from jax.sharding import PartitionSpec as P

LANES = 128
LOW = 7
MASK = 127
F32 = jnp.float32
BF16 = jnp.bfloat16
I32 = jnp.int32
I16 = jnp.int16
FAR = 1e9
TOP = 32768
NT = (((1,), (1,)), ((), ()))
BLOCK = 512
LATE_BLOCK = 256
COST = 1


class Sizes:
    def __init__(self, owners, rows, slots):
        self.owners, self.rows, self.slots = owners, rows, slots
        self.window = slots // 4
        self.chunks = rows // LANES
        self.user_rows = -(-8 * owners // LANES)
        self.code_rows = -(-(3 * self.chunks + 2 * self.user_rows) // 16) * 16
        self.span = min(owners, 8)
        self.shifts = 1 if owners <= self.span else 2
        self.capacity = 2 * rows // owners
        self.per_group = LANES // self.capacity
        self.groups = owners // self.per_group
        self.narrow = owners * slots <= 32768


def iota(shape, axis):
    return lax.broadcasted_iota(I32, shape, axis)


def ones_where(condition):
    return jnp.where(condition, F32(1), F32(0)).astype(BF16)


def dot(a, b):
    return jnp.dot(a, b, preferred_element_type=F32)


def loop(count, body, carry):
    if count <= 8:
        for i in range(count):
            carry = body(i, carry)
        return carry
    return lax.fori_loop(0, count, body, carry)


def send_kernel(z, me_ref, rate_ref, events_ref, weight_ref, route_ref, bucket_ref, segment_ref, block_ref, own_ref):
    groups = rate_ref.shape[0]
    lane = iota((1, LANES), 1)
    rate = jnp.full((1, LANES), rate_ref[0], F32)
    for g in range(1, groups):
        rate = jnp.where(lane >= g * (LANES // groups), rate_ref[g], rate)
    route = route_ref[...]
    bucket = bucket_ref[...]
    place = (route * z.slots + bucket).astype(F32)
    first = ((route >> (z.span.bit_length() - 1)) * (z.span * z.slots)).astype(F32)
    me = jnp.full((8 - 1, LANES), me_ref[0], I32).astype(F32)
    own_ref[0:16, :] = jnp.concatenate([place, first, rate, me], axis=0)
    spot = place - first - F32(z.span * z.slots // 2)
    columns = jnp.concatenate([weight_ref[...], spot], axis=0).T
    for r in range(z.chunks):
        part = slice(r * LANES, (r + 1) * LANES)
        weighted = (columns[:, r : r + 1] * events_ref[part, :].astype(F32)).astype(BF16)
        grown = weighted.astype(F32) * jnp.exp(columns[:, z.chunks + r : z.chunks + r + 1] * rate)
        block_ref[part, :] = grown.astype(BF16)
    ones = jnp.ones((8, LANES), BF16)
    high, low = [], []
    users = min(LANES, 8 * z.owners)
    for u in range(z.user_rows):
        user = iota((users, LANES), 0) + u * LANES
        below = jnp.zeros((users, LANES), F32)
        for r in range(z.slots // LANES):
            below += jnp.where(segment_ref[r : r + 1, :] < user, F32(1), F32(0))
        count = lax.dot_general(ones, below.astype(BF16), NT, preferred_element_type=F32)[0:1]
        if users < LANES:
            count = jnp.concatenate([count, jnp.full((1, LANES - users), z.slots, F32)], axis=1)
        own_ref[16 + u : 17 + u, :] = count
        count = count.astype(I32)
        high.append(count >> LOW)
        low.append(count & MASK)
    spare = z.code_rows - 3 * z.chunks - 2 * z.user_rows
    pad = [jnp.zeros((spare, LANES), I32)] if spare else []
    codes = jnp.concatenate([route, bucket >> LOW, bucket & MASK] + high + low + pad, axis=0)
    block_ref[z.rows : z.rows + z.code_rows, :] = codes.astype(F32).astype(BF16)


class Pieces:
    def __init__(self, z, form, refs):
        self.z, refs = z, list(refs)
        self.parts = [[refs.pop(0) for _ in range(n)] for n in form]
        self.count = len(form) if len(form) != 1 else self.parts[0][0].shape[0]
        self.per_group = 1 if len(form) != 1 else z.per_group
        self.groups = self.count // self.per_group

    def block(self, s):
        return (self.parts[s], 0) if len(self.parts) != 1 else (self.parts[0], s)

    def codes(self, s):
        parts, i = self.block(s)
        first = parts[0].shape[1] - self.z.code_rows
        return parts[0][i, first : first + self.z.code_rows, :].astype(F32)

    def rows(self, s):
        parts, i = self.block(s)
        first = parts[0][i, 0 : parts[0].shape[1] - self.z.code_rows, :]
        return jnp.concatenate([first] + [part[i] for part in parts[1:]], axis=0)

    def place(self, s):
        n, tile = self.z.chunks, self.codes(s)
        return tile[0:n] * F32(self.z.slots) + F32(LANES) * tile[n : 2 * n] + tile[2 * n : 3 * n]

    def below(self, s, u):
        tile, at = self.codes(s), 3 * self.z.chunks + u
        return F32(LANES) * tile[at : at + 1] + tile[at + self.z.user_rows : at + self.z.user_rows + 1]


class Runs:
    def __init__(self, z, starts):
        self.z, self.starts = z, starts
        users = min(LANES, 8 * z.owners)
        self.columns = [jnp.broadcast_to(row, (8, LANES)).T[:users, 0:1] for row in starts]
        self.steps = []
        for u, row in enumerate(starts):
            before = pltpu.roll(row, 1, 1)
            first = starts[u - 1][:, LANES - 1 : LANES] if u else jnp.zeros((1, 1), F32)
            step = (row - jnp.where(iota((1, LANES), 1) == 0, first, before)).astype(I32)
            pair = [jnp.broadcast_to(part, (LANES, LANES)) for part in (step >> LOW, step & MASK)]
            self.steps.append(jnp.concatenate(pair, axis=0).astype(F32).astype(BF16))

    def start(self, position):
        total = jnp.zeros((position.shape[0], 2 * LANES), F32)
        for row, step in zip(self.starts, self.steps):
            total += lax.dot_general(ones_where(row <= position), step, NT, preferred_element_type=F32)
        return F32(LANES) * total[:, :LANES] + total[:, LANES:]

    def start_row(self, row):
        start = jnp.zeros((1, LANES), F32)
        for column in self.columns:
            start = jnp.maximum(start, jnp.max(jnp.where(column <= row, column, F32(0)), axis=0, keepdims=True))
        return start

    def until(self, row):
        after = jnp.full((1, LANES), FAR, F32)
        for column in self.columns:
            later = jnp.where(column > row, column, F32(FAR))
            after = jnp.minimum(after, jnp.min(later, axis=0, keepdims=True))
        return jnp.minimum(row + F32(self.z.window), after - F32(1))


def root(z, distance):
    return lax.rsqrt(jnp.minimum(distance, F32(z.window)) + F32(1))


def pack(z, pieces, base, marks_ref, codes_ref, rows_ref, from_ref):
    if not pieces.count:
        return
    spare = jnp.zeros((8 - z.chunks, LANES), F32)

    def mark(s, carry):
        local = pieces.place(s) - base
        near = local.astype(I32)
        codes_ref[s] = jnp.concatenate([near >> LOW, near & MASK], axis=0).astype(F32)
        own = (local >= 0) & (local < F32(z.slots))
        tail = (local >= F32(-z.window)) & (local < 0)
        marks_ref[0, s] = jnp.concatenate([jnp.where(own, F32(1), F32(0)), spare], axis=0)
        marks_ref[1, s] = jnp.concatenate([jnp.where(tail, F32(1), F32(0)), spare], axis=0)
        return carry

    loop(pieces.count, mark, 0)
    upper = ones_where(iota((LANES, LANES), 0) < iota((LANES, LANES), 1))
    full = jnp.ones((LANES, LANES), BF16)
    lines = pieces.count * 8
    at, by = iota((lines, lines), 0), iota((lines, lines), 1)
    earlier = ones_where(((at >> 3) == (by >> 3)) & (by < at))
    source = iota((lines, LANES), 0) >> 3
    offset = ((source & (pieces.per_group - 1)) * z.capacity).astype(F32)
    for kind in range(2):
        marked = marks_ref[kind].reshape(lines, LANES)
        mark = marked.astype(BF16)
        rank = dot(mark, upper) + dot(earlier, dot(mark, full).astype(BF16)) + offset
        marks_ref[kind] = jnp.where(marked > 0, rank, F32(-1)).reshape(pieces.count, 8, LANES)

    spots = iota((LANES, LANES), 0).astype(F32)
    code_line = iota((2 * z.chunks, LANES), 0) & (z.chunks - 1)
    for kind in range(2):
        for g in range(pieces.groups):

            def add(i, carry):
                values, places = carry
                s = g * pieces.per_group + i
                ranks = marks_ref[kind, s]
                codes = codes_ref[s]
                hot = jnp.concatenate([ones_where(spots == ranks[r : r + 1]) for r in range(z.chunks)], axis=1)
                wide = [jnp.where(code_line == r, codes, F32(0)).astype(BF16) for r in range(z.chunks)]
                values += dot(hot, pieces.rows(s))
                places += lax.dot_general(jnp.concatenate(wide, axis=1), hot, NT, preferred_element_type=F32)
                return values, places

            zero = (jnp.zeros((LANES, LANES), F32), jnp.zeros((2 * z.chunks, LANES), F32))
            values, places = loop(pieces.per_group, add, zero)
            line = kind * pieces.groups + g
            rows_ref[line * LANES : (line + 1) * LANES, :] = values.astype(BF16)
            high = jnp.sum(places[: z.chunks], axis=0, keepdims=True)
            low = jnp.sum(places[z.chunks :], axis=0, keepdims=True)
            from_ref[line : line + 1, :] = F32(LANES) * high + low


def held(position, bounds):
    one, nothing = BF16(1), BF16(0)
    masks = [jnp.where(position - first <= length, one, nothing) for first, length in bounds]
    return jnp.concatenate(masks, axis=1)


def within(top, span, rows):
    if top.dtype == I16:
        one, nothing = BF16(1), BF16(0)
        return jnp.concatenate([jnp.where(top - row <= span, one, nothing) for row in rows], axis=1)
    return jnp.concatenate([ones_where((top - row >= 0) & (top - row <= span)) for row in rows], axis=1)


def wide_columns(*sets):
    count = sets[0].shape[0]
    columns = jnp.concatenate(sets, axis=0).T
    wide = lambda at: jnp.broadcast_to(columns[:, at : at + 1], (LANES, LANES))
    return [jnp.concatenate([wide(i * count + r) for r in range(count)], axis=0) for i in range(len(sets))]


def anchors(z, me):
    middle = F32(z.span * z.slots // 2)
    span_of = lambda owner: (owner.astype(I32) >> (z.span.bit_length() - 1)).astype(F32) * F32(z.span)
    own = (me - span_of(me)) * F32(z.slots) - middle
    tail = (me - span_of(me - F32(1))) * F32(z.slots) - middle
    return own, tail


def short(row):
    return row.astype(I32).astype(I16)


def early_kernel(z, form, before, *refs):
    count = sum(form)
    own_ref, pieces = refs[0], Pieces(z, form, refs[1 : 1 + count])
    refs = refs[1 + count :]
    if before:
        before_ref, sums_ref, rows_ref, from_ref, marks_ref, codes_ref = refs
    else:
        sums_ref, scale_ref, rows_ref, from_ref, high_ref, factor_ref, marks_ref, codes_ref = refs
    rate, me = own_ref[8:9, :], own_ref[9:10, :]
    runs = Runs(z, [own_ref[16 + u : 17 + u, :] for u in range(z.user_rows)])
    pack(z, pieces, me * F32(z.slots), marks_ref, codes_ref, rows_ref, from_ref)
    own_anchor, _ = anchors(z, me)
    inner = iota((BLOCK, LANES), 0)
    fall = jnp.exp(-rate * inner.astype(F32))
    bounds = []
    for g in range(pieces.groups if pieces.count else 0):
        begin = from_ref[g : g + 1, :]
        bounds.append((short(begin), short(runs.until(begin) - begin - F32(TOP))))
    for b in range(z.slots // BLOCK):
        part = slice(b * BLOCK, (b + 1) * BLOCK)
        if bounds:
            mask = held((inner + (b * BLOCK - TOP)).astype(I16), bounds)
            value = dot(mask, rows_ref[0 : len(bounds) * LANES, :])
        else:
            value = jnp.zeros((BLOCK, LANES), F32)
        sums_ref[part, :] = value + before_ref[part, :] if before else value
        if not before:
            first = F32(b * BLOCK)
            position = inner.astype(F32) + first
            start = runs.start(position)
            if b * BLOCK < z.window:
                scale_ref[part, :] = start
            else:
                scale_ref[part, :] = fall * jnp.exp(-rate * (first + own_anchor)) * root(z, position - start)
    if not before:
        position, span_start = wide_columns(own_ref[0 : z.chunks, :], own_ref[z.chunks : 2 * z.chunks, :])
        for shift in range(z.shifts):
            part = slice(shift * z.rows, (shift + 1) * z.rows)
            center = span_start + F32(z.span * z.slots // 2 - shift * z.span * z.slots)
            factor_ref[part, :] = jnp.exp(-rate * (position - center))
            top = position if shift == 0 else span_start - F32(1)
            high_ref[part, :] = short(top - F32(TOP)) if z.narrow else top


def late_kernel(z, earlier, form, late, *refs):
    own_ref, sums_ref, scale_ref, high_ref, factor_ref = refs[:5]
    tails = [refs[5 + 2 * i : 7 + 2 * i] for i in range(len(earlier))]
    refs = refs[5 + 2 * len(earlier) :]
    count = sum(form)
    table_out, feature_out, rows_ref, from_ref, marks_ref, codes_ref, table_ref, feature_ref, sems = refs[count:]
    pieces, last = Pieces(z, form, refs[:count]), Pieces(z, form[-late:], refs[count - sum(form[-late:]) : count])
    rate, me = own_ref[8:9, :], own_ref[9:10, :]
    base = me * F32(z.slots)
    starts = []
    for u in range(z.user_rows):
        add = lambda s, total: total + pieces.below(s, u)
        starts.append(loop(pieces.count, add, jnp.zeros((1, LANES), F32)))
    runs = Runs(z, starts)
    copies = []

    def send(ref, out, part):
        copies.append(pltpu.make_async_copy(ref.at[part, :], out.at[part, :], sems.at[len(copies)]))
        copies[-1].start()

    place = own_ref[0 : z.chunks, :]
    start = jnp.concatenate([runs.start_row(place[r : r + 1]) for r in range(z.chunks)], axis=0)
    distance = place - start
    reach = jnp.minimum(distance, F32(z.window))
    scale, reach = wide_columns(root(z, distance), reach - F32(TOP) if z.narrow else reach)
    position, span_start = (None, None) if z.narrow else wide_columns(place, own_ref[z.chunks : 2 * z.chunks, :])
    kind = short if z.narrow else lambda row: row
    total = jnp.zeros((z.rows, LANES), F32)
    for shift in range(z.shifts):
        part = slice(shift * z.rows, (shift + 1) * z.rows)
        top = high_ref[part, :]
        if z.narrow:
            span = short(reach)
        else:
            low = position - reach
            span = top - (jnp.maximum(low, span_start) if shift == 0 else low)

        def add(s, value):
            rows = pieces.place(s)
            mask = within(top, span, [kind(rows[r : r + 1]) for r in range(z.chunks)])
            return value + dot(mask, pieces.rows(s))

        total += loop(pieces.count, add, jnp.zeros((z.rows, LANES), F32)) * factor_ref[part, :]
    feature_ref[...] = (total * scale).astype(BF16)
    send(feature_ref, feature_out, slice(0, z.rows))

    pack(z, last, base, marks_ref, codes_ref, rows_ref, from_ref)
    own_anchor, tail_anchor = anchors(z, me)
    inner = iota((LATE_BLOCK, LANES), 0)
    fall = jnp.exp(-rate * inner.astype(F32))
    first_start = jnp.max(runs.start_row(base), axis=1, keepdims=True) - base
    bounds = []
    listed = [(from_ref, 0, 2 * last.groups)] + [(ref, count, count) for (_, ref), count in zip(tails, earlier)]
    for ref, first, lines in listed:
        for g in range(first, first + lines):
            begin = ref[g : g + 1, :]
            bounds.append((short(begin), short(runs.until(begin + base) - (begin + base) - F32(TOP))))
    n = last.groups
    own_rows = rows_ref[0 : n * LANES, :]
    tail_rows = [rows_ref[n * LANES : 2 * n * LANES, :]]
    tail_rows += [ref[count * LANES : 2 * count * LANES, :] for (ref, _), count in zip(tails, earlier)]
    tail_rows = jnp.concatenate(tail_rows, axis=0)
    for b in range(z.slots // LATE_BLOCK):
        part = slice(b * LATE_BLOCK, (b + 1) * LATE_BLOCK)
        position = (inner + (b * LATE_BLOCK - TOP)).astype(I16)
        first = F32(b * LATE_BLOCK)
        value = sums_ref[part, :]
        if b * LATE_BLOCK >= z.window:
            value = (value + dot(held(position, bounds[:n]), own_rows)) * scale_ref[part, :]
        else:
            own_fall = jnp.exp(-rate * (first + own_anchor))
            if z.shifts == 1:
                value += dot(held(position, bounds), jnp.concatenate([own_rows, tail_rows], axis=0))
                value *= own_fall
            else:
                value = (value + dot(held(position, bounds[:n]), own_rows)) * own_fall
                value += dot(held(position, bounds[n:]), tail_rows) * jnp.exp(-rate * (first + tail_anchor))
            start = scale_ref[part, :]
            start = jnp.where(start > 0, start, first_start)
            value = value * fall * root(z, inner.astype(F32) + first - start)
        table_ref[part, :] = value.astype(BF16)
        if (b + 1) * LATE_BLOCK % z.window == 0:
            send(table_ref, table_out, slice((b + 1) * LATE_BLOCK - z.window, (b + 1) * LATE_BLOCK))
    for copy in copies:
        copy.wait()


def swap(block, axis, distance):
    return lax.ppermute(block, axis, [(i, i ^ distance) for i in range(lax.axis_size(axis))])


def spread(blocks, axis):
    distance = lax.axis_size(axis) // 2
    while distance:
        blocks = blocks + [swap(block, axis, distance) for block in blocks]
        distance //= 2
    return blocks


def on_device(events, event_weight, route, bucket, segment, decay_rate):
    rows, width = events.shape
    key_count, shard_count = lax.axis_size("key"), lax.axis_size("shard")
    owners = key_count * shard_count
    slots = segment.shape[0]
    z = Sizes(owners, rows, slots)
    block_rows = rows + z.code_rows
    smem = pl.BlockSpec(memory_space=pltpu.SMEM)
    vmem = pl.BlockSpec(memory_space=pltpu.VMEM)
    shape = jax.ShapeDtypeStruct
    grant = pltpu.CompilerParams(vmem_limit_bytes=(16 if owners <= 8 else 48) * 1024 * 1024)
    me = (lax.axis_index("key") * shard_count + lax.axis_index("shard")).astype(I32).reshape(1)
    block, own = pl.pallas_call(
        functools.partial(send_kernel, z),
        out_shape=(
            shape((block_rows, width), BF16),
            shape((16 + z.user_rows + 7, LANES), F32),
        ),
        in_specs=[smem, smem] + [vmem] * 5,
        out_specs=(vmem, vmem),
        compiler_params=pltpu.CompilerParams(vmem_limit_bytes=56 * 1024 * 1024),
        name="weigh",
    )(
        me, decay_rate, events, event_weight.reshape(z.chunks, LANES), route.reshape(z.chunks, LANES),
        bucket.reshape(z.chunks, LANES), segment.reshape(slots // LANES, LANES),
    )

    def flat(blocks):
        return [part[None] if part.ndim == 2 else part for parts in blocks for part in parts]

    def sums(blocks, before=()):
        blocks, form, count = flat(blocks), tuple(map(len, blocks)), len(blocks)
        lines = max(8, 2 * count)
        whole = shape((slots, width), F32)
        kept = (shape((lines * LANES, LANES), BF16), shape((lines, LANES), F32))
        factors = shape((z.shifts * rows, width), F32)
        tops = shape((z.shifts * rows, width), I16 if z.narrow else F32)
        return pl.pallas_call(
            functools.partial(early_kernel, z, form, len(before)),
            out_shape=(whole,) + kept if before else (whole, whole) + kept + (tops, factors),
            in_specs=[vmem] * (1 + len(blocks) + len(before)),
            out_specs=(vmem,) * (3 if before else 6),
            scratch_shapes=[
                pltpu.VMEM((2, max(1, count), 8, LANES), F32),
                pltpu.VMEM((max(1, count), 2 * z.chunks, LANES), F32),
            ],
            compiler_params=grant,
            cost_estimate=pl.CostEstimate(flops=COST * count, bytes_accessed=0, transcendentals=0),
            name="more_sums" if before else "first_sums",
        )(own, *blocks, *before)

    if (key_count, shard_count) == (4, 2):
        tie = lax.optimization_barrier
        far = swap(block, "key", 2)
        side = swap(block, "shard", 1)
        near = swap(block, "key", 1)
        side_near = swap(side, "key", 1)
        total, scale, *tail, tops, factors = sums([(block,)])
        far, total = tie((far, total))
        last = swap(far, "key", 1)
        side_far = swap(far, "shard", 1)
        total, *tail2 = sums([(side,), (near,)], (total,))
        last, total = tie((last, total))
        side_last = swap(last, "shard", 1)
        second = [(far,), (last,), (side_far,)]
        total, *tail3 = sums(second, (total,))
        total, *tail4 = sums([(side_near,)], (total,))
        early = [(block,), (side,), (near,)] + second + [(side_near,)]
        earlier, tails, late = (1, 2, 3, 1), tail + tail2 + tail3 + tail4, [(side_last,)]
    else:
        blocks = spread(spread([block], "key"), "shard")
        total, scale, _, _, tops, factors = sums([])
        early, earlier, tails = [], (), []
        late = [(jnp.concatenate(blocks, axis=0).reshape(owners, block_rows, width),)]
    late_lines = 2 * (len(late) if earlier else z.groups)
    late_count = len(late) if earlier else owners
    form = tuple(map(len, early + late))
    return pl.pallas_call(
        functools.partial(late_kernel, z, earlier, form, len(late)),
        out_shape=(shape((slots, width), BF16), shape((rows, width), BF16)),
        in_specs=[vmem] * (5 + len(tails) + sum(form)),
        out_specs=(pl.BlockSpec(memory_space=pl.ANY),) * 2,
        scratch_shapes=[
            pltpu.VMEM((late_lines * LANES, LANES), BF16),
            pltpu.VMEM((late_lines, LANES), F32),
            pltpu.VMEM((2, late_count, 8, LANES), F32),
            pltpu.VMEM((late_count, 2 * z.chunks, LANES), F32),
            pltpu.VMEM((slots, width), BF16),
            pltpu.VMEM((rows, width), BF16),
            pltpu.SemaphoreType.DMA((1 + slots // z.window,)),
        ],
        compiler_params=grant,
        name="table_and_rows",
    )(own, total, scale, tops, factors, *tails, *flat(early + late))


def solution(mesh):
    placed = (
        P(("groups", "key", "shard"), "lane"),
        P(("groups", "key", "shard")),
        P(("groups", "key", "shard"), None),
        P(("groups", "key", "shard")),
        P(("groups", "key", "shard")),
        P("lane"),
    )
    return jax.shard_map(
        on_device,
        mesh=mesh,
        in_specs=placed,
        out_specs=(P(("groups", "key", "shard"), "lane"), P(("groups", "key", "shard"), "lane")),
        check_vma=False,
    )
```

```python
import functools
import jax
import jax.numpy as jnp
from jax import lax
from jax.experimental import pallas as pl
from jax.experimental.pallas import tpu as pltpu
from jax.sharding import PartitionSpec as P

LANES = 128
LOW = 7
MASK = 127
F32 = jnp.float32
BF16 = jnp.bfloat16
I32 = jnp.int32
I16 = jnp.int16
FAR = 1e9
TOP = 32768
NT = (((1,), (1,)), ((), ()))
BLOCK = 512
LATE_BLOCK = 256
COST = 1


class Sizes:
    def __init__(self, owners, rows, slots):
        self.owners, self.rows, self.slots = owners, rows, slots
        self.window = slots // 4
        self.chunks = rows // LANES
        self.user_rows = -(-8 * owners // LANES)
        self.code_rows = -(-(3 * self.chunks + 2 * self.user_rows) // 16) * 16
        self.span = min(owners, 8)
        self.shifts = 1 if owners <= self.span else 2
        self.capacity = 2 * rows // owners
        self.per_group = LANES // self.capacity
        self.groups = owners // self.per_group
        self.narrow = owners * slots <= 32768


def iota(shape, axis):
    return lax.broadcasted_iota(I32, shape, axis)


def ones_where(condition):
    return jnp.where(condition, F32(1), F32(0)).astype(BF16)


def dot(a, b):
    return jnp.dot(a, b, preferred_element_type=F32)


def loop(count, body, carry):
    if count <= 8:
        for i in range(count):
            carry = body(i, carry)
        return carry
    return lax.fori_loop(0, count, body, carry)


def send_kernel(z, me_ref, rate_ref, events_ref, weight_ref, route_ref, bucket_ref, segment_ref, block_ref, own_ref):
    groups = rate_ref.shape[0]
    lane = iota((1, LANES), 1)
    rate = jnp.full((1, LANES), rate_ref[0], F32)
    for g in range(1, groups):
        rate = jnp.where(lane >= g * (LANES // groups), rate_ref[g], rate)
    route = route_ref[...]
    bucket = bucket_ref[...]
    place = (route * z.slots + bucket).astype(F32)
    first = ((route >> (z.span.bit_length() - 1)) * (z.span * z.slots)).astype(F32)
    me = jnp.full((8 - 1, LANES), me_ref[0], I32).astype(F32)
    own_ref[0:16, :] = jnp.concatenate([place, first, rate, me], axis=0)
    spot = place - first - F32(z.span * z.slots // 2)
    columns = jnp.concatenate([weight_ref[...], spot], axis=0).T
    for r in range(z.chunks):
        part = slice(r * LANES, (r + 1) * LANES)
        weighted = (columns[:, r : r + 1] * events_ref[part, :].astype(F32)).astype(BF16)
        grown = weighted.astype(F32) * jnp.exp(columns[:, z.chunks + r : z.chunks + r + 1] * rate)
        block_ref[part, :] = grown.astype(BF16)
    ones = jnp.ones((8, LANES), BF16)
    high, low = [], []
    users = min(LANES, 8 * z.owners)
    for u in range(z.user_rows):
        user = iota((users, LANES), 0) + u * LANES
        below = jnp.zeros((users, LANES), F32)
        for r in range(z.slots // LANES):
            below += jnp.where(segment_ref[r : r + 1, :] < user, F32(1), F32(0))
        count = lax.dot_general(ones, below.astype(BF16), NT, preferred_element_type=F32)[0:1]
        if users < LANES:
            count = jnp.concatenate([count, jnp.full((1, LANES - users), z.slots, F32)], axis=1)
        own_ref[16 + u : 17 + u, :] = count
        count = count.astype(I32)
        high.append(count >> LOW)
        low.append(count & MASK)
    spare = z.code_rows - 3 * z.chunks - 2 * z.user_rows
    pad = [jnp.zeros((spare, LANES), I32)] if spare else []
    codes = jnp.concatenate([route, bucket >> LOW, bucket & MASK] + high + low + pad, axis=0)
    block_ref[z.rows : z.rows + z.code_rows, :] = codes.astype(F32).astype(BF16)


class Pieces:
    def __init__(self, z, form, refs):
        self.z, refs = z, list(refs)
        self.parts = [[refs.pop(0) for _ in range(n)] for n in form]
        self.count = len(form) if len(form) != 1 else self.parts[0][0].shape[0]
        self.per_group = 1 if len(form) != 1 else z.per_group
        self.groups = self.count // self.per_group

    def block(self, s):
        return (self.parts[s], 0) if len(self.parts) != 1 else (self.parts[0], s)

    def codes(self, s):
        parts, i = self.block(s)
        first = parts[0].shape[1] - self.z.code_rows
        return parts[0][i, first : first + self.z.code_rows, :].astype(F32)

    def rows(self, s):
        parts, i = self.block(s)
        first = parts[0][i, 0 : parts[0].shape[1] - self.z.code_rows, :]
        return jnp.concatenate([first] + [part[i] for part in parts[1:]], axis=0)

    def place(self, s):
        n, tile = self.z.chunks, self.codes(s)
        return tile[0:n] * F32(self.z.slots) + F32(LANES) * tile[n : 2 * n] + tile[2 * n : 3 * n]

    def below(self, s, u):
        tile, at = self.codes(s), 3 * self.z.chunks + u
        return F32(LANES) * tile[at : at + 1] + tile[at + self.z.user_rows : at + self.z.user_rows + 1]


class Runs:
    def __init__(self, z, starts):
        self.z, self.starts = z, starts
        users = min(LANES, 8 * z.owners)
        self.columns = [jnp.broadcast_to(row, (8, LANES)).T[:users, 0:1] for row in starts]
        self.steps = []
        for u, row in enumerate(starts):
            before = pltpu.roll(row, 1, 1)
            first = starts[u - 1][:, LANES - 1 : LANES] if u else jnp.zeros((1, 1), F32)
            step = (row - jnp.where(iota((1, LANES), 1) == 0, first, before)).astype(I32)
            pair = [jnp.broadcast_to(part, (LANES, LANES)) for part in (step >> LOW, step & MASK)]
            self.steps.append(jnp.concatenate(pair, axis=0).astype(F32).astype(BF16))

    def start(self, position):
        total = jnp.zeros((position.shape[0], 2 * LANES), F32)
        for row, step in zip(self.starts, self.steps):
            total += lax.dot_general(ones_where(row <= position), step, NT, preferred_element_type=F32)
        return F32(LANES) * total[:, :LANES] + total[:, LANES:]

    def start_row(self, row):
        start = jnp.zeros((1, LANES), F32)
        for column in self.columns:
            start = jnp.maximum(start, jnp.max(jnp.where(column <= row, column, F32(0)), axis=0, keepdims=True))
        return start

    def until(self, row):
        after = jnp.full((1, LANES), FAR, F32)
        for column in self.columns:
            later = jnp.where(column > row, column, F32(FAR))
            after = jnp.minimum(after, jnp.min(later, axis=0, keepdims=True))
        return jnp.minimum(row + F32(self.z.window), after - F32(1))


def root(z, distance):
    return lax.rsqrt(jnp.minimum(distance, F32(z.window)) + F32(1))


def pack(z, pieces, base, marks_ref, codes_ref, rows_ref, from_ref):
    if not pieces.count:
        return
    spare = jnp.zeros((8 - z.chunks, LANES), F32)

    def mark(s, carry):
        local = pieces.place(s) - base
        near = local.astype(I32)
        codes_ref[s] = jnp.concatenate([near >> LOW, near & MASK], axis=0).astype(F32)
        own = (local >= 0) & (local < F32(z.slots))
        tail = (local >= F32(-z.window)) & (local < 0)
        marks_ref[0, s] = jnp.concatenate([jnp.where(own, F32(1), F32(0)), spare], axis=0)
        marks_ref[1, s] = jnp.concatenate([jnp.where(tail, F32(1), F32(0)), spare], axis=0)
        return carry

    loop(pieces.count, mark, 0)
    upper = ones_where(iota((LANES, LANES), 0) < iota((LANES, LANES), 1))
    full = jnp.ones((LANES, LANES), BF16)
    lines = pieces.count * 8
    at, by = iota((lines, lines), 0), iota((lines, lines), 1)
    earlier = ones_where(((at >> 3) == (by >> 3)) & (by < at))
    source = iota((lines, LANES), 0) >> 3
    offset = ((source & (pieces.per_group - 1)) * z.capacity).astype(F32)
    for kind in range(2):
        marked = marks_ref[kind].reshape(lines, LANES)
        mark = marked.astype(BF16)
        rank = dot(mark, upper) + dot(earlier, dot(mark, full).astype(BF16)) + offset
        marks_ref[kind] = jnp.where(marked > 0, rank, F32(-1)).reshape(pieces.count, 8, LANES)

    spots = iota((LANES, LANES), 0).astype(F32)
    code_line = iota((2 * z.chunks, LANES), 0) & (z.chunks - 1)
    for kind in range(2):
        for g in range(pieces.groups):

            def add(i, carry):
                values, places = carry
                s = g * pieces.per_group + i
                ranks = marks_ref[kind, s]
                codes = codes_ref[s]
                hot = jnp.concatenate([ones_where(spots == ranks[r : r + 1]) for r in range(z.chunks)], axis=1)
                wide = [jnp.where(code_line == r, codes, F32(0)).astype(BF16) for r in range(z.chunks)]
                values += dot(hot, pieces.rows(s))
                places += lax.dot_general(jnp.concatenate(wide, axis=1), hot, NT, preferred_element_type=F32)
                return values, places

            zero = (jnp.zeros((LANES, LANES), F32), jnp.zeros((2 * z.chunks, LANES), F32))
            values, places = loop(pieces.per_group, add, zero)
            line = kind * pieces.groups + g
            rows_ref[line * LANES : (line + 1) * LANES, :] = values.astype(BF16)
            high = jnp.sum(places[: z.chunks], axis=0, keepdims=True)
            low = jnp.sum(places[z.chunks :], axis=0, keepdims=True)
            from_ref[line : line + 1, :] = F32(LANES) * high + low


def held(position, bounds):
    one, nothing = BF16(1), BF16(0)
    masks = [jnp.where(position - first <= length, one, nothing) for first, length in bounds]
    return jnp.concatenate(masks, axis=1)


def within(top, span, rows):
    if top.dtype == I16:
        one, nothing = BF16(1), BF16(0)
        return jnp.concatenate([jnp.where(top - row <= span, one, nothing) for row in rows], axis=1)
    return jnp.concatenate([ones_where((top - row >= 0) & (top - row <= span)) for row in rows], axis=1)


def wide_columns(*sets):
    count = sets[0].shape[0]
    columns = jnp.concatenate(sets, axis=0).T
    wide = lambda at: jnp.broadcast_to(columns[:, at : at + 1], (LANES, LANES))
    return [jnp.concatenate([wide(i * count + r) for r in range(count)], axis=0) for i in range(len(sets))]


def anchors(z, me):
    middle = F32(z.span * z.slots // 2)
    span_of = lambda owner: (owner.astype(I32) >> (z.span.bit_length() - 1)).astype(F32) * F32(z.span)
    own = (me - span_of(me)) * F32(z.slots) - middle
    tail = (me - span_of(me - F32(1))) * F32(z.slots) - middle
    return own, tail


def short(row):
    return row.astype(I32).astype(I16)


def early_kernel(z, form, before, *refs):
    count = sum(form)
    own_ref, pieces = refs[0], Pieces(z, form, refs[1 : 1 + count])
    refs = refs[1 + count :]
    if before:
        before_ref, sums_ref, rows_ref, from_ref, marks_ref, codes_ref = refs
    else:
        sums_ref, scale_ref, rows_ref, from_ref, high_ref, factor_ref, marks_ref, codes_ref = refs
    rate, me = own_ref[8:9, :], own_ref[9:10, :]
    runs = Runs(z, [own_ref[16 + u : 17 + u, :] for u in range(z.user_rows)])
    pack(z, pieces, me * F32(z.slots), marks_ref, codes_ref, rows_ref, from_ref)
    own_anchor, _ = anchors(z, me)
    inner = iota((BLOCK, LANES), 0)
    fall = jnp.exp(-rate * inner.astype(F32))
    bounds = []
    for g in range(pieces.groups if pieces.count else 0):
        begin = from_ref[g : g + 1, :]
        bounds.append((short(begin), short(runs.until(begin) - begin - F32(TOP))))
    for b in range(z.slots // BLOCK):
        part = slice(b * BLOCK, (b + 1) * BLOCK)
        if bounds:
            mask = held((inner + (b * BLOCK - TOP)).astype(I16), bounds)
            value = dot(mask, rows_ref[0 : len(bounds) * LANES, :])
        else:
            value = jnp.zeros((BLOCK, LANES), F32)
        sums_ref[part, :] = value + before_ref[part, :] if before else value
        if not before:
            first = F32(b * BLOCK)
            position = inner.astype(F32) + first
            start = runs.start(position)
            if b * BLOCK < z.window:
                scale_ref[part, :] = start
            else:
                scale_ref[part, :] = fall * jnp.exp(-rate * (first + own_anchor)) * root(z, position - start)
    if not before:
        position, span_start = wide_columns(own_ref[0 : z.chunks, :], own_ref[z.chunks : 2 * z.chunks, :])
        for shift in range(z.shifts):
            part = slice(shift * z.rows, (shift + 1) * z.rows)
            center = span_start + F32(z.span * z.slots // 2 - shift * z.span * z.slots)
            factor_ref[part, :] = jnp.exp(-rate * (position - center))
            top = position if shift == 0 else span_start - F32(1)
            high_ref[part, :] = short(top - F32(TOP)) if z.narrow else top


def late_kernel(z, earlier, form, late, *refs):
    own_ref, sums_ref, scale_ref, high_ref, factor_ref = refs[:5]
    tails = [refs[5 + 2 * i : 7 + 2 * i] for i in range(len(earlier))]
    refs = refs[5 + 2 * len(earlier) :]
    count = sum(form)
    table_out, feature_out, rows_ref, from_ref, marks_ref, codes_ref, table_ref, feature_ref, sems = refs[count:]
    pieces, last = Pieces(z, form, refs[:count]), Pieces(z, form[-late:], refs[count - sum(form[-late:]) : count])
    rate, me = own_ref[8:9, :], own_ref[9:10, :]
    base = me * F32(z.slots)
    starts = []
    for u in range(z.user_rows):
        add = lambda s, total: total + pieces.below(s, u)
        starts.append(loop(pieces.count, add, jnp.zeros((1, LANES), F32)))
    runs = Runs(z, starts)
    copies = []

    def send(ref, out, part):
        copies.append(pltpu.make_async_copy(ref.at[part, :], out.at[part, :], sems.at[len(copies)]))
        copies[-1].start()

    place = own_ref[0 : z.chunks, :]
    start = jnp.concatenate([runs.start_row(place[r : r + 1]) for r in range(z.chunks)], axis=0)
    distance = place - start
    reach = jnp.minimum(distance, F32(z.window))
    scale, reach = wide_columns(root(z, distance), reach - F32(TOP) if z.narrow else reach)
    position, span_start = (None, None) if z.narrow else wide_columns(place, own_ref[z.chunks : 2 * z.chunks, :])
    kind = short if z.narrow else lambda row: row
    for t in range(0, z.rows, LATE_BLOCK):
        block = slice(t, t + LATE_BLOCK)
        total = jnp.zeros((LATE_BLOCK, LANES), F32)
        for shift in range(z.shifts):
            part = slice(shift * z.rows + t, shift * z.rows + t + LATE_BLOCK)
            top = high_ref[part, :]
            if z.narrow:
                span = short(reach[block])
            else:
                low = position[block] - reach[block]
                span = top - (jnp.maximum(low, span_start[block]) if shift == 0 else low)

            def add(s, value):
                rows = pieces.place(s)
                mask = within(top, span, [kind(rows[r : r + 1]) for r in range(z.chunks)])
                return value + dot(mask, pieces.rows(s))

            total += loop(pieces.count, add, jnp.zeros((LATE_BLOCK, LANES), F32)) * factor_ref[part, :]
        feature_ref[block, :] = (total * scale[block]).astype(BF16)
    send(feature_ref, feature_out, slice(0, z.rows))

    pack(z, last, base, marks_ref, codes_ref, rows_ref, from_ref)
    own_anchor, tail_anchor = anchors(z, me)
    inner = iota((LATE_BLOCK, LANES), 0)
    fall = jnp.exp(-rate * inner.astype(F32))
    first_start = jnp.max(runs.start_row(base), axis=1, keepdims=True) - base
    bounds = []
    listed = [(from_ref, 0, 2 * last.groups)] + [(ref, count, count) for (_, ref), count in zip(tails, earlier)]
    for ref, first, lines in listed:
        for g in range(first, first + lines):
            begin = ref[g : g + 1, :]
            bounds.append((short(begin), short(runs.until(begin + base) - (begin + base) - F32(TOP))))
    n = last.groups
    own_rows = rows_ref[0 : n * LANES, :]
    tail_rows = [rows_ref[n * LANES : 2 * n * LANES, :]]
    tail_rows += [ref[count * LANES : 2 * count * LANES, :] for (ref, _), count in zip(tails, earlier)]
    tail_rows = jnp.concatenate(tail_rows, axis=0)
    for b in range(z.slots // LATE_BLOCK):
        part = slice(b * LATE_BLOCK, (b + 1) * LATE_BLOCK)
        position = (inner + (b * LATE_BLOCK - TOP)).astype(I16)
        first = F32(b * LATE_BLOCK)
        value = sums_ref[part, :]
        if b * LATE_BLOCK >= z.window:
            value = (value + dot(held(position, bounds[:n]), own_rows)) * scale_ref[part, :]
        else:
            own_fall = jnp.exp(-rate * (first + own_anchor))
            if z.shifts == 1:
                value += dot(held(position, bounds), jnp.concatenate([own_rows, tail_rows], axis=0))
                value *= own_fall
            else:
                value = (value + dot(held(position, bounds[:n]), own_rows)) * own_fall
                value += dot(held(position, bounds[n:]), tail_rows) * jnp.exp(-rate * (first + tail_anchor))
            start = scale_ref[part, :]
            start = jnp.where(start > 0, start, first_start)
            value = value * fall * root(z, inner.astype(F32) + first - start)
        table_ref[part, :] = value.astype(BF16)
        if (b + 1) * LATE_BLOCK % z.window == 0:
            send(table_ref, table_out, slice((b + 1) * LATE_BLOCK - z.window, (b + 1) * LATE_BLOCK))
    for copy in copies:
        copy.wait()


def swap(block, axis, distance):
    return lax.ppermute(block, axis, [(i, i ^ distance) for i in range(lax.axis_size(axis))])


def spread(blocks, axis):
    distance = lax.axis_size(axis) // 2
    while distance:
        blocks = blocks + [swap(block, axis, distance) for block in blocks]
        distance //= 2
    return blocks


def on_device(events, event_weight, route, bucket, segment, decay_rate):
    rows, width = events.shape
    key_count, shard_count = lax.axis_size("key"), lax.axis_size("shard")
    owners = key_count * shard_count
    slots = segment.shape[0]
    z = Sizes(owners, rows, slots)
    block_rows = rows + z.code_rows
    smem = pl.BlockSpec(memory_space=pltpu.SMEM)
    vmem = pl.BlockSpec(memory_space=pltpu.VMEM)
    shape = jax.ShapeDtypeStruct
    grant = pltpu.CompilerParams(vmem_limit_bytes=(16 if owners <= 8 else 48) * 1024 * 1024)
    me = (lax.axis_index("key") * shard_count + lax.axis_index("shard")).astype(I32).reshape(1)
    block, own = pl.pallas_call(
        functools.partial(send_kernel, z),
        out_shape=(
            shape((block_rows, width), BF16),
            shape((16 + z.user_rows + 7, LANES), F32),
        ),
        in_specs=[smem, smem] + [vmem] * 5,
        out_specs=(vmem, vmem),
        compiler_params=pltpu.CompilerParams(vmem_limit_bytes=56 * 1024 * 1024),
        name="weigh",
    )(
        me, decay_rate, events, event_weight.reshape(z.chunks, LANES), route.reshape(z.chunks, LANES),
        bucket.reshape(z.chunks, LANES), segment.reshape(slots // LANES, LANES),
    )

    def flat(blocks):
        return [part[None] if part.ndim == 2 else part for parts in blocks for part in parts]

    def sums(blocks, before=()):
        blocks, form, count = flat(blocks), tuple(map(len, blocks)), len(blocks)
        lines = max(8, 2 * count)
        whole = shape((slots, width), F32)
        kept = (shape((lines * LANES, LANES), BF16), shape((lines, LANES), F32))
        factors = shape((z.shifts * rows, width), F32)
        tops = shape((z.shifts * rows, width), I16 if z.narrow else F32)
        return pl.pallas_call(
            functools.partial(early_kernel, z, form, len(before)),
            out_shape=(whole,) + kept if before else (whole, whole) + kept + (tops, factors),
            in_specs=[vmem] * (1 + len(blocks) + len(before)),
            out_specs=(vmem,) * (3 if before else 6),
            scratch_shapes=[
                pltpu.VMEM((2, max(1, count), 8, LANES), F32),
                pltpu.VMEM((max(1, count), 2 * z.chunks, LANES), F32),
            ],
            compiler_params=grant,
            cost_estimate=pl.CostEstimate(flops=COST * count, bytes_accessed=0, transcendentals=0),
            name="more_sums" if before else "first_sums",
        )(own, *blocks, *before)

    if (key_count, shard_count) == (4, 2):
        tie = lax.optimization_barrier
        far = swap(block, "key", 2)
        side = swap(block, "shard", 1)
        near = swap(block, "key", 1)
        side_near = swap(side, "key", 1)
        total, scale, *tail, tops, factors = sums([(block,)])
        far, total = tie((far, total))
        last = swap(far, "key", 1)
        side_far = swap(far, "shard", 1)
        total, *tail2 = sums([(side,), (near,)], (total,))
        last, total = tie((last, total))
        side_last = swap(last, "shard", 1)
        second = [(far,), (last,), (side_far,)]
        late = [(side_near,), (side_last,)]
        total, *tail3 = sums(second, (total,))
        early, earlier, tails = [(block,), (side,), (near,)] + second, (1, 2, 3), tail + tail2 + tail3
    else:
        blocks = spread(spread([block], "key"), "shard")
        total, scale, _, _, tops, factors = sums([])
        early, earlier, tails = [], (), []
        late = [(jnp.concatenate(blocks, axis=0).reshape(owners, block_rows, width),)]
    late_lines = 2 * (len(late) if earlier else z.groups)
    late_count = len(late) if earlier else owners
    form = tuple(map(len, early + late))
    return pl.pallas_call(
        functools.partial(late_kernel, z, earlier, form, len(late)),
        out_shape=(shape((slots, width), BF16), shape((rows, width), BF16)),
        in_specs=[vmem] * (5 + len(tails) + sum(form)),
        out_specs=(pl.BlockSpec(memory_space=pl.ANY),) * 2,
        scratch_shapes=[
            pltpu.VMEM((late_lines * LANES, LANES), BF16),
            pltpu.VMEM((late_lines, LANES), F32),
            pltpu.VMEM((2, late_count, 8, LANES), F32),
            pltpu.VMEM((late_count, 2 * z.chunks, LANES), F32),
            pltpu.VMEM((slots, width), BF16),
            pltpu.VMEM((rows, width), BF16),
            pltpu.SemaphoreType.DMA((1 + slots // z.window,)),
        ],
        compiler_params=grant,
        name="table_and_rows",
    )(own, total, scale, tops, factors, *tails, *flat(early + late))


def solution(mesh):
    placed = (
        P(("groups", "key", "shard"), "lane"),
        P(("groups", "key", "shard")),
        P(("groups", "key", "shard"), None),
        P(("groups", "key", "shard")),
        P(("groups", "key", "shard")),
        P("lane"),
    )
    return jax.shard_map(
        on_device,
        mesh=mesh,
        in_specs=placed,
        out_specs=(P(("groups", "key", "shard"), "lane"), P(("groups", "key", "shard"), "lane")),
        check_vma=False,
    )
```

```python
import functools
import jax
import jax.numpy as jnp
from jax import lax
from jax.experimental import pallas as pl
from jax.experimental.pallas import tpu as pltpu
from jax.sharding import PartitionSpec as P

LANES = 128
LOW = 7
MASK = 127
F32 = jnp.float32
BF16 = jnp.bfloat16
I32 = jnp.int32
I16 = jnp.int16
FAR = 1e9
TOP = 32768
NT = (((1,), (1,)), ((), ()))
BLOCK = 512
LATE_BLOCK = 256
COST = 1


class Sizes:
    def __init__(self, owners, rows, slots):
        self.owners, self.rows, self.slots = owners, rows, slots
        self.window = slots // 4
        self.chunks = rows // LANES
        self.user_rows = -(-8 * owners // LANES)
        self.code_rows = -(-(3 * self.chunks + 2 * self.user_rows) // 16) * 16
        self.span = min(owners, 8)
        self.shifts = 1 if owners <= self.span else 2
        self.capacity = 2 * rows // owners
        self.per_group = LANES // self.capacity
        self.groups = owners // self.per_group
        self.narrow = owners * slots <= 32768


def iota(shape, axis):
    return lax.broadcasted_iota(I32, shape, axis)


def ones_where(condition):
    return jnp.where(condition, F32(1), F32(0)).astype(BF16)


def dot(a, b):
    return jnp.dot(a, b, preferred_element_type=F32)


def loop(count, body, carry):
    if count <= 8:
        for i in range(count):
            carry = body(i, carry)
        return carry
    return lax.fori_loop(0, count, body, carry)


def send_kernel(z, me_ref, rate_ref, events_ref, weight_ref, route_ref, bucket_ref, segment_ref, block_ref, own_ref):
    groups = rate_ref.shape[0]
    lane = iota((1, LANES), 1)
    rate = jnp.full((1, LANES), rate_ref[0], F32)
    for g in range(1, groups):
        rate = jnp.where(lane >= g * (LANES // groups), rate_ref[g], rate)
    route = route_ref[...]
    bucket = bucket_ref[...]
    place = (route * z.slots + bucket).astype(F32)
    first = ((route >> (z.span.bit_length() - 1)) * (z.span * z.slots)).astype(F32)
    me = jnp.full((8 - 1, LANES), me_ref[0], I32).astype(F32)
    own_ref[0:16, :] = jnp.concatenate([place, first, rate, me], axis=0)
    spot = place - first - F32(z.span * z.slots // 2)
    columns = jnp.concatenate([weight_ref[...], spot], axis=0).T
    for r in range(z.chunks):
        part = slice(r * LANES, (r + 1) * LANES)
        weighted = (columns[:, r : r + 1] * events_ref[part, :].astype(F32)).astype(BF16)
        grown = weighted.astype(F32) * jnp.exp(columns[:, z.chunks + r : z.chunks + r + 1] * rate)
        block_ref[part, :] = grown.astype(BF16)
    ones = jnp.ones((8, LANES), BF16)
    high, low = [], []
    users = min(LANES, 8 * z.owners)
    for u in range(z.user_rows):
        user = iota((users, LANES), 0) + u * LANES
        below = jnp.zeros((users, LANES), F32)
        for r in range(z.slots // LANES):
            below += jnp.where(segment_ref[r : r + 1, :] < user, F32(1), F32(0))
        count = lax.dot_general(ones, below.astype(BF16), NT, preferred_element_type=F32)[0:1]
        if users < LANES:
            count = jnp.concatenate([count, jnp.full((1, LANES - users), z.slots, F32)], axis=1)
        own_ref[16 + u : 17 + u, :] = count
        count = count.astype(I32)
        high.append(count >> LOW)
        low.append(count & MASK)
    spare = z.code_rows - 3 * z.chunks - 2 * z.user_rows
    pad = [jnp.zeros((spare, LANES), I32)] if spare else []
    codes = jnp.concatenate([route, bucket >> LOW, bucket & MASK] + high + low + pad, axis=0)
    block_ref[z.rows : z.rows + z.code_rows, :] = codes.astype(F32).astype(BF16)


class Pieces:
    def __init__(self, z, form, refs):
        self.z, refs = z, list(refs)
        self.parts = [[refs.pop(0) for _ in range(n)] for n in form]
        self.count = len(form) if len(form) != 1 else self.parts[0][0].shape[0]
        self.per_group = 1 if len(form) != 1 else z.per_group
        self.groups = self.count // self.per_group

    def block(self, s):
        return (self.parts[s], 0) if len(self.parts) != 1 else (self.parts[0], s)

    def codes(self, s):
        parts, i = self.block(s)
        first = parts[0].shape[1] - self.z.code_rows
        return parts[0][i, first : first + self.z.code_rows, :].astype(F32)

    def rows(self, s):
        parts, i = self.block(s)
        first = parts[0][i, 0 : parts[0].shape[1] - self.z.code_rows, :]
        return jnp.concatenate([first] + [part[i] for part in parts[1:]], axis=0)

    def place(self, s):
        n, tile = self.z.chunks, self.codes(s)
        return tile[0:n] * F32(self.z.slots) + F32(LANES) * tile[n : 2 * n] + tile[2 * n : 3 * n]

    def below(self, s, u):
        tile, at = self.codes(s), 3 * self.z.chunks + u
        return F32(LANES) * tile[at : at + 1] + tile[at + self.z.user_rows : at + self.z.user_rows + 1]


class Runs:
    def __init__(self, z, starts):
        self.z, self.starts = z, starts
        users = min(LANES, 8 * z.owners)
        self.columns = [jnp.broadcast_to(row, (8, LANES)).T[:users, 0:1] for row in starts]
        self.steps = []
        for u, row in enumerate(starts):
            before = pltpu.roll(row, 1, 1)
            first = starts[u - 1][:, LANES - 1 : LANES] if u else jnp.zeros((1, 1), F32)
            step = (row - jnp.where(iota((1, LANES), 1) == 0, first, before)).astype(I32)
            pair = [jnp.broadcast_to(part, (LANES, LANES)) for part in (step >> LOW, step & MASK)]
            self.steps.append(jnp.concatenate(pair, axis=0).astype(F32).astype(BF16))

    def start(self, position):
        total = jnp.zeros((position.shape[0], 2 * LANES), F32)
        for row, step in zip(self.starts, self.steps):
            total += lax.dot_general(ones_where(row <= position), step, NT, preferred_element_type=F32)
        return F32(LANES) * total[:, :LANES] + total[:, LANES:]

    def start_row(self, row):
        start = jnp.zeros((1, LANES), F32)
        for column in self.columns:
            start = jnp.maximum(start, jnp.max(jnp.where(column <= row, column, F32(0)), axis=0, keepdims=True))
        return start

    def until(self, row):
        after = jnp.full((1, LANES), FAR, F32)
        for column in self.columns:
            later = jnp.where(column > row, column, F32(FAR))
            after = jnp.minimum(after, jnp.min(later, axis=0, keepdims=True))
        return jnp.minimum(row + F32(self.z.window), after - F32(1))


def root(z, distance):
    return lax.rsqrt(jnp.minimum(distance, F32(z.window)) + F32(1))


def pack(z, pieces, base, marks_ref, codes_ref, rows_ref, from_ref):
    if not pieces.count:
        return
    spare = jnp.zeros((8 - z.chunks, LANES), F32)

    def mark(s, carry):
        local = pieces.place(s) - base
        near = local.astype(I32)
        codes_ref[s] = jnp.concatenate([near >> LOW, near & MASK], axis=0).astype(F32)
        own = (local >= 0) & (local < F32(z.slots))
        tail = (local >= F32(-z.window)) & (local < 0)
        marks_ref[0, s] = jnp.concatenate([jnp.where(own, F32(1), F32(0)), spare], axis=0)
        marks_ref[1, s] = jnp.concatenate([jnp.where(tail, F32(1), F32(0)), spare], axis=0)
        return carry

    loop(pieces.count, mark, 0)
    upper = ones_where(iota((LANES, LANES), 0) < iota((LANES, LANES), 1))
    full = jnp.ones((LANES, LANES), BF16)
    lines = pieces.count * 8
    at, by = iota((lines, lines), 0), iota((lines, lines), 1)
    earlier = ones_where(((at >> 3) == (by >> 3)) & (by < at))
    source = iota((lines, LANES), 0) >> 3
    offset = ((source & (pieces.per_group - 1)) * z.capacity).astype(F32)
    for kind in range(2):
        marked = marks_ref[kind].reshape(lines, LANES)
        mark = marked.astype(BF16)
        rank = dot(mark, upper) + dot(earlier, dot(mark, full).astype(BF16)) + offset
        marks_ref[kind] = jnp.where(marked > 0, rank, F32(-1)).reshape(pieces.count, 8, LANES)

    spots = iota((LANES, LANES), 0).astype(F32)
    code_line = iota((2 * z.chunks, LANES), 0) & (z.chunks - 1)
    for kind in range(2):
        for g in range(pieces.groups):

            def add(i, carry):
                values, places = carry
                s = g * pieces.per_group + i
                ranks = marks_ref[kind, s]
                codes = codes_ref[s]
                hot = jnp.concatenate([ones_where(spots == ranks[r : r + 1]) for r in range(z.chunks)], axis=1)
                wide = [jnp.where(code_line == r, codes, F32(0)).astype(BF16) for r in range(z.chunks)]
                values += dot(hot, pieces.rows(s))
                places += lax.dot_general(jnp.concatenate(wide, axis=1), hot, NT, preferred_element_type=F32)
                return values, places

            zero = (jnp.zeros((LANES, LANES), F32), jnp.zeros((2 * z.chunks, LANES), F32))
            values, places = loop(pieces.per_group, add, zero)
            line = kind * pieces.groups + g
            rows_ref[line * LANES : (line + 1) * LANES, :] = values.astype(BF16)
            high = jnp.sum(places[: z.chunks], axis=0, keepdims=True)
            low = jnp.sum(places[z.chunks :], axis=0, keepdims=True)
            from_ref[line : line + 1, :] = F32(LANES) * high + low


def tiles(values):
    return values.reshape(values.shape[0] // 16, 16, LANES)


def tile_of(row):
    return jnp.broadcast_to(row.astype(I32), (16, LANES)).astype(I16)


def held(position, bounds):
    one, nothing, count = BF16(1), BF16(0), position.shape[0]
    position = tiles(position)
    masks = [jnp.where(position - first[None] <= length[None], one, nothing) for first, length in bounds]
    return jnp.concatenate([mask.reshape(count, LANES) for mask in masks], axis=1)


def within(top, span, rows):
    if top.dtype == I16:
        one, nothing, count = BF16(1), BF16(0), top.shape[0]
        top, span = tiles(top), tiles(span)
        masks = [jnp.where(top - tile_of(row)[None] <= span, one, nothing) for row in rows]
        return jnp.concatenate([mask.reshape(count, LANES) for mask in masks], axis=1)
    return jnp.concatenate([ones_where((top - row >= 0) & (top - row <= span)) for row in rows], axis=1)


def wide_columns(*sets):
    count = sets[0].shape[0]
    columns = jnp.concatenate(sets, axis=0).T
    wide = lambda at: jnp.broadcast_to(columns[:, at : at + 1], (LANES, LANES))
    return [jnp.concatenate([wide(i * count + r) for r in range(count)], axis=0) for i in range(len(sets))]


def anchors(z, me):
    middle = F32(z.span * z.slots // 2)
    span_of = lambda owner: (owner.astype(I32) >> (z.span.bit_length() - 1)).astype(F32) * F32(z.span)
    own = (me - span_of(me)) * F32(z.slots) - middle
    tail = (me - span_of(me - F32(1))) * F32(z.slots) - middle
    return own, tail


def short(row):
    return row.astype(I32).astype(I16)


def early_kernel(z, form, before, *refs):
    count = sum(form)
    own_ref, pieces = refs[0], Pieces(z, form, refs[1 : 1 + count])
    refs = refs[1 + count :]
    if before:
        before_ref, sums_ref, rows_ref, from_ref, marks_ref, codes_ref = refs
    else:
        sums_ref, scale_ref, rows_ref, from_ref, high_ref, factor_ref, marks_ref, codes_ref = refs
    rate, me = own_ref[8:9, :], own_ref[9:10, :]
    runs = Runs(z, [own_ref[16 + u : 17 + u, :] for u in range(z.user_rows)])
    pack(z, pieces, me * F32(z.slots), marks_ref, codes_ref, rows_ref, from_ref)
    own_anchor, _ = anchors(z, me)
    inner = iota((BLOCK, LANES), 0)
    fall = jnp.exp(-rate * inner.astype(F32))
    bounds = []
    for g in range(pieces.groups if pieces.count else 0):
        begin = from_ref[g : g + 1, :]
        bounds.append((tile_of(begin), tile_of(runs.until(begin) - begin - F32(TOP))))
    for b in range(z.slots // BLOCK):
        part = slice(b * BLOCK, (b + 1) * BLOCK)
        if bounds:
            mask = held((inner + (b * BLOCK - TOP)).astype(I16), bounds)
            value = dot(mask, rows_ref[0 : len(bounds) * LANES, :])
        else:
            value = jnp.zeros((BLOCK, LANES), F32)
        sums_ref[part, :] = value + before_ref[part, :] if before else value
        if not before:
            first = F32(b * BLOCK)
            position = inner.astype(F32) + first
            start = runs.start(position)
            if b * BLOCK < z.window:
                scale_ref[part, :] = start
            else:
                scale_ref[part, :] = fall * jnp.exp(-rate * (first + own_anchor)) * root(z, position - start)
    if not before:
        position, span_start = wide_columns(own_ref[0 : z.chunks, :], own_ref[z.chunks : 2 * z.chunks, :])
        for shift in range(z.shifts):
            part = slice(shift * z.rows, (shift + 1) * z.rows)
            center = span_start + F32(z.span * z.slots // 2 - shift * z.span * z.slots)
            factor_ref[part, :] = jnp.exp(-rate * (position - center))
            top = position if shift == 0 else span_start - F32(1)
            high_ref[part, :] = short(top - F32(TOP)) if z.narrow else top


def late_kernel(z, earlier, form, late, *refs):
    own_ref, sums_ref, scale_ref, high_ref, factor_ref = refs[:5]
    tails = [refs[5 + 2 * i : 7 + 2 * i] for i in range(len(earlier))]
    refs = refs[5 + 2 * len(earlier) :]
    count = sum(form)
    table_out, feature_out, rows_ref, from_ref, marks_ref, codes_ref, table_ref, feature_ref, sems = refs[count:]
    pieces, last = Pieces(z, form, refs[:count]), Pieces(z, form[-late:], refs[count - sum(form[-late:]) : count])
    rate, me = own_ref[8:9, :], own_ref[9:10, :]
    base = me * F32(z.slots)
    starts = []
    for u in range(z.user_rows):
        add = lambda s, total: total + pieces.below(s, u)
        starts.append(loop(pieces.count, add, jnp.zeros((1, LANES), F32)))
    runs = Runs(z, starts)
    copies = []

    def send(ref, out, part):
        copies.append(pltpu.make_async_copy(ref.at[part, :], out.at[part, :], sems.at[len(copies)]))
        copies[-1].start()

    place = own_ref[0 : z.chunks, :]
    start = jnp.concatenate([runs.start_row(place[r : r + 1]) for r in range(z.chunks)], axis=0)
    distance = place - start
    reach = jnp.minimum(distance, F32(z.window))
    scale, reach = wide_columns(root(z, distance), reach - F32(TOP) if z.narrow else reach)
    position, span_start = (None, None) if z.narrow else wide_columns(place, own_ref[z.chunks : 2 * z.chunks, :])
    total = jnp.zeros((z.rows, LANES), F32)
    for shift in range(z.shifts):
        part = slice(shift * z.rows, (shift + 1) * z.rows)
        top = high_ref[part, :]
        if z.narrow:
            span = short(reach)
        else:
            low = position - reach
            span = top - (jnp.maximum(low, span_start) if shift == 0 else low)

        def add(s, value):
            rows = pieces.place(s)
            mask = within(top, span, [rows[r : r + 1] for r in range(z.chunks)])
            return value + dot(mask, pieces.rows(s))

        total += loop(pieces.count, add, jnp.zeros((z.rows, LANES), F32)) * factor_ref[part, :]
    feature_ref[...] = (total * scale).astype(BF16)
    send(feature_ref, feature_out, slice(0, z.rows))

    pack(z, last, base, marks_ref, codes_ref, rows_ref, from_ref)
    own_anchor, tail_anchor = anchors(z, me)
    inner = iota((LATE_BLOCK, LANES), 0)
    fall = jnp.exp(-rate * inner.astype(F32))
    first_start = jnp.max(runs.start_row(base), axis=1, keepdims=True) - base
    bounds = []
    listed = [(from_ref, 0, 2 * last.groups)] + [(ref, count, count) for (_, ref), count in zip(tails, earlier)]
    for ref, first, lines in listed:
        for g in range(first, first + lines):
            begin = ref[g : g + 1, :]
            bounds.append((tile_of(begin), tile_of(runs.until(begin + base) - (begin + base) - F32(TOP))))
    n = last.groups
    own_rows = rows_ref[0 : n * LANES, :]
    tail_rows = [rows_ref[n * LANES : 2 * n * LANES, :]]
    tail_rows += [ref[count * LANES : 2 * count * LANES, :] for (ref, _), count in zip(tails, earlier)]
    tail_rows = jnp.concatenate(tail_rows, axis=0)
    for b in range(z.slots // LATE_BLOCK):
        part = slice(b * LATE_BLOCK, (b + 1) * LATE_BLOCK)
        position = (inner + (b * LATE_BLOCK - TOP)).astype(I16)
        first = F32(b * LATE_BLOCK)
        value = sums_ref[part, :]
        if b * LATE_BLOCK >= z.window:
            value = (value + dot(held(position, bounds[:n]), own_rows)) * scale_ref[part, :]
        else:
            own_fall = jnp.exp(-rate * (first + own_anchor))
            if z.shifts == 1:
                value += dot(held(position, bounds), jnp.concatenate([own_rows, tail_rows], axis=0))
                value *= own_fall
            else:
                value = (value + dot(held(position, bounds[:n]), own_rows)) * own_fall
                value += dot(held(position, bounds[n:]), tail_rows) * jnp.exp(-rate * (first + tail_anchor))
            start = scale_ref[part, :]
            start = jnp.where(start > 0, start, first_start)
            value = value * fall * root(z, inner.astype(F32) + first - start)
        table_ref[part, :] = value.astype(BF16)
        if (b + 1) * LATE_BLOCK % z.window == 0:
            send(table_ref, table_out, slice((b + 1) * LATE_BLOCK - z.window, (b + 1) * LATE_BLOCK))
    for copy in copies:
        copy.wait()


def swap(block, axis, distance):
    return lax.ppermute(block, axis, [(i, i ^ distance) for i in range(lax.axis_size(axis))])


def spread(blocks, axis):
    distance = lax.axis_size(axis) // 2
    while distance:
        blocks = blocks + [swap(block, axis, distance) for block in blocks]
        distance //= 2
    return blocks


def on_device(events, event_weight, route, bucket, segment, decay_rate):
    rows, width = events.shape
    key_count, shard_count = lax.axis_size("key"), lax.axis_size("shard")
    owners = key_count * shard_count
    slots = segment.shape[0]
    z = Sizes(owners, rows, slots)
    block_rows = rows + z.code_rows
    smem = pl.BlockSpec(memory_space=pltpu.SMEM)
    vmem = pl.BlockSpec(memory_space=pltpu.VMEM)
    shape = jax.ShapeDtypeStruct
    grant = pltpu.CompilerParams(vmem_limit_bytes=(16 if owners <= 8 else 48) * 1024 * 1024)
    me = (lax.axis_index("key") * shard_count + lax.axis_index("shard")).astype(I32).reshape(1)
    block, own = pl.pallas_call(
        functools.partial(send_kernel, z),
        out_shape=(
            shape((block_rows, width), BF16),
            shape((16 + z.user_rows + 7, LANES), F32),
        ),
        in_specs=[smem, smem] + [vmem] * 5,
        out_specs=(vmem, vmem),
        compiler_params=pltpu.CompilerParams(vmem_limit_bytes=56 * 1024 * 1024),
        name="weigh",
    )(
        me, decay_rate, events, event_weight.reshape(z.chunks, LANES), route.reshape(z.chunks, LANES),
        bucket.reshape(z.chunks, LANES), segment.reshape(slots // LANES, LANES),
    )

    def flat(blocks):
        return [part[None] if part.ndim == 2 else part for parts in blocks for part in parts]

    def sums(blocks, before=()):
        blocks, form, count = flat(blocks), tuple(map(len, blocks)), len(blocks)
        lines = max(8, 2 * count)
        whole = shape((slots, width), F32)
        kept = (shape((lines * LANES, LANES), BF16), shape((lines, LANES), F32))
        factors = shape((z.shifts * rows, width), F32)
        tops = shape((z.shifts * rows, width), I16 if z.narrow else F32)
        return pl.pallas_call(
            functools.partial(early_kernel, z, form, len(before)),
            out_shape=(whole,) + kept if before else (whole, whole) + kept + (tops, factors),
            in_specs=[vmem] * (1 + len(blocks) + len(before)),
            out_specs=(vmem,) * (3 if before else 6),
            scratch_shapes=[
                pltpu.VMEM((2, max(1, count), 8, LANES), F32),
                pltpu.VMEM((max(1, count), 2 * z.chunks, LANES), F32),
            ],
            compiler_params=grant,
            cost_estimate=pl.CostEstimate(flops=COST * count, bytes_accessed=0, transcendentals=0),
            name="more_sums" if before else "first_sums",
        )(own, *blocks, *before)

    if (key_count, shard_count) == (4, 2):
        tie = lax.optimization_barrier
        far = swap(block, "key", 2)
        side = swap(block, "shard", 1)
        near = swap(block, "key", 1)
        side_near = swap(side, "key", 1)
        total, scale, *tail, tops, factors = sums([(block,)])
        far, total = tie((far, total))
        last = swap(far, "key", 1)
        side_far = swap(far, "shard", 1)
        total, *tail2 = sums([(side,), (near,)], (total,))
        last, total = tie((last, total))
        side_last = swap(last, "shard", 1)
        second = [(far,), (last,), (side_far,)]
        late = [(side_near,), (side_last,)]
        total, *tail3 = sums(second, (total,))
        early, earlier, tails = [(block,), (side,), (near,)] + second, (1, 2, 3), tail + tail2 + tail3
    else:
        blocks = spread(spread([block], "key"), "shard")
        total, scale, _, _, tops, factors = sums([])
        early, earlier, tails = [], (), []
        late = [(jnp.concatenate(blocks, axis=0).reshape(owners, block_rows, width),)]
    late_lines = 2 * (len(late) if earlier else z.groups)
    late_count = len(late) if earlier else owners
    form = tuple(map(len, early + late))
    return pl.pallas_call(
        functools.partial(late_kernel, z, earlier, form, len(late)),
        out_shape=(shape((slots, width), BF16), shape((rows, width), BF16)),
        in_specs=[vmem] * (5 + len(tails) + sum(form)),
        out_specs=(pl.BlockSpec(memory_space=pl.ANY),) * 2,
        scratch_shapes=[
            pltpu.VMEM((late_lines * LANES, LANES), BF16),
            pltpu.VMEM((late_lines, LANES), F32),
            pltpu.VMEM((2, late_count, 8, LANES), F32),
            pltpu.VMEM((late_count, 2 * z.chunks, LANES), F32),
            pltpu.VMEM((slots, width), BF16),
            pltpu.VMEM((rows, width), BF16),
            pltpu.SemaphoreType.DMA((1 + slots // z.window,)),
        ],
        compiler_params=grant,
        name="table_and_rows",
    )(own, total, scale, tops, factors, *tails, *flat(early + late))


def solution(mesh):
    placed = (
        P(("groups", "key", "shard"), "lane"),
        P(("groups", "key", "shard")),
        P(("groups", "key", "shard"), None),
        P(("groups", "key", "shard")),
        P(("groups", "key", "shard")),
        P("lane"),
    )
    return jax.shard_map(
        on_device,
        mesh=mesh,
        in_specs=placed,
        out_specs=(P(("groups", "key", "shard"), "lane"), P(("groups", "key", "shard"), "lane")),
        check_vma=False,
    )
```

```python
import functools
import jax
import jax.numpy as jnp
from jax import lax
from jax.experimental import pallas as pl
from jax.experimental.pallas import tpu as pltpu
from jax.sharding import PartitionSpec as P

LANES = 128
LOW = 7
MASK = 127
F32 = jnp.float32
BF16 = jnp.bfloat16
I32 = jnp.int32
I16 = jnp.int16
FAR = 1e9
TOP = 32768
NT = (((1,), (1,)), ((), ()))
BLOCK = 512
LATE_BLOCK = 256
TALL_FIRST = 512
TALL = 1024
COST = 1


class Sizes:
    def __init__(self, owners, rows, slots):
        self.owners, self.rows, self.slots = owners, rows, slots
        self.window = slots // 4
        self.chunks = rows // LANES
        self.user_rows = -(-8 * owners // LANES)
        self.code_rows = -(-(3 * self.chunks + 2 * self.user_rows) // 16) * 16
        self.span = min(owners, 8)
        self.shifts = 1 if owners <= self.span else 2
        self.capacity = 2 * rows // owners
        self.per_group = LANES // self.capacity
        self.groups = owners // self.per_group
        self.narrow = owners * slots <= 32768


def iota(shape, axis):
    return lax.broadcasted_iota(I32, shape, axis)


def ones_where(condition):
    return jnp.where(condition, F32(1), F32(0)).astype(BF16)


def dot(a, b):
    return jnp.dot(a, b, preferred_element_type=F32)


def loop(count, body, carry):
    if count <= 8:
        for i in range(count):
            carry = body(i, carry)
        return carry
    return lax.fori_loop(0, count, body, carry)


def send_kernel(z, me_ref, rate_ref, events_ref, weight_ref, route_ref, bucket_ref, segment_ref, block_ref, own_ref):
    groups = rate_ref.shape[0]
    lane = iota((1, LANES), 1)
    rate = jnp.full((1, LANES), rate_ref[0], F32)
    for g in range(1, groups):
        rate = jnp.where(lane >= g * (LANES // groups), rate_ref[g], rate)
    route = route_ref[...]
    bucket = bucket_ref[...]
    place = (route * z.slots + bucket).astype(F32)
    first = ((route >> (z.span.bit_length() - 1)) * (z.span * z.slots)).astype(F32)
    me = jnp.full((8 - 1, LANES), me_ref[0], I32).astype(F32)
    own_ref[0:16, :] = jnp.concatenate([place, first, rate, me], axis=0)
    spot = place - first - F32(z.span * z.slots // 2)
    columns = jnp.concatenate([weight_ref[...], spot], axis=0).T
    for r in range(z.chunks):
        part = slice(r * LANES, (r + 1) * LANES)
        weighted = (columns[:, r : r + 1] * events_ref[part, :].astype(F32)).astype(BF16)
        grown = weighted.astype(F32) * jnp.exp(columns[:, z.chunks + r : z.chunks + r + 1] * rate)
        block_ref[part, :] = grown.astype(BF16)
    ones = jnp.ones((8, LANES), BF16)
    high, low = [], []
    users = min(LANES, 8 * z.owners)
    for u in range(z.user_rows):
        user = iota((users, LANES), 0) + u * LANES
        below = jnp.zeros((users, LANES), F32)
        for r in range(z.slots // LANES):
            below += jnp.where(segment_ref[r : r + 1, :] < user, F32(1), F32(0))
        count = lax.dot_general(ones, below.astype(BF16), NT, preferred_element_type=F32)[0:1]
        if users < LANES:
            count = jnp.concatenate([count, jnp.full((1, LANES - users), z.slots, F32)], axis=1)
        own_ref[16 + u : 17 + u, :] = count
        count = count.astype(I32)
        high.append(count >> LOW)
        low.append(count & MASK)
    spare = z.code_rows - 3 * z.chunks - 2 * z.user_rows
    pad = [jnp.zeros((spare, LANES), I32)] if spare else []
    codes = jnp.concatenate([route, bucket >> LOW, bucket & MASK] + high + low + pad, axis=0)
    block_ref[z.rows : z.rows + z.code_rows, :] = codes.astype(F32).astype(BF16)


class Pieces:
    def __init__(self, z, form, refs):
        self.z, refs = z, list(refs)
        self.parts = [[refs.pop(0) for _ in range(n)] for n in form]
        self.count = len(form) if len(form) != 1 else self.parts[0][0].shape[0]
        self.per_group = 1 if len(form) != 1 else z.per_group
        self.groups = self.count // self.per_group

    def block(self, s):
        return (self.parts[s], 0) if len(self.parts) != 1 else (self.parts[0], s)

    def codes(self, s):
        parts, i = self.block(s)
        first = parts[0].shape[1] - self.z.code_rows
        return parts[0][i, first : first + self.z.code_rows, :].astype(F32)

    def rows(self, s):
        parts, i = self.block(s)
        first = parts[0][i, 0 : parts[0].shape[1] - self.z.code_rows, :]
        return jnp.concatenate([first] + [part[i] for part in parts[1:]], axis=0)

    def place(self, s):
        n, tile = self.z.chunks, self.codes(s)
        return tile[0:n] * F32(self.z.slots) + F32(LANES) * tile[n : 2 * n] + tile[2 * n : 3 * n]

    def below(self, s, u):
        tile, at = self.codes(s), 3 * self.z.chunks + u
        return F32(LANES) * tile[at : at + 1] + tile[at + self.z.user_rows : at + self.z.user_rows + 1]


class Runs:
    def __init__(self, z, starts):
        self.z, self.starts = z, starts
        users = min(LANES, 8 * z.owners)
        self.columns = [jnp.broadcast_to(row, (8, LANES)).T[:users, 0:1] for row in starts]
        self.steps = []
        for u, row in enumerate(starts):
            before = pltpu.roll(row, 1, 1)
            first = starts[u - 1][:, LANES - 1 : LANES] if u else jnp.zeros((1, 1), F32)
            step = (row - jnp.where(iota((1, LANES), 1) == 0, first, before)).astype(I32)
            pair = [jnp.broadcast_to(part, (LANES, LANES)) for part in (step >> LOW, step & MASK)]
            self.steps.append(jnp.concatenate(pair, axis=0).astype(F32).astype(BF16))

    def start(self, position):
        total = jnp.zeros((position.shape[0], 2 * LANES), F32)
        for row, step in zip(self.starts, self.steps):
            total += lax.dot_general(ones_where(row <= position), step, NT, preferred_element_type=F32)
        return F32(LANES) * total[:, :LANES] + total[:, LANES:]

    def start_row(self, row):
        start = jnp.zeros((1, LANES), F32)
        for column in self.columns:
            start = jnp.maximum(start, jnp.max(jnp.where(column <= row, column, F32(0)), axis=0, keepdims=True))
        return start

    def until(self, row):
        after = jnp.full((1, LANES), FAR, F32)
        for column in self.columns:
            later = jnp.where(column > row, column, F32(FAR))
            after = jnp.minimum(after, jnp.min(later, axis=0, keepdims=True))
        return jnp.minimum(row + F32(self.z.window), after - F32(1))


def root(z, distance):
    return lax.rsqrt(jnp.minimum(distance, F32(z.window)) + F32(1))


def pack(z, pieces, base, marks_ref, codes_ref, rows_ref, from_ref):
    if not pieces.count:
        return
    spare = jnp.zeros((8 - z.chunks, LANES), F32)

    def mark(s, carry):
        local = pieces.place(s) - base
        near = local.astype(I32)
        codes_ref[s] = jnp.concatenate([near >> LOW, near & MASK], axis=0).astype(F32)
        own = (local >= 0) & (local < F32(z.slots))
        tail = (local >= F32(-z.window)) & (local < 0)
        marks_ref[0, s] = jnp.concatenate([jnp.where(own, F32(1), F32(0)), spare], axis=0)
        marks_ref[1, s] = jnp.concatenate([jnp.where(tail, F32(1), F32(0)), spare], axis=0)
        return carry

    loop(pieces.count, mark, 0)
    upper = ones_where(iota((LANES, LANES), 0) < iota((LANES, LANES), 1))
    full = jnp.ones((LANES, LANES), BF16)
    lines = pieces.count * 8
    at, by = iota((lines, lines), 0), iota((lines, lines), 1)
    earlier = ones_where(((at >> 3) == (by >> 3)) & (by < at))
    source = iota((lines, LANES), 0) >> 3
    offset = ((source & (pieces.per_group - 1)) * z.capacity).astype(F32)
    for kind in range(2):
        marked = marks_ref[kind].reshape(lines, LANES)
        mark = marked.astype(BF16)
        rank = dot(mark, upper) + dot(earlier, dot(mark, full).astype(BF16)) + offset
        marks_ref[kind] = jnp.where(marked > 0, rank, F32(-1)).reshape(pieces.count, 8, LANES)

    spots = iota((LANES, LANES), 0).astype(F32)
    code_line = iota((2 * z.chunks, LANES), 0) & (z.chunks - 1)
    for kind in range(2):
        for g in range(pieces.groups):

            def add(i, carry):
                values, places = carry
                s = g * pieces.per_group + i
                ranks = marks_ref[kind, s]
                codes = codes_ref[s]
                hot = jnp.concatenate([ones_where(spots == ranks[r : r + 1]) for r in range(z.chunks)], axis=1)
                wide = [jnp.where(code_line == r, codes, F32(0)).astype(BF16) for r in range(z.chunks)]
                values += dot(hot, pieces.rows(s))
                places += lax.dot_general(jnp.concatenate(wide, axis=1), hot, NT, preferred_element_type=F32)
                return values, places

            zero = (jnp.zeros((LANES, LANES), F32), jnp.zeros((2 * z.chunks, LANES), F32))
            values, places = loop(pieces.per_group, add, zero)
            line = kind * pieces.groups + g
            rows_ref[line * LANES : (line + 1) * LANES, :] = values.astype(BF16)
            high = jnp.sum(places[: z.chunks], axis=0, keepdims=True)
            low = jnp.sum(places[z.chunks :], axis=0, keepdims=True)
            from_ref[line : line + 1, :] = F32(LANES) * high + low


def tiles(values):
    return values.reshape(values.shape[0] // 16, 16, LANES)


def tile_of(row):
    return jnp.broadcast_to(row.astype(I32), (16, LANES)).astype(I16)


def held(position, bounds):
    one, nothing, count = BF16(1), BF16(0), position.shape[0]
    position = tiles(position)
    masks = [jnp.where(position - first[None] <= length[None], one, nothing) for first, length in bounds]
    return jnp.concatenate([mask.reshape(count, LANES) for mask in masks], axis=1)


def within(top, span, rows):
    if top.dtype == I16:
        one, nothing, count = BF16(1), BF16(0), top.shape[0]
        top, span = tiles(top), tiles(span)
        masks = [jnp.where(top - tile_of(row)[None] <= span, one, nothing) for row in rows]
        return jnp.concatenate([mask.reshape(count, LANES) for mask in masks], axis=1)
    return jnp.concatenate([ones_where((top - row >= 0) & (top - row <= span)) for row in rows], axis=1)


def wide_columns(*sets):
    count = sets[0].shape[0]
    columns = jnp.concatenate(sets, axis=0).T
    wide = lambda at: jnp.broadcast_to(columns[:, at : at + 1], (LANES, LANES))
    return [jnp.concatenate([wide(i * count + r) for r in range(count)], axis=0) for i in range(len(sets))]


def anchors(z, me):
    middle = F32(z.span * z.slots // 2)
    span_of = lambda owner: (owner.astype(I32) >> (z.span.bit_length() - 1)).astype(F32) * F32(z.span)
    own = (me - span_of(me)) * F32(z.slots) - middle
    tail = (me - span_of(me - F32(1))) * F32(z.slots) - middle
    return own, tail


def short(row):
    return row.astype(I32).astype(I16)


def early_kernel(z, form, before, *refs):
    count = sum(form)
    own_ref, pieces = refs[0], Pieces(z, form, refs[1 : 1 + count])
    refs = refs[1 + count :]
    if before:
        before_ref, sums_ref, rows_ref, from_ref, marks_ref, codes_ref = refs
    else:
        sums_ref, scale_ref, rows_ref, from_ref, high_ref, factor_ref, marks_ref, codes_ref = refs
    rate, me = own_ref[8:9, :], own_ref[9:10, :]
    runs = Runs(z, [own_ref[16 + u : 17 + u, :] for u in range(z.user_rows)])
    pack(z, pieces, me * F32(z.slots), marks_ref, codes_ref, rows_ref, from_ref)
    own_anchor, _ = anchors(z, me)
    inner = iota((BLOCK, LANES), 0)
    fall = jnp.exp(-rate * inner.astype(F32))
    bounds = []
    for g in range(pieces.groups if pieces.count else 0):
        begin = from_ref[g : g + 1, :]
        bounds.append((tile_of(begin), tile_of(runs.until(begin) - begin - F32(TOP))))
    for b in range(z.slots // BLOCK):
        part = slice(b * BLOCK, (b + 1) * BLOCK)
        if bounds:
            mask = held((inner + (b * BLOCK - TOP)).astype(I16), bounds)
            value = dot(mask, rows_ref[0 : len(bounds) * LANES, :])
        else:
            value = jnp.zeros((BLOCK, LANES), F32)
        sums_ref[part, :] = value + before_ref[part, :] if before else value
        if not before:
            first = F32(b * BLOCK)
            position = inner.astype(F32) + first
            start = runs.start(position)
            if b * BLOCK < z.window:
                scale_ref[part, :] = start
            else:
                scale_ref[part, :] = fall * jnp.exp(-rate * (first + own_anchor)) * root(z, position - start)
    if not before:
        position, span_start = wide_columns(own_ref[0 : z.chunks, :], own_ref[z.chunks : 2 * z.chunks, :])
        for shift in range(z.shifts):
            part = slice(shift * z.rows, (shift + 1) * z.rows)
            center = span_start + F32(z.span * z.slots // 2 - shift * z.span * z.slots)
            factor_ref[part, :] = jnp.exp(-rate * (position - center))
            top = position if shift == 0 else span_start - F32(1)
            high_ref[part, :] = short(top - F32(TOP)) if z.narrow else top


def late_kernel(z, earlier, form, late, *refs):
    own_ref, sums_ref, scale_ref, high_ref, factor_ref = refs[:5]
    tails = [refs[5 + 2 * i : 7 + 2 * i] for i in range(len(earlier))]
    refs = refs[5 + 2 * len(earlier) :]
    count = sum(form)
    table_out, feature_out, rows_ref, from_ref, marks_ref, codes_ref, table_ref, feature_ref, sems = refs[count:]
    pieces, last = Pieces(z, form, refs[:count]), Pieces(z, form[-late:], refs[count - sum(form[-late:]) : count])
    rate, me = own_ref[8:9, :], own_ref[9:10, :]
    base = me * F32(z.slots)
    starts = []
    for u in range(z.user_rows):
        add = lambda s, total: total + pieces.below(s, u)
        starts.append(loop(pieces.count, add, jnp.zeros((1, LANES), F32)))
    runs = Runs(z, starts)
    copies = []

    def send(ref, out, part):
        copies.append(pltpu.make_async_copy(ref.at[part, :], out.at[part, :], sems.at[len(copies)]))
        copies[-1].start()

    place = own_ref[0 : z.chunks, :]
    start = jnp.concatenate([runs.start_row(place[r : r + 1]) for r in range(z.chunks)], axis=0)
    distance = place - start
    reach = jnp.minimum(distance, F32(z.window))
    scale, reach = wide_columns(root(z, distance), reach - F32(TOP) if z.narrow else reach)
    position, span_start = (None, None) if z.narrow else wide_columns(place, own_ref[z.chunks : 2 * z.chunks, :])
    total = jnp.zeros((z.rows, LANES), F32)
    for shift in range(z.shifts):
        part = slice(shift * z.rows, (shift + 1) * z.rows)
        top = high_ref[part, :]
        if z.narrow:
            span = short(reach)
        else:
            low = position - reach
            span = top - (jnp.maximum(low, span_start) if shift == 0 else low)

        def add(s, value):
            rows = pieces.place(s)
            mask = within(top, span, [rows[r : r + 1] for r in range(z.chunks)])
            return value + dot(mask, pieces.rows(s))

        total += loop(pieces.count, add, jnp.zeros((z.rows, LANES), F32)) * factor_ref[part, :]
    feature_ref[...] = (total * scale).astype(BF16)
    send(feature_ref, feature_out, slice(0, z.rows))

    pack(z, last, base, marks_ref, codes_ref, rows_ref, from_ref)
    own_anchor, tail_anchor = anchors(z, me)
    inner = iota((LATE_BLOCK, LANES), 0)
    fall = jnp.exp(-rate * inner.astype(F32))
    first_start = jnp.max(runs.start_row(base), axis=1, keepdims=True) - base
    bounds = []
    listed = [(from_ref, 0, 2 * last.groups)] + [(ref, count, count) for (_, ref), count in zip(tails, earlier)]
    for ref, first, lines in listed:
        for g in range(first, first + lines):
            begin = ref[g : g + 1, :]
            bounds.append((tile_of(begin), tile_of(runs.until(begin + base) - (begin + base) - F32(TOP))))
    n = last.groups
    own_rows = rows_ref[0 : n * LANES, :]
    tail_rows = [rows_ref[n * LANES : 2 * n * LANES, :]]
    tail_rows += [ref[count * LANES : 2 * count * LANES, :] for (ref, _), count in zip(tails, earlier)]
    tail_rows = jnp.concatenate(tail_rows, axis=0)
    masks = lambda first, tall, bounds: held((iota((tall, LANES), 0) + (first - TOP)).astype(I16), bounds)
    first = 0
    while first < z.slots:
        inside = first < z.window
        tall = min(TALL_FIRST if inside else TALL, z.window)
        if inside and z.shifts == 1:
            sums = dot(masks(first, tall, bounds), jnp.concatenate([own_rows, tail_rows], axis=0))
        else:
            sums = dot(masks(first, tall, bounds[:n]), own_rows)
        if inside and z.shifts > 1:
            tail_sums = dot(masks(first, tall, bounds[n:]), tail_rows)
        for k in range(0, tall, LATE_BLOCK):
            at = first + k
            part = slice(at, at + LATE_BLOCK)
            value = sums_ref[part, :] + sums[k : k + LATE_BLOCK]
            if inside:
                value *= jnp.exp(-rate * (F32(at) + own_anchor))
                if z.shifts > 1:
                    value += tail_sums[k : k + LATE_BLOCK] * jnp.exp(-rate * (F32(at) + tail_anchor))
                start = scale_ref[part, :]
                start = jnp.where(start > 0, start, first_start)
                value = value * fall * root(z, inner.astype(F32) + F32(at) - start)
            else:
                value = value * scale_ref[part, :]
            table_ref[part, :] = value.astype(BF16)
        first += tall
        if first % z.window == 0:
            send(table_ref, table_out, slice(first - z.window, first))
    for copy in copies:
        copy.wait()


def swap(block, axis, distance):
    return lax.ppermute(block, axis, [(i, i ^ distance) for i in range(lax.axis_size(axis))])


def spread(blocks, axis):
    distance = lax.axis_size(axis) // 2
    while distance:
        blocks = blocks + [swap(block, axis, distance) for block in blocks]
        distance //= 2
    return blocks


def on_device(events, event_weight, route, bucket, segment, decay_rate):
    rows, width = events.shape
    key_count, shard_count = lax.axis_size("key"), lax.axis_size("shard")
    owners = key_count * shard_count
    slots = segment.shape[0]
    z = Sizes(owners, rows, slots)
    block_rows = rows + z.code_rows
    smem = pl.BlockSpec(memory_space=pltpu.SMEM)
    vmem = pl.BlockSpec(memory_space=pltpu.VMEM)
    shape = jax.ShapeDtypeStruct
    grant = pltpu.CompilerParams(vmem_limit_bytes=(16 if owners <= 8 else 48) * 1024 * 1024)
    me = (lax.axis_index("key") * shard_count + lax.axis_index("shard")).astype(I32).reshape(1)
    block, own = pl.pallas_call(
        functools.partial(send_kernel, z),
        out_shape=(
            shape((block_rows, width), BF16),
            shape((16 + z.user_rows + 7, LANES), F32),
        ),
        in_specs=[smem, smem] + [vmem] * 5,
        out_specs=(vmem, vmem),
        compiler_params=pltpu.CompilerParams(vmem_limit_bytes=56 * 1024 * 1024),
        name="weigh",
    )(
        me, decay_rate, events, event_weight.reshape(z.chunks, LANES), route.reshape(z.chunks, LANES),
        bucket.reshape(z.chunks, LANES), segment.reshape(slots // LANES, LANES),
    )

    def flat(blocks):
        return [part[None] if part.ndim == 2 else part for parts in blocks for part in parts]

    def sums(blocks, before=()):
        blocks, form, count = flat(blocks), tuple(map(len, blocks)), len(blocks)
        lines = max(8, 2 * count)
        whole = shape((slots, width), F32)
        kept = (shape((lines * LANES, LANES), BF16), shape((lines, LANES), F32))
        factors = shape((z.shifts * rows, width), F32)
        tops = shape((z.shifts * rows, width), I16 if z.narrow else F32)
        return pl.pallas_call(
            functools.partial(early_kernel, z, form, len(before)),
            out_shape=(whole,) + kept if before else (whole, whole) + kept + (tops, factors),
            in_specs=[vmem] * (1 + len(blocks) + len(before)),
            out_specs=(vmem,) * (3 if before else 6),
            scratch_shapes=[
                pltpu.VMEM((2, max(1, count), 8, LANES), F32),
                pltpu.VMEM((max(1, count), 2 * z.chunks, LANES), F32),
            ],
            compiler_params=grant,
            cost_estimate=pl.CostEstimate(flops=COST * count, bytes_accessed=0, transcendentals=0),
            name="more_sums" if before else "first_sums",
        )(own, *blocks, *before)

    if (key_count, shard_count) == (4, 2):
        tie = lax.optimization_barrier
        far = swap(block, "key", 2)
        side = swap(block, "shard", 1)
        near = swap(block, "key", 1)
        side_near = swap(side, "key", 1)
        total, scale, *tail, tops, factors = sums([(block,)])
        far, total = tie((far, total))
        last = swap(far, "key", 1)
        side_far = swap(far, "shard", 1)
        total, *tail2 = sums([(side,), (near,)], (total,))
        last, total = tie((last, total))
        side_last = swap(last, "shard", 1)
        second = [(far,), (last,), (side_far,)]
        late = [(side_near,), (side_last,)]
        total, *tail3 = sums(second, (total,))
        early, earlier, tails = [(block,), (side,), (near,)] + second, (1, 2, 3), tail + tail2 + tail3
    else:
        blocks = spread(spread([block], "key"), "shard")
        total, scale, _, _, tops, factors = sums([])
        early, earlier, tails = [], (), []
        late = [(jnp.concatenate(blocks, axis=0).reshape(owners, block_rows, width),)]
    late_lines = 2 * (len(late) if earlier else z.groups)
    late_count = len(late) if earlier else owners
    form = tuple(map(len, early + late))
    return pl.pallas_call(
        functools.partial(late_kernel, z, earlier, form, len(late)),
        out_shape=(shape((slots, width), BF16), shape((rows, width), BF16)),
        in_specs=[vmem] * (5 + len(tails) + sum(form)),
        out_specs=(pl.BlockSpec(memory_space=pl.ANY),) * 2,
        scratch_shapes=[
            pltpu.VMEM((late_lines * LANES, LANES), BF16),
            pltpu.VMEM((late_lines, LANES), F32),
            pltpu.VMEM((2, late_count, 8, LANES), F32),
            pltpu.VMEM((late_count, 2 * z.chunks, LANES), F32),
            pltpu.VMEM((slots, width), BF16),
            pltpu.VMEM((rows, width), BF16),
            pltpu.SemaphoreType.DMA((1 + slots // z.window,)),
        ],
        compiler_params=grant,
        name="table_and_rows",
    )(own, total, scale, tops, factors, *tails, *flat(early + late))


def solution(mesh):
    placed = (
        P(("groups", "key", "shard"), "lane"),
        P(("groups", "key", "shard")),
        P(("groups", "key", "shard"), None),
        P(("groups", "key", "shard")),
        P(("groups", "key", "shard")),
        P("lane"),
    )
    return jax.shard_map(
        on_device,
        mesh=mesh,
        in_specs=placed,
        out_specs=(P(("groups", "key", "shard"), "lane"), P(("groups", "key", "shard"), "lane")),
        check_vma=False,
    )
```

```python
import functools
import jax
import jax.numpy as jnp
from jax import lax
from jax.experimental import pallas as pl
from jax.experimental.pallas import tpu as pltpu
from jax.sharding import PartitionSpec as P

LANES = 128
LOW = 7
MASK = 127
F32 = jnp.float32
BF16 = jnp.bfloat16
I32 = jnp.int32
I16 = jnp.int16
FAR = 1e9
TOP = 32768
NT = (((1,), (1,)), ((), ()))
BLOCK = 512
LATE_BLOCK = 256
COST = 1


class Sizes:
    def __init__(self, owners, rows, slots):
        self.owners, self.rows, self.slots = owners, rows, slots
        self.window = slots // 4
        self.chunks = rows // LANES
        self.user_rows = -(-8 * owners // LANES)
        self.code_rows = -(-(3 * self.chunks + 2 * self.user_rows) // 16) * 16
        self.span = min(owners, 8)
        self.shifts = 1 if owners <= self.span else 2
        self.capacity = 2 * rows // owners
        self.per_group = LANES // self.capacity
        self.groups = owners // self.per_group
        self.narrow = owners * slots <= 32768


def iota(shape, axis):
    return lax.broadcasted_iota(I32, shape, axis)


def ones_where(condition):
    return jnp.where(condition, F32(1), F32(0)).astype(BF16)


def dot(a, b):
    return jnp.dot(a, b, preferred_element_type=F32)


def loop(count, body, carry):
    if count <= 8:
        for i in range(count):
            carry = body(i, carry)
        return carry
    return lax.fori_loop(0, count, body, carry)


def send_kernel(z, me_ref, rate_ref, events_ref, weight_ref, route_ref, bucket_ref, segment_ref, block_ref, own_ref):
    groups = rate_ref.shape[0]
    lane = iota((1, LANES), 1)
    rate = jnp.full((1, LANES), rate_ref[0], F32)
    for g in range(1, groups):
        rate = jnp.where(lane >= g * (LANES // groups), rate_ref[g], rate)
    route = route_ref[...]
    bucket = bucket_ref[...]
    place = (route * z.slots + bucket).astype(F32)
    first = ((route >> (z.span.bit_length() - 1)) * (z.span * z.slots)).astype(F32)
    me = jnp.full((8 - 1, LANES), me_ref[0], I32).astype(F32)
    own_ref[0:16, :] = jnp.concatenate([place, first, rate, me], axis=0)
    spot = place - first - F32(z.span * z.slots // 2)
    columns = jnp.concatenate([weight_ref[...], spot], axis=0).T
    for r in range(z.chunks):
        part = slice(r * LANES, (r + 1) * LANES)
        weighted = (columns[:, r : r + 1] * events_ref[part, :].astype(F32)).astype(BF16)
        grown = weighted.astype(F32) * jnp.exp(columns[:, z.chunks + r : z.chunks + r + 1] * rate)
        block_ref[part, :] = grown.astype(BF16)
    ones = jnp.ones((8, LANES), BF16)
    high, low = [], []
    users = min(LANES, 8 * z.owners)
    for u in range(z.user_rows):
        user = iota((users, LANES), 0) + u * LANES
        below = jnp.zeros((users, LANES), F32)
        for r in range(z.slots // LANES):
            below += jnp.where(segment_ref[r : r + 1, :] < user, F32(1), F32(0))
        count = lax.dot_general(ones, below.astype(BF16), NT, preferred_element_type=F32)[0:1]
        if users < LANES:
            count = jnp.concatenate([count, jnp.full((1, LANES - users), z.slots, F32)], axis=1)
        own_ref[16 + u : 17 + u, :] = count
        count = count.astype(I32)
        high.append(count >> LOW)
        low.append(count & MASK)
    spare = z.code_rows - 3 * z.chunks - 2 * z.user_rows
    pad = [jnp.zeros((spare, LANES), I32)] if spare else []
    codes = jnp.concatenate([route, bucket >> LOW, bucket & MASK] + high + low + pad, axis=0)
    block_ref[z.rows : z.rows + z.code_rows, :] = codes.astype(F32).astype(BF16)


class Pieces:
    def __init__(self, z, form, refs):
        self.z, refs = z, list(refs)
        self.parts = [[refs.pop(0) for _ in range(n)] for n in form]
        self.count = len(form) if len(form) != 1 else self.parts[0][0].shape[0]
        self.per_group = 1 if len(form) != 1 else z.per_group
        self.groups = self.count // self.per_group

    def block(self, s):
        return (self.parts[s], 0) if len(self.parts) != 1 else (self.parts[0], s)

    def codes(self, s):
        parts, i = self.block(s)
        first = parts[0].shape[1] - self.z.code_rows
        return parts[0][i, first : first + self.z.code_rows, :].astype(F32)

    def rows(self, s):
        parts, i = self.block(s)
        first = parts[0][i, 0 : parts[0].shape[1] - self.z.code_rows, :]
        return jnp.concatenate([first] + [part[i] for part in parts[1:]], axis=0)

    def place(self, s):
        n, tile = self.z.chunks, self.codes(s)
        return tile[0:n] * F32(self.z.slots) + F32(LANES) * tile[n : 2 * n] + tile[2 * n : 3 * n]

    def below(self, s, u):
        tile, at = self.codes(s), 3 * self.z.chunks + u
        return F32(LANES) * tile[at : at + 1] + tile[at + self.z.user_rows : at + self.z.user_rows + 1]


class Runs:
    def __init__(self, z, starts):
        self.z, self.starts = z, starts
        users = min(LANES, 8 * z.owners)
        self.columns = [jnp.broadcast_to(row, (8, LANES)).T[:users, 0:1] for row in starts]
        self.steps = []
        for u, row in enumerate(starts):
            before = pltpu.roll(row, 1, 1)
            first = starts[u - 1][:, LANES - 1 : LANES] if u else jnp.zeros((1, 1), F32)
            step = (row - jnp.where(iota((1, LANES), 1) == 0, first, before)).astype(I32)
            pair = [jnp.broadcast_to(part, (LANES, LANES)) for part in (step >> LOW, step & MASK)]
            self.steps.append(jnp.concatenate(pair, axis=0).astype(F32).astype(BF16))

    def start(self, position):
        total = jnp.zeros((position.shape[0], 2 * LANES), F32)
        for row, step in zip(self.starts, self.steps):
            total += lax.dot_general(ones_where(row <= position), step, NT, preferred_element_type=F32)
        return F32(LANES) * total[:, :LANES] + total[:, LANES:]

    def start_row(self, row):
        start = jnp.zeros((1, LANES), F32)
        for column in self.columns:
            start = jnp.maximum(start, jnp.max(jnp.where(column <= row, column, F32(0)), axis=0, keepdims=True))
        return start

    def until(self, row):
        after = jnp.full((1, LANES), FAR, F32)
        for column in self.columns:
            later = jnp.where(column > row, column, F32(FAR))
            after = jnp.minimum(after, jnp.min(later, axis=0, keepdims=True))
        return jnp.minimum(row + F32(self.z.window), after - F32(1))


def root(z, distance):
    return lax.rsqrt(jnp.minimum(distance, F32(z.window)) + F32(1))


def pack(z, pieces, base, marks_ref, codes_ref, rows_ref, from_ref):
    if not pieces.count:
        return
    spare = jnp.zeros((8 - z.chunks, LANES), F32)

    def mark(s, carry):
        local = pieces.place(s) - base
        near = local.astype(I32)
        codes_ref[s] = jnp.concatenate([near >> LOW, near & MASK], axis=0).astype(F32)
        own = (local >= 0) & (local < F32(z.slots))
        tail = (local >= F32(-z.window)) & (local < 0)
        marks_ref[0, s] = jnp.concatenate([jnp.where(own, F32(1), F32(0)), spare], axis=0)
        marks_ref[1, s] = jnp.concatenate([jnp.where(tail, F32(1), F32(0)), spare], axis=0)
        return carry

    loop(pieces.count, mark, 0)
    upper = ones_where(iota((LANES, LANES), 0) < iota((LANES, LANES), 1))
    full = jnp.ones((LANES, LANES), BF16)
    lines = pieces.count * 8
    at, by = iota((lines, lines), 0), iota((lines, lines), 1)
    earlier = ones_where(((at >> 3) == (by >> 3)) & (by < at))
    source = iota((lines, LANES), 0) >> 3
    offset = ((source & (pieces.per_group - 1)) * z.capacity).astype(F32)
    for kind in range(2):
        marked = marks_ref[kind].reshape(lines, LANES)
        mark = marked.astype(BF16)
        rank = dot(mark, upper) + dot(earlier, dot(mark, full).astype(BF16)) + offset
        marks_ref[kind] = jnp.where(marked > 0, rank, F32(-1)).reshape(pieces.count, 8, LANES)

    spots = iota((LANES, LANES), 0).astype(F32)
    code_line = iota((2 * z.chunks, LANES), 0) & (z.chunks - 1)
    for kind in range(2):
        for g in range(pieces.groups):

            def add(i, carry):
                values, places = carry
                s = g * pieces.per_group + i
                ranks = marks_ref[kind, s]
                codes = codes_ref[s]
                hot = jnp.concatenate([ones_where(spots == ranks[r : r + 1]) for r in range(z.chunks)], axis=1)
                wide = [jnp.where(code_line == r, codes, F32(0)).astype(BF16) for r in range(z.chunks)]
                values += dot(hot, pieces.rows(s))
                places += lax.dot_general(jnp.concatenate(wide, axis=1), hot, NT, preferred_element_type=F32)
                return values, places

            zero = (jnp.zeros((LANES, LANES), F32), jnp.zeros((2 * z.chunks, LANES), F32))
            values, places = loop(pieces.per_group, add, zero)
            line = kind * pieces.groups + g
            rows_ref[line * LANES : (line + 1) * LANES, :] = values.astype(BF16)
            high = jnp.sum(places[: z.chunks], axis=0, keepdims=True)
            low = jnp.sum(places[z.chunks :], axis=0, keepdims=True)
            from_ref[line : line + 1, :] = F32(LANES) * high + low


def tiles(values):
    return values.reshape(values.shape[0] // 16, 16, LANES)


def tile_of(row):
    return jnp.broadcast_to(row.astype(I32), (16, LANES)).astype(I16)


def held(position, bounds):
    one, nothing, count = BF16(1), BF16(0), position.shape[0]
    position = tiles(position)
    masks = [jnp.where(position - first[None] <= length[None], one, nothing) for first, length in bounds]
    return jnp.concatenate([mask.reshape(count, LANES) for mask in masks], axis=1)


def within(top, span, rows):
    if top.dtype == I16:
        one, nothing, count = BF16(1), BF16(0), top.shape[0]
        top, span = tiles(top), tiles(span)
        masks = [jnp.where(top - tile_of(row)[None] <= span, one, nothing) for row in rows]
        return jnp.concatenate([mask.reshape(count, LANES) for mask in masks], axis=1)
    return jnp.concatenate([ones_where((top - row >= 0) & (top - row <= span)) for row in rows], axis=1)


def wide_columns(*sets):
    count = sets[0].shape[0]
    columns = jnp.concatenate(sets, axis=0).T
    wide = lambda at: jnp.broadcast_to(columns[:, at : at + 1], (LANES, LANES))
    return [jnp.concatenate([wide(i * count + r) for r in range(count)], axis=0) for i in range(len(sets))]


def anchors(z, me):
    middle = F32(z.span * z.slots // 2)
    span_of = lambda owner: (owner.astype(I32) >> (z.span.bit_length() - 1)).astype(F32) * F32(z.span)
    own = (me - span_of(me)) * F32(z.slots) - middle
    tail = (me - span_of(me - F32(1))) * F32(z.slots) - middle
    return own, tail


def short(row):
    return row.astype(I32).astype(I16)


def early_kernel(z, form, before, *refs):
    count = sum(form)
    own_ref, pieces = refs[0], Pieces(z, form, refs[1 : 1 + count])
    refs = refs[1 + count :]
    if before:
        before_ref, sums_ref, rows_ref, from_ref, marks_ref, codes_ref = refs
    else:
        sums_ref, scale_ref, rows_ref, from_ref, high_ref, factor_ref, marks_ref, codes_ref = refs
    rate, me = own_ref[8:9, :], own_ref[9:10, :]
    runs = Runs(z, [own_ref[16 + u : 17 + u, :] for u in range(z.user_rows)])
    pack(z, pieces, me * F32(z.slots), marks_ref, codes_ref, rows_ref, from_ref)
    own_anchor, _ = anchors(z, me)
    inner = iota((BLOCK, LANES), 0)
    fall = jnp.exp(-rate * inner.astype(F32))
    bounds = []
    for g in range(pieces.groups if pieces.count else 0):
        begin = from_ref[g : g + 1, :]
        bounds.append((tile_of(begin), tile_of(runs.until(begin) - begin - F32(TOP))))
    for b in range(z.slots // BLOCK):
        part = slice(b * BLOCK, (b + 1) * BLOCK)
        if bounds:
            mask = held((inner + (b * BLOCK - TOP)).astype(I16), bounds)
            value = dot(mask, rows_ref[0 : len(bounds) * LANES, :])
        else:
            value = jnp.zeros((BLOCK, LANES), F32)
        sums_ref[part, :] = value + before_ref[part, :] if before else value
        if not before:
            first = F32(b * BLOCK)
            position = inner.astype(F32) + first
            start = runs.start(position)
            if b * BLOCK < z.window:
                scale_ref[part, :] = start
            else:
                scale_ref[part, :] = fall * jnp.exp(-rate * (first + own_anchor)) * root(z, position - start)
    if not before:
        position, span_start = wide_columns(own_ref[0 : z.chunks, :], own_ref[z.chunks : 2 * z.chunks, :])
        for shift in range(z.shifts):
            part = slice(shift * z.rows, (shift + 1) * z.rows)
            center = span_start + F32(z.span * z.slots // 2 - shift * z.span * z.slots)
            factor_ref[part, :] = jnp.exp(-rate * (position - center))
            top = position if shift == 0 else span_start - F32(1)
            high_ref[part, :] = short(top - F32(TOP)) if z.narrow else top


def late_kernel(z, earlier, form, late, *refs):
    own_ref, sums_ref, scale_ref, high_ref, factor_ref = refs[:5]
    tails = [refs[5 + 2 * i : 7 + 2 * i] for i in range(len(earlier))]
    refs = refs[5 + 2 * len(earlier) :]
    count = sum(form)
    table_out, feature_out, rows_ref, from_ref, marks_ref, codes_ref, table_ref, feature_ref, sems = refs[count:]
    pieces, last = Pieces(z, form, refs[:count]), Pieces(z, form[-late:], refs[count - sum(form[-late:]) : count])
    rate, me = own_ref[8:9, :], own_ref[9:10, :]
    base = me * F32(z.slots)
    starts = []
    for u in range(z.user_rows):
        add = lambda s, total: total + pieces.below(s, u)
        starts.append(loop(pieces.count, add, jnp.zeros((1, LANES), F32)))
    runs = Runs(z, starts)
    copies = []

    def send(ref, out, part):
        copies.append(pltpu.make_async_copy(ref.at[part, :], out.at[part, :], sems.at[len(copies)]))
        copies[-1].start()

    place = own_ref[0 : z.chunks, :]
    start = jnp.concatenate([runs.start_row(place[r : r + 1]) for r in range(z.chunks)], axis=0)
    distance = place - start
    reach = jnp.minimum(distance, F32(z.window))
    scale, reach = wide_columns(root(z, distance), reach - F32(TOP) if z.narrow else reach)
    position, span_start = (None, None) if z.narrow else wide_columns(place, own_ref[z.chunks : 2 * z.chunks, :])
    total = jnp.zeros((z.rows, LANES), F32)
    for shift in range(z.shifts):
        part = slice(shift * z.rows, (shift + 1) * z.rows)
        top = high_ref[part, :]
        if z.narrow:
            span = short(reach)
        else:
            low = position - reach
            span = top - (jnp.maximum(low, span_start) if shift == 0 else low)

        def add(s, value):
            rows = pieces.place(s)
            mask = within(top, span, [rows[r : r + 1] for r in range(z.chunks)])
            return value + dot(mask, pieces.rows(s))

        if z.narrow:
            sources = range(pieces.count)
            lines = [row for s in sources for row in jnp.split(pieces.place(s), z.chunks, axis=0)]
            value = dot(within(top, span, lines), jnp.concatenate([pieces.rows(s) for s in sources], axis=0))
        else:
            value = loop(pieces.count, add, jnp.zeros((z.rows, LANES), F32))
        total += value * factor_ref[part, :]
    feature_ref[...] = (total * scale).astype(BF16)
    send(feature_ref, feature_out, slice(0, z.rows))

    pack(z, last, base, marks_ref, codes_ref, rows_ref, from_ref)
    own_anchor, tail_anchor = anchors(z, me)
    inner = iota((LATE_BLOCK, LANES), 0)
    fall = jnp.exp(-rate * inner.astype(F32))
    first_start = jnp.max(runs.start_row(base), axis=1, keepdims=True) - base
    bounds = []
    listed = [(from_ref, 0, 2 * last.groups)] + [(ref, count, count) for (_, ref), count in zip(tails, earlier)]
    for ref, first, lines in listed:
        for g in range(first, first + lines):
            begin = ref[g : g + 1, :]
            bounds.append((tile_of(begin), tile_of(runs.until(begin + base) - (begin + base) - F32(TOP))))
    n = last.groups
    own_rows = rows_ref[0 : n * LANES, :]
    tail_rows = [rows_ref[n * LANES : 2 * n * LANES, :]]
    tail_rows += [ref[count * LANES : 2 * count * LANES, :] for (ref, _), count in zip(tails, earlier)]
    tail_rows = jnp.concatenate(tail_rows, axis=0)
    for b in range(z.slots // LATE_BLOCK):
        part = slice(b * LATE_BLOCK, (b + 1) * LATE_BLOCK)
        position = (inner + (b * LATE_BLOCK - TOP)).astype(I16)
        first = F32(b * LATE_BLOCK)
        value = sums_ref[part, :]
        if b * LATE_BLOCK >= z.window:
            value = (value + dot(held(position, bounds[:n]), own_rows)) * scale_ref[part, :]
        else:
            own_fall = jnp.exp(-rate * (first + own_anchor))
            if z.shifts == 1:
                value += dot(held(position, bounds), jnp.concatenate([own_rows, tail_rows], axis=0))
                value *= own_fall
            else:
                value = (value + dot(held(position, bounds[:n]), own_rows)) * own_fall
                value += dot(held(position, bounds[n:]), tail_rows) * jnp.exp(-rate * (first + tail_anchor))
            start = scale_ref[part, :]
            start = jnp.where(start > 0, start, first_start)
            value = value * fall * root(z, inner.astype(F32) + first - start)
        table_ref[part, :] = value.astype(BF16)
        if (b + 1) * LATE_BLOCK % z.window == 0:
            send(table_ref, table_out, slice((b + 1) * LATE_BLOCK - z.window, (b + 1) * LATE_BLOCK))
    for copy in copies:
        copy.wait()


def swap(block, axis, distance):
    return lax.ppermute(block, axis, [(i, i ^ distance) for i in range(lax.axis_size(axis))])


def spread(blocks, axis):
    distance = lax.axis_size(axis) // 2
    while distance:
        blocks = blocks + [swap(block, axis, distance) for block in blocks]
        distance //= 2
    return blocks


def on_device(events, event_weight, route, bucket, segment, decay_rate):
    rows, width = events.shape
    key_count, shard_count = lax.axis_size("key"), lax.axis_size("shard")
    owners = key_count * shard_count
    slots = segment.shape[0]
    z = Sizes(owners, rows, slots)
    block_rows = rows + z.code_rows
    smem = pl.BlockSpec(memory_space=pltpu.SMEM)
    vmem = pl.BlockSpec(memory_space=pltpu.VMEM)
    shape = jax.ShapeDtypeStruct
    grant = pltpu.CompilerParams(vmem_limit_bytes=(16 if owners <= 8 else 48) * 1024 * 1024)
    me = (lax.axis_index("key") * shard_count + lax.axis_index("shard")).astype(I32).reshape(1)
    block, own = pl.pallas_call(
        functools.partial(send_kernel, z),
        out_shape=(
            shape((block_rows, width), BF16),
            shape((16 + z.user_rows + 7, LANES), F32),
        ),
        in_specs=[smem, smem] + [vmem] * 5,
        out_specs=(vmem, vmem),
        compiler_params=pltpu.CompilerParams(vmem_limit_bytes=56 * 1024 * 1024),
        name="weigh",
    )(
        me, decay_rate, events, event_weight.reshape(z.chunks, LANES), route.reshape(z.chunks, LANES),
        bucket.reshape(z.chunks, LANES), segment.reshape(slots // LANES, LANES),
    )

    def flat(blocks):
        return [part[None] if part.ndim == 2 else part for parts in blocks for part in parts]

    def sums(blocks, before=()):
        blocks, form, count = flat(blocks), tuple(map(len, blocks)), len(blocks)
        lines = max(8, 2 * count)
        whole = shape((slots, width), F32)
        kept = (shape((lines * LANES, LANES), BF16), shape((lines, LANES), F32))
        factors = shape((z.shifts * rows, width), F32)
        tops = shape((z.shifts * rows, width), I16 if z.narrow else F32)
        return pl.pallas_call(
            functools.partial(early_kernel, z, form, len(before)),
            out_shape=(whole,) + kept if before else (whole, whole) + kept + (tops, factors),
            in_specs=[vmem] * (1 + len(blocks) + len(before)),
            out_specs=(vmem,) * (3 if before else 6),
            scratch_shapes=[
                pltpu.VMEM((2, max(1, count), 8, LANES), F32),
                pltpu.VMEM((max(1, count), 2 * z.chunks, LANES), F32),
            ],
            compiler_params=grant,
            cost_estimate=pl.CostEstimate(flops=COST * count, bytes_accessed=0, transcendentals=0),
            name="more_sums" if before else "first_sums",
        )(own, *blocks, *before)

    if (key_count, shard_count) == (4, 2):
        tie = lax.optimization_barrier
        far = swap(block, "key", 2)
        side = swap(block, "shard", 1)
        near = swap(block, "key", 1)
        side_near = swap(side, "key", 1)
        total, scale, *tail, tops, factors = sums([(block,)])
        far, total = tie((far, total))
        last = swap(far, "key", 1)
        side_far = swap(far, "shard", 1)
        total, *tail2 = sums([(side,), (near,)], (total,))
        last, total = tie((last, total))
        side_last = swap(last, "shard", 1)
        second = [(far,), (last,), (side_far,)]
        late = [(side_near,), (side_last,)]
        total, *tail3 = sums(second, (total,))
        early, earlier, tails = [(block,), (side,), (near,)] + second, (1, 2, 3), tail + tail2 + tail3
    else:
        blocks = spread(spread([block], "key"), "shard")
        total, scale, _, _, tops, factors = sums([])
        early, earlier, tails = [], (), []
        late = [(jnp.concatenate(blocks, axis=0).reshape(owners, block_rows, width),)]
    late_lines = 2 * (len(late) if earlier else z.groups)
    late_count = len(late) if earlier else owners
    form = tuple(map(len, early + late))
    return pl.pallas_call(
        functools.partial(late_kernel, z, earlier, form, len(late)),
        out_shape=(shape((slots, width), BF16), shape((rows, width), BF16)),
        in_specs=[vmem] * (5 + len(tails) + sum(form)),
        out_specs=(pl.BlockSpec(memory_space=pl.ANY),) * 2,
        scratch_shapes=[
            pltpu.VMEM((late_lines * LANES, LANES), BF16),
            pltpu.VMEM((late_lines, LANES), F32),
            pltpu.VMEM((2, late_count, 8, LANES), F32),
            pltpu.VMEM((late_count, 2 * z.chunks, LANES), F32),
            pltpu.VMEM((slots, width), BF16),
            pltpu.VMEM((rows, width), BF16),
            pltpu.SemaphoreType.DMA((1 + slots // z.window,)),
        ],
        compiler_params=grant,
        name="table_and_rows",
    )(own, total, scale, tops, factors, *tails, *flat(early + late))


def solution(mesh):
    placed = (
        P(("groups", "key", "shard"), "lane"),
        P(("groups", "key", "shard")),
        P(("groups", "key", "shard"), None),
        P(("groups", "key", "shard")),
        P(("groups", "key", "shard")),
        P("lane"),
    )
    return jax.shard_map(
        on_device,
        mesh=mesh,
        in_specs=placed,
        out_specs=(P(("groups", "key", "shard"), "lane"), P(("groups", "key", "shard"), "lane")),
        check_vma=False,
    )
```

```python
import functools
import jax
import jax.numpy as jnp
from jax import lax
from jax.experimental import pallas as pl
from jax.experimental.pallas import tpu as pltpu
from jax.sharding import PartitionSpec as P

LANES = 128
LOW = 7
MASK = 127
F32 = jnp.float32
BF16 = jnp.bfloat16
I32 = jnp.int32
I16 = jnp.int16
FAR = 1e9
TOP = 32768
NT = (((1,), (1,)), ((), ()))
BLOCK = 512
LATE_BLOCK = 256
COST = 1


class Sizes:
    def __init__(self, owners, rows, slots):
        self.owners, self.rows, self.slots = owners, rows, slots
        self.window = slots // 4
        self.chunks = rows // LANES
        self.user_rows = -(-8 * owners // LANES)
        self.code_rows = -(-(3 * self.chunks + 2 * self.user_rows) // 16) * 16
        self.span = min(owners, 8)
        self.shifts = 1 if owners <= self.span else 2
        self.capacity = 2 * rows // owners
        self.per_group = LANES // self.capacity
        self.groups = owners // self.per_group
        self.narrow = owners * slots <= 32768


def iota(shape, axis):
    return lax.broadcasted_iota(I32, shape, axis)


def ones_where(condition):
    return jnp.where(condition, F32(1), F32(0)).astype(BF16)


def dot(a, b):
    return jnp.dot(a, b, preferred_element_type=F32)


def loop(count, body, carry):
    if count <= 8:
        for i in range(count):
            carry = body(i, carry)
        return carry
    return lax.fori_loop(0, count, body, carry)


def send_kernel(z, me_ref, rate_ref, events_ref, weight_ref, route_ref, bucket_ref, segment_ref, block_ref, own_ref):
    groups = rate_ref.shape[0]
    lane = iota((1, LANES), 1)
    rate = jnp.full((1, LANES), rate_ref[0], F32)
    for g in range(1, groups):
        rate = jnp.where(lane >= g * (LANES // groups), rate_ref[g], rate)
    route = route_ref[...]
    bucket = bucket_ref[...]
    place = (route * z.slots + bucket).astype(F32)
    first = ((route >> (z.span.bit_length() - 1)) * (z.span * z.slots)).astype(F32)
    me = jnp.full((8 - 1, LANES), me_ref[0], I32).astype(F32)
    own_ref[0:16, :] = jnp.concatenate([place, first, rate, me], axis=0)
    spot = place - first - F32(z.span * z.slots // 2)
    columns = jnp.concatenate([weight_ref[...], spot], axis=0).T
    for r in range(z.chunks):
        part = slice(r * LANES, (r + 1) * LANES)
        weighted = (columns[:, r : r + 1] * events_ref[part, :].astype(F32)).astype(BF16)
        grown = weighted.astype(F32) * jnp.exp(columns[:, z.chunks + r : z.chunks + r + 1] * rate)
        block_ref[part, :] = grown.astype(BF16)
    ones = jnp.ones((8, LANES), BF16)
    high, low = [], []
    users = min(LANES, 8 * z.owners)
    for u in range(z.user_rows):
        user = iota((users, LANES), 0) + u * LANES
        below = jnp.zeros((users, LANES), F32)
        for r in range(z.slots // LANES):
            below += jnp.where(segment_ref[r : r + 1, :] < user, F32(1), F32(0))
        count = lax.dot_general(ones, below.astype(BF16), NT, preferred_element_type=F32)[0:1]
        if users < LANES:
            count = jnp.concatenate([count, jnp.full((1, LANES - users), z.slots, F32)], axis=1)
        own_ref[16 + u : 17 + u, :] = count
        count = count.astype(I32)
        high.append(count >> LOW)
        low.append(count & MASK)
    spare = z.code_rows - 3 * z.chunks - 2 * z.user_rows
    pad = [jnp.zeros((spare, LANES), I32)] if spare else []
    codes = jnp.concatenate([route, bucket >> LOW, bucket & MASK] + high + low + pad, axis=0)
    block_ref[z.rows : z.rows + z.code_rows, :] = codes.astype(F32).astype(BF16)


class Pieces:
    def __init__(self, z, form, refs):
        self.z, refs = z, list(refs)
        self.parts = [[refs.pop(0) for _ in range(n)] for n in form]
        self.count = len(form) if len(form) != 1 else self.parts[0][0].shape[0]
        self.per_group = 1 if len(form) != 1 else z.per_group
        self.groups = self.count // self.per_group

    def block(self, s):
        return (self.parts[s], 0) if len(self.parts) != 1 else (self.parts[0], s)

    def codes(self, s):
        parts, i = self.block(s)
        first = parts[0].shape[1] - self.z.code_rows
        return parts[0][i, first : first + self.z.code_rows, :].astype(F32)

    def rows(self, s):
        parts, i = self.block(s)
        first = parts[0][i, 0 : parts[0].shape[1] - self.z.code_rows, :]
        return jnp.concatenate([first] + [part[i] for part in parts[1:]], axis=0)

    def place(self, s):
        n, tile = self.z.chunks, self.codes(s)
        return tile[0:n] * F32(self.z.slots) + F32(LANES) * tile[n : 2 * n] + tile[2 * n : 3 * n]

    def below(self, s, u):
        tile, at = self.codes(s), 3 * self.z.chunks + u
        return F32(LANES) * tile[at : at + 1] + tile[at + self.z.user_rows : at + self.z.user_rows + 1]


class Runs:
    def __init__(self, z, starts):
        self.z, self.starts = z, starts
        users = min(LANES, 8 * z.owners)
        self.columns = [jnp.broadcast_to(row, (8, LANES)).T[:users, 0:1] for row in starts]
        self.steps = []
        for u, row in enumerate(starts):
            before = pltpu.roll(row, 1, 1)
            first = starts[u - 1][:, LANES - 1 : LANES] if u else jnp.zeros((1, 1), F32)
            step = (row - jnp.where(iota((1, LANES), 1) == 0, first, before)).astype(I32)
            pair = [jnp.broadcast_to(part, (LANES, LANES)) for part in (step >> LOW, step & MASK)]
            self.steps.append(jnp.concatenate(pair, axis=0).astype(F32).astype(BF16))

    def start(self, position):
        total = jnp.zeros((position.shape[0], 2 * LANES), F32)
        for row, step in zip(self.starts, self.steps):
            total += lax.dot_general(ones_where(row <= position), step, NT, preferred_element_type=F32)
        return F32(LANES) * total[:, :LANES] + total[:, LANES:]

    def start_row(self, row):
        start = jnp.zeros((1, LANES), F32)
        for column in self.columns:
            start = jnp.maximum(start, jnp.max(jnp.where(column <= row, column, F32(0)), axis=0, keepdims=True))
        return start

    def until(self, row):
        after = jnp.full((1, LANES), FAR, F32)
        for column in self.columns:
            later = jnp.where(column > row, column, F32(FAR))
            after = jnp.minimum(after, jnp.min(later, axis=0, keepdims=True))
        return jnp.minimum(row + F32(self.z.window), after - F32(1))


def root(z, distance):
    return lax.rsqrt(jnp.minimum(distance, F32(z.window)) + F32(1))


def pack(z, pieces, base, marks_ref, codes_ref, rows_ref, from_ref):
    if not pieces.count:
        return
    spare = jnp.zeros((8 - z.chunks, LANES), F32)

    def mark(s, carry):
        local = pieces.place(s) - base
        near = local.astype(I32)
        codes_ref[s] = jnp.concatenate([near >> LOW, near & MASK], axis=0).astype(F32)
        own = (local >= 0) & (local < F32(z.slots))
        tail = (local >= F32(-z.window)) & (local < 0)
        marks_ref[0, s] = jnp.concatenate([jnp.where(own, F32(1), F32(0)), spare], axis=0)
        marks_ref[1, s] = jnp.concatenate([jnp.where(tail, F32(1), F32(0)), spare], axis=0)
        return carry

    loop(pieces.count, mark, 0)
    upper = ones_where(iota((LANES, LANES), 0) < iota((LANES, LANES), 1))
    full = jnp.ones((LANES, LANES), BF16)
    lines = pieces.count * 8
    at, by = iota((lines, lines), 0), iota((lines, lines), 1)
    earlier = ones_where(((at >> 3) == (by >> 3)) & (by < at))
    source = iota((lines, LANES), 0) >> 3
    offset = ((source & (pieces.per_group - 1)) * z.capacity).astype(F32)
    for kind in range(2):
        marked = marks_ref[kind].reshape(lines, LANES)
        mark = marked.astype(BF16)
        rank = dot(mark, upper) + dot(earlier, dot(mark, full).astype(BF16)) + offset
        marks_ref[kind] = jnp.where(marked > 0, rank, F32(-1)).reshape(pieces.count, 8, LANES)

    spots = iota((LANES, LANES), 0).astype(F32)
    code_line = iota((2 * z.chunks, LANES), 0) & (z.chunks - 1)
    for kind in range(2):
        for g in range(pieces.groups):

            def add(i, carry):
                values, places = carry
                s = g * pieces.per_group + i
                ranks = marks_ref[kind, s]
                codes = codes_ref[s]
                hot = jnp.concatenate([ones_where(spots == ranks[r : r + 1]) for r in range(z.chunks)], axis=1)
                wide = [jnp.where(code_line == r, codes, F32(0)).astype(BF16) for r in range(z.chunks)]
                values += dot(hot, pieces.rows(s))
                places += lax.dot_general(jnp.concatenate(wide, axis=1), hot, NT, preferred_element_type=F32)
                return values, places

            zero = (jnp.zeros((LANES, LANES), F32), jnp.zeros((2 * z.chunks, LANES), F32))
            values, places = loop(pieces.per_group, add, zero)
            line = kind * pieces.groups + g
            rows_ref[line * LANES : (line + 1) * LANES, :] = values.astype(BF16)
            high = jnp.sum(places[: z.chunks], axis=0, keepdims=True)
            low = jnp.sum(places[z.chunks :], axis=0, keepdims=True)
            from_ref[line : line + 1, :] = F32(LANES) * high + low


def tiles(values):
    return values.reshape(values.shape[0] // 16, 16, LANES)


def tile_of(row):
    return jnp.broadcast_to(row.astype(I32), (16, LANES)).astype(I16)


def held(position, bounds):
    one, nothing, count = BF16(1), BF16(0), position.shape[0]
    position = tiles(position)
    masks = [jnp.where(position - first[None] <= length[None], one, nothing) for first, length in bounds]
    return jnp.concatenate([mask.reshape(count, LANES) for mask in masks], axis=1)


def within(top, span, rows):
    if top.dtype == I16:
        one, nothing, count = BF16(1), BF16(0), top.shape[0]
        top, span = tiles(top), tiles(span)
        masks = [jnp.where(top - tile_of(row)[None] <= span, one, nothing) for row in rows]
        return jnp.concatenate([mask.reshape(count, LANES) for mask in masks], axis=1)
    return jnp.concatenate([ones_where((top - row >= 0) & (top - row <= span)) for row in rows], axis=1)


def wide_columns(*sets):
    count = sets[0].shape[0]
    columns = jnp.concatenate(sets, axis=0).T
    wide = lambda at: jnp.broadcast_to(columns[:, at : at + 1], (LANES, LANES))
    return [jnp.concatenate([wide(i * count + r) for r in range(count)], axis=0) for i in range(len(sets))]


def anchors(z, me):
    middle = F32(z.span * z.slots // 2)
    span_of = lambda owner: (owner.astype(I32) >> (z.span.bit_length() - 1)).astype(F32) * F32(z.span)
    own = (me - span_of(me)) * F32(z.slots) - middle
    tail = (me - span_of(me - F32(1))) * F32(z.slots) - middle
    return own, tail


def short(row):
    return row.astype(I32).astype(I16)


def early_kernel(z, form, before, *refs):
    count = sum(form)
    own_ref, pieces = refs[0], Pieces(z, form, refs[1 : 1 + count])
    refs = refs[1 + count :]
    if before:
        before_ref, sums_ref, rows_ref, from_ref, marks_ref, codes_ref = refs
    else:
        sums_ref, scale_ref, rows_ref, from_ref, high_ref, factor_ref, marks_ref, codes_ref = refs
    rate, me = own_ref[8:9, :], own_ref[9:10, :]
    runs = Runs(z, [own_ref[16 + u : 17 + u, :] for u in range(z.user_rows)])
    pack(z, pieces, me * F32(z.slots), marks_ref, codes_ref, rows_ref, from_ref)
    own_anchor, _ = anchors(z, me)
    inner = iota((BLOCK, LANES), 0)
    fall = jnp.exp(-rate * inner.astype(F32))
    bounds = []
    for g in range(pieces.groups if pieces.count else 0):
        begin = from_ref[g : g + 1, :]
        bounds.append((tile_of(begin), tile_of(runs.until(begin) - begin - F32(TOP))))
    for b in range(z.slots // BLOCK):
        part = slice(b * BLOCK, (b + 1) * BLOCK)
        if bounds:
            mask = held((inner + (b * BLOCK - TOP)).astype(I16), bounds)
            value = dot(mask, rows_ref[0 : len(bounds) * LANES, :])
        else:
            value = jnp.zeros((BLOCK, LANES), F32)
        sums_ref[part, :] = value + before_ref[part, :] if before else value
        if not before:
            first = F32(b * BLOCK)
            position = inner.astype(F32) + first
            start = runs.start(position)
            if b * BLOCK < z.window:
                scale_ref[part, :] = start
            else:
                scale_ref[part, :] = fall * jnp.exp(-rate * (first + own_anchor)) * root(z, position - start)
    if not before:
        position, span_start = wide_columns(own_ref[0 : z.chunks, :], own_ref[z.chunks : 2 * z.chunks, :])
        for shift in range(z.shifts):
            part = slice(shift * z.rows, (shift + 1) * z.rows)
            center = span_start + F32(z.span * z.slots // 2 - shift * z.span * z.slots)
            factor_ref[part, :] = jnp.exp(-rate * (position - center))
            top = position if shift == 0 else span_start - F32(1)
            high_ref[part, :] = short(top - F32(TOP)) if z.narrow else top


def late_kernel(z, earlier, form, late, *refs):
    own_ref, sums_ref, scale_ref, high_ref, factor_ref = refs[:5]
    tails = [refs[5 + 2 * i : 7 + 2 * i] for i in range(len(earlier))]
    refs = refs[5 + 2 * len(earlier) :]
    count = sum(form)
    table_out, feature_out, rows_ref, from_ref, marks_ref, codes_ref, table_ref, feature_ref, sems = refs[count:]
    pieces, last = Pieces(z, form, refs[:count]), Pieces(z, form[-late:], refs[count - sum(form[-late:]) : count])
    rate, me = own_ref[8:9, :], own_ref[9:10, :]
    base = me * F32(z.slots)
    starts = []
    for u in range(z.user_rows):
        add = lambda s, total: total + pieces.below(s, u)
        starts.append(loop(pieces.count, add, jnp.zeros((1, LANES), F32)))
    runs = Runs(z, starts)
    copies = []

    def send(ref, out, part):
        copies.append(pltpu.make_async_copy(ref.at[part, :], out.at[part, :], sems.at[len(copies)]))
        copies[-1].start()

    pack(z, last, base, marks_ref, codes_ref, rows_ref, from_ref)
    own_anchor, tail_anchor = anchors(z, me)
    inner = iota((LATE_BLOCK, LANES), 0)
    fall = jnp.exp(-rate * inner.astype(F32))
    first_start = jnp.max(runs.start_row(base), axis=1, keepdims=True) - base
    bounds = []
    listed = [(from_ref, 0, 2 * last.groups)] + [(ref, count, count) for (_, ref), count in zip(tails, earlier)]
    for ref, first, lines in listed:
        for g in range(first, first + lines):
            begin = ref[g : g + 1, :]
            bounds.append((tile_of(begin), tile_of(runs.until(begin + base) - (begin + base) - F32(TOP))))
    n = last.groups
    own_rows = rows_ref[0 : n * LANES, :]
    tail_rows = [rows_ref[n * LANES : 2 * n * LANES, :]]
    tail_rows += [ref[count * LANES : 2 * count * LANES, :] for (ref, _), count in zip(tails, earlier)]
    tail_rows = jnp.concatenate(tail_rows, axis=0)

    place = own_ref[0 : z.chunks, :]
    start = jnp.concatenate([runs.start_row(place[r : r + 1]) for r in range(z.chunks)], axis=0)
    distance = place - start
    reach = jnp.minimum(distance, F32(z.window))
    scale, reach = wide_columns(root(z, distance), reach - F32(TOP) if z.narrow else reach)
    position, span_start = (None, None) if z.narrow else wide_columns(place, own_ref[z.chunks : 2 * z.chunks, :])
    total = jnp.zeros((z.rows, LANES), F32)
    for shift in range(z.shifts):
        part = slice(shift * z.rows, (shift + 1) * z.rows)
        top = high_ref[part, :]
        if z.narrow:
            span = short(reach)
        else:
            low = position - reach
            span = top - (jnp.maximum(low, span_start) if shift == 0 else low)

        def add(s, value):
            rows = pieces.place(s)
            mask = within(top, span, [rows[r : r + 1] for r in range(z.chunks)])
            return value + dot(mask, pieces.rows(s))

        total += loop(pieces.count, add, jnp.zeros((z.rows, LANES), F32)) * factor_ref[part, :]
    feature_ref[...] = (total * scale).astype(BF16)

    for b in range(z.slots // LATE_BLOCK):
        part = slice(b * LATE_BLOCK, (b + 1) * LATE_BLOCK)
        position = (inner + (b * LATE_BLOCK - TOP)).astype(I16)
        first = F32(b * LATE_BLOCK)
        value = sums_ref[part, :]
        if b * LATE_BLOCK >= z.window:
            value = (value + dot(held(position, bounds[:n]), own_rows)) * scale_ref[part, :]
        else:
            own_fall = jnp.exp(-rate * (first + own_anchor))
            if z.shifts == 1:
                value += dot(held(position, bounds), jnp.concatenate([own_rows, tail_rows], axis=0))
                value *= own_fall
            else:
                value = (value + dot(held(position, bounds[:n]), own_rows)) * own_fall
                value += dot(held(position, bounds[n:]), tail_rows) * jnp.exp(-rate * (first + tail_anchor))
            start = scale_ref[part, :]
            start = jnp.where(start > 0, start, first_start)
            value = value * fall * root(z, inner.astype(F32) + first - start)
        table_ref[part, :] = value.astype(BF16)
        if (b + 1) * LATE_BLOCK % z.window == 0:
            send(table_ref, table_out, slice((b + 1) * LATE_BLOCK - z.window, (b + 1) * LATE_BLOCK))
            if len(copies) == 1:
                send(feature_ref, feature_out, slice(0, z.rows))
    for copy in copies:
        copy.wait()


def swap(block, axis, distance):
    return lax.ppermute(block, axis, [(i, i ^ distance) for i in range(lax.axis_size(axis))])


def spread(blocks, axis):
    distance = lax.axis_size(axis) // 2
    while distance:
        blocks = blocks + [swap(block, axis, distance) for block in blocks]
        distance //= 2
    return blocks


def on_device(events, event_weight, route, bucket, segment, decay_rate):
    rows, width = events.shape
    key_count, shard_count = lax.axis_size("key"), lax.axis_size("shard")
    owners = key_count * shard_count
    slots = segment.shape[0]
    z = Sizes(owners, rows, slots)
    block_rows = rows + z.code_rows
    smem = pl.BlockSpec(memory_space=pltpu.SMEM)
    vmem = pl.BlockSpec(memory_space=pltpu.VMEM)
    shape = jax.ShapeDtypeStruct
    grant = pltpu.CompilerParams(vmem_limit_bytes=(16 if owners <= 8 else 48) * 1024 * 1024)
    me = (lax.axis_index("key") * shard_count + lax.axis_index("shard")).astype(I32).reshape(1)
    block, own = pl.pallas_call(
        functools.partial(send_kernel, z),
        out_shape=(
            shape((block_rows, width), BF16),
            shape((16 + z.user_rows + 7, LANES), F32),
        ),
        in_specs=[smem, smem] + [vmem] * 5,
        out_specs=(vmem, vmem),
        compiler_params=pltpu.CompilerParams(vmem_limit_bytes=56 * 1024 * 1024),
        name="weigh",
    )(
        me, decay_rate, events, event_weight.reshape(z.chunks, LANES), route.reshape(z.chunks, LANES),
        bucket.reshape(z.chunks, LANES), segment.reshape(slots // LANES, LANES),
    )

    def flat(blocks):
        return [part[None] if part.ndim == 2 else part for parts in blocks for part in parts]

    def sums(blocks, before=()):
        blocks, form, count = flat(blocks), tuple(map(len, blocks)), len(blocks)
        lines = max(8, 2 * count)
        whole = shape((slots, width), F32)
        kept = (shape((lines * LANES, LANES), BF16), shape((lines, LANES), F32))
        factors = shape((z.shifts * rows, width), F32)
        tops = shape((z.shifts * rows, width), I16 if z.narrow else F32)
        return pl.pallas_call(
            functools.partial(early_kernel, z, form, len(before)),
            out_shape=(whole,) + kept if before else (whole, whole) + kept + (tops, factors),
            in_specs=[vmem] * (1 + len(blocks) + len(before)),
            out_specs=(vmem,) * (3 if before else 6),
            scratch_shapes=[
                pltpu.VMEM((2, max(1, count), 8, LANES), F32),
                pltpu.VMEM((max(1, count), 2 * z.chunks, LANES), F32),
            ],
            compiler_params=grant,
            cost_estimate=pl.CostEstimate(flops=COST * count, bytes_accessed=0, transcendentals=0),
            name="more_sums" if before else "first_sums",
        )(own, *blocks, *before)

    if (key_count, shard_count) == (4, 2):
        tie = lax.optimization_barrier
        far = swap(block, "key", 2)
        side = swap(block, "shard", 1)
        near = swap(block, "key", 1)
        side_near = swap(side, "key", 1)
        total, scale, *tail, tops, factors = sums([(block,)])
        far, total = tie((far, total))
        last = swap(far, "key", 1)
        side_far = swap(far, "shard", 1)
        total, *tail2 = sums([(side,), (near,)], (total,))
        last, total = tie((last, total))
        side_last = swap(last, "shard", 1)
        second = [(far,), (last,), (side_far,)]
        late = [(side_near,), (side_last,)]
        total, *tail3 = sums(second, (total,))
        early, earlier, tails = [(block,), (side,), (near,)] + second, (1, 2, 3), tail + tail2 + tail3
    else:
        blocks = spread(spread([block], "key"), "shard")
        total, scale, _, _, tops, factors = sums([])
        early, earlier, tails = [], (), []
        late = [(jnp.concatenate(blocks, axis=0).reshape(owners, block_rows, width),)]
    late_lines = 2 * (len(late) if earlier else z.groups)
    late_count = len(late) if earlier else owners
    form = tuple(map(len, early + late))
    return pl.pallas_call(
        functools.partial(late_kernel, z, earlier, form, len(late)),
        out_shape=(shape((slots, width), BF16), shape((rows, width), BF16)),
        in_specs=[vmem] * (5 + len(tails) + sum(form)),
        out_specs=(pl.BlockSpec(memory_space=pl.ANY),) * 2,
        scratch_shapes=[
            pltpu.VMEM((late_lines * LANES, LANES), BF16),
            pltpu.VMEM((late_lines, LANES), F32),
            pltpu.VMEM((2, late_count, 8, LANES), F32),
            pltpu.VMEM((late_count, 2 * z.chunks, LANES), F32),
            pltpu.VMEM((slots, width), BF16),
            pltpu.VMEM((rows, width), BF16),
            pltpu.SemaphoreType.DMA((1 + slots // z.window,)),
        ],
        compiler_params=grant,
        name="table_and_rows",
    )(own, total, scale, tops, factors, *tails, *flat(early + late))


def solution(mesh):
    placed = (
        P(("groups", "key", "shard"), "lane"),
        P(("groups", "key", "shard")),
        P(("groups", "key", "shard"), None),
        P(("groups", "key", "shard")),
        P(("groups", "key", "shard")),
        P("lane"),
    )
    return jax.shard_map(
        on_device,
        mesh=mesh,
        in_specs=placed,
        out_specs=(P(("groups", "key", "shard"), "lane"), P(("groups", "key", "shard"), "lane")),
        check_vma=False,
    )
```

```python
import functools
import jax
import jax.numpy as jnp
from jax import lax
from jax.experimental import pallas as pl
from jax.experimental.pallas import tpu as pltpu
from jax.sharding import PartitionSpec as P

LANES = 128
LOW = 7
MASK = 127
F32 = jnp.float32
BF16 = jnp.bfloat16
I32 = jnp.int32
I16 = jnp.int16
FAR = 1e9
TOP = 32768
NT = (((1,), (1,)), ((), ()))
BLOCK = 512
LATE_BLOCK = 256
COST = 1


class Sizes:
    def __init__(self, owners, rows, slots):
        self.owners, self.rows, self.slots = owners, rows, slots
        self.window = slots // 4
        self.chunks = rows // LANES
        self.user_rows = -(-8 * owners // LANES)
        self.code_rows = -(-(3 * self.chunks + 2 * self.user_rows) // 16) * 16
        self.span = min(owners, 8)
        self.shifts = 1 if owners <= self.span else 2
        self.capacity = 2 * rows // owners
        self.per_group = LANES // self.capacity
        self.groups = owners // self.per_group
        self.narrow = owners * slots <= 32768


def iota(shape, axis):
    return lax.broadcasted_iota(I32, shape, axis)


def ones_where(condition):
    return jnp.where(condition, F32(1), F32(0)).astype(BF16)


def dot(a, b):
    return jnp.dot(a, b, preferred_element_type=F32)


def loop(count, body, carry):
    if count <= 8:
        for i in range(count):
            carry = body(i, carry)
        return carry
    return lax.fori_loop(0, count, body, carry)


def send_kernel(z, me_ref, rate_ref, events_ref, weight_ref, route_ref, bucket_ref, segment_ref, block_ref, own_ref):
    groups = rate_ref.shape[0]
    lane = iota((1, LANES), 1)
    rate = jnp.full((1, LANES), rate_ref[0], F32)
    for g in range(1, groups):
        rate = jnp.where(lane >= g * (LANES // groups), rate_ref[g], rate)
    route = route_ref[...]
    bucket = bucket_ref[...]
    place = (route * z.slots + bucket).astype(F32)
    first = ((route >> (z.span.bit_length() - 1)) * (z.span * z.slots)).astype(F32)
    me = jnp.full((8 - 1, LANES), me_ref[0], I32).astype(F32)
    own_ref[0:16, :] = jnp.concatenate([place, first, rate, me], axis=0)
    spot = place - first - F32(z.span * z.slots // 2)
    columns = jnp.concatenate([weight_ref[...], spot], axis=0).T
    for r in range(z.chunks):
        part = slice(r * LANES, (r + 1) * LANES)
        weighted = (columns[:, r : r + 1] * events_ref[part, :].astype(F32)).astype(BF16)
        grown = weighted.astype(F32) * jnp.exp(columns[:, z.chunks + r : z.chunks + r + 1] * rate)
        block_ref[part, :] = grown.astype(BF16)
    ones = jnp.ones((8, LANES), BF16)
    high, low = [], []
    users = min(LANES, 8 * z.owners)
    for u in range(z.user_rows):
        user = iota((users, LANES), 0) + u * LANES
        below = jnp.zeros((users, LANES), F32)
        for r in range(z.slots // LANES):
            below += jnp.where(segment_ref[r : r + 1, :] < user, F32(1), F32(0))
        count = lax.dot_general(ones, below.astype(BF16), NT, preferred_element_type=F32)[0:1]
        if users < LANES:
            count = jnp.concatenate([count, jnp.full((1, LANES - users), z.slots, F32)], axis=1)
        own_ref[16 + u : 17 + u, :] = count
        count = count.astype(I32)
        high.append(count >> LOW)
        low.append(count & MASK)
    spare = z.code_rows - 3 * z.chunks - 2 * z.user_rows
    pad = [jnp.zeros((spare, LANES), I32)] if spare else []
    codes = jnp.concatenate([route, bucket >> LOW, bucket & MASK] + high + low + pad, axis=0)
    block_ref[z.rows : z.rows + z.code_rows, :] = codes.astype(F32).astype(BF16)


class Pieces:
    def __init__(self, z, form, refs):
        self.z, refs = z, list(refs)
        self.parts = [[refs.pop(0) for _ in range(n)] for n in form]
        self.count = len(form) if len(form) != 1 else self.parts[0][0].shape[0]
        self.per_group = 1 if len(form) != 1 else z.per_group
        self.groups = self.count // self.per_group

    def block(self, s):
        return (self.parts[s], 0) if len(self.parts) != 1 else (self.parts[0], s)

    def codes(self, s):
        parts, i = self.block(s)
        first = parts[0].shape[1] - self.z.code_rows
        return parts[0][i, first : first + self.z.code_rows, :].astype(F32)

    def rows(self, s):
        parts, i = self.block(s)
        first = parts[0][i, 0 : parts[0].shape[1] - self.z.code_rows, :]
        return jnp.concatenate([first] + [part[i] for part in parts[1:]], axis=0)

    def place(self, s):
        n, tile = self.z.chunks, self.codes(s)
        return tile[0:n] * F32(self.z.slots) + F32(LANES) * tile[n : 2 * n] + tile[2 * n : 3 * n]

    def below(self, s, u):
        tile, at = self.codes(s), 3 * self.z.chunks + u
        return F32(LANES) * tile[at : at + 1] + tile[at + self.z.user_rows : at + self.z.user_rows + 1]


class Runs:
    def __init__(self, z, starts):
        self.z, self.starts = z, starts
        users = min(LANES, 8 * z.owners)
        self.columns = [jnp.broadcast_to(row, (8, LANES)).T[:users, 0:1] for row in starts]
        self.steps = []
        for u, row in enumerate(starts):
            before = pltpu.roll(row, 1, 1)
            first = starts[u - 1][:, LANES - 1 : LANES] if u else jnp.zeros((1, 1), F32)
            step = (row - jnp.where(iota((1, LANES), 1) == 0, first, before)).astype(I32)
            pair = [jnp.broadcast_to(part, (LANES, LANES)) for part in (step >> LOW, step & MASK)]
            self.steps.append(jnp.concatenate(pair, axis=0).astype(F32).astype(BF16))

    def start(self, position):
        total = jnp.zeros((position.shape[0], 2 * LANES), F32)
        for row, step in zip(self.starts, self.steps):
            total += lax.dot_general(ones_where(row <= position), step, NT, preferred_element_type=F32)
        return F32(LANES) * total[:, :LANES] + total[:, LANES:]

    def start_row(self, row):
        start = jnp.zeros((1, LANES), F32)
        for column in self.columns:
            start = jnp.maximum(start, jnp.max(jnp.where(column <= row, column, F32(0)), axis=0, keepdims=True))
        return start

    def until(self, row):
        after = jnp.full((1, LANES), FAR, F32)
        for column in self.columns:
            later = jnp.where(column > row, column, F32(FAR))
            after = jnp.minimum(after, jnp.min(later, axis=0, keepdims=True))
        return jnp.minimum(row + F32(self.z.window), after - F32(1))


def root(z, distance):
    return lax.rsqrt(jnp.minimum(distance, F32(z.window)) + F32(1))


def pack(z, pieces, base, marks_ref, codes_ref, rows_ref, from_ref):
    if not pieces.count:
        return
    spare = jnp.zeros((8 - z.chunks, LANES), F32)

    def mark(s, carry):
        local = pieces.place(s) - base
        near = local.astype(I32)
        codes_ref[s] = jnp.concatenate([near >> LOW, near & MASK], axis=0).astype(F32)
        own = (local >= 0) & (local < F32(z.slots))
        tail = (local >= F32(-z.window)) & (local < 0)
        marks_ref[0, s] = jnp.concatenate([jnp.where(own, F32(1), F32(0)), spare], axis=0)
        marks_ref[1, s] = jnp.concatenate([jnp.where(tail, F32(1), F32(0)), spare], axis=0)
        return carry

    loop(pieces.count, mark, 0)
    upper = ones_where(iota((LANES, LANES), 0) < iota((LANES, LANES), 1))
    full = jnp.ones((LANES, LANES), BF16)
    lines = pieces.count * 8
    at, by = iota((lines, lines), 0), iota((lines, lines), 1)
    earlier = ones_where(((at >> 3) == (by >> 3)) & (by < at))
    source = iota((lines, LANES), 0) >> 3
    offset = ((source & (pieces.per_group - 1)) * z.capacity).astype(F32)
    for kind in range(2):
        marked = marks_ref[kind].reshape(lines, LANES)
        mark = marked.astype(BF16)
        rank = dot(mark, upper) + dot(earlier, dot(mark, full).astype(BF16)) + offset
        marks_ref[kind] = jnp.where(marked > 0, rank, F32(-1)).reshape(pieces.count, 8, LANES)

    spots = iota((LANES, LANES), 0).astype(F32)
    code_line = iota((2 * z.chunks, LANES), 0) & (z.chunks - 1)
    for kind in range(2):
        for g in range(pieces.groups):

            def add(i, carry):
                values, places = carry
                s = g * pieces.per_group + i
                ranks = marks_ref[kind, s]
                codes = codes_ref[s]
                hot = jnp.concatenate([ones_where(spots == ranks[r : r + 1]) for r in range(z.chunks)], axis=1)
                wide = [jnp.where(code_line == r, codes, F32(0)).astype(BF16) for r in range(z.chunks)]
                values += dot(hot, pieces.rows(s))
                places += lax.dot_general(jnp.concatenate(wide, axis=1), hot, NT, preferred_element_type=F32)
                return values, places

            zero = (jnp.zeros((LANES, LANES), F32), jnp.zeros((2 * z.chunks, LANES), F32))
            values, places = loop(pieces.per_group, add, zero)
            line = kind * pieces.groups + g
            rows_ref[line * LANES : (line + 1) * LANES, :] = values.astype(BF16)
            high = jnp.sum(places[: z.chunks], axis=0, keepdims=True)
            low = jnp.sum(places[z.chunks :], axis=0, keepdims=True)
            from_ref[line : line + 1, :] = F32(LANES) * high + low


def tiles(values):
    return values.reshape(values.shape[0] // 16, 16, LANES)


def tile_of(row):
    return jnp.broadcast_to(row.astype(I32), (16, LANES)).astype(I16)


def held(position, bounds):
    one, nothing, count = BF16(1), BF16(0), position.shape[0]
    position = tiles(position)
    masks = [jnp.where(position - first[None] <= length[None], one, nothing) for first, length in bounds]
    return jnp.concatenate([mask.reshape(count, LANES) for mask in masks], axis=1)


def within(top, span, rows):
    if top.dtype == I16:
        one, nothing, count = BF16(1), BF16(0), top.shape[0]
        top, span = tiles(top), tiles(span)
        masks = [jnp.where(top - tile_of(row)[None] <= span, one, nothing) for row in rows]
        return jnp.concatenate([mask.reshape(count, LANES) for mask in masks], axis=1)
    return jnp.concatenate([ones_where((top - row >= 0) & (top - row <= span)) for row in rows], axis=1)


def wide_columns(*sets):
    count = sets[0].shape[0]
    columns = jnp.concatenate(sets, axis=0).T
    wide = lambda at: jnp.broadcast_to(columns[:, at : at + 1], (LANES, LANES))
    return [jnp.concatenate([wide(i * count + r) for r in range(count)], axis=0) for i in range(len(sets))]


def anchors(z, me):
    middle = F32(z.span * z.slots // 2)
    span_of = lambda owner: (owner.astype(I32) >> (z.span.bit_length() - 1)).astype(F32) * F32(z.span)
    own = (me - span_of(me)) * F32(z.slots) - middle
    tail = (me - span_of(me - F32(1))) * F32(z.slots) - middle
    return own, tail


def short(row):
    return row.astype(I32).astype(I16)


def early_kernel(z, form, before, *refs):
    count = sum(form)
    own_ref, pieces = refs[0], Pieces(z, form, refs[1 : 1 + count])
    refs = refs[1 + count :]
    if before:
        before_ref, sums_ref, rows_ref, from_ref, marks_ref, codes_ref = refs
    else:
        sums_ref, scale_ref, rows_ref, from_ref, high_ref, factor_ref, marks_ref, codes_ref = refs
    rate, me = own_ref[8:9, :], own_ref[9:10, :]
    runs = Runs(z, [own_ref[16 + u : 17 + u, :] for u in range(z.user_rows)])
    pack(z, pieces, me * F32(z.slots), marks_ref, codes_ref, rows_ref, from_ref)
    own_anchor, _ = anchors(z, me)
    inner = iota((BLOCK, LANES), 0)
    fall = jnp.exp(-rate * inner.astype(F32))
    bounds = []
    for g in range(pieces.groups if pieces.count else 0):
        begin = from_ref[g : g + 1, :]
        bounds.append((tile_of(begin), tile_of(runs.until(begin) - begin - F32(TOP))))
    for b in range(z.slots // BLOCK):
        part = slice(b * BLOCK, (b + 1) * BLOCK)
        if bounds:
            mask = held((inner + (b * BLOCK - TOP)).astype(I16), bounds)
            value = dot(mask, rows_ref[0 : len(bounds) * LANES, :])
        else:
            value = jnp.zeros((BLOCK, LANES), F32)
        sums_ref[part, :] = value + before_ref[part, :] if before else value
        if not before:
            first = F32(b * BLOCK)
            position = inner.astype(F32) + first
            start = runs.start(position)
            if b * BLOCK < z.window:
                scale_ref[part, :] = start
            else:
                scale_ref[part, :] = fall * jnp.exp(-rate * (first + own_anchor)) * root(z, position - start)
    if not before:
        position, span_start = wide_columns(own_ref[0 : z.chunks, :], own_ref[z.chunks : 2 * z.chunks, :])
        for shift in range(z.shifts):
            part = slice(shift * z.rows, (shift + 1) * z.rows)
            center = span_start + F32(z.span * z.slots // 2 - shift * z.span * z.slots)
            factor_ref[part, :] = jnp.exp(-rate * (position - center))
            top = position if shift == 0 else span_start - F32(1)
            high_ref[part, :] = short(top - F32(TOP)) if z.narrow else top


def late_kernel(z, earlier, form, late, *refs):
    own_ref, sums_ref, scale_ref, high_ref, factor_ref = refs[:5]
    tails = [refs[5 + 2 * i : 7 + 2 * i] for i in range(len(earlier))]
    refs = refs[5 + 2 * len(earlier) :]
    count = sum(form)
    table_out, feature_out, rows_ref, from_ref, marks_ref, codes_ref, table_ref, feature_ref, sems = refs[count:]
    pieces, last = Pieces(z, form, refs[:count]), Pieces(z, form[-late:], refs[count - sum(form[-late:]) : count])
    rate, me = own_ref[8:9, :], own_ref[9:10, :]
    base = me * F32(z.slots)
    starts = []
    for u in range(z.user_rows):
        add = lambda s, total: total + pieces.below(s, u)
        starts.append(loop(pieces.count, add, jnp.zeros((1, LANES), F32)))
    runs = Runs(z, starts)
    copies = []

    def send(ref, out, part):
        copies.append(pltpu.make_async_copy(ref.at[part, :], out.at[part, :], sems.at[len(copies)]))
        copies[-1].start()

    pack(z, last, base, marks_ref, codes_ref, rows_ref, from_ref)
    own_anchor, tail_anchor = anchors(z, me)
    inner = iota((LATE_BLOCK, LANES), 0)
    fall = jnp.exp(-rate * inner.astype(F32))
    first_start = jnp.max(runs.start_row(base), axis=1, keepdims=True) - base
    bounds = []
    listed = [(from_ref, 0, 2 * last.groups)] + [(ref, count, count) for (_, ref), count in zip(tails, earlier)]
    for ref, first, lines in listed:
        for g in range(first, first + lines):
            begin = ref[g : g + 1, :]
            bounds.append((tile_of(begin), tile_of(runs.until(begin + base) - (begin + base) - F32(TOP))))
    n = last.groups
    own_rows = rows_ref[0 : n * LANES, :]
    tail_rows = [rows_ref[n * LANES : 2 * n * LANES, :]]
    tail_rows += [ref[count * LANES : 2 * count * LANES, :] for (ref, _), count in zip(tails, earlier)]
    tail_rows = jnp.concatenate(tail_rows, axis=0)
    for b in range(z.slots // LATE_BLOCK):
        part = slice(b * LATE_BLOCK, (b + 1) * LATE_BLOCK)
        position = (inner + (b * LATE_BLOCK - TOP)).astype(I16)
        first = F32(b * LATE_BLOCK)
        value = sums_ref[part, :]
        if b * LATE_BLOCK >= z.window:
            value = (value + dot(held(position, bounds[:n]), own_rows)) * scale_ref[part, :]
        else:
            own_fall = jnp.exp(-rate * (first + own_anchor))
            if z.shifts == 1:
                value += dot(held(position, bounds), jnp.concatenate([own_rows, tail_rows], axis=0))
                value *= own_fall
            else:
                value = (value + dot(held(position, bounds[:n]), own_rows)) * own_fall
                value += dot(held(position, bounds[n:]), tail_rows) * jnp.exp(-rate * (first + tail_anchor))
            start = scale_ref[part, :]
            start = jnp.where(start > 0, start, first_start)
            value = value * fall * root(z, inner.astype(F32) + first - start)
        table_ref[part, :] = value.astype(BF16)
        if (b + 1) * LATE_BLOCK % z.window == 0:
            send(table_ref, table_out, slice((b + 1) * LATE_BLOCK - z.window, (b + 1) * LATE_BLOCK))

    place = own_ref[0 : z.chunks, :]
    start = jnp.concatenate([runs.start_row(place[r : r + 1]) for r in range(z.chunks)], axis=0)
    distance = place - start
    reach = jnp.minimum(distance, F32(z.window))
    scale, reach = wide_columns(root(z, distance), reach - F32(TOP) if z.narrow else reach)
    position, span_start = (None, None) if z.narrow else wide_columns(place, own_ref[z.chunks : 2 * z.chunks, :])
    total = jnp.zeros((z.rows, LANES), F32)
    for shift in range(z.shifts):
        part = slice(shift * z.rows, (shift + 1) * z.rows)
        top = high_ref[part, :]
        if z.narrow:
            span = short(reach)
        else:
            low = position - reach
            span = top - (jnp.maximum(low, span_start) if shift == 0 else low)

        def add(s, value):
            rows = pieces.place(s)
            mask = within(top, span, [rows[r : r + 1] for r in range(z.chunks)])
            return value + dot(mask, pieces.rows(s))

        total += loop(pieces.count, add, jnp.zeros((z.rows, LANES), F32)) * factor_ref[part, :]
    feature_ref[...] = (total * scale).astype(BF16)
    send(feature_ref, feature_out, slice(0, z.rows))
    for copy in copies:
        copy.wait()


def swap(block, axis, distance):
    return lax.ppermute(block, axis, [(i, i ^ distance) for i in range(lax.axis_size(axis))])


def spread(blocks, axis):
    distance = lax.axis_size(axis) // 2
    while distance:
        blocks = blocks + [swap(block, axis, distance) for block in blocks]
        distance //= 2
    return blocks


def on_device(events, event_weight, route, bucket, segment, decay_rate):
    rows, width = events.shape
    key_count, shard_count = lax.axis_size("key"), lax.axis_size("shard")
    owners = key_count * shard_count
    slots = segment.shape[0]
    z = Sizes(owners, rows, slots)
    block_rows = rows + z.code_rows
    smem = pl.BlockSpec(memory_space=pltpu.SMEM)
    vmem = pl.BlockSpec(memory_space=pltpu.VMEM)
    shape = jax.ShapeDtypeStruct
    grant = pltpu.CompilerParams(vmem_limit_bytes=(16 if owners <= 8 else 48) * 1024 * 1024)
    me = (lax.axis_index("key") * shard_count + lax.axis_index("shard")).astype(I32).reshape(1)
    block, own = pl.pallas_call(
        functools.partial(send_kernel, z),
        out_shape=(
            shape((block_rows, width), BF16),
            shape((16 + z.user_rows + 7, LANES), F32),
        ),
        in_specs=[smem, smem] + [vmem] * 5,
        out_specs=(vmem, vmem),
        compiler_params=pltpu.CompilerParams(vmem_limit_bytes=56 * 1024 * 1024),
        name="weigh",
    )(
        me, decay_rate, events, event_weight.reshape(z.chunks, LANES), route.reshape(z.chunks, LANES),
        bucket.reshape(z.chunks, LANES), segment.reshape(slots // LANES, LANES),
    )

    def flat(blocks):
        return [part[None] if part.ndim == 2 else part for parts in blocks for part in parts]

    def sums(blocks, before=()):
        blocks, form, count = flat(blocks), tuple(map(len, blocks)), len(blocks)
        lines = max(8, 2 * count)
        whole = shape((slots, width), F32)
        kept = (shape((lines * LANES, LANES), BF16), shape((lines, LANES), F32))
        factors = shape((z.shifts * rows, width), F32)
        tops = shape((z.shifts * rows, width), I16 if z.narrow else F32)
        return pl.pallas_call(
            functools.partial(early_kernel, z, form, len(before)),
            out_shape=(whole,) + kept if before else (whole, whole) + kept + (tops, factors),
            in_specs=[vmem] * (1 + len(blocks) + len(before)),
            out_specs=(vmem,) * (3 if before else 6),
            scratch_shapes=[
                pltpu.VMEM((2, max(1, count), 8, LANES), F32),
                pltpu.VMEM((max(1, count), 2 * z.chunks, LANES), F32),
            ],
            compiler_params=grant,
            cost_estimate=pl.CostEstimate(flops=COST * count, bytes_accessed=0, transcendentals=0),
            name="more_sums" if before else "first_sums",
        )(own, *blocks, *before)

    if (key_count, shard_count) == (4, 2):
        tie = lax.optimization_barrier
        far = swap(block, "key", 2)
        side = swap(block, "shard", 1)
        near = swap(block, "key", 1)
        side_near = swap(side, "key", 1)
        total, scale, *tail, tops, factors = sums([(block,)])
        far, total = tie((far, total))
        last = swap(far, "key", 1)
        side_far = swap(far, "shard", 1)
        total, *tail2 = sums([(side,), (near,)], (total,))
        last, total = tie((last, total))
        side_last = swap(last, "shard", 1)
        second = [(far,), (last,), (side_far,)]
        late = [(side_near,), (side_last,)]
        total, *tail3 = sums(second, (total,))
        early, earlier, tails = [(block,), (side,), (near,)] + second, (1, 2, 3), tail + tail2 + tail3
    else:
        blocks = spread(spread([block], "key"), "shard")
        total, scale, _, _, tops, factors = sums([])
        early, earlier, tails = [], (), []
        late = [(jnp.concatenate(blocks, axis=0).reshape(owners, block_rows, width),)]
    late_lines = 2 * (len(late) if earlier else z.groups)
    late_count = len(late) if earlier else owners
    form = tuple(map(len, early + late))
    return pl.pallas_call(
        functools.partial(late_kernel, z, earlier, form, len(late)),
        out_shape=(shape((slots, width), BF16), shape((rows, width), BF16)),
        in_specs=[vmem] * (5 + len(tails) + sum(form)),
        out_specs=(pl.BlockSpec(memory_space=pl.ANY),) * 2,
        scratch_shapes=[
            pltpu.VMEM((late_lines * LANES, LANES), BF16),
            pltpu.VMEM((late_lines, LANES), F32),
            pltpu.VMEM((2, late_count, 8, LANES), F32),
            pltpu.VMEM((late_count, 2 * z.chunks, LANES), F32),
            pltpu.VMEM((slots, width), BF16),
            pltpu.VMEM((rows, width), BF16),
            pltpu.SemaphoreType.DMA((1 + slots // z.window,)),
        ],
        compiler_params=grant,
        name="table_and_rows",
    )(own, total, scale, tops, factors, *tails, *flat(early + late))


def solution(mesh):
    placed = (
        P(("groups", "key", "shard"), "lane"),
        P(("groups", "key", "shard")),
        P(("groups", "key", "shard"), None),
        P(("groups", "key", "shard")),
        P(("groups", "key", "shard")),
        P("lane"),
    )
    return jax.shard_map(
        on_device,
        mesh=mesh,
        in_specs=placed,
        out_specs=(P(("groups", "key", "shard"), "lane"), P(("groups", "key", "shard"), "lane")),
        check_vma=False,
    )
```

```python
import functools
import jax
import jax.numpy as jnp
from jax import lax
from jax.experimental import pallas as pl
from jax.experimental.pallas import tpu as pltpu
from jax.sharding import PartitionSpec as P

LANES = 128
LOW = 7
MASK = 127
F32 = jnp.float32
BF16 = jnp.bfloat16
I32 = jnp.int32
I16 = jnp.int16
FAR = 1e9
TOP = 32768
NT = (((1,), (1,)), ((), ()))
BLOCK = 512
LATE_BLOCK = 256
COST = 1


class Sizes:
    def __init__(self, owners, rows, slots):
        self.owners, self.rows, self.slots = owners, rows, slots
        self.window = slots // 4
        self.chunks = rows // LANES
        self.user_rows = -(-8 * owners // LANES)
        self.code_rows = -(-(3 * self.chunks + 2 * self.user_rows) // 16) * 16
        self.span = min(owners, 8)
        self.shifts = 1 if owners <= self.span else 2
        self.capacity = 2 * rows // owners
        self.per_group = LANES // self.capacity
        self.groups = owners // self.per_group
        self.narrow = owners * slots <= 32768


def iota(shape, axis):
    return lax.broadcasted_iota(I32, shape, axis)


def ones_where(condition):
    return jnp.where(condition, F32(1), F32(0)).astype(BF16)


def dot(a, b):
    return jnp.dot(a, b, preferred_element_type=F32)


def loop(count, body, carry):
    if count <= 8:
        for i in range(count):
            carry = body(i, carry)
        return carry
    return lax.fori_loop(0, count, body, carry)


def send_kernel(z, me_ref, rate_ref, events_ref, weight_ref, route_ref, bucket_ref, segment_ref, block_ref, own_ref):
    groups = rate_ref.shape[0]
    lane = iota((1, LANES), 1)
    rate = jnp.full((1, LANES), rate_ref[0], F32)
    for g in range(1, groups):
        rate = jnp.where(lane >= g * (LANES // groups), rate_ref[g], rate)
    route = route_ref[...]
    bucket = bucket_ref[...]
    place = (route * z.slots + bucket).astype(F32)
    first = ((route >> (z.span.bit_length() - 1)) * (z.span * z.slots)).astype(F32)
    me = jnp.full((8 - 1, LANES), me_ref[0], I32).astype(F32)
    own_ref[0:16, :] = jnp.concatenate([place, first, rate, me], axis=0)
    spot = place - first - F32(z.span * z.slots // 2)
    columns = jnp.concatenate([weight_ref[...], spot], axis=0).T
    for r in range(z.chunks):
        part = slice(r * LANES, (r + 1) * LANES)
        weighted = (columns[:, r : r + 1] * events_ref[part, :].astype(F32)).astype(BF16)
        grown = weighted.astype(F32) * jnp.exp(columns[:, z.chunks + r : z.chunks + r + 1] * rate)
        block_ref[part, :] = grown.astype(BF16)
    ones = jnp.ones((8, LANES), BF16)
    high, low = [], []
    users = min(LANES, 8 * z.owners)
    for u in range(z.user_rows):
        user = iota((users, LANES), 0) + u * LANES
        below = jnp.zeros((users, LANES), F32)
        for r in range(z.slots // LANES):
            below += jnp.where(segment_ref[r : r + 1, :] < user, F32(1), F32(0))
        count = lax.dot_general(ones, below.astype(BF16), NT, preferred_element_type=F32)[0:1]
        if users < LANES:
            count = jnp.concatenate([count, jnp.full((1, LANES - users), z.slots, F32)], axis=1)
        own_ref[16 + u : 17 + u, :] = count
        count = count.astype(I32)
        high.append(count >> LOW)
        low.append(count & MASK)
    spare = z.code_rows - 3 * z.chunks - 2 * z.user_rows
    pad = [jnp.zeros((spare, LANES), I32)] if spare else []
    codes = jnp.concatenate([route, bucket >> LOW, bucket & MASK] + high + low + pad, axis=0)
    block_ref[z.rows : z.rows + z.code_rows, :] = codes.astype(F32).astype(BF16)


class Pieces:
    def __init__(self, z, form, refs):
        self.z, refs = z, list(refs)
        self.parts = [[refs.pop(0) for _ in range(n)] for n in form]
        self.count = len(form) if len(form) != 1 else self.parts[0][0].shape[0]
        self.per_group = 1 if len(form) != 1 else z.per_group
        self.groups = self.count // self.per_group

    def block(self, s):
        return (self.parts[s], 0) if len(self.parts) != 1 else (self.parts[0], s)

    def codes(self, s):
        parts, i = self.block(s)
        first = parts[0].shape[1] - self.z.code_rows
        return parts[0][i, first : first + self.z.code_rows, :].astype(F32)

    def rows(self, s):
        parts, i = self.block(s)
        first = parts[0][i, 0 : parts[0].shape[1] - self.z.code_rows, :]
        return jnp.concatenate([first] + [part[i] for part in parts[1:]], axis=0)

    def place(self, s):
        n, tile = self.z.chunks, self.codes(s)
        return tile[0:n] * F32(self.z.slots) + F32(LANES) * tile[n : 2 * n] + tile[2 * n : 3 * n]

    def below(self, s, u):
        tile, at = self.codes(s), 3 * self.z.chunks + u
        return F32(LANES) * tile[at : at + 1] + tile[at + self.z.user_rows : at + self.z.user_rows + 1]


class Runs:
    def __init__(self, z, starts):
        self.z, self.starts = z, starts
        users = min(LANES, 8 * z.owners)
        self.columns = [jnp.broadcast_to(row, (8, LANES)).T[:users, 0:1] for row in starts]
        self.steps = []
        for u, row in enumerate(starts):
            before = pltpu.roll(row, 1, 1)
            first = starts[u - 1][:, LANES - 1 : LANES] if u else jnp.zeros((1, 1), F32)
            step = (row - jnp.where(iota((1, LANES), 1) == 0, first, before)).astype(I32)
            pair = [jnp.broadcast_to(part, (LANES, LANES)) for part in (step >> LOW, step & MASK)]
            self.steps.append(jnp.concatenate(pair, axis=0).astype(F32).astype(BF16))

    def start(self, position):
        total = jnp.zeros((position.shape[0], 2 * LANES), F32)
        for row, step in zip(self.starts, self.steps):
            total += lax.dot_general(ones_where(row <= position), step, NT, preferred_element_type=F32)
        return F32(LANES) * total[:, :LANES] + total[:, LANES:]

    def start_row(self, row):
        start = jnp.zeros((1, LANES), F32)
        for column in self.columns:
            start = jnp.maximum(start, jnp.max(jnp.where(column <= row, column, F32(0)), axis=0, keepdims=True))
        return start

    def until(self, row):
        after = jnp.full((1, LANES), FAR, F32)
        for column in self.columns:
            later = jnp.where(column > row, column, F32(FAR))
            after = jnp.minimum(after, jnp.min(later, axis=0, keepdims=True))
        return jnp.minimum(row + F32(self.z.window), after - F32(1))


def root(z, distance):
    return lax.rsqrt(jnp.minimum(distance, F32(z.window)) + F32(1))


def pack(z, pieces, base, marks_ref, codes_ref, rows_ref, from_ref):
    if not pieces.count:
        return
    spare = jnp.zeros((8 - z.chunks, LANES), F32)

    def mark(s, carry):
        local = pieces.place(s) - base
        near = local.astype(I32)
        codes_ref[s] = jnp.concatenate([near >> LOW, near & MASK], axis=0).astype(F32)
        own = (local >= 0) & (local < F32(z.slots))
        tail = (local >= F32(-z.window)) & (local < 0)
        marks_ref[0, s] = jnp.concatenate([jnp.where(own, F32(1), F32(0)), spare], axis=0)
        marks_ref[1, s] = jnp.concatenate([jnp.where(tail, F32(1), F32(0)), spare], axis=0)
        return carry

    loop(pieces.count, mark, 0)
    upper = ones_where(iota((LANES, LANES), 0) < iota((LANES, LANES), 1))
    full = jnp.ones((LANES, LANES), BF16)
    lines = pieces.count * 8
    at, by = iota((lines, lines), 0), iota((lines, lines), 1)
    earlier = ones_where(((at >> 3) == (by >> 3)) & (by < at))
    source = iota((lines, LANES), 0) >> 3
    offset = ((source & (pieces.per_group - 1)) * z.capacity).astype(F32)
    for kind in range(2):
        marked = marks_ref[kind].reshape(lines, LANES)
        mark = marked.astype(BF16)
        rank = dot(mark, upper) + dot(earlier, dot(mark, full).astype(BF16)) + offset
        marks_ref[kind] = jnp.where(marked > 0, rank, F32(-1)).reshape(pieces.count, 8, LANES)

    spots = iota((LANES, LANES), 0).astype(F32)
    code_line = iota((2 * z.chunks, LANES), 0) & (z.chunks - 1)
    for kind in range(2):
        for g in range(pieces.groups):

            def add(i, carry):
                values, places = carry
                s = g * pieces.per_group + i
                ranks = marks_ref[kind, s]
                codes = codes_ref[s]
                hot = jnp.concatenate([ones_where(spots == ranks[r : r + 1]) for r in range(z.chunks)], axis=1)
                wide = [jnp.where(code_line == r, codes, F32(0)).astype(BF16) for r in range(z.chunks)]
                values += dot(hot, pieces.rows(s))
                places += lax.dot_general(jnp.concatenate(wide, axis=1), hot, NT, preferred_element_type=F32)
                return values, places

            zero = (jnp.zeros((LANES, LANES), F32), jnp.zeros((2 * z.chunks, LANES), F32))
            values, places = loop(pieces.per_group, add, zero)
            line = kind * pieces.groups + g
            rows_ref[line * LANES : (line + 1) * LANES, :] = values.astype(BF16)
            high = jnp.sum(places[: z.chunks], axis=0, keepdims=True)
            low = jnp.sum(places[z.chunks :], axis=0, keepdims=True)
            from_ref[line : line + 1, :] = F32(LANES) * high + low


def tiles(values):
    return values.reshape(values.shape[0] // 16, 16, LANES)


def tile_of(row):
    return jnp.broadcast_to(row.astype(I32), (16, LANES)).astype(I16)


def held(position, bounds):
    one, nothing, count = BF16(1), BF16(0), position.shape[0]
    position = tiles(position)
    masks = [jnp.where(position - first[None] <= length[None], one, nothing) for first, length in bounds]
    return jnp.concatenate([mask.reshape(count, LANES) for mask in masks], axis=1)


def within(top, span, rows):
    if top.dtype == I16:
        one, nothing, count = BF16(1), BF16(0), top.shape[0]
        top, span = tiles(top), tiles(span)
        masks = [jnp.where(top - tile_of(row)[None] <= span, one, nothing) for row in rows]
        return jnp.concatenate([mask.reshape(count, LANES) for mask in masks], axis=1)
    return jnp.concatenate([ones_where((top - row >= 0) & (top - row <= span)) for row in rows], axis=1)


def wide_columns(*sets):
    count = sets[0].shape[0]
    columns = jnp.concatenate(sets, axis=0).T
    wide = lambda at: jnp.broadcast_to(columns[:, at : at + 1], (LANES, LANES))
    return [jnp.concatenate([wide(i * count + r) for r in range(count)], axis=0) for i in range(len(sets))]


def anchors(z, me):
    middle = F32(z.span * z.slots // 2)
    span_of = lambda owner: (owner.astype(I32) >> (z.span.bit_length() - 1)).astype(F32) * F32(z.span)
    own = (me - span_of(me)) * F32(z.slots) - middle
    tail = (me - span_of(me - F32(1))) * F32(z.slots) - middle
    return own, tail


def short(row):
    return row.astype(I32).astype(I16)


def early_kernel(z, form, before, *refs):
    count = sum(form)
    own_ref, pieces = refs[0], Pieces(z, form, refs[1 : 1 + count])
    refs = refs[1 + count :]
    if before:
        before_ref, sums_ref, rows_ref, from_ref, marks_ref, codes_ref = refs
    else:
        sums_ref, scale_ref, rows_ref, from_ref, high_ref, factor_ref, marks_ref, codes_ref = refs
    rate, me = own_ref[8:9, :], own_ref[9:10, :]
    runs = Runs(z, [own_ref[16 + u : 17 + u, :] for u in range(z.user_rows)])
    pack(z, pieces, me * F32(z.slots), marks_ref, codes_ref, rows_ref, from_ref)
    own_anchor, _ = anchors(z, me)
    inner = iota((BLOCK, LANES), 0)
    fall = jnp.exp(-rate * inner.astype(F32))
    bounds = []
    for g in range(pieces.groups if pieces.count else 0):
        begin = from_ref[g : g + 1, :]
        bounds.append((tile_of(begin), tile_of(runs.until(begin) - begin - F32(TOP))))
    for b in range(z.slots // BLOCK):
        part = slice(b * BLOCK, (b + 1) * BLOCK)
        if bounds:
            mask = held((inner + (b * BLOCK - TOP)).astype(I16), bounds)
            value = dot(mask, rows_ref[0 : len(bounds) * LANES, :])
        else:
            value = jnp.zeros((BLOCK, LANES), F32)
        sums_ref[part, :] = value + before_ref[part, :] if before else value
        if not before:
            first = F32(b * BLOCK)
            position = inner.astype(F32) + first
            start = runs.start(position)
            if b * BLOCK < z.window:
                scale_ref[part, :] = start
            else:
                scale_ref[part, :] = fall * jnp.exp(-rate * (first + own_anchor)) * root(z, position - start)
    if not before:
        position, span_start = wide_columns(own_ref[0 : z.chunks, :], own_ref[z.chunks : 2 * z.chunks, :])
        for shift in range(z.shifts):
            part = slice(shift * z.rows, (shift + 1) * z.rows)
            center = span_start + F32(z.span * z.slots // 2 - shift * z.span * z.slots)
            factor_ref[part, :] = jnp.exp(-rate * (position - center))
            top = position if shift == 0 else span_start - F32(1)
            high_ref[part, :] = short(top - F32(TOP)) if z.narrow else top


def late_kernel(z, earlier, form, late, *refs):
    own_ref, sums_ref, scale_ref, high_ref, factor_ref = refs[:5]
    tails = [refs[5 + 2 * i : 7 + 2 * i] for i in range(len(earlier))]
    refs = refs[5 + 2 * len(earlier) :]
    count = sum(form)
    table_out, feature_out, rows_ref, from_ref, marks_ref, codes_ref, table_ref, feature_ref, sems = refs[count:]
    pieces, last = Pieces(z, form, refs[:count]), Pieces(z, form[-late:], refs[count - sum(form[-late:]) : count])
    rate, me = own_ref[8:9, :], own_ref[9:10, :]
    base = me * F32(z.slots)
    starts = []
    for u in range(z.user_rows):
        add = lambda s, total: total + pieces.below(s, u)
        starts.append(loop(pieces.count, add, jnp.zeros((1, LANES), F32)))
    runs = Runs(z, starts)
    copies = []

    def send(ref, out, part):
        copies.append(pltpu.make_async_copy(ref.at[part, :], out.at[part, :], sems.at[len(copies)]))
        copies[-1].start()

    pack(z, last, base, marks_ref, codes_ref, rows_ref, from_ref)
    own_anchor, tail_anchor = anchors(z, me)
    inner = iota((LATE_BLOCK, LANES), 0)
    fall = jnp.exp(-rate * inner.astype(F32))
    first_start = jnp.max(runs.start_row(base), axis=1, keepdims=True) - base
    bounds = []
    listed = [(from_ref, 0, 2 * last.groups)] + [(ref, count, count) for (_, ref), count in zip(tails, earlier)]
    for ref, first, lines in listed:
        for g in range(first, first + lines):
            begin = ref[g : g + 1, :]
            bounds.append((tile_of(begin), tile_of(runs.until(begin + base) - (begin + base) - F32(TOP))))
    n = last.groups
    own_rows = rows_ref[0 : n * LANES, :]
    tail_rows = [rows_ref[n * LANES : 2 * n * LANES, :]]
    tail_rows += [ref[count * LANES : 2 * count * LANES, :] for (ref, _), count in zip(tails, earlier)]
    tail_rows = jnp.concatenate(tail_rows, axis=0)
    for b in range(z.slots // LATE_BLOCK):
        part = slice(b * LATE_BLOCK, (b + 1) * LATE_BLOCK)
        position = (inner + (b * LATE_BLOCK - TOP)).astype(I16)
        first = F32(b * LATE_BLOCK)
        value = sums_ref[part, :]
        if b * LATE_BLOCK >= z.window:
            value = (value + dot(held(position, bounds[:n]), own_rows)) * scale_ref[part, :]
        else:
            own_fall = jnp.exp(-rate * (first + own_anchor))
            if z.shifts == 1:
                value += dot(held(position, bounds), jnp.concatenate([own_rows, tail_rows], axis=0))
                value *= own_fall
            else:
                value = (value + dot(held(position, bounds[:n]), own_rows)) * own_fall
                value += dot(held(position, bounds[n:]), tail_rows) * jnp.exp(-rate * (first + tail_anchor))
            start = scale_ref[part, :]
            start = jnp.where(start > 0, start, first_start)
            value = value * fall * root(z, inner.astype(F32) + first - start)
        table_ref[part, :] = value.astype(BF16)

    send(table_ref, table_out, slice(0, z.slots))

    place = own_ref[0 : z.chunks, :]
    start = jnp.concatenate([runs.start_row(place[r : r + 1]) for r in range(z.chunks)], axis=0)
    distance = place - start
    reach = jnp.minimum(distance, F32(z.window))
    scale, reach = wide_columns(root(z, distance), reach - F32(TOP) if z.narrow else reach)
    position, span_start = (None, None) if z.narrow else wide_columns(place, own_ref[z.chunks : 2 * z.chunks, :])
    total = jnp.zeros((z.rows, LANES), F32)
    for shift in range(z.shifts):
        part = slice(shift * z.rows, (shift + 1) * z.rows)
        top = high_ref[part, :]
        if z.narrow:
            span = short(reach)
        else:
            low = position - reach
            span = top - (jnp.maximum(low, span_start) if shift == 0 else low)

        def add(s, value):
            rows = pieces.place(s)
            mask = within(top, span, [rows[r : r + 1] for r in range(z.chunks)])
            return value + dot(mask, pieces.rows(s))

        total += loop(pieces.count, add, jnp.zeros((z.rows, LANES), F32)) * factor_ref[part, :]
    feature_ref[...] = (total * scale).astype(BF16)
    send(feature_ref, feature_out, slice(0, z.rows))
    for copy in copies:
        copy.wait()


def swap(block, axis, distance):
    return lax.ppermute(block, axis, [(i, i ^ distance) for i in range(lax.axis_size(axis))])


def spread(blocks, axis):
    distance = lax.axis_size(axis) // 2
    while distance:
        blocks = blocks + [swap(block, axis, distance) for block in blocks]
        distance //= 2
    return blocks


def on_device(events, event_weight, route, bucket, segment, decay_rate):
    rows, width = events.shape
    key_count, shard_count = lax.axis_size("key"), lax.axis_size("shard")
    owners = key_count * shard_count
    slots = segment.shape[0]
    z = Sizes(owners, rows, slots)
    block_rows = rows + z.code_rows
    smem = pl.BlockSpec(memory_space=pltpu.SMEM)
    vmem = pl.BlockSpec(memory_space=pltpu.VMEM)
    shape = jax.ShapeDtypeStruct
    grant = pltpu.CompilerParams(vmem_limit_bytes=(16 if owners <= 8 else 48) * 1024 * 1024)
    me = (lax.axis_index("key") * shard_count + lax.axis_index("shard")).astype(I32).reshape(1)
    block, own = pl.pallas_call(
        functools.partial(send_kernel, z),
        out_shape=(
            shape((block_rows, width), BF16),
            shape((16 + z.user_rows + 7, LANES), F32),
        ),
        in_specs=[smem, smem] + [vmem] * 5,
        out_specs=(vmem, vmem),
        compiler_params=pltpu.CompilerParams(vmem_limit_bytes=56 * 1024 * 1024),
        name="weigh",
    )(
        me, decay_rate, events, event_weight.reshape(z.chunks, LANES), route.reshape(z.chunks, LANES),
        bucket.reshape(z.chunks, LANES), segment.reshape(slots // LANES, LANES),
    )

    def flat(blocks):
        return [part[None] if part.ndim == 2 else part for parts in blocks for part in parts]

    def sums(blocks, before=()):
        blocks, form, count = flat(blocks), tuple(map(len, blocks)), len(blocks)
        lines = max(8, 2 * count)
        whole = shape((slots, width), F32)
        kept = (shape((lines * LANES, LANES), BF16), shape((lines, LANES), F32))
        factors = shape((z.shifts * rows, width), F32)
        tops = shape((z.shifts * rows, width), I16 if z.narrow else F32)
        return pl.pallas_call(
            functools.partial(early_kernel, z, form, len(before)),
            out_shape=(whole,) + kept if before else (whole, whole) + kept + (tops, factors),
            in_specs=[vmem] * (1 + len(blocks) + len(before)),
            out_specs=(vmem,) * (3 if before else 6),
            scratch_shapes=[
                pltpu.VMEM((2, max(1, count), 8, LANES), F32),
                pltpu.VMEM((max(1, count), 2 * z.chunks, LANES), F32),
            ],
            compiler_params=grant,
            cost_estimate=pl.CostEstimate(flops=COST * count, bytes_accessed=0, transcendentals=0),
            name="more_sums" if before else "first_sums",
        )(own, *blocks, *before)

    if (key_count, shard_count) == (4, 2):
        tie = lax.optimization_barrier
        far = swap(block, "key", 2)
        side = swap(block, "shard", 1)
        near = swap(block, "key", 1)
        side_near = swap(side, "key", 1)
        total, scale, *tail, tops, factors = sums([(block,)])
        far, total = tie((far, total))
        last = swap(far, "key", 1)
        side_far = swap(far, "shard", 1)
        total, *tail2 = sums([(side,), (near,)], (total,))
        last, total = tie((last, total))
        side_last = swap(last, "shard", 1)
        second = [(far,), (last,), (side_far,)]
        late = [(side_near,), (side_last,)]
        total, *tail3 = sums(second, (total,))
        early, earlier, tails = [(block,), (side,), (near,)] + second, (1, 2, 3), tail + tail2 + tail3
    else:
        blocks = spread(spread([block], "key"), "shard")
        total, scale, _, _, tops, factors = sums([])
        early, earlier, tails = [], (), []
        late = [(jnp.concatenate(blocks, axis=0).reshape(owners, block_rows, width),)]
    late_lines = 2 * (len(late) if earlier else z.groups)
    late_count = len(late) if earlier else owners
    form = tuple(map(len, early + late))
    return pl.pallas_call(
        functools.partial(late_kernel, z, earlier, form, len(late)),
        out_shape=(shape((slots, width), BF16), shape((rows, width), BF16)),
        in_specs=[vmem] * (5 + len(tails) + sum(form)),
        out_specs=(pl.BlockSpec(memory_space=pl.ANY),) * 2,
        scratch_shapes=[
            pltpu.VMEM((late_lines * LANES, LANES), BF16),
            pltpu.VMEM((late_lines, LANES), F32),
            pltpu.VMEM((2, late_count, 8, LANES), F32),
            pltpu.VMEM((late_count, 2 * z.chunks, LANES), F32),
            pltpu.VMEM((slots, width), BF16),
            pltpu.VMEM((rows, width), BF16),
            pltpu.SemaphoreType.DMA((2,)),
        ],
        compiler_params=grant,
        name="table_and_rows",
    )(own, total, scale, tops, factors, *tails, *flat(early + late))


def solution(mesh):
    placed = (
        P(("groups", "key", "shard"), "lane"),
        P(("groups", "key", "shard")),
        P(("groups", "key", "shard"), None),
        P(("groups", "key", "shard")),
        P(("groups", "key", "shard")),
        P("lane"),
    )
    return jax.shard_map(
        on_device,
        mesh=mesh,
        in_specs=placed,
        out_specs=(P(("groups", "key", "shard"), "lane"), P(("groups", "key", "shard"), "lane")),
        check_vma=False,
    )
```
